32 devices in a mesh: tp: 4 (over y, x), ep: 8 (over z, core).
Axes of the slice: x: 2, y: 2, z: 4, core: 2. Of those that a mesh axis runs over, the one named last changes fastest.
Arguments:
- tokens: bfloat16 [1024, 5120], P('ep', 'tp'), may hold values from -6 to 6
- cotangent: bfloat16 [1024, 5120], P('ep', 'tp'), may hold values from -6 to 6
- expert_ids: int32 [1024, 3], P('ep'), may hold values from 0 to 7, all different within a row; in each aligned block of 128 rows (0 to 127, 128 to 255, ...) at most 60 rows name the same one
- gate_weights: float32 [1024, 4], P('ep'), may hold values from 0.1 to 1
- shadow_mask: int32 [1024], P('ep'), may hold values 0 or 1
- w_gate: bfloat16 [8, 5120, 1536], P('ep', None, 'tp'), may hold values from -0.078125 to 0.078125
- w_up: bfloat16 [8, 5120, 1536], P('ep', None, 'tp'), may hold values from -0.078125 to 0.078125
- w_down: bfloat16 [8, 1536, 5120], P('ep', 'tp'), may hold values from -0.15625 to 0.15625
- s_gate: bfloat16 [5120, 1536], P('ep', 'tp'), may hold values from -0.078125 to 0.078125
- s_up: bfloat16 [5120, 1536], P('ep', 'tp'), may hold values from -0.078125 to 0.078125
- s_down: bfloat16 [1536, 5120], P('tp', 'ep'), may hold values from -0.15625 to 0.15625
Outputs:
- mixed: bfloat16 [1024, 5120], P('ep', 'tp')
- grad_gate: bfloat16 [8, 5120, 1536], P('ep', None, 'tp')
- grad_up: bfloat16 [8, 5120, 1536], P('ep', None, 'tp')
- grad_down: bfloat16 [8, 1536, 5120], P('ep', 'tp')
- grad_s_gate: bfloat16 [5120, 1536], P('ep', 'tp')
- grad_s_up: bfloat16 [5120, 1536], P('ep', 'tp')
- grad_s_down: bfloat16 [1536, 5120], P('tp', 'ep')
The draws below stay inside these ranges and needn't reach their ends.
Inputs may be any that keep to these rules, and one draw needn't show every extreme that they name: `expert_ids`: each row names 3 different experts. Among the 128 rows of one device no expert is named more than 60 times, and in every draw some expert is named exactly 60 times by the rows of some device.
All inputs are finite; a program needn't handle non-finite values. No bound on the sum of `shadow_mask` on one device may be relied on, other than what follows from the above.
Results may differ from the reference program's by a relative error of at most 0.028.
Values may be sent and summed in bfloat16 or wider, within the bound.
No kernel may reach another device: no remote copies, remote signals or barrier semaphores. Data moves between devices by JAX's collectives and lax.ppermute only.
A program may use at most 192 MiB of HBM per device.

```python
import math
import jax
import jax.numpy as jnp
import numpy as np
from jax import lax

D = 5120
FF = 1536
TOK_DEV = 128
TOP_OLD = 3
EXPERTS = 8
CAP = 60
TOKENS = 1024
N_TP = 4
N_EP = 8


def set_ends(result, rng, low, largest):
    longest = result.shape.index(max(result.shape))
    spots = []
    for shift in (0, 1):
        where = [jax.random.randint(jax.random.fold_in(rng, axis), (), 0, length) for axis, length in enumerate(result.shape)]
        where[longest] = (where[longest] + shift) % result.shape[longest]
        spots.append(tuple(where))
    return result.at[spots[0]].set(low).at[spots[1]].set(largest)


def strengthened(entries, key, source, target, blocks, factor):
    owner, partner = [(jnp.arange(entries.shape[dim]) // (entries.shape[dim] // blocks)).reshape([-1 if axis == dim else 1 for axis in range(entries.ndim)]) for dim in (source, target)]
    chosen = jax.random.permutation(key, blocks)[partner]
    strong = (owner == chosen) | (owner == (partner + blocks // 2) % blocks)
    return jnp.where(strong, factor * entries, entries)


def levels(rng, dims, shards, low, largest):
    def one(axis_at, shards_of):
        draws = jax.random.uniform(jax.random.fold_in(jax.random.fold_in(rng, 6), axis_at), (shards_of,), jnp.float32, low / len(shards), largest / len(shards))
        return jnp.repeat(jnp.exp(draws), dims[axis_at] // shards_of).reshape((-1,) + (1,) * (len(dims) - axis_at - 1))

    gain = one(*shards[0])
    for cut in shards[1:]:
        gain = gain * one(*cut)
    return gain


def assign_block(own_key, own, number, rows, amount, top, bound, lean):
    order = jax.random.permutation(own_key, amount)
    heavy_load, ordinary = load_shares(amount, rows * top, bound, lean, True), load_shares(amount, rows * top, bound, lean, False)
    places = jnp.arange(amount)

    def named(tallies, rotation):
        used = int((tallies > 0).sum())
        fixed = max(1, used // 4)
        moved = fixed + (places - fixed + rotation * (used - fixed)) % max(1, amount - fixed)
        return jnp.zeros((amount,), jnp.int32).at[order[jnp.where(places < fixed, places, moved)]].set(jnp.asarray(tallies, jnp.int32))

    tallies = jnp.where(number % 4 == 0, named(heavy_load, number // 4), named(ordinary, number - number // 4 - 1))
    mixed = jax.random.permutation(jax.random.fold_in(own, 3), amount)
    source_of, receiver = mixed[0:amount // 2 * 2:2], mixed[1:amount // 2 * 2:2]
    slack = jnp.minimum(tallies[source_of] - 1, bound - tallies[receiver]) // 2
    slack = jnp.where((source_of == order[0]) | (receiver == order[0]) | (tallies[receiver] == 0), 0, jnp.maximum(slack, 0))
    moved = jax.random.randint(jax.random.fold_in(own, 4), (amount // 2,), 0, 1 << 20) % (slack + 1)
    tallies = tallies.at[source_of].add(-moved).at[receiver].add(moved)
    labels = jnp.searchsorted(jnp.cumsum(tallies), jnp.arange(rows * top), side="right").astype(jnp.int32)
    table = labels.reshape(top, rows).T
    table = table[jax.random.permutation(jax.random.fold_in(own, 1), rows)]
    rotation = jax.random.randint(jax.random.fold_in(own, 2), (rows, 1), 0, top)
    return jnp.take_along_axis(table, (jnp.arange(top)[None, :] + rotation) % top, axis=1)


def load_shares(number_of, total, most, skew, full):
    loads = [(1 << 20) // math.isqrt(rank ** skew) + 1 for rank in range(1, number_of + 1)]
    largest = most if full else min(most, max(-(-total // number_of), total * loads[0] // sum(loads)))
    least = 1 if total - largest >= number_of - 1 else 0
    counts, rest = [largest] + [least] * (number_of - 1), total - largest - least * (number_of - 1)
    while rest > 0:
        movable = [i for i in range(1, number_of) if counts[i] < largest] or [i for i in range(1, number_of) if counts[i] < most]
        mass, left = sum([loads[i] for i in movable]), rest
        for i in movable:
            extra = min(most - counts[i], max(1, left * loads[i] // mass), rest)
            counts[i] = counts[i] + extra
            rest = rest - extra
    return np.array(counts)


def noise(stream_key, dims, scale, most, pieces=(), held_as=jnp.bfloat16):
    entries = jax.random.normal(stream_key, dims, jnp.float32) * scale
    if len(pieces) > 0:
        entries = levels(stream_key, dims, pieces, -0.22, 0.18) * entries
    return jnp.clip(entries, min=-most, max=most).astype(held_as)


def bell_draw_with(stream_key, extent, spread, reach, shards, heavy, kind=jnp.bfloat16):
    entries = spread * jax.random.normal(stream_key, extent, jnp.float32)
    if shards:
        entries = entries * levels(stream_key, extent, shards, -0.22, 0.18)
    return jnp.clip(strengthened(entries, jax.random.fold_in(stream_key, 3), *heavy), -reach, reach).astype(kind)


def setup_inputs(seed: int = 0) -> dict:
    splits = jax.random.split(jax.random.key(seed), 12)
    tokens = bell_draw_with(splits[0], (TOKENS, D), 1.0, 6.0, ((0, 8), (1, 4)), (0, 1, 8, 2.0))
    cotangent = bell_draw_with(splits[1], (TOKENS, D), 1.0, 6.0, ((0, 8), (1, 4)), (0, 1, 8, 2.0))
    expert_ids_keys = jax.random.split(jax.random.fold_in(splits[2], 1), TOKENS // TOK_DEV)
    expert_ids_turns = jax.random.permutation(jax.random.fold_in(splits[2], 3), TOKENS // TOK_DEV)
    expert_ids = jax.vmap(lambda own, number: assign_block(jax.random.fold_in(splits[2], 2), own, number, TOK_DEV, EXPERTS, TOP_OLD, CAP, 2))(expert_ids_keys, expert_ids_turns).reshape((TOKENS, TOP_OLD))
    gate_weights = jnp.clip(jnp.exp(math.log(1.0) - 2.3025851 * jax.random.uniform(splits[3], (TOKENS, TOP_OLD + 1), jnp.float32) ** levels(splits[3], (TOKENS, TOP_OLD + 1), ((0, 8),), -0.2, 0.2)), 0.1, 1.0)
    shadow_mask = set_ends((jax.random.randint(splits[4], (TOKENS,), 0, 20) < 9).astype(jnp.int32), jax.random.fold_in(splits[4], 1), 0, 1)
    w_gate = noise(splits[5], (EXPERTS, D, FF), D ** -0.5, 0.078125, ((0, 8), (2, 4)))
    w_up = noise(splits[6], (EXPERTS, D, FF), D ** -0.5, 0.078125, ((0, 8), (2, 4)))
    w_down = noise(splits[7], (EXPERTS, FF, D), FF ** -0.5, 0.15625, ((0, 8), (1, 4)))
    s_gate = noise(splits[8], (D, FF), D ** -0.5, 0.078125, ((0, 8), (1, 4)))
    s_up = noise(splits[9], (D, FF), D ** -0.5, 0.078125, ((0, 8), (1, 4)))
    s_down = noise(splits[10], (FF, D), FF ** -0.5, 0.15625, ((0, 4), (1, 8)))
    return dict(tokens=tokens, cotangent=cotangent, expert_ids=expert_ids, gate_weights=gate_weights, shadow_mask=shadow_mask, w_gate=w_gate, w_up=w_up, w_down=w_down, s_gate=s_gate, s_up=s_up, s_down=s_down)


def contract_rows(left, right):
    return lax.dot_general(left, right, (((0,), (0,)), ((), ())), preferred_element_type=jnp.float32)


def swiglu_pass(rows_x, rows_dout, weight_gate, weight_up, weight_down):
    pre_gate = jnp.dot(rows_x, weight_gate, preferred_element_type=jnp.float32)
    pre_up = jnp.dot(rows_x, weight_up, preferred_element_type=jnp.float32)
    sigmoid_gate = jax.nn.sigmoid(pre_gate)
    activated = pre_gate * sigmoid_gate
    hidden = (activated * pre_up).astype(jnp.bfloat16)
    row_count = rows_x.shape[0]
    per_block = weight_down.shape[0] // N_TP
    quarters = jnp.einsum('rqh,qhd->qrd', hidden.astype(jnp.float32).reshape(row_count, N_TP, per_block),
                          weight_down.astype(jnp.float32).reshape(N_TP, per_block, weight_down.shape[1]),
                          precision=lax.Precision.HIGHEST)
    rounded = lax.optimization_barrier(quarters.astype(jnp.bfloat16))
    output = jnp.sum(rounded.astype(jnp.float32), axis=0)
    hidden_grad = lax.dot_general(rows_dout, weight_down, (((1,), (1,)), ((), ())), preferred_element_type=jnp.float32)
    grad_pre_gate = (hidden_grad * pre_up * sigmoid_gate * (1.0 + pre_gate * (1.0 - sigmoid_gate))).astype(jnp.bfloat16)
    grad_pre_up = (hidden_grad * activated).astype(jnp.bfloat16)
    return (output, contract_rows(rows_x, grad_pre_gate), contract_rows(rows_x, grad_pre_up),
            contract_rows(hidden, rows_dout))


def reference(tokens, cotangent, expert_ids, gate_weights, shadow_mask, w_gate, w_up, w_down, s_gate, s_up, s_down):
    picks = expert_ids.reshape(N_EP, TOK_DEV * TOP_OLD)
    onehot = (picks[:, :, None] == jnp.arange(EXPERTS, dtype=jnp.int32)[None, None, :]).astype(jnp.int32)
    slot_rank = jnp.sum((jnp.cumsum(onehot, axis=1) - onehot) * onehot, axis=2)
    position = (jnp.arange(N_EP, dtype=jnp.int32)[:, None] * CAP + slot_rank).reshape(-1).astype(jnp.int32)
    token_of = jnp.repeat(jnp.arange(TOKENS, dtype=jnp.int32), TOP_OLD)
    picks_flat = expert_ids.reshape(-1).astype(jnp.int32)
    row_token = jnp.zeros((EXPERTS, N_EP * CAP), jnp.int32).at[picks_flat, position].set(token_of)
    row_weight = jnp.zeros((EXPERTS, N_EP * CAP), jnp.float32).at[picks_flat, position].set(
        gate_weights[:, :TOP_OLD].reshape(-1))
    row_filled = jnp.zeros((EXPERTS, N_EP * CAP), jnp.float32).at[picks_flat, position].set(1.0)

    def one_expert(item):
        weight_gate, weight_up, weight_down, token_index, weight_row, filled = item
        rows_x = tokens[token_index] * filled[:, None].astype(jnp.bfloat16)
        rows_dout = (weight_row[:, None] * cotangent[token_index].astype(jnp.float32)).astype(jnp.bfloat16)
        output, grad_g, grad_u, grad_d = swiglu_pass(rows_x, rows_dout, weight_gate, weight_up, weight_down)
        return output, grad_g.astype(jnp.bfloat16), grad_u.astype(jnp.bfloat16), grad_d.astype(jnp.bfloat16)

    outputs, grad_gate, grad_up, grad_down = lax.map(
        one_expert, (w_gate, w_up, w_down, row_token, row_weight, row_filled))
    mixed_old = jnp.zeros((TOKENS, D), jnp.float32).at[row_token.reshape(-1)].add(
        (row_weight[:, :, None] * outputs).reshape(-1, D))

    shadow_weight = (gate_weights[:, TOP_OLD] * shadow_mask.astype(jnp.float32)).reshape(N_EP, TOK_DEV)
    blocks_x = tokens.reshape(N_EP, TOK_DEV, D)
    blocks_dy = cotangent.reshape(N_EP, TOK_DEV, D)

    def shadow_block(carry, item):
        block_x, block_dy, block_weight = item
        block_dout = (block_weight[:, None] * block_dy.astype(jnp.float32)).astype(jnp.bfloat16)
        output, grad_g, grad_u, grad_d = swiglu_pass(block_x, block_dout, s_gate, s_up, s_down)
        sums = tuple(total + lax.optimization_barrier(piece.astype(jnp.bfloat16)).astype(jnp.float32)
                     for total, piece in zip(carry, (grad_g, grad_u, grad_d)))
        return sums, block_weight[:, None] * output

    start = (jnp.zeros((D, FF), jnp.float32), jnp.zeros((D, FF), jnp.float32), jnp.zeros((FF, D), jnp.float32))
    shadow_sums, shadow_out = lax.scan(shadow_block, start, (blocks_x, blocks_dy, shadow_weight))
    mixed = (mixed_old + shadow_out.reshape(TOKENS, D)).astype(jnp.bfloat16)
    return (mixed, grad_gate, grad_up, grad_down, shadow_sums[0].astype(jnp.bfloat16),
            shadow_sums[1].astype(jnp.bfloat16), shadow_sums[2].astype(jnp.bfloat16))
```

```python
import jax
import jax.numpy as jnp
from jax import lax
from jax.sharding import PartitionSpec as P


def contract_rows(left, right):
    return lax.dot_general(
        left, right, (((0,), (0,)), ((), ())), preferred_element_type=jnp.float32
    )


def split_parts(values):
    upper_part = values.astype(jnp.bfloat16)
    lower_part = (values - upper_part.astype(jnp.float32)).astype(jnp.bfloat16)
    return (upper_part, lower_part)


def weigh_rows(weight_table, rows):
    weight_upper, weight_lower = split_parts(weight_table)
    return jnp.dot(weight_upper, rows, preferred_element_type=jnp.float32) + jnp.dot(
        weight_lower, rows, preferred_element_type=jnp.float32
    )


def expert_pass(rows_x, rows_dout, weight_gate, weight_up, weight_down):
    pre_gate = jnp.dot(rows_x, weight_gate, preferred_element_type=jnp.float32)
    pre_up = jnp.dot(rows_x, weight_up, preferred_element_type=jnp.float32)
    sigmoid_gate = jax.nn.sigmoid(pre_gate)
    activated = pre_gate * sigmoid_gate
    hidden = (activated * pre_up).astype(jnp.bfloat16)
    partial_out = jnp.dot(hidden, weight_down, preferred_element_type=jnp.float32).astype(
        jnp.bfloat16
    )
    hidden_grad = lax.dot_general(
        rows_dout, weight_down, (((1,), (1,)), ((), ())), preferred_element_type=jnp.float32
    )
    grad_pre_gate = (
        hidden_grad * pre_up * sigmoid_gate * (1.0 + pre_gate * (1.0 - sigmoid_gate))
    ).astype(jnp.bfloat16)
    grad_pre_up = (hidden_grad * activated).astype(jnp.bfloat16)
    return (partial_out, hidden, grad_pre_gate, grad_pre_up)


def shards(
    tokens,
    cotangent,
    expert_ids,
    gate_weights,
    shadow_mask,
    w_gate,
    w_up,
    w_down,
    s_gate,
    s_up,
    s_down,
):
    ep_count = lax.axis_size("ep")
    tok_count, top_count = expert_ids.shape
    quarter_width = tokens.shape[1]
    width = quarter_width * lax.axis_size("tp")
    expert_count = w_gate.shape[0] * ep_count
    capacity = (5 * tok_count * top_count + 4 * expert_count - 1) // (4 * expert_count)
    slot_count = expert_count * capacity
    picks_flat = expert_ids.reshape(-1)
    onehot = (picks_flat[:, None] == jnp.arange(expert_count, dtype=jnp.int32)[None, :]).astype(
        jnp.int32
    )
    slot_rank = jnp.sum((jnp.cumsum(onehot, axis=0) - onehot) * onehot, axis=1)
    slot_index = (picks_flat * capacity + slot_rank).reshape(tok_count, top_count)
    matches = jnp.arange(slot_count, dtype=jnp.int32)[:, None, None] == slot_index[None, :, :]
    dispatch = jnp.any(matches, axis=2).astype(jnp.bfloat16)
    weighting = jnp.sum(jnp.where(matches, gate_weights[None, :, :top_count], 0.0), axis=2)
    slot_gate = jnp.sum(weighting, axis=1)
    shadow_weight = gate_weights[:, top_count] * shadow_mask.astype(jnp.float32)
    x_full, dy_full = (
        lax.all_gather(tokens, "tp", axis=1, tiled=True),
        lax.all_gather(cotangent, "tp", axis=1, tiled=True),
    )
    rows_x = jnp.dot(dispatch, tokens, preferred_element_type=jnp.float32).astype(jnp.bfloat16)
    rows_dy = jnp.dot(dispatch, cotangent, preferred_element_type=jnp.float32)
    rows_dout = (slot_gate[:, None] * rows_dy).astype(jnp.bfloat16)
    recv_x, recv_dout = (
        lax.all_to_all(
            rows_x.reshape(ep_count, -1, quarter_width),
            "ep",
            split_axis=0,
            concat_axis=0,
            tiled=True,
        ),
        lax.all_to_all(
            rows_dout.reshape(ep_count, -1, quarter_width),
            "ep",
            split_axis=0,
            concat_axis=0,
            tiled=True,
        ),
    )
    expert_x, expert_dout = (
        lax.all_gather(recv_x.reshape(-1, quarter_width), "tp", axis=1, tiled=True),
        lax.all_gather(recv_dout.reshape(-1, quarter_width), "tp", axis=1, tiled=True),
    )
    partial_out, hidden, grad_pre_gate, grad_pre_up = expert_pass(
        expert_x, expert_dout, w_gate[0], w_up[0], w_down[0]
    )
    grad_gate = contract_rows(expert_x, grad_pre_gate).astype(jnp.bfloat16)[None]
    grad_up = contract_rows(expert_x, grad_pre_up).astype(jnp.bfloat16)[None]
    grad_down = contract_rows(hidden, expert_dout).astype(jnp.bfloat16)[None]
    full_gate, full_up, full_down = (
        lax.all_gather(s_gate, "ep", axis=0, tiled=True),
        lax.all_gather(s_up, "ep", axis=0, tiled=True),
        lax.all_gather(s_down, "ep", axis=1, tiled=True),
    )
    shadow_dout = (shadow_weight[:, None] * dy_full.astype(jnp.float32)).astype(jnp.bfloat16)
    shadow_out, shadow_hidden, shadow_gate_pre, shadow_up_pre = expert_pass(
        x_full, shadow_dout, full_gate, full_up, full_down
    )
    shadow_sums = lax.psum_scatter(
        jnp.concatenate(
            [
                contract_rows(x_full, shadow_gate_pre),
                contract_rows(x_full, shadow_up_pre),
                contract_rows(shadow_dout, shadow_hidden),
            ],
            axis=1,
        ).astype(jnp.bfloat16),
        "ep",
        scatter_dimension=0,
        tiled=True,
    ).astype(jnp.float32)
    hidden_part = s_gate.shape[1]
    grad_s_gate = shadow_sums[:, :hidden_part].astype(jnp.bfloat16)
    grad_s_up = shadow_sums[:, hidden_part : 2 * hidden_part].astype(jnp.bfloat16)
    grad_s_down = shadow_sums[:, 2 * hidden_part :].T.astype(jnp.bfloat16)
    back_rows = lax.all_to_all(
        partial_out.reshape(ep_count, -1, width), "ep", split_axis=0, concat_axis=0, tiled=True
    ).reshape(-1, width)
    term = weigh_rows(weighting.T, back_rows)
    term = term + shadow_weight[:, None] * shadow_out.astype(jnp.float32)
    mixed = lax.psum_scatter(term.astype(jnp.bfloat16), "tp", scatter_dimension=1, tiled=True)
    return (mixed, grad_gate, grad_up, grad_down, grad_s_gate, grad_s_up, grad_s_down)


def swap_pairs(count, bit):
    return [(i, i ^ bit) for i in range(count)]


def ring_pairs(count, shift):
    return [(i, (i + shift) % count) for i in range(count)]


def pick_one(choices, index):
    chosen = choices[-1]
    for i in range(len(choices) - 2, -1, -1):
        chosen = jnp.where(index == i, choices[i], chosen)
    return chosen


def exchange_blocks(blocks, axis):
    count = lax.axis_size(axis)
    me = lax.axis_index(axis)
    own = lax.dynamic_index_in_dim(blocks, me, 0, keepdims=True)
    result = lax.dynamic_update_slice_in_dim(jnp.zeros_like(blocks), own, me, 0)
    for shift in range(1, count):
        piece = lax.dynamic_index_in_dim(blocks, (me + shift) % count, 0, keepdims=True)
        piece = lax.ppermute(piece, axis, ring_pairs(count, shift))
        result = lax.dynamic_update_slice_in_dim(result, piece, (me - shift) % count, 0)
    return result


def gather_tokens(own):
    tp_count, ep_count = lax.axis_size("tp"), lax.axis_size("ep")
    along, across = swap_pairs(tp_count, 1), swap_pairs(tp_count, 2)
    column = lax.axis_index("tp")
    half = own.shape[0] // 2
    own_blocks, other_blocks = [], []
    piece = own
    for step in range(ep_count // 2):
        if step:
            piece = lax.ppermute(piece, "ep", ring_pairs(ep_count, 2))
        from_x = lax.ppermute(piece, "tp", along)
        from_y = lax.ppermute(piece, "tp", across)
        diag_top = lax.ppermute(from_x[:half], "tp", across)
        diag_low = lax.ppermute(from_y[half:], "tp", along)
        diag = jnp.concatenate([diag_top, diag_low], axis=0)
        parts = (piece, from_x, from_y, diag)
        block = jnp.concatenate([pick_one(parts, column ^ q) for q in range(tp_count)], axis=1)
        own_blocks.append(block)
        other_blocks.append(lax.ppermute(block, "ep", swap_pairs(ep_count, 1)))
    return jnp.concatenate(own_blocks + other_blocks, axis=0)


def return_tokens(weighted, down_parts):
    tp_count, ep_count = lax.axis_size("tp"), lax.axis_size("ep")
    along, across = swap_pairs(tp_count, 1), swap_pairs(tp_count, 2)
    steps = ep_count // 2
    rows = weighted.shape[0] // ep_count
    half = rows // 2
    carried = None
    for step in list(range(1, steps)) + [0]:
        mine = weighted[step * rows : (step + 1) * rows]
        theirs = weighted[(steps + step) * rows : (steps + step + 1) * rows]
        sent = jnp.concatenate(
            [jnp.dot(theirs, part, preferred_element_type=jnp.float32).astype(jnp.bfloat16) for part in down_parts],
            axis=1,
        )
        got = lax.ppermute(sent, "ep", swap_pairs(ep_count, 1)).astype(jnp.float32)
        width = down_parts[0].shape[1]
        own, to_x, to_y, to_diag = [
            jnp.dot(mine, part, preferred_element_type=jnp.float32) + got[:, i * width : (i + 1) * width]
            for i, part in enumerate(down_parts)
        ]
        to_diag = to_diag.astype(jnp.bfloat16)
        top = lax.ppermute(to_diag[:half], "tp", along).astype(jnp.float32)
        low = lax.ppermute(to_diag[half:], "tp", across).astype(jnp.float32)
        to_y = jnp.concatenate([to_y[:half] + top, to_y[half:]], axis=0).astype(jnp.bfloat16)
        to_x = jnp.concatenate([to_x[:half], to_x[half:] + low], axis=0).astype(jnp.bfloat16)
        total = (
            own
            + lax.ppermute(to_x, "tp", along).astype(jnp.float32)
            + lax.ppermute(to_y, "tp", across).astype(jnp.float32)
        )
        if carried is not None:
            total = total + carried.astype(jnp.float32)
        if step:
            carried = lax.ppermute(total.astype(jnp.bfloat16), "ep", ring_pairs(ep_count, 2))
    return total.astype(jnp.bfloat16)


def contract_last(left, right):
    return lax.dot_general(
        left, right, (((1,), (1,)), ((), ())), preferred_element_type=jnp.float32
    )


def activation(pre_gate, pre_up, weight):
    sigmoid_gate = jax.nn.sigmoid(pre_gate)
    activated = pre_gate * sigmoid_gate
    hidden = (weight * activated * pre_up).astype(jnp.bfloat16)
    slope = weight * pre_up * sigmoid_gate * (1.0 + pre_gate * (1.0 - sigmoid_gate))
    return hidden, slope, weight * activated


def dense_shards(
    tokens,
    cotangent,
    expert_ids,
    gate_weights,
    shadow_mask,
    w_gate,
    w_up,
    w_down,
    s_gate,
    s_up,
    s_down,
):
    ep_count, tp_count = lax.axis_size("ep"), lax.axis_size("tp")
    ep_index, tp_index = lax.axis_index("ep"), lax.axis_index("tp")
    tok_count, top_count = expert_ids.shape
    quarter = tokens.shape[1]
    width = quarter * tp_count
    hidden_part = w_gate.shape[2]
    shadow_part = hidden_part // ep_count
    block_width = s_gate.shape[0]

    picked = expert_ids[:, :, None] == jnp.arange(ep_count, dtype=jnp.int32)[None, None, :]
    table = jnp.sum(jnp.where(picked, gate_weights[:, :top_count, None], 0.0), axis=1)
    shadow_weight = gate_weights[:, top_count] * shadow_mask.astype(jnp.float32)
    table = jnp.concatenate([table, shadow_weight[:, None]], axis=1).T
    tables = lax.all_gather(table, "ep", axis=0)
    steps = ep_count // 2
    order = [(ep_index - 2 * s) % ep_count for s in range(steps)]
    order = jnp.stack(order + [index ^ 1 for index in order])
    place = (order[:, None] == jnp.arange(ep_count)[None, :])[:, :, None]
    expert_column = lax.dynamic_index_in_dim(tables, ep_index, 1, keepdims=False)
    w_expert = jnp.sum(jnp.where(place, expert_column[None], 0.0), axis=1).reshape(-1, 1)
    w_shadow = jnp.sum(jnp.where(place, tables[:, ep_count][None], 0.0), axis=1).reshape(-1, 1)

    shadow_blocks = jnp.concatenate(
        [
            s_gate.T.reshape(ep_count, shadow_part, block_width),
            s_up.T.reshape(ep_count, shadow_part, block_width),
            s_down.reshape(ep_count, shadow_part, block_width),
        ],
        axis=1,
    )
    shadow_rows = exchange_blocks(shadow_blocks, "ep").transpose(1, 0, 2).reshape(-1, width)
    shadow_in, shadow_down = shadow_rows[: 2 * shadow_part], shadow_rows[2 * shadow_part :]

    down_full = jnp.concatenate([w_down[0], shadow_down], axis=0)
    down_quarters = [down_full[:, q * quarter : (q + 1) * quarter] for q in range(tp_count)]
    down_parts = [pick_one(down_quarters, tp_index ^ r) for r in range(tp_count)]

    x_all = gather_tokens(tokens)
    dy_all = gather_tokens(cotangent)

    pre_gate = jnp.dot(x_all, w_gate[0], preferred_element_type=jnp.float32)
    pre_up = jnp.dot(x_all, w_up[0], preferred_element_type=jnp.float32)
    pre_shadow = contract_last(x_all, shadow_in)
    hidden, slope, activated = activation(pre_gate, pre_up, w_expert)
    hidden_s, slope_s, activated_s = activation(
        pre_shadow[:, :shadow_part], pre_shadow[:, shadow_part:], w_shadow
    )
    mixed = return_tokens(jnp.concatenate([hidden, hidden_s], axis=1), down_parts)

    grad_hidden_s = contract_last(dy_all, shadow_down)
    grad_pre_s = jnp.concatenate(
        [grad_hidden_s * slope_s, grad_hidden_s * activated_s], axis=1
    ).astype(jnp.bfloat16)
    grad_in_s = contract_rows(grad_pre_s, x_all).astype(jnp.bfloat16)
    grad_down_s = contract_rows(hidden_s, dy_all).astype(jnp.bfloat16)
    grad_s = jnp.concatenate([grad_in_s, grad_down_s], axis=0)
    grad_s = grad_s.reshape(3 * shadow_part, ep_count, block_width).transpose(1, 0, 2)
    grad_s = exchange_blocks(grad_s, "ep")
    grad_s_gate = grad_s[:, :shadow_part].reshape(hidden_part, block_width).T
    grad_s_up = grad_s[:, shadow_part : 2 * shadow_part].reshape(hidden_part, block_width).T
    grad_s_down = grad_s[:, 2 * shadow_part :].reshape(hidden_part, block_width)

    grad_hidden = contract_last(dy_all, w_down[0])
    grad_pre_gate = (grad_hidden * slope).astype(jnp.bfloat16)
    grad_pre_up = (grad_hidden * activated).astype(jnp.bfloat16)
    grad_gate = contract_rows(x_all, grad_pre_gate).astype(jnp.bfloat16)[None]
    grad_up = contract_rows(x_all, grad_pre_up).astype(jnp.bfloat16)[None]
    grad_down = contract_rows(hidden, dy_all).astype(jnp.bfloat16)[None]
    return (mixed, grad_gate, grad_up, grad_down, grad_s_gate, grad_s_up, grad_s_down)


def solution(mesh):
    tp_count, ep_count = mesh.shape["tp"], mesh.shape["ep"]
    dense = tp_count == 4 and ep_count % 2 == 0 and ep_count <= 8
    return jax.shard_map(
        dense_shards if dense else shards,
        mesh=mesh,
        in_specs=(
            P("ep", "tp"),
            P("ep", "tp"),
            P("ep", None),
            P("ep", None),
            P("ep"),
            P("ep", None, "tp"),
            P("ep", None, "tp"),
            P("ep", "tp", None),
            P("ep", "tp"),
            P("ep", "tp"),
            P("tp", "ep"),
        ),
        out_specs=(
            P("ep", "tp"),
            P("ep", None, "tp"),
            P("ep", None, "tp"),
            P("ep", "tp", None),
            P("ep", "tp"),
            P("ep", "tp"),
            P("tp", "ep"),
        ),
        check_vma=False,
    )
```

```python
import jax
import jax.numpy as jnp
from jax import lax
from jax.experimental import pallas as pl
from jax.sharding import PartitionSpec as P


def contract_rows(left, right):
    return lax.dot_general(
        left, right, (((0,), (0,)), ((), ())), preferred_element_type=jnp.float32
    )


def split_parts(values):
    upper_part = values.astype(jnp.bfloat16)
    lower_part = (values - upper_part.astype(jnp.float32)).astype(jnp.bfloat16)
    return (upper_part, lower_part)


def weigh_rows(weight_table, rows):
    weight_upper, weight_lower = split_parts(weight_table)
    return jnp.dot(weight_upper, rows, preferred_element_type=jnp.float32) + jnp.dot(
        weight_lower, rows, preferred_element_type=jnp.float32
    )


def expert_pass(rows_x, rows_dout, weight_gate, weight_up, weight_down):
    pre_gate = jnp.dot(rows_x, weight_gate, preferred_element_type=jnp.float32)
    pre_up = jnp.dot(rows_x, weight_up, preferred_element_type=jnp.float32)
    sigmoid_gate = jax.nn.sigmoid(pre_gate)
    activated = pre_gate * sigmoid_gate
    hidden = (activated * pre_up).astype(jnp.bfloat16)
    partial_out = jnp.dot(hidden, weight_down, preferred_element_type=jnp.float32).astype(
        jnp.bfloat16
    )
    hidden_grad = lax.dot_general(
        rows_dout, weight_down, (((1,), (1,)), ((), ())), preferred_element_type=jnp.float32
    )
    grad_pre_gate = (
        hidden_grad * pre_up * sigmoid_gate * (1.0 + pre_gate * (1.0 - sigmoid_gate))
    ).astype(jnp.bfloat16)
    grad_pre_up = (hidden_grad * activated).astype(jnp.bfloat16)
    return (partial_out, hidden, grad_pre_gate, grad_pre_up)


def shards(
    tokens,
    cotangent,
    expert_ids,
    gate_weights,
    shadow_mask,
    w_gate,
    w_up,
    w_down,
    s_gate,
    s_up,
    s_down,
):
    ep_count = lax.axis_size("ep")
    tok_count, top_count = expert_ids.shape
    quarter_width = tokens.shape[1]
    width = quarter_width * lax.axis_size("tp")
    expert_count = w_gate.shape[0] * ep_count
    capacity = (5 * tok_count * top_count + 4 * expert_count - 1) // (4 * expert_count)
    slot_count = expert_count * capacity
    picks_flat = expert_ids.reshape(-1)
    onehot = (picks_flat[:, None] == jnp.arange(expert_count, dtype=jnp.int32)[None, :]).astype(
        jnp.int32
    )
    slot_rank = jnp.sum((jnp.cumsum(onehot, axis=0) - onehot) * onehot, axis=1)
    slot_index = (picks_flat * capacity + slot_rank).reshape(tok_count, top_count)
    matches = jnp.arange(slot_count, dtype=jnp.int32)[:, None, None] == slot_index[None, :, :]
    dispatch = jnp.any(matches, axis=2).astype(jnp.bfloat16)
    weighting = jnp.sum(jnp.where(matches, gate_weights[None, :, :top_count], 0.0), axis=2)
    slot_gate = jnp.sum(weighting, axis=1)
    shadow_weight = gate_weights[:, top_count] * shadow_mask.astype(jnp.float32)
    x_full, dy_full = (
        lax.all_gather(tokens, "tp", axis=1, tiled=True),
        lax.all_gather(cotangent, "tp", axis=1, tiled=True),
    )
    rows_x = jnp.dot(dispatch, tokens, preferred_element_type=jnp.float32).astype(jnp.bfloat16)
    rows_dy = jnp.dot(dispatch, cotangent, preferred_element_type=jnp.float32)
    rows_dout = (slot_gate[:, None] * rows_dy).astype(jnp.bfloat16)
    recv_x, recv_dout = (
        lax.all_to_all(
            rows_x.reshape(ep_count, -1, quarter_width),
            "ep",
            split_axis=0,
            concat_axis=0,
            tiled=True,
        ),
        lax.all_to_all(
            rows_dout.reshape(ep_count, -1, quarter_width),
            "ep",
            split_axis=0,
            concat_axis=0,
            tiled=True,
        ),
    )
    expert_x, expert_dout = (
        lax.all_gather(recv_x.reshape(-1, quarter_width), "tp", axis=1, tiled=True),
        lax.all_gather(recv_dout.reshape(-1, quarter_width), "tp", axis=1, tiled=True),
    )
    partial_out, hidden, grad_pre_gate, grad_pre_up = expert_pass(
        expert_x, expert_dout, w_gate[0], w_up[0], w_down[0]
    )
    grad_gate = contract_rows(expert_x, grad_pre_gate).astype(jnp.bfloat16)[None]
    grad_up = contract_rows(expert_x, grad_pre_up).astype(jnp.bfloat16)[None]
    grad_down = contract_rows(hidden, expert_dout).astype(jnp.bfloat16)[None]
    full_gate, full_up, full_down = (
        lax.all_gather(s_gate, "ep", axis=0, tiled=True),
        lax.all_gather(s_up, "ep", axis=0, tiled=True),
        lax.all_gather(s_down, "ep", axis=1, tiled=True),
    )
    shadow_dout = (shadow_weight[:, None] * dy_full.astype(jnp.float32)).astype(jnp.bfloat16)
    shadow_out, shadow_hidden, shadow_gate_pre, shadow_up_pre = expert_pass(
        x_full, shadow_dout, full_gate, full_up, full_down
    )
    shadow_sums = lax.psum_scatter(
        jnp.concatenate(
            [
                contract_rows(x_full, shadow_gate_pre),
                contract_rows(x_full, shadow_up_pre),
                contract_rows(shadow_dout, shadow_hidden),
            ],
            axis=1,
        ).astype(jnp.bfloat16),
        "ep",
        scatter_dimension=0,
        tiled=True,
    ).astype(jnp.float32)
    hidden_part = s_gate.shape[1]
    grad_s_gate = shadow_sums[:, :hidden_part].astype(jnp.bfloat16)
    grad_s_up = shadow_sums[:, hidden_part : 2 * hidden_part].astype(jnp.bfloat16)
    grad_s_down = shadow_sums[:, 2 * hidden_part :].T.astype(jnp.bfloat16)
    back_rows = lax.all_to_all(
        partial_out.reshape(ep_count, -1, width), "ep", split_axis=0, concat_axis=0, tiled=True
    ).reshape(-1, width)
    term = weigh_rows(weighting.T, back_rows)
    term = term + shadow_weight[:, None] * shadow_out.astype(jnp.float32)
    mixed = lax.psum_scatter(term.astype(jnp.bfloat16), "tp", scatter_dimension=1, tiled=True)
    return (mixed, grad_gate, grad_up, grad_down, grad_s_gate, grad_s_up, grad_s_down)


def swap_pairs(count, bit):
    return [(i, i ^ bit) for i in range(count)]


def ring_pairs(count, shift):
    return [(i, (i + shift) % count) for i in range(count)]


def after(arrays, *earlier):
    def nothing(*refs):
        del refs

    count = len(arrays)
    return pl.pallas_call(
        nothing,
        out_shape=[jax.ShapeDtypeStruct(a.shape, a.dtype) for a in arrays],
        in_specs=[pl.BlockSpec(memory_space=pl.ANY)] * (count + len(earlier)),
        out_specs=[pl.BlockSpec(memory_space=pl.ANY)] * count,
        input_output_aliases={i: i for i in range(count)},
        cost_estimate=pl.CostEstimate(flops=0, bytes_accessed=0, transcendentals=0),
        name="after",
    )(*arrays, *earlier)


def pick_one(choices, index):
    chosen = choices[-1]
    for i in range(len(choices) - 2, -1, -1):
        chosen = jnp.where(index == i, choices[i], chosen)
    return chosen


def send_blocks(blocks, axis):
    count = lax.axis_size(axis)
    me = lax.axis_index(axis)
    pieces = [lax.dynamic_index_in_dim(blocks, me, 0, keepdims=True)]
    for shift in range(1, count):
        piece = lax.dynamic_index_in_dim(blocks, (me + shift) % count, 0, keepdims=True)
        pieces.append(lax.ppermute(piece, axis, ring_pairs(count, shift)))
    return pieces


def place_blocks(pieces, axis):
    count = lax.axis_size(axis)
    me = lax.axis_index(axis)
    result = jnp.zeros((count,) + pieces[0].shape[1:], pieces[0].dtype)
    for shift, piece in enumerate(pieces):
        result = lax.dynamic_update_slice_in_dim(result, piece, (me - shift) % count, 0)
    return result


def send_along_z(own):
    ep_count = lax.axis_size("ep")
    return [own] + [lax.ppermute(own, "ep", ring_pairs(ep_count, 2 * s)) for s in range(1, ep_count // 2)]


def swap_cores(block):
    return lax.ppermute(block, "ep", swap_pairs(lax.axis_size("ep"), 1))


def send_plane(piece):
    along, across = [swap_pairs(lax.axis_size("tp"), bit) for bit in (1, 2)]
    half = piece.shape[0] // 2
    from_x = lax.ppermute(piece, "tp", along)
    from_y = lax.ppermute(piece, "tp", across)
    diag_top = lax.ppermute(from_x[:half], "tp", across)
    diag_low = lax.ppermute(from_y[half:], "tp", along)
    return piece, from_x, from_y, diag_top, diag_low


def join_plane(piece, from_x, from_y, diag_top, diag_low):
    parts = (piece, from_x, from_y, jnp.concatenate([diag_top, diag_low], axis=0))
    column = lax.axis_index("tp")
    return jnp.concatenate([pick_one(parts, column ^ q) for q in range(len(parts))], axis=1)


def dot32(left, right):
    return jnp.dot(left, right, preferred_element_type=jnp.float32)


def contract_last(left, right):
    return lax.dot_general(
        left, right, (((1,), (1,)), ((), ())), preferred_element_type=jnp.float32
    )


def activation(pre_gate, pre_up, weight):
    sigmoid_gate = jax.nn.sigmoid(pre_gate)
    activated = pre_gate * sigmoid_gate
    hidden = (weight * activated * pre_up).astype(jnp.bfloat16)
    slope = weight * pre_up * sigmoid_gate * (1.0 + pre_gate * (1.0 - sigmoid_gate))
    return hidden, slope, weight * activated


def dense_shards(
    tokens,
    cotangent,
    expert_ids,
    gate_weights,
    shadow_mask,
    w_gate,
    w_up,
    w_down,
    s_gate,
    s_up,
    s_down,
):
    ep_count, tp_count = lax.axis_size("ep"), lax.axis_size("tp")
    ep_index, tp_index = lax.axis_index("ep"), lax.axis_index("tp")
    tok_count, top_count = expert_ids.shape
    quarter = tokens.shape[1]
    width = quarter * tp_count
    hidden_part = w_gate.shape[2]
    shadow_part = hidden_part // ep_count
    block_width = s_gate.shape[0]
    steps = ep_count // 2
    half = tok_count // 2
    along, across = swap_pairs(tp_count, 1), swap_pairs(tp_count, 2)

    x_z = send_along_z(tokens)
    x_plane = [send_plane(piece) for piece in x_z]
    x_own = [join_plane(*parts) for parts in x_plane]
    x_other = [swap_cores(block) for block in x_own]

    picked = expert_ids[:, :, None] == jnp.arange(ep_count, dtype=jnp.int32)[None, None, :]
    table = jnp.sum(jnp.where(picked, gate_weights[:, :top_count, None], 0.0), axis=1)
    shadow_weight = gate_weights[:, top_count] * shadow_mask.astype(jnp.float32)
    table = jnp.concatenate([table, shadow_weight[:, None]], axis=1).T
    table = jnp.pad(table, ((0, 16 - (ep_count + 1) % 16), (0, 0)))
    (table,) = after([table], x_z[1])
    table_own = jnp.concatenate([piece[None] for piece in send_along_z(table)], axis=0)
    tables = jnp.stack([table_own, swap_cores(table_own)])
    w_expert = lax.dynamic_index_in_dim(tables, ep_index, 2, keepdims=False)
    w_shadow = tables[:, :, ep_count]
    w_expert = [w_expert[:, s].reshape(-1, 1) for s in range(steps)]
    w_shadow = [w_shadow[:, s].reshape(-1, 1) for s in range(steps)]

    (dy_first,) = after([cotangent], x_plane[0][1], x_plane[0][2])
    (dy_later,) = after([cotangent], x_z[-1])
    dy_z = [dy_first] + send_along_z(dy_later)[1:]
    dy_plane = [send_plane(dy_z[0])]
    for s in range(1, steps):
        (piece,) = after([dy_z[s]], x_plane[-1][1], x_plane[-1][2])
        dy_plane.append(send_plane(piece))

    shadow_blocks = jnp.concatenate(
        [
            s_gate.T.reshape(ep_count, shadow_part, block_width),
            s_up.T.reshape(ep_count, shadow_part, block_width),
            s_down.reshape(ep_count, shadow_part, block_width),
        ],
        axis=1,
    )
    (shadow_blocks,) = after([shadow_blocks], x_z[-1], dy_z[1])
    shadow_rows = place_blocks(send_blocks(shadow_blocks, "ep"), "ep")
    shadow_rows = shadow_rows.transpose(1, 0, 2).reshape(-1, width)
    shadow_in, shadow_down = shadow_rows[: 2 * shadow_part], shadow_rows[2 * shadow_part :]

    x_slots, dy_slots, forward = [], [], []
    for s in range(steps):
        x_slot = jnp.concatenate([x_own[s], x_other[s]], axis=0)
        x_slots.append(x_slot)
        forward.append(activation(dot32(x_slot, w_gate[0]), dot32(x_slot, w_up[0]), w_expert[s]))
        dy_own = join_plane(*after(dy_plane[s], forward[s][0]))
        dy_slots.append(jnp.concatenate([dy_own, swap_cores(dy_own)], axis=0))
    x_all = jnp.concatenate(x_slots, axis=0)

    pre_shadow = contract_last(x_all, shadow_in)
    hidden_s, slope_s, activated_s = activation(
        pre_shadow[:, :shadow_part], pre_shadow[:, shadow_part:], jnp.concatenate(w_shadow, axis=0)
    )

    down_full = jnp.concatenate([w_down[0], shadow_down], axis=0)
    down_quarters = [down_full[:, q * quarter : (q + 1) * quarter] for q in range(tp_count)]
    down_parts = [pick_one(down_quarters, tp_index ^ r) for r in range(tp_count)]
    got, arrived, sums = [], [], []
    for s in list(range(1, steps)) + [0]:
        rows = slice(2 * s * tok_count, 2 * (s + 1) * tok_count)
        weighted = jnp.concatenate([forward[s][0], hidden_s[rows]], axis=1)
        mine, theirs = weighted[:tok_count], weighted[tok_count:]
        sent = jnp.concatenate([dot32(theirs, part).astype(jnp.bfloat16) for part in down_parts], axis=1)
        got.append(swap_cores(sent))
        own, to_x, to_y, to_diag = [
            dot32(mine, part) + got[-1][:, i * quarter : (i + 1) * quarter].astype(jnp.float32)
            for i, part in enumerate(down_parts)
        ]
        to_diag = to_diag.astype(jnp.bfloat16)
        top = lax.ppermute(to_diag[:half], "tp", along).astype(jnp.float32)
        low = lax.ppermute(to_diag[half:], "tp", across).astype(jnp.float32)
        to_y = jnp.concatenate([to_y[:half] + top, to_y[half:]], axis=0).astype(jnp.bfloat16)
        to_x = jnp.concatenate([to_x[:half], to_x[half:] + low], axis=0).astype(jnp.bfloat16)
        from_x, from_y = lax.ppermute(to_x, "tp", along), lax.ppermute(to_y, "tp", across)
        arrived.append((from_x, from_y))
        total = own + from_x.astype(jnp.float32) + from_y.astype(jnp.float32)
        if s:
            total = lax.ppermute(total.astype(jnp.bfloat16), "ep", ring_pairs(ep_count, -2 * s))
        sums.append(total.astype(jnp.float32))
    mixed = sum(sums).astype(jnp.bfloat16)

    dy_all = jnp.concatenate(dy_slots, axis=0)
    (hidden_s, dy_all) = after([hidden_s, dy_all], got[0])
    grad_hidden_s = contract_last(dy_all, shadow_down)
    grad_pre_s = jnp.concatenate(
        [grad_hidden_s * slope_s, grad_hidden_s * activated_s], axis=1
    ).astype(jnp.bfloat16)
    grad_in_s = contract_rows(grad_pre_s, x_all).astype(jnp.bfloat16)
    grad_down_s = contract_rows(hidden_s, dy_all).astype(jnp.bfloat16)
    grad_s = jnp.concatenate([grad_in_s, grad_down_s], axis=0)
    grad_s = grad_s.reshape(3 * shadow_part, ep_count, block_width).transpose(1, 0, 2)
    grad_s = send_blocks(grad_s, "ep")

    grad_hidden = contract_last(dy_all, w_down[0])
    slope = jnp.concatenate([f[1] for f in forward], axis=0)
    activated = jnp.concatenate([f[2] for f in forward], axis=0)
    hidden = jnp.concatenate([f[0] for f in forward], axis=0)
    grad_pre_gate = (grad_hidden * slope).astype(jnp.bfloat16)
    grad_pre_up = (grad_hidden * activated).astype(jnp.bfloat16)
    (grad_pre_gate,) = after([grad_pre_gate], *arrived[0])
    grad_gate = contract_rows(x_all, grad_pre_gate).astype(jnp.bfloat16)[None]
    (grad_pre_up,) = after([grad_pre_up], *arrived[1])
    grad_up = contract_rows(x_all, grad_pre_up).astype(jnp.bfloat16)[None]
    (hidden,) = after([hidden], *arrived[2])
    grad_down = contract_rows(hidden, dy_all).astype(jnp.bfloat16)[None]

    grad_s = place_blocks(after(grad_s, *arrived[2]), "ep")
    grad_s_gate = grad_s[:, :shadow_part].reshape(hidden_part, block_width).T
    grad_s_up = grad_s[:, shadow_part : 2 * shadow_part].reshape(hidden_part, block_width).T
    grad_s_down = grad_s[:, 2 * shadow_part :].reshape(hidden_part, block_width)
    return (mixed, grad_gate, grad_up, grad_down, grad_s_gate, grad_s_up, grad_s_down)


def solution(mesh):
    tp_count, ep_count = mesh.shape["tp"], mesh.shape["ep"]
    dense = tp_count == 4 and ep_count % 2 == 0 and ep_count <= 8
    return jax.shard_map(
        dense_shards if dense else shards,
        mesh=mesh,
        in_specs=(
            P("ep", "tp"),
            P("ep", "tp"),
            P("ep", None),
            P("ep", None),
            P("ep"),
            P("ep", None, "tp"),
            P("ep", None, "tp"),
            P("ep", "tp", None),
            P("ep", "tp"),
            P("ep", "tp"),
            P("tp", "ep"),
        ),
        out_specs=(
            P("ep", "tp"),
            P("ep", None, "tp"),
            P("ep", None, "tp"),
            P("ep", "tp", None),
            P("ep", "tp"),
            P("ep", "tp"),
            P("tp", "ep"),
        ),
        check_vma=False,
    )
```

```python
import math

import jax
import jax.numpy as jnp
from jax import lax
from jax.experimental import pallas as pl
from jax.experimental.pallas import tpu as pltpu
from jax.sharding import PartitionSpec as P


def contract_rows(left, right):
    return lax.dot_general(
        left, right, (((0,), (0,)), ((), ())), preferred_element_type=jnp.float32
    )


def split_parts(values):
    upper_part = values.astype(jnp.bfloat16)
    lower_part = (values - upper_part.astype(jnp.float32)).astype(jnp.bfloat16)
    return (upper_part, lower_part)


def weigh_rows(weight_table, rows):
    weight_upper, weight_lower = split_parts(weight_table)
    return jnp.dot(weight_upper, rows, preferred_element_type=jnp.float32) + jnp.dot(
        weight_lower, rows, preferred_element_type=jnp.float32
    )


def expert_pass(rows_x, rows_dout, weight_gate, weight_up, weight_down):
    pre_gate = jnp.dot(rows_x, weight_gate, preferred_element_type=jnp.float32)
    pre_up = jnp.dot(rows_x, weight_up, preferred_element_type=jnp.float32)
    sigmoid_gate = jax.nn.sigmoid(pre_gate)
    activated = pre_gate * sigmoid_gate
    hidden = (activated * pre_up).astype(jnp.bfloat16)
    partial_out = jnp.dot(hidden, weight_down, preferred_element_type=jnp.float32).astype(
        jnp.bfloat16
    )
    hidden_grad = lax.dot_general(
        rows_dout, weight_down, (((1,), (1,)), ((), ())), preferred_element_type=jnp.float32
    )
    grad_pre_gate = (
        hidden_grad * pre_up * sigmoid_gate * (1.0 + pre_gate * (1.0 - sigmoid_gate))
    ).astype(jnp.bfloat16)
    grad_pre_up = (hidden_grad * activated).astype(jnp.bfloat16)
    return (partial_out, hidden, grad_pre_gate, grad_pre_up)


def shards(
    tokens,
    cotangent,
    expert_ids,
    gate_weights,
    shadow_mask,
    w_gate,
    w_up,
    w_down,
    s_gate,
    s_up,
    s_down,
):
    ep_count = lax.axis_size("ep")
    tok_count, top_count = expert_ids.shape
    quarter_width = tokens.shape[1]
    width = quarter_width * lax.axis_size("tp")
    expert_count = w_gate.shape[0] * ep_count
    capacity = (5 * tok_count * top_count + 4 * expert_count - 1) // (4 * expert_count)
    slot_count = expert_count * capacity
    picks_flat = expert_ids.reshape(-1)
    onehot = (picks_flat[:, None] == jnp.arange(expert_count, dtype=jnp.int32)[None, :]).astype(
        jnp.int32
    )
    slot_rank = jnp.sum((jnp.cumsum(onehot, axis=0) - onehot) * onehot, axis=1)
    slot_index = (picks_flat * capacity + slot_rank).reshape(tok_count, top_count)
    matches = jnp.arange(slot_count, dtype=jnp.int32)[:, None, None] == slot_index[None, :, :]
    dispatch = jnp.any(matches, axis=2).astype(jnp.bfloat16)
    weighting = jnp.sum(jnp.where(matches, gate_weights[None, :, :top_count], 0.0), axis=2)
    slot_gate = jnp.sum(weighting, axis=1)
    shadow_weight = gate_weights[:, top_count] * shadow_mask.astype(jnp.float32)
    x_full, dy_full = (
        lax.all_gather(tokens, "tp", axis=1, tiled=True),
        lax.all_gather(cotangent, "tp", axis=1, tiled=True),
    )
    rows_x = jnp.dot(dispatch, tokens, preferred_element_type=jnp.float32).astype(jnp.bfloat16)
    rows_dy = jnp.dot(dispatch, cotangent, preferred_element_type=jnp.float32)
    rows_dout = (slot_gate[:, None] * rows_dy).astype(jnp.bfloat16)
    recv_x, recv_dout = (
        lax.all_to_all(
            rows_x.reshape(ep_count, -1, quarter_width),
            "ep",
            split_axis=0,
            concat_axis=0,
            tiled=True,
        ),
        lax.all_to_all(
            rows_dout.reshape(ep_count, -1, quarter_width),
            "ep",
            split_axis=0,
            concat_axis=0,
            tiled=True,
        ),
    )
    expert_x, expert_dout = (
        lax.all_gather(recv_x.reshape(-1, quarter_width), "tp", axis=1, tiled=True),
        lax.all_gather(recv_dout.reshape(-1, quarter_width), "tp", axis=1, tiled=True),
    )
    partial_out, hidden, grad_pre_gate, grad_pre_up = expert_pass(
        expert_x, expert_dout, w_gate[0], w_up[0], w_down[0]
    )
    grad_gate = contract_rows(expert_x, grad_pre_gate).astype(jnp.bfloat16)[None]
    grad_up = contract_rows(expert_x, grad_pre_up).astype(jnp.bfloat16)[None]
    grad_down = contract_rows(hidden, expert_dout).astype(jnp.bfloat16)[None]
    full_gate, full_up, full_down = (
        lax.all_gather(s_gate, "ep", axis=0, tiled=True),
        lax.all_gather(s_up, "ep", axis=0, tiled=True),
        lax.all_gather(s_down, "ep", axis=1, tiled=True),
    )
    shadow_dout = (shadow_weight[:, None] * dy_full.astype(jnp.float32)).astype(jnp.bfloat16)
    shadow_out, shadow_hidden, shadow_gate_pre, shadow_up_pre = expert_pass(
        x_full, shadow_dout, full_gate, full_up, full_down
    )
    shadow_sums = lax.psum_scatter(
        jnp.concatenate(
            [
                contract_rows(x_full, shadow_gate_pre),
                contract_rows(x_full, shadow_up_pre),
                contract_rows(shadow_dout, shadow_hidden),
            ],
            axis=1,
        ).astype(jnp.bfloat16),
        "ep",
        scatter_dimension=0,
        tiled=True,
    ).astype(jnp.float32)
    hidden_part = s_gate.shape[1]
    grad_s_gate = shadow_sums[:, :hidden_part].astype(jnp.bfloat16)
    grad_s_up = shadow_sums[:, hidden_part : 2 * hidden_part].astype(jnp.bfloat16)
    grad_s_down = shadow_sums[:, 2 * hidden_part :].T.astype(jnp.bfloat16)
    back_rows = lax.all_to_all(
        partial_out.reshape(ep_count, -1, width), "ep", split_axis=0, concat_axis=0, tiled=True
    ).reshape(-1, width)
    term = weigh_rows(weighting.T, back_rows)
    term = term + shadow_weight[:, None] * shadow_out.astype(jnp.float32)
    mixed = lax.psum_scatter(term.astype(jnp.bfloat16), "tp", scatter_dimension=1, tiled=True)
    return (mixed, grad_gate, grad_up, grad_down, grad_s_gate, grad_s_up, grad_s_down)


ANY = pl.BlockSpec(memory_space=pl.ANY)
VMEM_LIMIT = 48 * 1024 * 1024


def swap_pairs(count, bit):
    return [(i, i ^ bit) for i in range(count)]


def ring_pairs(count, shift):
    return [(i, (i + shift) % count) for i in range(count)]


def dot32(left, right):
    return jnp.dot(left, right, preferred_element_type=jnp.float32)


def contract_last(left, right):
    return lax.dot_general(
        left, right, (((1,), (1,)), ((), ())), preferred_element_type=jnp.float32
    )


def shape_of(*dims, dtype=jnp.bfloat16):
    return jax.ShapeDtypeStruct(dims, dtype)


def after(arrays, *earlier):
    def nothing(*refs):
        del refs

    count = len(arrays)
    return pl.pallas_call(
        nothing,
        out_shape=[jax.ShapeDtypeStruct(a.shape, a.dtype) for a in arrays],
        in_specs=[ANY] * (count + len(earlier)),
        out_specs=[ANY] * count,
        input_output_aliases={i: i for i in range(count)},
        cost_estimate=pl.CostEstimate(flops=0, bytes_accessed=0, transcendentals=0),
        name="after",
    )(*arrays, *earlier)


def kernel_call(body, grid, in_specs, out_specs, out_shape, operands, scratch, flops, name, column=None, earlier=()):
    count = len(operands)

    def run(column_ref, *refs):
        del column_ref
        body(*refs[:count], *refs[count + len(earlier) :])

    column = jnp.zeros((1,), jnp.int32) if column is None else column.reshape(1).astype(jnp.int32)
    moved = sum(a.size * a.dtype.itemsize for a in operands)
    moved += sum(math.prod(a.shape) * a.dtype.itemsize for a in out_shape)
    return pl.pallas_call(
        run,
        out_shape=out_shape,
        grid_spec=pltpu.PrefetchScalarGridSpec(
            num_scalar_prefetch=1,
            grid=grid,
            in_specs=list(in_specs) + [ANY] * len(earlier),
            out_specs=out_specs,
            scratch_shapes=scratch,
        ),
        compiler_params=pltpu.CompilerParams(vmem_limit_bytes=VMEM_LIMIT),
        cost_estimate=pl.CostEstimate(flops=int(flops), bytes_accessed=int(moved), transcendentals=0),
        name=name,
    )(column, *operands, *earlier)


def whole(array):
    return pl.BlockSpec(array.shape, lambda *_: (0,) * len(array.shape))


def join_plane(column, piece, from_x, from_y, diag_top, diag_low):
    rows, quarter = piece.shape
    half = rows // 2
    places = ((0, 0, rows), (1, 0, rows), (2, 0, rows), (3, 0, half), (3, half, half))

    def body(column_ref, *refs):
        sources, out, done = refs[:5], refs[5], refs[6]
        copies = []
        for i, (bit, start, count) in enumerate(places):
            offset = pl.multiple_of((column_ref[0] ^ bit) * quarter, 128)
            target = out.at[pl.ds(start, count), pl.ds(offset, quarter)]
            copies.append(pltpu.make_async_copy(sources[i], target, done.at[i]))
            copies[-1].start()
        for copy in copies:
            copy.wait()

    return pl.pallas_call(
        body,
        out_shape=shape_of(rows, 4 * quarter),
        in_specs=[pl.BlockSpec(memory_space=pltpu.SMEM)] + [ANY] * 5,
        out_specs=ANY,
        scratch_shapes=[pltpu.SemaphoreType.DMA((5,))],
        cost_estimate=pl.CostEstimate(flops=0, bytes_accessed=16 * rows * quarter, transcendentals=0),
        name="join_plane",
    )(column.reshape(1).astype(jnp.int32), piece, from_x, from_y, diag_top, diag_low)


def row_specs(groups, tile):
    def spec(index, rows):
        return pl.BlockSpec((rows, tile), lambda k, *_: (index, k))

    return [spec(index, rows) for _, index, rows in groups]


def apply_gate(pre_gate, pre_up, weight):
    sigmoid_gate = jax.nn.sigmoid(pre_gate)
    activated = pre_gate * sigmoid_gate
    hidden = (weight * activated * pre_up).astype(jnp.bfloat16)
    slope = weight * pre_up * sigmoid_gate * (1.0 + pre_gate * (1.0 - sigmoid_gate))
    return hidden, slope, weight * activated


def forward_rows(groups, w_gate, w_up, weight, tile, earlier=()):
    rows = sum(g[2] for g in groups)
    width, units = w_gate.shape
    steps = width // tile

    def body(*refs):
        n = len(groups)
        gate_ref, up_ref, weight_ref, hidden_ref, slope_ref, act_ref, both, acc = refs[n:]
        step = pl.program_id(0)
        both[:, :units] = gate_ref[...]
        both[:, units:] = up_ref[...]
        start = 0
        for ref, (_, _, count) in zip(refs[:n], groups):
            part = pl.ds(start, count)
            value = dot32(ref[...], both[...])

            @pl.when(step == 0)
            def _():
                acc[part, :] = value

            @pl.when(step > 0)
            def _():
                acc[part, :] += value

            start += count

        @pl.when(step == steps - 1)
        def _():
            chunk = 64

            @pl.loop(0, rows // chunk)
            def _(i):
                part = pl.ds(pl.multiple_of(i * chunk, chunk), chunk)
                hidden, slope, act = apply_gate(acc[part, :units], acc[part, units:], weight_ref[part, :])
                hidden_ref[part, :] = hidden
                slope_ref[part, :] = slope
                act_ref[part, :] = act

    tile_spec = pl.BlockSpec((tile, units), lambda k, *_: (k, 0))
    out_spec = pl.BlockSpec((rows, units), lambda *_: (0, 0))
    return kernel_call(
        body,
        (steps,),
        row_specs(groups, tile) + [tile_spec, tile_spec, whole(weight)],
        [out_spec] * 3,
        [shape_of(rows, units), shape_of(rows, units, dtype=jnp.float32), shape_of(rows, units, dtype=jnp.float32)],
        [g[0] for g in groups] + [w_gate, w_up, weight],
        [pltpu.VMEM((tile, 2 * units), jnp.bfloat16), pltpu.VMEM((rows, 2 * units), jnp.float32)],
        4 * rows * width * units,
        "forward_rows",
        earlier=earlier,
    )


def forward_shadow(groups, shadow_rows, weight, tile, earlier=()):
    rows = sum(g[2] for g in groups)
    width = shadow_rows.shape[1]
    units = shadow_rows.shape[0] // 3
    steps = width // tile
    apart = 128

    def body(*refs):
        n = len(groups)
        rows_ref, weight_ref, hidden_ref, slope_ref, act_ref, both, acc = refs[n:]
        step = pl.program_id(0)

        @pl.when(step == 0)
        def _():
            both[...] = jnp.zeros_like(both)

        both[:units, :] = rows_ref[:units, :]
        both[apart : apart + units, :] = rows_ref[units : 2 * units, :]
        start = 0
        for ref, (_, _, count) in zip(refs[:n], groups):
            part = pl.ds(start, count)
            value = contract_last(ref[...], both[...])

            @pl.when(step == 0)
            def _():
                acc[part, :] = value

            @pl.when(step > 0)
            def _():
                acc[part, :] += value

            start += count

        @pl.when(step == steps - 1)
        def _():
            chunk = 128

            @pl.loop(0, rows // chunk)
            def _(i):
                part = pl.ds(pl.multiple_of(i * chunk, chunk), chunk)
                hidden, slope, act = apply_gate(acc[part, :apart], acc[part, apart:], weight_ref[part, :])
                hidden_ref[part, :] = hidden[:, :units]
                slope_ref[part, :] = slope[:, :units]
                act_ref[part, :] = act[:, :units]

    out_spec = pl.BlockSpec((rows, units), lambda *_: (0, 0))
    return kernel_call(
        body,
        (steps,),
        row_specs(groups, tile) + [pl.BlockSpec((3 * units, tile), lambda k, *_: (0, k)), whole(weight)],
        [out_spec] * 3,
        [shape_of(rows, units), shape_of(rows, units, dtype=jnp.float32), shape_of(rows, units, dtype=jnp.float32)],
        [g[0] for g in groups] + [shadow_rows, weight],
        [pltpu.VMEM((2 * apart, tile), jnp.bfloat16), pltpu.VMEM((rows, 2 * apart), jnp.float32)],
        4 * rows * width * apart,
        "forward_shadow",
        earlier=earlier,
    )


def output_other(weighted, down, column, parts, quarter, earlier=()):
    rows, units = weighted.shape
    count = rows // 2 // parts

    def body(weighted_ref, down_ref, *outs):
        for i, out in enumerate(outs):
            out[...] = dot32(weighted_ref[i * count : (i + 1) * count, :], down_ref[...]).astype(jnp.bfloat16)

    return kernel_call(
        body,
        (4,),
        [
            pl.BlockSpec((rows // 2, units), lambda *_: (1, 0)),
            pl.BlockSpec((units, quarter), lambda q, column_ref: (0, column_ref[0] ^ q)),
        ],
        [pl.BlockSpec((count, quarter), lambda q, *_: (0, q))] * parts,
        [shape_of(count, 4 * quarter)] * parts,
        [weighted, down],
        [],
        rows * units * quarter * 4,
        "output_other",
        column=column,
        earlier=earlier,
    )


def output_own(weighted, got, down, column, part, quarter, earlier=()):
    count, units = got.shape[0], weighted.shape[1]
    half = count // 2

    def body(weighted_ref, got_ref, down_ref, own, to_x, to_y, diag_top, diag_low):
        q = pl.program_id(0)
        value = dot32(weighted_ref[...], down_ref[...]) + got_ref[...].astype(jnp.float32)

        @pl.when(q == 0)
        def _():
            own[...] = value

        @pl.when(q == 1)
        def _():
            to_x[...] = value.astype(jnp.bfloat16)

        @pl.when(q == 2)
        def _():
            to_y[...] = value.astype(jnp.bfloat16)

        @pl.when(q == 3)
        def _():
            diag_top[...] = value[:half].astype(jnp.bfloat16)
            diag_low[...] = value[half:].astype(jnp.bfloat16)

    full = pl.BlockSpec((count, quarter), lambda *_: (0, 0))
    part_spec = pl.BlockSpec((half, quarter), lambda *_: (0, 0))
    return kernel_call(
        body,
        (4,),
        [
            pl.BlockSpec((count, units), lambda *_: (part, 0)),
            pl.BlockSpec((count, quarter), lambda q, *_: (0, q)),
            pl.BlockSpec((units, quarter), lambda q, column_ref: (0, column_ref[0] ^ q)),
        ],
        [full, full, full, part_spec, part_spec],
        [shape_of(count, quarter, dtype=jnp.float32), shape_of(count, quarter), shape_of(count, quarter)]
        + [shape_of(half, quarter)] * 2,
        [weighted, got, down],
        [],
        2 * count * units * quarter * 4,
        "output_own",
        column=column,
        earlier=earlier,
    )


def backward_rows(groups, down, slopes, acts, slope_s, act_s, tile, earlier=()):
    rows = sum(g[2] for g in groups)
    units_all, width = down.shape
    units = slopes[0].shape[1]
    units_s = units_all - units
    steps = width // tile
    apart = 128
    firsts = [0]
    for slope in slopes:
        firsts.append(firsts[-1] + slope.shape[0])

    def body(*refs):
        n, m = len(groups), len(slopes)
        down_ref = refs[n]
        slope_refs, act_refs = refs[n + 1 : n + 1 + m], refs[n + 1 + m : n + 1 + 2 * m]
        slope_s_ref, act_s_ref, pre_ref, pre_s_ref, acc = refs[n + 1 + 2 * m :]
        step = pl.program_id(0)
        start = 0
        for ref, (_, _, count) in zip(refs[:n], groups):
            part = pl.ds(start, count)
            value = contract_last(ref[...], down_ref[...])

            @pl.when(step == 0)
            def _():
                acc[part, :] = value

            @pl.when(step > 0)
            def _():
                acc[part, :] += value

            start += count

        @pl.when(step == steps - 1)
        def _():
            chunk = 64
            for j in range(m):

                @pl.loop(0, slopes[j].shape[0] // chunk)
                def _(i):
                    source = pl.ds(pl.multiple_of(i * chunk, chunk), chunk)
                    part = pl.ds(pl.multiple_of(firsts[j] + i * chunk, chunk), chunk)
                    grad = acc[part, :units]
                    pre_ref[part, :units] = (grad * slope_refs[j][source, :]).astype(jnp.bfloat16)
                    pre_ref[part, units:] = (grad * act_refs[j][source, :]).astype(jnp.bfloat16)

            pre_s_ref[...] = jnp.zeros_like(pre_s_ref)

            @pl.loop(0, rows // chunk)
            def _(i):
                part = pl.ds(pl.multiple_of(i * chunk, chunk), chunk)
                grad = acc[part, units:]
                pre_s_ref[part, :units_s] = (grad * slope_s_ref[part, :]).astype(jnp.bfloat16)
                pre_s_ref[part, apart : apart + units_s] = (grad * act_s_ref[part, :]).astype(jnp.bfloat16)

    return kernel_call(
        body,
        (steps,),
        row_specs(groups, tile)
        + [pl.BlockSpec((units_all, tile), lambda k, *_: (0, k))]
        + [whole(a) for a in list(slopes) + list(acts) + [slope_s, act_s]],
        [pl.BlockSpec((rows, 2 * units), lambda *_: (0, 0)), pl.BlockSpec((rows, 2 * apart), lambda *_: (0, 0))],
        [shape_of(rows, 2 * units), shape_of(rows, 2 * apart)],
        [g[0] for g in groups] + [down] + list(slopes) + list(acts) + [slope_s, act_s],
        [pltpu.VMEM((rows, units_all), jnp.float32)],
        2 * rows * width * units_all,
        "backward_rows",
        earlier=earlier,
    )


def stage_rows(refs, groups, held):
    start = 0
    for ref, (_, _, count) in zip(refs, groups):
        held[pl.ds(start, count), :] = ref[...]
        start += count
    return held[...]


def shadow_grads(x_groups, dy_groups, pre_s, hidden_s, tile, earlier=()):
    rows, wide = pre_s.shape
    units = hidden_s.shape[1]
    width = x_groups[0][0].shape[1]
    apart = wide // 2

    def body(*refs):
        n = len(x_groups)
        pre_ref, hidden_ref, out, held = refs[2 * n :]
        value = contract_rows(pre_ref[...], stage_rows(refs[:n], x_groups, held))
        out[:units, :] = value[:units].astype(jnp.bfloat16)
        out[units : 2 * units, :] = value[apart : apart + units].astype(jnp.bfloat16)
        value = contract_rows(hidden_ref[...], stage_rows(refs[n : 2 * n], dy_groups, held))
        out[2 * units :, :] = value.astype(jnp.bfloat16)

    (out,) = kernel_call(
        body,
        (width // tile,),
        row_specs(x_groups, tile) + row_specs(dy_groups, tile) + [whole(pre_s), whole(hidden_s)],
        [pl.BlockSpec((3 * units, tile), lambda k, *_: (0, k))],
        [shape_of(3 * units, width)],
        [g[0] for g in x_groups + dy_groups] + [pre_s, hidden_s],
        [pltpu.VMEM((rows, tile), jnp.bfloat16)],
        2 * rows * width * (wide + units),
        "shadow_grads",
        earlier=earlier,
    )
    return out


def input_grads(groups, pre, tile, earlier=()):
    rows, both = pre.shape
    units = both // 2
    width = groups[0][0].shape[1]

    def body(*refs):
        n = len(groups)
        pre_ref, gate_ref, up_ref, held = refs[n:]
        value = contract_rows(stage_rows(refs[:n], groups, held), pre_ref[...])
        gate_ref[...] = value[:, :units].astype(jnp.bfloat16)
        up_ref[...] = value[:, units:].astype(jnp.bfloat16)

    return kernel_call(
        body,
        (width // tile,),
        row_specs(groups, tile) + [whole(pre)],
        [pl.BlockSpec((tile, units), lambda k, *_: (k, 0))] * 2,
        [shape_of(width, units)] * 2,
        [g[0] for g in groups] + [pre],
        [pltpu.VMEM((rows, tile), jnp.bfloat16)],
        2 * rows * width * both,
        "input_grads",
        earlier=earlier,
    )


def down_grad(groups, hidden, tile, earlier=()):
    rows, units = hidden.shape
    width = groups[0][0].shape[1]

    def body(*refs):
        n = len(groups)
        hidden_ref, out, held = refs[n:]
        out[...] = contract_rows(hidden_ref[...], stage_rows(refs[:n], groups, held)).astype(jnp.bfloat16)

    (out,) = kernel_call(
        body,
        (width // tile,),
        row_specs(groups, tile) + [whole(hidden)],
        [pl.BlockSpec((units, tile), lambda k, *_: (0, k))],
        [shape_of(units, width)],
        [g[0] for g in groups] + [hidden],
        [pltpu.VMEM((rows, tile), jnp.bfloat16)],
        2 * rows * width * units,
        "down_grad",
        earlier=earlier,
    )
    return out


def send_along_z(own):
    ep_count = lax.axis_size("ep")
    return [lax.ppermute(own, "ep", ring_pairs(ep_count, 2 * s)) for s in range(1, ep_count // 2)]


def swap_cores(block):
    return lax.ppermute(block, "ep", swap_pairs(lax.axis_size("ep"), 1))


def send_plane(piece):
    along, across = [swap_pairs(lax.axis_size("tp"), bit) for bit in (1, 2)]
    half = piece.shape[0] // 2
    from_x = lax.ppermute(piece, "tp", along)
    from_y = lax.ppermute(piece, "tp", across)
    diag_top = lax.ppermute(from_x[:half], "tp", across)
    diag_low = lax.ppermute(from_y[half:], "tp", along)
    return piece, from_x, from_y, diag_top, diag_low


def exchange_start(blocks):
    ep_count, me = lax.axis_size("ep"), lax.axis_index("ep")
    chips, chip, core = ep_count // 2, me // 2, me % 2
    pairs = blocks.reshape(chips, 2, *blocks.shape[1:])
    kept = jnp.where(core == 0, pairs[:, 0], pairs[:, 1])
    given = jnp.where(core == 0, pairs[:, 1], pairs[:, 0])
    taken = swap_cores(given)
    both = jnp.stack([jnp.where(core == 0, kept, taken), jnp.where(core == 0, taken, kept)], axis=1)
    pieces = [lax.dynamic_index_in_dim(both, chip, 0)]
    for shift in range(1, chips):
        piece = lax.dynamic_index_in_dim(both, (chip + shift) % chips, 0)
        pieces.append(lax.ppermute(piece, "ep", ring_pairs(ep_count, 2 * shift)))
    return pieces


def exchange_end(pieces):
    chip = lax.axis_index("ep") // 2
    chips = len(pieces)
    result = jnp.zeros((chips,) + pieces[0].shape[1:], pieces[0].dtype)
    for shift, piece in enumerate(pieces):
        result = lax.dynamic_update_slice_in_dim(result, piece, (chip - shift) % chips, 0)
    return result.reshape(2 * chips, *result.shape[2:])


def dense_shards(
    tokens,
    cotangent,
    expert_ids,
    gate_weights,
    shadow_mask,
    w_gate,
    w_up,
    w_down,
    s_gate,
    s_up,
    s_down,
):
    ep_count, tp_count = lax.axis_size("ep"), lax.axis_size("tp")
    ep_index, tp_index = lax.axis_index("ep"), lax.axis_index("tp")
    tok_count, top_count = expert_ids.shape
    quarter = tokens.shape[1]
    width = quarter * tp_count
    hidden_part = w_gate.shape[2]
    shadow_part = hidden_part // ep_count
    block_width = s_gate.shape[0]
    steps = ep_count // 2
    later = (steps - 1) * tok_count
    tile = width // 8
    along, across = swap_pairs(tp_count, 1), swap_pairs(tp_count, 2)

    x_z = send_along_z(tokens)
    near_plane = send_plane(jnp.concatenate([tokens, cotangent], axis=0))
    near_own = join_plane(tp_index, *near_plane)
    near_other = swap_cores(near_own)
    x_plane = send_plane(jnp.concatenate(x_z, axis=0))
    x_own = join_plane(tp_index, *x_plane)
    x_other = swap_cores(x_own)

    picked = expert_ids[:, :, None] == jnp.arange(ep_count, dtype=jnp.int32)[None, None, :]
    table = jnp.sum(jnp.where(picked, gate_weights[:, :top_count, None], 0.0), axis=1)
    shadow_weight = gate_weights[:, top_count] * shadow_mask.astype(jnp.float32)
    table = jnp.concatenate([table, shadow_weight[:, None]], axis=1).T
    table = jnp.pad(table, ((0, -(ep_count + 1) % 8), (0, 0)))
    (table,) = after([table], x_z[-1])
    table_own = jnp.concatenate([piece[None] for piece in [table] + send_along_z(table)], axis=0)
    tables = jnp.stack([table_own, swap_cores(table_own)])
    w_expert = lax.dynamic_index_in_dim(tables, ep_index, 2, keepdims=False)
    w_shadow = tables[:, :, ep_count]
    w_expert_near, w_expert_far = w_expert[:, 0].reshape(-1, 1), w_expert[:, 1:].reshape(-1, 1)
    w_shadow = jnp.concatenate([w_shadow[:, 0].reshape(-1, 1), w_shadow[:, 1:].reshape(-1, 1)], axis=0)

    (dy_later,) = after([cotangent], x_z[-1])
    dy_z = send_along_z(dy_later)
    (dy_far,) = after([jnp.concatenate(dy_z, axis=0)], x_plane[1], x_plane[2])
    dy_plane = send_plane(dy_far)

    shadow_blocks = jnp.concatenate(
        [
            s_gate.T.reshape(ep_count, shadow_part, block_width),
            s_up.T.reshape(ep_count, shadow_part, block_width),
            s_down.reshape(ep_count, shadow_part, block_width),
        ],
        axis=1,
    )
    (shadow_blocks,) = after([shadow_blocks], dy_z[-1])
    shadow_rows = exchange_end(exchange_start(shadow_blocks))
    shadow_rows = shadow_rows.transpose(1, 0, 2).reshape(-1, width)

    x_near = [(near_own, 0, tok_count), (near_other, 0, tok_count)]
    x_far = [(x_own, 0, later), (x_other, 0, later)]
    x_groups = x_near + x_far
    hidden_near, slope_near, act_near = forward_rows(x_near, w_gate[0], w_up[0], w_expert_near, 2 * tile)
    hidden_far, slope_far, act_far = forward_rows(
        x_far, w_gate[0], w_up[0], w_expert_far, 2 * tile, earlier=[hidden_near]
    )
    hidden_s, slope_s, act_s = forward_shadow(x_groups, shadow_rows, w_shadow, 2 * tile, earlier=[hidden_far])

    down = jnp.concatenate([w_down[0], shadow_rows[2 * shadow_part :]], axis=0)
    near = jnp.concatenate([hidden_near, hidden_s[: 2 * tok_count]], axis=1)
    far = jnp.concatenate([hidden_far, hidden_s[2 * tok_count :]], axis=1)
    weighted = jnp.concatenate([far[:later], near[:tok_count], far[later:], near[tok_count:]], axis=0)
    parts = 2 if steps % 2 == 0 else 1
    sent = output_other(weighted, down, tp_index, parts, quarter)
    got = [swap_cores(array) for array in sent]

    dy_own = join_plane(tp_index, *dy_plane)
    dy_other = swap_cores(dy_own)
    dy_groups = [(near_own, 1, tok_count), (near_other, 1, tok_count), (dy_own, 0, later), (dy_other, 0, later)]
    pre, pre_s = backward_rows(
        dy_groups, down, [slope_near, slope_far], [act_near, act_far], slope_s, act_s, tile, earlier=sent
    )

    sums, fence = [], ()
    for part in range(parts):
        own, to_x, to_y, diag_top, diag_low = output_own(
            weighted, got[part], down, tp_index, part, quarter, earlier=fence
        )
        half = own.shape[0] // 2
        top = lax.ppermute(diag_top, "tp", along).astype(jnp.float32)
        low = lax.ppermute(diag_low, "tp", across).astype(jnp.float32)
        if part == 0:
            grad_s = shadow_grads(x_groups, dy_groups, pre_s, hidden_s, tile, earlier=[diag_low])
            grad_s = grad_s.reshape(3 * shadow_part, ep_count, block_width).transpose(1, 0, 2)
            grad_s = exchange_start(grad_s)
        to_y = jnp.concatenate([(to_y[:half] + top).astype(jnp.bfloat16), to_y[half:]], axis=0)
        to_x = jnp.concatenate([to_x[:half], (to_x[half:] + low).astype(jnp.bfloat16)], axis=0)
        from_x, from_y = lax.ppermute(to_x, "tp", along), lax.ppermute(to_y, "tp", across)
        fence = (to_x, to_y)
        sums.append((own, from_x, from_y, diag_low, to_x))
    grad_gate, grad_up = input_grads(x_groups, pre, tile, earlier=[sums[0][4], sums[-1][3]])

    def slot_rows(i):
        own, from_x, from_y = sums[i * parts // steps][:3]
        part = slice(i % (steps // parts) * tok_count, (i % (steps // parts) + 1) * tok_count)
        return own[part] + from_x[part].astype(jnp.float32) + from_y[part].astype(jnp.float32)

    total = slot_rows(steps - 1)
    for s in range(1, steps):
        piece = slot_rows(s - 1).astype(jnp.bfloat16)
        total = total + lax.ppermute(piece, "ep", ring_pairs(ep_count, -2 * s)).astype(jnp.float32)
    mixed = total.astype(jnp.bfloat16)

    hidden = jnp.concatenate([hidden_near, hidden_far], axis=0)
    grad_down = down_grad(dy_groups, hidden, tile, earlier=[sums[-1][4], grad_gate])

    grad_s = exchange_end(after(grad_s, grad_down))
    grad_s_gate = grad_s[:, :shadow_part].reshape(hidden_part, block_width).T
    grad_s_up = grad_s[:, shadow_part : 2 * shadow_part].reshape(hidden_part, block_width).T
    grad_s_down = grad_s[:, 2 * shadow_part :].reshape(hidden_part, block_width)
    return (
        mixed,
        grad_gate[None],
        grad_up[None],
        grad_down[None],
        grad_s_gate,
        grad_s_up,
        grad_s_down,
    )


def solution(mesh):
    tp_count, ep_count = mesh.shape["tp"], mesh.shape["ep"]
    dense = tp_count == 4 and ep_count % 2 == 0 and ep_count <= 8
    return jax.shard_map(
        dense_shards if dense else shards,
        mesh=mesh,
        in_specs=(
            P("ep", "tp"),
            P("ep", "tp"),
            P("ep", None),
            P("ep", None),
            P("ep"),
            P("ep", None, "tp"),
            P("ep", None, "tp"),
            P("ep", "tp", None),
            P("ep", "tp"),
            P("ep", "tp"),
            P("tp", "ep"),
        ),
        out_specs=(
            P("ep", "tp"),
            P("ep", None, "tp"),
            P("ep", None, "tp"),
            P("ep", "tp", None),
            P("ep", "tp"),
            P("ep", "tp"),
            P("tp", "ep"),
        ),
        check_vma=False,
    )
```

```python
import functools
import math

import jax
import jax.numpy as jnp
from jax import lax
from jax.experimental import pallas as pl
from jax.experimental.pallas import tpu as pltpu
from jax.sharding import PartitionSpec as P


def contract_rows(left, right):
    return lax.dot_general(
        left, right, (((0,), (0,)), ((), ())), preferred_element_type=jnp.float32
    )


def split_parts(values):
    upper_part = values.astype(jnp.bfloat16)
    lower_part = (values - upper_part.astype(jnp.float32)).astype(jnp.bfloat16)
    return (upper_part, lower_part)


def weigh_rows(weight_table, rows):
    weight_upper, weight_lower = split_parts(weight_table)
    return jnp.dot(weight_upper, rows, preferred_element_type=jnp.float32) + jnp.dot(
        weight_lower, rows, preferred_element_type=jnp.float32
    )


def expert_pass(rows_x, rows_dout, weight_gate, weight_up, weight_down):
    pre_gate = jnp.dot(rows_x, weight_gate, preferred_element_type=jnp.float32)
    pre_up = jnp.dot(rows_x, weight_up, preferred_element_type=jnp.float32)
    sigmoid_gate = jax.nn.sigmoid(pre_gate)
    activated = pre_gate * sigmoid_gate
    hidden = (activated * pre_up).astype(jnp.bfloat16)
    partial_out = jnp.dot(hidden, weight_down, preferred_element_type=jnp.float32).astype(
        jnp.bfloat16
    )
    hidden_grad = lax.dot_general(
        rows_dout, weight_down, (((1,), (1,)), ((), ())), preferred_element_type=jnp.float32
    )
    grad_pre_gate = (
        hidden_grad * pre_up * sigmoid_gate * (1.0 + pre_gate * (1.0 - sigmoid_gate))
    ).astype(jnp.bfloat16)
    grad_pre_up = (hidden_grad * activated).astype(jnp.bfloat16)
    return (partial_out, hidden, grad_pre_gate, grad_pre_up)


def shards(
    tokens,
    cotangent,
    expert_ids,
    gate_weights,
    shadow_mask,
    w_gate,
    w_up,
    w_down,
    s_gate,
    s_up,
    s_down,
):
    ep_count = lax.axis_size("ep")
    tok_count, top_count = expert_ids.shape
    quarter_width = tokens.shape[1]
    width = quarter_width * lax.axis_size("tp")
    expert_count = w_gate.shape[0] * ep_count
    capacity = (5 * tok_count * top_count + 4 * expert_count - 1) // (4 * expert_count)
    slot_count = expert_count * capacity
    picks_flat = expert_ids.reshape(-1)
    onehot = (picks_flat[:, None] == jnp.arange(expert_count, dtype=jnp.int32)[None, :]).astype(
        jnp.int32
    )
    slot_rank = jnp.sum((jnp.cumsum(onehot, axis=0) - onehot) * onehot, axis=1)
    slot_index = (picks_flat * capacity + slot_rank).reshape(tok_count, top_count)
    matches = jnp.arange(slot_count, dtype=jnp.int32)[:, None, None] == slot_index[None, :, :]
    dispatch = jnp.any(matches, axis=2).astype(jnp.bfloat16)
    weighting = jnp.sum(jnp.where(matches, gate_weights[None, :, :top_count], 0.0), axis=2)
    slot_gate = jnp.sum(weighting, axis=1)
    shadow_weight = gate_weights[:, top_count] * shadow_mask.astype(jnp.float32)
    x_full, dy_full = (
        lax.all_gather(tokens, "tp", axis=1, tiled=True),
        lax.all_gather(cotangent, "tp", axis=1, tiled=True),
    )
    rows_x = jnp.dot(dispatch, tokens, preferred_element_type=jnp.float32).astype(jnp.bfloat16)
    rows_dy = jnp.dot(dispatch, cotangent, preferred_element_type=jnp.float32)
    rows_dout = (slot_gate[:, None] * rows_dy).astype(jnp.bfloat16)
    recv_x, recv_dout = (
        lax.all_to_all(
            rows_x.reshape(ep_count, -1, quarter_width),
            "ep",
            split_axis=0,
            concat_axis=0,
            tiled=True,
        ),
        lax.all_to_all(
            rows_dout.reshape(ep_count, -1, quarter_width),
            "ep",
            split_axis=0,
            concat_axis=0,
            tiled=True,
        ),
    )
    expert_x, expert_dout = (
        lax.all_gather(recv_x.reshape(-1, quarter_width), "tp", axis=1, tiled=True),
        lax.all_gather(recv_dout.reshape(-1, quarter_width), "tp", axis=1, tiled=True),
    )
    partial_out, hidden, grad_pre_gate, grad_pre_up = expert_pass(
        expert_x, expert_dout, w_gate[0], w_up[0], w_down[0]
    )
    grad_gate = contract_rows(expert_x, grad_pre_gate).astype(jnp.bfloat16)[None]
    grad_up = contract_rows(expert_x, grad_pre_up).astype(jnp.bfloat16)[None]
    grad_down = contract_rows(hidden, expert_dout).astype(jnp.bfloat16)[None]
    full_gate, full_up, full_down = (
        lax.all_gather(s_gate, "ep", axis=0, tiled=True),
        lax.all_gather(s_up, "ep", axis=0, tiled=True),
        lax.all_gather(s_down, "ep", axis=1, tiled=True),
    )
    shadow_dout = (shadow_weight[:, None] * dy_full.astype(jnp.float32)).astype(jnp.bfloat16)
    shadow_out, shadow_hidden, shadow_gate_pre, shadow_up_pre = expert_pass(
        x_full, shadow_dout, full_gate, full_up, full_down
    )
    shadow_sums = lax.psum_scatter(
        jnp.concatenate(
            [
                contract_rows(x_full, shadow_gate_pre),
                contract_rows(x_full, shadow_up_pre),
                contract_rows(shadow_dout, shadow_hidden),
            ],
            axis=1,
        ).astype(jnp.bfloat16),
        "ep",
        scatter_dimension=0,
        tiled=True,
    ).astype(jnp.float32)
    hidden_part = s_gate.shape[1]
    grad_s_gate = shadow_sums[:, :hidden_part].astype(jnp.bfloat16)
    grad_s_up = shadow_sums[:, hidden_part : 2 * hidden_part].astype(jnp.bfloat16)
    grad_s_down = shadow_sums[:, 2 * hidden_part :].T.astype(jnp.bfloat16)
    back_rows = lax.all_to_all(
        partial_out.reshape(ep_count, -1, width), "ep", split_axis=0, concat_axis=0, tiled=True
    ).reshape(-1, width)
    term = weigh_rows(weighting.T, back_rows)
    term = term + shadow_weight[:, None] * shadow_out.astype(jnp.float32)
    mixed = lax.psum_scatter(term.astype(jnp.bfloat16), "tp", scatter_dimension=1, tiled=True)
    return (mixed, grad_gate, grad_up, grad_down, grad_s_gate, grad_s_up, grad_s_down)


ANY = pl.BlockSpec(memory_space=pl.ANY)
VMEM_LIMIT = 48 * 1024 * 1024


def swap_pairs(count, bit):
    return [(i, i ^ bit) for i in range(count)]


def ring_pairs(count, shift):
    return [(i, (i + shift) % count) for i in range(count)]


def dot32(left, right):
    return jnp.dot(left, right, preferred_element_type=jnp.float32)


def contract_last(left, right):
    return lax.dot_general(
        left, right, (((1,), (1,)), ((), ())), preferred_element_type=jnp.float32
    )


def shape_of(*dims, dtype=jnp.bfloat16):
    return jax.ShapeDtypeStruct(dims, dtype)


def after(arrays, *earlier):
    def nothing(*refs):
        del refs

    count = len(arrays)
    return pl.pallas_call(
        nothing,
        out_shape=[jax.ShapeDtypeStruct(a.shape, a.dtype) for a in arrays],
        in_specs=[ANY] * (count + len(earlier)),
        out_specs=[ANY] * count,
        input_output_aliases={i: i for i in range(count)},
        cost_estimate=pl.CostEstimate(flops=0, bytes_accessed=0, transcendentals=0),
        name="after",
    )(*arrays, *earlier)


def kernel_call(body, grid, in_specs, out_specs, out_shape, operands, scratch, flops, name, column=None, earlier=()):
    count = len(operands)

    def run(column_ref, *refs):
        del column_ref
        body(*refs[:count], *refs[count + len(earlier) :])

    column = jnp.zeros((1,), jnp.int32) if column is None else column.reshape(1).astype(jnp.int32)
    moved = sum(a.size * a.dtype.itemsize for a in operands)
    moved += sum(math.prod(a.shape) * a.dtype.itemsize for a in out_shape)
    return pl.pallas_call(
        run,
        out_shape=out_shape,
        grid_spec=pltpu.PrefetchScalarGridSpec(
            num_scalar_prefetch=1,
            grid=grid,
            in_specs=list(in_specs) + [ANY] * len(earlier),
            out_specs=out_specs,
            scratch_shapes=scratch,
        ),
        compiler_params=pltpu.CompilerParams(vmem_limit_bytes=VMEM_LIMIT),
        cost_estimate=pl.CostEstimate(flops=int(flops), bytes_accessed=int(moved), transcendentals=0),
        name=name,
    )(column, *operands, *earlier)


def whole(array):
    return pl.BlockSpec(array.shape, lambda *_: (0,) * len(array.shape))


def join_plane(column, piece, from_x, from_y, diag_top, diag_low, earlier=()):
    rows, quarter = piece.shape
    chunk = rows // 4

    def body(column_ref, *refs):
        sources, out = refs[:5], refs[-1]
        i = pl.program_id(0)

        def store(own_column, from_diag):
            for bit, source in enumerate(sources[:3] + (from_diag,)):
                place = own_column ^ bit
                out[:, place * quarter : (place + 1) * quarter] = source[...]

        for own_column in range(4):
            here = column_ref[0] == own_column
            pl.when(here & (i < 2))(functools.partial(store, own_column, sources[3]))
            pl.when(here & (i >= 2))(functools.partial(store, own_column, sources[4]))

    spec = pl.BlockSpec((chunk, quarter), lambda i, *_: (i, 0))
    return pl.pallas_call(
        body,
        out_shape=shape_of(rows, 4 * quarter),
        grid_spec=pltpu.PrefetchScalarGridSpec(
            num_scalar_prefetch=1,
            grid=(4,),
            in_specs=[
                spec,
                spec,
                spec,
                pl.BlockSpec((chunk, quarter), lambda i, *_: (jnp.minimum(i, 1), 0)),
                pl.BlockSpec((chunk, quarter), lambda i, *_: (jnp.maximum(i - 2, 0), 0)),
            ]
            + [ANY] * len(earlier),
            out_specs=pl.BlockSpec((chunk, 4 * quarter), lambda i, *_: (i, 0)),
        ),
        cost_estimate=pl.CostEstimate(flops=0, bytes_accessed=16 * rows * quarter, transcendentals=0),
        name="join_plane",
    )(column.reshape(1).astype(jnp.int32), piece, from_x, from_y, diag_top, diag_low, *earlier)


def row_specs(groups, tile):
    def spec(index, rows):
        return pl.BlockSpec((rows, tile), lambda k, *_: (index, k))

    return [spec(index, rows) for _, index, rows in groups]


def apply_gate(pre_gate, pre_up, weight):
    sigmoid_gate = jax.nn.sigmoid(pre_gate)
    activated = pre_gate * sigmoid_gate
    hidden = (weight * activated * pre_up).astype(jnp.bfloat16)
    slope = weight * pre_up * sigmoid_gate * (1.0 + pre_gate * (1.0 - sigmoid_gate))
    return hidden, slope, weight * activated


def forward_rows(groups, w_gate, w_up, weight, tile, earlier=()):
    rows = sum(g[2] for g in groups)
    width, units = w_gate.shape
    steps = width // tile

    def body(*refs):
        n = len(groups)
        gate_ref, up_ref, weight_ref, hidden_ref, slope_ref, act_ref, both, acc = refs[n:]
        step = pl.program_id(0)
        both[:, :units] = gate_ref[...]
        both[:, units:] = up_ref[...]
        start = 0
        for ref, (_, _, count) in zip(refs[:n], groups):
            part = pl.ds(start, count)
            value = dot32(ref[...], both[...])

            @pl.when(step == 0)
            def _():
                acc[part, :] = value

            @pl.when(step > 0)
            def _():
                acc[part, :] += value

            start += count

        @pl.when(step == steps - 1)
        def _():
            chunk = 64

            @pl.loop(0, rows // chunk)
            def _(i):
                part = pl.ds(pl.multiple_of(i * chunk, chunk), chunk)
                hidden, slope, act = apply_gate(acc[part, :units], acc[part, units:], weight_ref[part, :])
                hidden_ref[part, :] = hidden
                slope_ref[part, :] = slope
                act_ref[part, :] = act

    tile_spec = pl.BlockSpec((tile, units), lambda k, *_: (k, 0))
    out_spec = pl.BlockSpec((rows, units), lambda *_: (0, 0))
    return kernel_call(
        body,
        (steps,),
        row_specs(groups, tile) + [tile_spec, tile_spec, whole(weight)],
        [out_spec] * 3,
        [shape_of(rows, units), shape_of(rows, units, dtype=jnp.float32), shape_of(rows, units, dtype=jnp.float32)],
        [g[0] for g in groups] + [w_gate, w_up, weight],
        [pltpu.VMEM((tile, 2 * units), jnp.bfloat16), pltpu.VMEM((rows, 2 * units), jnp.float32)],
        4 * rows * width * units,
        "forward_rows",
        earlier=earlier,
    )


def forward_shadow(groups, shadow_rows, weight, tile, earlier=()):
    rows = sum(g[2] for g in groups)
    width = shadow_rows.shape[1]
    units = shadow_rows.shape[0] // 3
    steps = width // tile
    apart = 128

    def body(*refs):
        n = len(groups)
        rows_ref, weight_ref, hidden_ref, slope_ref, act_ref, both, acc = refs[n:]
        step = pl.program_id(0)

        @pl.when(step == 0)
        def _():
            both[...] = jnp.zeros_like(both)

        both[:units, :] = rows_ref[:units, :]
        both[apart : apart + units, :] = rows_ref[units : 2 * units, :]
        start = 0
        for ref, (_, _, count) in zip(refs[:n], groups):
            part = pl.ds(start, count)
            value = contract_last(ref[...], both[...])

            @pl.when(step == 0)
            def _():
                acc[part, :] = value

            @pl.when(step > 0)
            def _():
                acc[part, :] += value

            start += count

        @pl.when(step == steps - 1)
        def _():
            chunk = 128

            @pl.loop(0, rows // chunk)
            def _(i):
                part = pl.ds(pl.multiple_of(i * chunk, chunk), chunk)
                hidden, slope, act = apply_gate(acc[part, :apart], acc[part, apart:], weight_ref[part, :])
                hidden_ref[part, :] = hidden[:, :units]
                slope_ref[part, :] = slope[:, :units]
                act_ref[part, :] = act[:, :units]

    out_spec = pl.BlockSpec((rows, units), lambda *_: (0, 0))
    return kernel_call(
        body,
        (steps,),
        row_specs(groups, tile) + [pl.BlockSpec((3 * units, tile), lambda k, *_: (0, k)), whole(weight)],
        [out_spec] * 3,
        [shape_of(rows, units), shape_of(rows, units, dtype=jnp.float32), shape_of(rows, units, dtype=jnp.float32)],
        [g[0] for g in groups] + [shadow_rows, weight],
        [pltpu.VMEM((2 * apart, tile), jnp.bfloat16), pltpu.VMEM((rows, 2 * apart), jnp.float32)],
        4 * rows * width * apart,
        "forward_shadow",
        earlier=earlier,
    )


def output_other(weighted, down, column, parts, quarter, earlier=()):
    rows, units = weighted.shape
    count = rows // 2 // parts

    def body(weighted_ref, down_ref, *outs):
        for i, out in enumerate(outs):
            out[...] = dot32(weighted_ref[i * count : (i + 1) * count, :], down_ref[...]).astype(jnp.bfloat16)

    return kernel_call(
        body,
        (4,),
        [
            pl.BlockSpec((rows // 2, units), lambda *_: (1, 0)),
            pl.BlockSpec((units, quarter), lambda q, column_ref: (0, column_ref[0] ^ q)),
        ],
        [pl.BlockSpec((count, quarter), lambda q, *_: (0, q))] * parts,
        [shape_of(count, 4 * quarter)] * parts,
        [weighted, down],
        [],
        rows * units * quarter * 4,
        "output_other",
        column=column,
        earlier=earlier,
    )


def output_own(weighted, got, down, column, part, quarter, earlier=()):
    count, units = got.shape[0], weighted.shape[1]
    half = count // 2

    def body(weighted_ref, got_ref, down_ref, own, to_x, to_y, diag_top, diag_low):
        q = pl.program_id(0)
        value = dot32(weighted_ref[...], down_ref[...]) + got_ref[...].astype(jnp.float32)

        @pl.when(q == 0)
        def _():
            own[...] = value

        @pl.when(q == 1)
        def _():
            to_x[...] = value.astype(jnp.bfloat16)

        @pl.when(q == 2)
        def _():
            to_y[...] = value.astype(jnp.bfloat16)

        @pl.when(q == 3)
        def _():
            diag_top[...] = value[:half].astype(jnp.bfloat16)
            diag_low[...] = value[half:].astype(jnp.bfloat16)

    full = pl.BlockSpec((count, quarter), lambda *_: (0, 0))
    part_spec = pl.BlockSpec((half, quarter), lambda *_: (0, 0))
    return kernel_call(
        body,
        (4,),
        [
            pl.BlockSpec((count, units), lambda *_: (part, 0)),
            pl.BlockSpec((count, quarter), lambda q, *_: (0, q)),
            pl.BlockSpec((units, quarter), lambda q, column_ref: (0, column_ref[0] ^ q)),
        ],
        [full, full, full, part_spec, part_spec],
        [shape_of(count, quarter, dtype=jnp.float32), shape_of(count, quarter), shape_of(count, quarter)]
        + [shape_of(half, quarter)] * 2,
        [weighted, got, down],
        [],
        2 * count * units * quarter * 4,
        "output_own",
        column=column,
        earlier=earlier,
    )


def backward_rows(groups, down, slopes, acts, slope_s, act_s, tile, earlier=()):
    rows = sum(g[2] for g in groups)
    units_all, width = down.shape
    units = slopes[0].shape[1]
    units_s = units_all - units
    steps = width // tile
    apart = 128
    firsts = [0]
    for slope in slopes:
        firsts.append(firsts[-1] + slope.shape[0])

    def body(*refs):
        n, m = len(groups), len(slopes)
        down_ref = refs[n]
        slope_refs, act_refs = refs[n + 1 : n + 1 + m], refs[n + 1 + m : n + 1 + 2 * m]
        slope_s_ref, act_s_ref, pre_ref, pre_s_ref, acc = refs[n + 1 + 2 * m :]
        step = pl.program_id(0)
        start = 0
        for ref, (_, _, count) in zip(refs[:n], groups):
            part = pl.ds(start, count)
            value = contract_last(ref[...], down_ref[...])

            @pl.when(step == 0)
            def _():
                acc[part, :] = value

            @pl.when(step > 0)
            def _():
                acc[part, :] += value

            start += count

        @pl.when(step == steps - 1)
        def _():
            chunk = 64
            for j in range(m):

                @pl.loop(0, slopes[j].shape[0] // chunk)
                def _(i):
                    source = pl.ds(pl.multiple_of(i * chunk, chunk), chunk)
                    part = pl.ds(pl.multiple_of(firsts[j] + i * chunk, chunk), chunk)
                    grad = acc[part, :units]
                    pre_ref[part, :units] = (grad * slope_refs[j][source, :]).astype(jnp.bfloat16)
                    pre_ref[part, units:] = (grad * act_refs[j][source, :]).astype(jnp.bfloat16)

            pre_s_ref[...] = jnp.zeros_like(pre_s_ref)

            @pl.loop(0, rows // chunk)
            def _(i):
                part = pl.ds(pl.multiple_of(i * chunk, chunk), chunk)
                grad = acc[part, units:]
                pre_s_ref[part, :units_s] = (grad * slope_s_ref[part, :]).astype(jnp.bfloat16)
                pre_s_ref[part, apart : apart + units_s] = (grad * act_s_ref[part, :]).astype(jnp.bfloat16)

    return kernel_call(
        body,
        (steps,),
        row_specs(groups, tile)
        + [pl.BlockSpec((units_all, tile), lambda k, *_: (0, k))]
        + [whole(a) for a in list(slopes) + list(acts) + [slope_s, act_s]],
        [pl.BlockSpec((rows, 2 * units), lambda *_: (0, 0)), pl.BlockSpec((rows, 2 * apart), lambda *_: (0, 0))],
        [shape_of(rows, 2 * units), shape_of(rows, 2 * apart)],
        [g[0] for g in groups] + [down] + list(slopes) + list(acts) + [slope_s, act_s],
        [pltpu.VMEM((rows, units_all), jnp.float32)],
        2 * rows * width * units_all,
        "backward_rows",
        earlier=earlier,
    )


def stage_rows(refs, groups, held):
    start = 0
    for ref, (_, _, count) in zip(refs, groups):
        held[pl.ds(start, count), :] = ref[...]
        start += count
    return held[...]


def shadow_grads(x_groups, dy_groups, pre_s, hidden_s, tile, earlier=()):
    rows, wide = pre_s.shape
    units = hidden_s.shape[1]
    width = x_groups[0][0].shape[1]
    apart = wide // 2

    def body(*refs):
        n = len(x_groups)
        pre_ref, hidden_ref, out, held = refs[2 * n :]
        value = contract_rows(pre_ref[...], stage_rows(refs[:n], x_groups, held))
        out[:units, :] = value[:units].astype(jnp.bfloat16)
        out[units : 2 * units, :] = value[apart : apart + units].astype(jnp.bfloat16)
        value = contract_rows(hidden_ref[...], stage_rows(refs[n : 2 * n], dy_groups, held))
        out[2 * units :, :] = value.astype(jnp.bfloat16)

    (out,) = kernel_call(
        body,
        (width // tile,),
        row_specs(x_groups, tile) + row_specs(dy_groups, tile) + [whole(pre_s), whole(hidden_s)],
        [pl.BlockSpec((3 * units, tile), lambda k, *_: (0, k))],
        [shape_of(3 * units, width)],
        [g[0] for g in x_groups + dy_groups] + [pre_s, hidden_s],
        [pltpu.VMEM((rows, tile), jnp.bfloat16)],
        2 * rows * width * (wide + units),
        "shadow_grads",
        earlier=earlier,
    )
    return out


def input_grads(groups, pre, tile, earlier=()):
    rows, both = pre.shape
    units = both // 2
    width = groups[0][0].shape[1]

    def body(*refs):
        n = len(groups)
        pre_ref, gate_ref, up_ref, held = refs[n:]
        value = contract_rows(stage_rows(refs[:n], groups, held), pre_ref[...])
        gate_ref[...] = value[:, :units].astype(jnp.bfloat16)
        up_ref[...] = value[:, units:].astype(jnp.bfloat16)

    return kernel_call(
        body,
        (width // tile,),
        row_specs(groups, tile) + [whole(pre)],
        [pl.BlockSpec((tile, units), lambda k, *_: (k, 0))] * 2,
        [shape_of(width, units)] * 2,
        [g[0] for g in groups] + [pre],
        [pltpu.VMEM((rows, tile), jnp.bfloat16)],
        2 * rows * width * both,
        "input_grads",
        earlier=earlier,
    )


def down_grad(groups, hidden, tile, earlier=()):
    rows, units = hidden.shape
    width = groups[0][0].shape[1]

    def body(*refs):
        n = len(groups)
        hidden_ref, out, held = refs[n:]
        out[...] = contract_rows(hidden_ref[...], stage_rows(refs[:n], groups, held)).astype(jnp.bfloat16)

    (out,) = kernel_call(
        body,
        (width // tile,),
        row_specs(groups, tile) + [whole(hidden)],
        [pl.BlockSpec((units, tile), lambda k, *_: (0, k))],
        [shape_of(units, width)],
        [g[0] for g in groups] + [hidden],
        [pltpu.VMEM((rows, tile), jnp.bfloat16)],
        2 * rows * width * units,
        "down_grad",
        earlier=earlier,
    )
    return out


def send_along_z(own):
    ep_count = lax.axis_size("ep")
    return [lax.ppermute(own, "ep", ring_pairs(ep_count, 2 * s)) for s in range(1, ep_count // 2)]


def swap_cores(block):
    return lax.ppermute(block, "ep", swap_pairs(lax.axis_size("ep"), 1))


def send_plane(piece):
    along, across = [swap_pairs(lax.axis_size("tp"), bit) for bit in (1, 2)]
    return piece, lax.ppermute(piece, "tp", along), lax.ppermute(piece, "tp", across)


def send_diagonal(piece, from_x, from_y):
    along, across = [swap_pairs(lax.axis_size("tp"), bit) for bit in (1, 2)]
    half = piece.shape[0] // 2
    diag_top = lax.ppermute(from_x[:half], "tp", across)
    diag_low = lax.ppermute(from_y[half:], "tp", along)
    return piece, from_x, from_y, diag_top, diag_low


def exchange_start(blocks):
    ep_count, me = lax.axis_size("ep"), lax.axis_index("ep")
    chips, chip, core = ep_count // 2, me // 2, me % 2
    pairs = blocks.reshape(chips, 2, *blocks.shape[1:])
    kept = jnp.where(core == 0, pairs[:, 0], pairs[:, 1])
    given = jnp.where(core == 0, pairs[:, 1], pairs[:, 0])
    taken = swap_cores(given)
    both = jnp.stack([jnp.where(core == 0, kept, taken), jnp.where(core == 0, taken, kept)], axis=1)
    pieces = [lax.dynamic_index_in_dim(both, chip, 0)]
    for shift in range(1, chips):
        piece = lax.dynamic_index_in_dim(both, (chip + shift) % chips, 0)
        pieces.append(lax.ppermute(piece, "ep", ring_pairs(ep_count, 2 * shift)))
    return pieces


def exchange_end(pieces):
    chip = lax.axis_index("ep") // 2
    chips = len(pieces)
    result = jnp.zeros((chips,) + pieces[0].shape[1:], pieces[0].dtype)
    for shift, piece in enumerate(pieces):
        result = lax.dynamic_update_slice_in_dim(result, piece, (chip - shift) % chips, 0)
    return result.reshape(2 * chips, *result.shape[2:])


def dense_shards(
    tokens,
    cotangent,
    expert_ids,
    gate_weights,
    shadow_mask,
    w_gate,
    w_up,
    w_down,
    s_gate,
    s_up,
    s_down,
):
    ep_count, tp_count = lax.axis_size("ep"), lax.axis_size("tp")
    ep_index, tp_index = lax.axis_index("ep"), lax.axis_index("tp")
    tok_count, top_count = expert_ids.shape
    quarter = tokens.shape[1]
    width = quarter * tp_count
    hidden_part = w_gate.shape[2]
    shadow_part = hidden_part // ep_count
    block_width = s_gate.shape[0]
    steps = ep_count // 2
    later = (steps - 1) * tok_count
    tile = width // 8
    along, across = swap_pairs(tp_count, 1), swap_pairs(tp_count, 2)

    x_z = send_along_z(tokens)
    near_plane = send_plane(jnp.concatenate([tokens, cotangent], axis=0))
    near_plane = send_diagonal(*near_plane)
    x_z = after(x_z, near_plane[1], near_plane[2])
    x_plane = send_plane(jnp.concatenate(x_z, axis=0))
    near_own = join_plane(tp_index, *near_plane)
    near_other = swap_cores(near_own)

    picked = expert_ids[:, :, None] == jnp.arange(ep_count, dtype=jnp.int32)[None, None, :]
    table = jnp.sum(jnp.where(picked, gate_weights[:, :top_count, None], 0.0), axis=1)
    shadow_weight = gate_weights[:, top_count] * shadow_mask.astype(jnp.float32)
    table = jnp.concatenate([table, shadow_weight[:, None]], axis=1).T
    table = jnp.pad(table, ((0, -(ep_count + 1) % 8), (0, 0)))
    (table,) = after([table], x_z[-1])
    table_own = jnp.concatenate([piece[None] for piece in [table] + send_along_z(table)], axis=0)
    tables = jnp.stack([table_own, swap_cores(table_own)])
    w_expert = lax.dynamic_index_in_dim(tables, ep_index, 2, keepdims=False)
    w_shadow = tables[:, :, ep_count]
    w_expert_near, w_expert_far = w_expert[:, 0].reshape(-1, 1), w_expert[:, 1:].reshape(-1, 1)
    w_shadow = jnp.concatenate([w_shadow[:, 0].reshape(-1, 1), w_shadow[:, 1:].reshape(-1, 1)], axis=0)

    (dy_later,) = after([cotangent], x_z[-1])
    dy_z = send_along_z(dy_later)

    shadow_blocks = jnp.concatenate(
        [
            s_gate.T.reshape(ep_count, shadow_part, block_width),
            s_up.T.reshape(ep_count, shadow_part, block_width),
            s_down.reshape(ep_count, shadow_part, block_width),
        ],
        axis=1,
    )
    (shadow_blocks,) = after([shadow_blocks], dy_z[-1])
    shadow_rows = exchange_end(exchange_start(shadow_blocks))
    shadow_rows = shadow_rows.transpose(1, 0, 2).reshape(-1, width)

    x_near = [(near_own, 0, tok_count), (near_other, 0, tok_count)]
    hidden_near, slope_near, act_near = forward_rows(x_near, w_gate[0], w_up[0], w_expert_near, 2 * tile)
    x_plane = after(x_plane, hidden_near)
    dy_far = after(dy_z, x_plane[1], x_plane[2])
    dy_plane = send_plane(jnp.concatenate(dy_far, axis=0))
    x_own = join_plane(tp_index, *send_diagonal(*x_plane))
    x_other = swap_cores(x_own)
    x_far = [(x_own, 0, later), (x_other, 0, later)]
    x_groups = x_near + x_far
    hidden_far, slope_far, act_far = forward_rows(x_far, w_gate[0], w_up[0], w_expert_far, 2 * tile)
    hidden_s, slope_s, act_s = forward_shadow(x_groups, shadow_rows, w_shadow, 2 * tile, earlier=[hidden_far])

    down = jnp.concatenate([w_down[0], shadow_rows[2 * shadow_part :]], axis=0)
    near = jnp.concatenate([hidden_near, hidden_s[: 2 * tok_count]], axis=1)
    far = jnp.concatenate([hidden_far, hidden_s[2 * tok_count :]], axis=1)
    weighted = jnp.concatenate([far[:later], near[:tok_count], far[later:], near[tok_count:]], axis=0)
    parts = 2 if steps % 2 == 0 else 1
    sent = output_other(weighted, down, tp_index, parts, quarter)
    got = [swap_cores(array) for array in sent]

    dy_plane = send_diagonal(*after(dy_plane, *sent))
    owns = [output_own(weighted, got[part], down, tp_index, part, quarter) for part in range(parts)]
    diagonals = [
        (lax.ppermute(own[3], "tp", along), lax.ppermute(own[4], "tp", across)) for own in owns
    ]

    dy_own = join_plane(tp_index, *dy_plane, earlier=[own[4] for own in owns])
    dy_other = swap_cores(dy_own)
    dy_groups = [(near_own, 1, tok_count), (near_other, 1, tok_count), (dy_own, 0, later), (dy_other, 0, later)]

    sums, fence = [], [dy_own]
    for part in range(parts):
        own, to_x, to_y, _, _ = owns[part]
        half = own.shape[0] // 2
        top, low = after(diagonals[part], *fence)
        to_y = jnp.concatenate(
            [(to_y[:half].astype(jnp.float32) + top.astype(jnp.float32)).astype(jnp.bfloat16), to_y[half:]], axis=0
        )
        to_x = jnp.concatenate(
            [to_x[:half], (to_x[half:].astype(jnp.float32) + low.astype(jnp.float32)).astype(jnp.bfloat16)], axis=0
        )
        from_x, from_y = lax.ppermute(to_x, "tp", along), lax.ppermute(to_y, "tp", across)
        sums.append((own, from_x, from_y))
        if part == 0:
            pre, pre_s = backward_rows(
                dy_groups, down, [slope_near, slope_far], [act_near, act_far], slope_s, act_s, tile,
                earlier=[to_x, to_y],
            )
        if part == parts - 1:
            grad_s = shadow_grads(x_groups, dy_groups, pre_s, hidden_s, tile, earlier=[to_x, to_y])
        fence = [pre]
    grad_s = grad_s.reshape(3 * shadow_part, ep_count, block_width).transpose(1, 0, 2)
    grad_s = exchange_start(grad_s)
    from_first = sums[0][1]
    grad_gate, grad_up = input_grads(x_groups, pre, tile, earlier=[grad_s[0], from_first])

    def slot_rows(i):
        own, from_x, from_y = sums[i * parts // steps][:3]
        part = slice(i % (steps // parts) * tok_count, (i % (steps // parts) + 1) * tok_count)
        return own[part] + from_x[part].astype(jnp.float32) + from_y[part].astype(jnp.float32)

    total = slot_rows(steps - 1)
    for s in range(1, steps):
        piece = slot_rows(s - 1).astype(jnp.bfloat16)
        total = total + lax.ppermute(piece, "ep", ring_pairs(ep_count, -2 * s)).astype(jnp.float32)
    mixed = total.astype(jnp.bfloat16)

    hidden = jnp.concatenate([hidden_near, hidden_far], axis=0)
    grad_down = down_grad(dy_groups, hidden, tile, earlier=[grad_gate, sums[-1][1]])

    grad_s = exchange_end(after(grad_s, grad_down))
    grad_s_gate = grad_s[:, :shadow_part].reshape(hidden_part, block_width).T
    grad_s_up = grad_s[:, shadow_part : 2 * shadow_part].reshape(hidden_part, block_width).T
    grad_s_down = grad_s[:, 2 * shadow_part :].reshape(hidden_part, block_width)
    return (
        mixed,
        grad_gate[None],
        grad_up[None],
        grad_down[None],
        grad_s_gate,
        grad_s_up,
        grad_s_down,
    )


def solution(mesh):
    tp_count, ep_count = mesh.shape["tp"], mesh.shape["ep"]
    dense = tp_count == 4 and ep_count % 2 == 0 and ep_count <= 8
    return jax.shard_map(
        dense_shards if dense else shards,
        mesh=mesh,
        in_specs=(
            P("ep", "tp"),
            P("ep", "tp"),
            P("ep", None),
            P("ep", None),
            P("ep"),
            P("ep", None, "tp"),
            P("ep", None, "tp"),
            P("ep", "tp", None),
            P("ep", "tp"),
            P("ep", "tp"),
            P("tp", "ep"),
        ),
        out_specs=(
            P("ep", "tp"),
            P("ep", None, "tp"),
            P("ep", None, "tp"),
            P("ep", "tp", None),
            P("ep", "tp"),
            P("ep", "tp"),
            P("tp", "ep"),
        ),
        check_vma=False,
    )
```

```python
import functools
import math

import jax
import jax.numpy as jnp
from jax import lax
from jax.experimental import pallas as pl
from jax.experimental.pallas import tpu as pltpu
from jax.sharding import PartitionSpec as P


def contract_rows(left, right):
    return lax.dot_general(
        left, right, (((0,), (0,)), ((), ())), preferred_element_type=jnp.float32
    )


def split_parts(values):
    upper_part = values.astype(jnp.bfloat16)
    lower_part = (values - upper_part.astype(jnp.float32)).astype(jnp.bfloat16)
    return (upper_part, lower_part)


def weigh_rows(weight_table, rows):
    weight_upper, weight_lower = split_parts(weight_table)
    return jnp.dot(weight_upper, rows, preferred_element_type=jnp.float32) + jnp.dot(
        weight_lower, rows, preferred_element_type=jnp.float32
    )


def expert_pass(rows_x, rows_dout, weight_gate, weight_up, weight_down):
    pre_gate = jnp.dot(rows_x, weight_gate, preferred_element_type=jnp.float32)
    pre_up = jnp.dot(rows_x, weight_up, preferred_element_type=jnp.float32)
    sigmoid_gate = jax.nn.sigmoid(pre_gate)
    activated = pre_gate * sigmoid_gate
    hidden = (activated * pre_up).astype(jnp.bfloat16)
    partial_out = jnp.dot(hidden, weight_down, preferred_element_type=jnp.float32).astype(
        jnp.bfloat16
    )
    hidden_grad = lax.dot_general(
        rows_dout, weight_down, (((1,), (1,)), ((), ())), preferred_element_type=jnp.float32
    )
    grad_pre_gate = (
        hidden_grad * pre_up * sigmoid_gate * (1.0 + pre_gate * (1.0 - sigmoid_gate))
    ).astype(jnp.bfloat16)
    grad_pre_up = (hidden_grad * activated).astype(jnp.bfloat16)
    return (partial_out, hidden, grad_pre_gate, grad_pre_up)


def shards(
    tokens,
    cotangent,
    expert_ids,
    gate_weights,
    shadow_mask,
    w_gate,
    w_up,
    w_down,
    s_gate,
    s_up,
    s_down,
):
    ep_count = lax.axis_size("ep")
    tok_count, top_count = expert_ids.shape
    quarter_width = tokens.shape[1]
    width = quarter_width * lax.axis_size("tp")
    expert_count = w_gate.shape[0] * ep_count
    capacity = (5 * tok_count * top_count + 4 * expert_count - 1) // (4 * expert_count)
    slot_count = expert_count * capacity
    picks_flat = expert_ids.reshape(-1)
    onehot = (picks_flat[:, None] == jnp.arange(expert_count, dtype=jnp.int32)[None, :]).astype(
        jnp.int32
    )
    slot_rank = jnp.sum((jnp.cumsum(onehot, axis=0) - onehot) * onehot, axis=1)
    slot_index = (picks_flat * capacity + slot_rank).reshape(tok_count, top_count)
    matches = jnp.arange(slot_count, dtype=jnp.int32)[:, None, None] == slot_index[None, :, :]
    dispatch = jnp.any(matches, axis=2).astype(jnp.bfloat16)
    weighting = jnp.sum(jnp.where(matches, gate_weights[None, :, :top_count], 0.0), axis=2)
    slot_gate = jnp.sum(weighting, axis=1)
    shadow_weight = gate_weights[:, top_count] * shadow_mask.astype(jnp.float32)
    x_full, dy_full = (
        lax.all_gather(tokens, "tp", axis=1, tiled=True),
        lax.all_gather(cotangent, "tp", axis=1, tiled=True),
    )
    rows_x = jnp.dot(dispatch, tokens, preferred_element_type=jnp.float32).astype(jnp.bfloat16)
    rows_dy = jnp.dot(dispatch, cotangent, preferred_element_type=jnp.float32)
    rows_dout = (slot_gate[:, None] * rows_dy).astype(jnp.bfloat16)
    recv_x, recv_dout = (
        lax.all_to_all(
            rows_x.reshape(ep_count, -1, quarter_width),
            "ep",
            split_axis=0,
            concat_axis=0,
            tiled=True,
        ),
        lax.all_to_all(
            rows_dout.reshape(ep_count, -1, quarter_width),
            "ep",
            split_axis=0,
            concat_axis=0,
            tiled=True,
        ),
    )
    expert_x, expert_dout = (
        lax.all_gather(recv_x.reshape(-1, quarter_width), "tp", axis=1, tiled=True),
        lax.all_gather(recv_dout.reshape(-1, quarter_width), "tp", axis=1, tiled=True),
    )
    partial_out, hidden, grad_pre_gate, grad_pre_up = expert_pass(
        expert_x, expert_dout, w_gate[0], w_up[0], w_down[0]
    )
    grad_gate = contract_rows(expert_x, grad_pre_gate).astype(jnp.bfloat16)[None]
    grad_up = contract_rows(expert_x, grad_pre_up).astype(jnp.bfloat16)[None]
    grad_down = contract_rows(hidden, expert_dout).astype(jnp.bfloat16)[None]
    full_gate, full_up, full_down = (
        lax.all_gather(s_gate, "ep", axis=0, tiled=True),
        lax.all_gather(s_up, "ep", axis=0, tiled=True),
        lax.all_gather(s_down, "ep", axis=1, tiled=True),
    )
    shadow_dout = (shadow_weight[:, None] * dy_full.astype(jnp.float32)).astype(jnp.bfloat16)
    shadow_out, shadow_hidden, shadow_gate_pre, shadow_up_pre = expert_pass(
        x_full, shadow_dout, full_gate, full_up, full_down
    )
    shadow_sums = lax.psum_scatter(
        jnp.concatenate(
            [
                contract_rows(x_full, shadow_gate_pre),
                contract_rows(x_full, shadow_up_pre),
                contract_rows(shadow_dout, shadow_hidden),
            ],
            axis=1,
        ).astype(jnp.bfloat16),
        "ep",
        scatter_dimension=0,
        tiled=True,
    ).astype(jnp.float32)
    hidden_part = s_gate.shape[1]
    grad_s_gate = shadow_sums[:, :hidden_part].astype(jnp.bfloat16)
    grad_s_up = shadow_sums[:, hidden_part : 2 * hidden_part].astype(jnp.bfloat16)
    grad_s_down = shadow_sums[:, 2 * hidden_part :].T.astype(jnp.bfloat16)
    back_rows = lax.all_to_all(
        partial_out.reshape(ep_count, -1, width), "ep", split_axis=0, concat_axis=0, tiled=True
    ).reshape(-1, width)
    term = weigh_rows(weighting.T, back_rows)
    term = term + shadow_weight[:, None] * shadow_out.astype(jnp.float32)
    mixed = lax.psum_scatter(term.astype(jnp.bfloat16), "tp", scatter_dimension=1, tiled=True)
    return (mixed, grad_gate, grad_up, grad_down, grad_s_gate, grad_s_up, grad_s_down)


ANY = pl.BlockSpec(memory_space=pl.ANY)
VMEM_LIMIT = 48 * 1024 * 1024
SHORT = pl.CostEstimate(flops=1, bytes_accessed=1, transcendentals=0)


def swap_pairs(count, bit):
    return [(i, i ^ bit) for i in range(count)]


def ring_pairs(count, shift):
    return [(i, (i + shift) % count) for i in range(count)]


def dot32(left, right):
    return jnp.dot(left, right, preferred_element_type=jnp.float32)


def contract_last(left, right):
    return lax.dot_general(
        left, right, (((1,), (1,)), ((), ())), preferred_element_type=jnp.float32
    )


def shape_of(*dims, dtype=jnp.bfloat16):
    return jax.ShapeDtypeStruct(dims, dtype)


def after(arrays, *earlier):
    def nothing(*refs):
        del refs

    count = len(arrays)
    return pl.pallas_call(
        nothing,
        out_shape=[jax.ShapeDtypeStruct(a.shape, a.dtype) for a in arrays],
        in_specs=[ANY] * (count + len(earlier)),
        out_specs=[ANY] * count,
        input_output_aliases={i: i for i in range(count)},
        cost_estimate=SHORT,
        name="after",
    )(*arrays, *earlier)


def kernel_call(body, grid, in_specs, out_specs, out_shape, operands, scratch, name, column=None, earlier=()):
    count = len(operands)

    def run(column_ref, *refs):
        del column_ref
        body(*refs[:count], *refs[count + len(earlier) :])

    column = jnp.zeros((1,), jnp.int32) if column is None else column.reshape(1).astype(jnp.int32)
    return pl.pallas_call(
        run,
        out_shape=out_shape,
        grid_spec=pltpu.PrefetchScalarGridSpec(
            num_scalar_prefetch=1,
            grid=grid,
            in_specs=list(in_specs) + [ANY] * len(earlier),
            out_specs=out_specs,
            scratch_shapes=scratch,
        ),
        compiler_params=pltpu.CompilerParams(vmem_limit_bytes=VMEM_LIMIT),
        cost_estimate=SHORT,
        name=name,
    )(column, *operands, *earlier)


def whole(array):
    return pl.BlockSpec(array.shape, lambda *_: (0,) * len(array.shape))


def join_plane(column, piece, from_x, from_y, *diagonal, earlier=()):
    rows, quarter = piece.shape
    chunk = rows // 4
    per = 4 // len(diagonal)

    def body(*refs):
        column_ref, sources, out = refs[0], refs[1:4], refs[-1]
        diagonal_refs = refs[4 : 4 + len(diagonal)]
        i = pl.program_id(0)

        def store(own_column, from_diag):
            for bit, source in enumerate(sources + (from_diag,)):
                place = own_column ^ bit
                out[:, place * quarter : (place + 1) * quarter] = source[...]

        for own_column in range(4):
            for j, from_diag in enumerate(diagonal_refs):
                here = (column_ref[0] == own_column) & (i // per == j)
                pl.when(here)(functools.partial(store, own_column, from_diag))

    def diagonal_spec(j):
        return pl.BlockSpec((chunk, quarter), lambda i, *_: (jnp.clip(i - j * per, 0, per - 1), 0))

    spec = pl.BlockSpec((chunk, quarter), lambda i, *_: (i, 0))
    return pl.pallas_call(
        body,
        out_shape=shape_of(rows, 4 * quarter),
        grid_spec=pltpu.PrefetchScalarGridSpec(
            num_scalar_prefetch=1,
            grid=(4,),
            in_specs=[spec] * 3 + [diagonal_spec(j) for j in range(len(diagonal))] + [ANY] * len(earlier),
            out_specs=pl.BlockSpec((chunk, 4 * quarter), lambda i, *_: (i, 0)),
        ),
        compiler_params=pltpu.CompilerParams(vmem_limit_bytes=16 * 1024 * 1024),
        cost_estimate=SHORT,
        name="join_plane",
    )(column.reshape(1).astype(jnp.int32), piece, from_x, from_y, *diagonal, *earlier)


def stack_pieces(pieces):
    rows, columns = pieces[0].shape

    def body(*refs):
        for i, ref in enumerate(refs[:-1]):
            @pl.when(pl.program_id(0) == i)
            def _():
                refs[-1][...] = ref[...]

    return pl.pallas_call(
        body,
        out_shape=shape_of(len(pieces) * rows, columns),
        grid=(len(pieces),),
        in_specs=[pl.BlockSpec((rows, columns), lambda i: (0, 0))] * len(pieces),
        out_specs=pl.BlockSpec((rows, columns), lambda i: (i, 0)),
        cost_estimate=SHORT,
        name="stack_pieces",
    )(*pieces)


def row_specs(groups, tile):
    def spec(index, rows):
        return pl.BlockSpec((rows, tile), lambda k, *_: (index, k))

    return [spec(index, rows) for _, index, rows in groups]


def apply_gate(pre_gate, pre_up):
    sigmoid_gate = jax.nn.sigmoid(pre_gate)
    activated = pre_gate * sigmoid_gate
    hidden = (activated * pre_up).astype(jnp.bfloat16)
    return hidden, pre_up * sigmoid_gate * (1.0 + pre_gate * (1.0 - sigmoid_gate)), activated


def clear_first(acc):
    @pl.when(pl.program_id(0) == 0)
    def _():
        acc[...] = jnp.zeros_like(acc)


def forward_rows(groups, w_both, tile, transposed=False, earlier=()):
    rows = sum(g[2] for g in groups)
    if transposed:
        units, width = w_both.shape[0] // 2, w_both.shape[1]
        tile_spec = pl.BlockSpec((2 * units, tile), lambda k, *_: (0, k))
    else:
        width, units = w_both.shape[0], w_both.shape[1] // 2
        tile_spec = pl.BlockSpec((tile, 2 * units), lambda k, *_: (k, 0))
    steps = width // tile

    def body(*refs):
        n = len(groups)
        both_ref, hidden_ref, slope_ref, act_ref, acc = refs[n:]
        clear_first(acc)
        start = 0
        for ref, (_, _, count) in zip(refs[:n], groups):
            part = pl.ds(start, count)
            if transposed:
                acc[part, :] += contract_last(ref[...], both_ref[...])
            else:
                acc[part, :] += dot32(ref[...], both_ref[...])
            start += count

        @pl.when(pl.program_id(0) == steps - 1)
        def _():
            chunk = 64

            @pl.loop(0, rows // chunk)
            def _(i):
                part = pl.ds(pl.multiple_of(i * chunk, chunk), chunk)
                hidden, slope, act = apply_gate(acc[part, :units], acc[part, units:])
                hidden_ref[part, :] = hidden
                slope_ref[part, :] = slope
                act_ref[part, :] = act

    out_spec = pl.BlockSpec((rows, units), lambda *_: (0, 0))
    return kernel_call(
        body,
        (steps,),
        row_specs(groups, tile) + [tile_spec],
        [out_spec] * 3,
        [shape_of(rows, units), shape_of(rows, units, dtype=jnp.float32), shape_of(rows, units, dtype=jnp.float32)],
        [g[0] for g in groups] + [w_both],
        [pltpu.VMEM((rows, 2 * units), jnp.float32)],
        "forward_rows",
        earlier=earlier,
    )


def output_other(weighted, down, column, parts, quarter, earlier=()):
    rows, units = weighted.shape
    count = rows // 2 // parts

    def body(weighted_ref, down_ref, *outs):
        for i, out in enumerate(outs):
            out[...] = dot32(weighted_ref[i * count : (i + 1) * count, :], down_ref[...]).astype(jnp.bfloat16)

    return kernel_call(
        body,
        (4,),
        [
            pl.BlockSpec((rows // 2, units), lambda *_: (1, 0)),
            pl.BlockSpec((units, quarter), lambda q, column_ref: (0, column_ref[0] ^ q)),
        ],
        [pl.BlockSpec((count, quarter), lambda q, *_: (0, q))] * parts,
        [shape_of(count, 4 * quarter)] * parts,
        [weighted, down],
        [],
        "output_other",
        column=column,
        earlier=earlier,
    )


def output_own(weighted, got, down, column, quarter, earlier=()):
    count, units = got[0].shape[0], weighted.shape[1]
    half, parts = count // 2, len(got)

    def body(weighted_ref, down_ref, *refs):
        q = pl.program_id(0)
        for i in range(parts):
            own, to_x, to_y, diag_top, diag_low = refs[parts + 5 * i : parts + 5 * i + 5]
            value = dot32(weighted_ref[i * count : (i + 1) * count, :], down_ref[...])
            value = value + refs[i][...].astype(jnp.float32)

            @pl.when(q == 3)
            def _():
                own[...] = value

            @pl.when(q == 2)
            def _():
                to_x[...] = value.astype(jnp.bfloat16)

            @pl.when(q == 1)
            def _():
                to_y[...] = value.astype(jnp.bfloat16)

            @pl.when(q == 0)
            def _():
                diag_top[...] = value[:half].astype(jnp.bfloat16)
                diag_low[...] = value[half:].astype(jnp.bfloat16)

    full = pl.BlockSpec((count, quarter), lambda *_: (0, 0))
    part_spec = pl.BlockSpec((half, quarter), lambda *_: (0, 0))
    out = kernel_call(
        body,
        (4,),
        [
            pl.BlockSpec((parts * count, units), lambda *_: (0, 0)),
            pl.BlockSpec((units, quarter), lambda q, column_ref: (0, column_ref[0] ^ 3 ^ q)),
        ]
        + [pl.BlockSpec((count, quarter), lambda q, *_: (0, 3 - q))] * parts,
        [full, full, full, part_spec, part_spec] * parts,
        (
            [shape_of(count, quarter, dtype=jnp.float32), shape_of(count, quarter), shape_of(count, quarter)]
            + [shape_of(half, quarter)] * 2
        )
        * parts,
        [weighted, down] + list(got),
        [],
        "output_own",
        column=column,
        earlier=earlier,
    )
    return [out[5 * i : 5 * i + 5] for i in range(parts)]


def backward_rows(groups, down, parts, slope_s, act_s, w_rows, w_shadow, tile, earlier=()):
    rows = sum(g[2] for g in groups)
    units_all, width = down.shape
    units_s = slope_s.shape[1]
    units = units_all - units_s
    steps = width // tile
    arrays = list({id(a): a for part in parts for a in part[:2]}.values())
    places = [[next(i for i, a in enumerate(arrays) if a is b) for b in part[:2]] for part in parts]

    def body(*refs):
        n, m = len(groups), len(arrays)
        down_ref = refs[n]
        array_refs = refs[n + 1 : n + 1 + m]
        slope_s_ref, act_s_ref, w_ref, w_s_ref, pre_ref, pre_s_ref, acc = refs[n + 1 + m :]
        clear_first(acc)
        start = 0
        for ref, (_, _, count) in zip(refs[:n], groups):
            acc[pl.ds(start, count), :] += contract_last(ref[...], down_ref[...])
            start += count

        @pl.when(pl.program_id(0) == steps - 1)
        def _():
            chunk = 64
            start = 0
            for (_, _, count), (_, _, first), (slope_at, act_at) in zip(groups, parts, places):

                @pl.loop(0, count // chunk)
                def _(i, start=start, first=first, slope_ref=array_refs[slope_at], act_ref=array_refs[act_at]):
                    source = pl.ds(pl.multiple_of(first + i * chunk, chunk), chunk)
                    part = pl.ds(pl.multiple_of(start + i * chunk, chunk), chunk)
                    grad = acc[part, :units] * w_ref[part, :]
                    pre_ref[part, :units] = (grad * slope_ref[source, :]).astype(jnp.bfloat16)
                    pre_ref[part, units:] = (grad * act_ref[source, :]).astype(jnp.bfloat16)
                    grad = acc[part, units:] * w_s_ref[part, :]
                    pre_s_ref[part, :units_s] = (grad * slope_s_ref[part, :]).astype(jnp.bfloat16)
                    pre_s_ref[part, units_s:] = (grad * act_s_ref[part, :]).astype(jnp.bfloat16)

                start += count

    extra = arrays + [slope_s, act_s, w_rows, w_shadow]
    return kernel_call(
        body,
        (steps,),
        row_specs(groups, tile) + [pl.BlockSpec((units_all, tile), lambda k, *_: (0, k))] + [whole(a) for a in extra],
        [pl.BlockSpec((rows, 2 * units), lambda *_: (0, 0)), pl.BlockSpec((rows, 2 * units_s), lambda *_: (0, 0))],
        [shape_of(rows, 2 * units), shape_of(rows, 2 * units_s)],
        [g[0] for g in groups] + [down] + extra,
        [pltpu.VMEM((rows, units_all), jnp.float32)],
        "backward_rows",
        earlier=earlier,
    )


def stage_rows(refs, groups, held):
    start = 0
    for ref, (_, _, count) in zip(refs, groups):
        held[pl.ds(start, count), :] = ref[...]
        start += count
    return held[...]


def shadow_grads(x_groups, dy_groups, pre_s, weighted, units, tile, earlier=()):
    rows, wide = pre_s.shape
    apart = wide // 2
    width = x_groups[0][0].shape[1]

    def body(*refs):
        n = len(x_groups)
        pre_ref, hidden_ref, out, held, pre_t, hidden_t = refs[2 * n :]

        @pl.when(pl.program_id(0) == 0)
        def _():
            pre_t[...] = pre_ref[...].T
            hidden_t[...] = hidden_ref[...].T

        value = dot32(pre_t[...], stage_rows(refs[:n], x_groups, held))
        out[:units, :] = value[:units].astype(jnp.bfloat16)
        out[units : 2 * units, :] = value[apart : apart + units].astype(jnp.bfloat16)
        value = dot32(hidden_t[...], stage_rows(refs[n : 2 * n], dy_groups, held))
        out[2 * units :, :] = value[:units].astype(jnp.bfloat16)

    (out,) = kernel_call(
        body,
        (width // tile,),
        row_specs(x_groups, tile)
        + row_specs(dy_groups, tile)
        + [whole(pre_s), pl.BlockSpec((rows, apart), lambda *_: (0, weighted.shape[1] // apart - 1))],
        [pl.BlockSpec((3 * units, tile), lambda k, *_: (0, k))],
        [shape_of(3 * units, width)],
        [g[0] for g in x_groups + dy_groups] + [pre_s, weighted],
        [
            pltpu.VMEM((rows, tile), jnp.bfloat16),
            pltpu.VMEM((wide, rows), jnp.bfloat16),
            pltpu.VMEM((apart, rows), jnp.bfloat16),
        ],
        "shadow_grads",
        earlier=earlier,
    )
    return out


def input_grads(groups, pre, tile, earlier=()):
    rows, both = pre.shape
    units = both // 2
    width = groups[0][0].shape[1]

    def body(*refs):
        n = len(groups)
        pre_ref, gate_ref, up_ref, held = refs[n:]
        value = contract_rows(stage_rows(refs[:n], groups, held), pre_ref[...])
        gate_ref[...] = value[:, :units].astype(jnp.bfloat16)
        up_ref[...] = value[:, units:].astype(jnp.bfloat16)

    return kernel_call(
        body,
        (width // tile,),
        row_specs(groups, tile) + [whole(pre)],
        [pl.BlockSpec((tile, units), lambda k, *_: (k, 0))] * 2,
        [shape_of(width, units)] * 2,
        [g[0] for g in groups] + [pre],
        [pltpu.VMEM((rows, tile), jnp.bfloat16)],
        "input_grads",
        earlier=earlier,
    )


def down_grad(groups, weighted, units, tile, earlier=()):
    rows = weighted.shape[0]
    width = groups[0][0].shape[1]

    def body(*refs):
        n = len(groups)
        hidden_ref, out, held, hidden_t = refs[n:]

        @pl.when(pl.program_id(0) == 0)
        def _():
            hidden_t[...] = hidden_ref[...].T

        out[...] = dot32(hidden_t[...], stage_rows(refs[:n], groups, held)).astype(jnp.bfloat16)

    (out,) = kernel_call(
        body,
        (width // tile,),
        row_specs(groups, tile) + [pl.BlockSpec((rows, units), lambda *_: (0, 0))],
        [pl.BlockSpec((units, tile), lambda k, *_: (0, k))],
        [shape_of(units, width)],
        [g[0] for g in groups] + [weighted],
        [pltpu.VMEM((rows, tile), jnp.bfloat16), pltpu.VMEM((units, rows), jnp.bfloat16)],
        "down_grad",
        earlier=earlier,
    )
    return out


def send_along_z(own):
    ep_count = lax.axis_size("ep")
    return [lax.ppermute(own, "ep", ring_pairs(ep_count, 2 * s)) for s in range(1, ep_count // 2)]


def swap_cores(block):
    return lax.ppermute(block, "ep", swap_pairs(lax.axis_size("ep"), 1))


def send_plane(piece, bits=(1, 2)):
    return [lax.ppermute(piece, "tp", swap_pairs(lax.axis_size("tp"), bit)) for bit in bits]


def send_diagonal(from_x, from_y):
    along, across = [swap_pairs(lax.axis_size("tp"), bit) for bit in (1, 2)]
    half = from_x.shape[0] // 2
    return lax.ppermute(from_x[:half], "tp", across), lax.ppermute(from_y[half:], "tp", along)


def exchange_cores(blocks):
    ep_count, core = lax.axis_size("ep"), lax.axis_index("ep") % 2
    pairs = blocks.reshape(ep_count // 2, 2, *blocks.shape[1:])
    kept = jnp.where(core == 0, pairs[:, 0], pairs[:, 1])
    given = jnp.where(core == 0, pairs[:, 1], pairs[:, 0])
    return kept, swap_cores(given)


def exchange_chips(kept, taken, earlier=()):
    ep_count, me = lax.axis_size("ep"), lax.axis_index("ep")
    chips, chip, core = ep_count // 2, me // 2, me % 2
    both = jnp.stack([jnp.where(core == 0, kept, taken), jnp.where(core == 0, taken, kept)], axis=1)
    pieces = [lax.dynamic_index_in_dim(both, (chip + shift) % chips, 0) for shift in range(chips)]
    if earlier:
        pieces = after(pieces, *earlier)
    return list(pieces[:1]) + [
        lax.ppermute(pieces[shift], "ep", ring_pairs(ep_count, 2 * shift)) for shift in range(1, chips)
    ]


def exchange_end(pieces):
    chip = lax.axis_index("ep") // 2
    chips = len(pieces)
    result = jnp.zeros((chips,) + pieces[0].shape[1:], pieces[0].dtype)
    for shift, piece in enumerate(pieces):
        result = lax.dynamic_update_slice_in_dim(result, piece, (chip - shift) % chips, 0)
    return result.reshape(2 * chips, *result.shape[2:])


def dense_shards(
    tokens,
    cotangent,
    expert_ids,
    gate_weights,
    shadow_mask,
    w_gate,
    w_up,
    w_down,
    s_gate,
    s_up,
    s_down,
):
    ep_count, tp_count = lax.axis_size("ep"), lax.axis_size("tp")
    ep_index, tp_index = lax.axis_index("ep"), lax.axis_index("tp")
    tok_count, top_count = expert_ids.shape
    quarter = tokens.shape[1]
    width = quarter * tp_count
    hidden_part = w_gate.shape[2]
    shadow_part = hidden_part // ep_count
    block_width = s_gate.shape[0]
    steps = ep_count // 2
    later = (steps - 1) * tok_count
    tile = width // 8
    along, across = swap_pairs(tp_count, 1), swap_pairs(tp_count, 2)

    x_z = send_along_z(tokens)
    near = jnp.concatenate([tokens, cotangent], axis=0)
    near_plane = send_plane(near, bits=(1, 2, 3))
    w_both = jnp.concatenate([w_gate[0], w_up[0]], axis=1)
    *x_z, near_x, near_y, near_d = after(x_z + near_plane, w_both)

    x_piece = stack_pieces(x_z)
    x_plane = send_plane(x_piece)
    (dy_first,) = after([cotangent], x_z[0])
    dy_z = send_along_z(dy_first)
    near_own = join_plane(tp_index, near, near_x, near_y, near_d)
    near_other = swap_cores(near_own)
    x_near = [(near_own, 0, tok_count), (near_other, 0, tok_count)]
    hidden_near, slope_near, act_near = forward_rows(x_near, w_both, 2 * tile)
    fenced = after([*x_plane, *dy_z], hidden_near)
    x_plane, dy_z = fenced[:2], fenced[2:]

    x_diagonal = send_diagonal(*x_plane)
    dy_piece = stack_pieces(dy_z)
    dy_plane = send_plane(dy_piece)
    picked = expert_ids[None, :, :] == jnp.arange(ep_count, dtype=jnp.int32)[:, None, None]
    table = jnp.sum(jnp.where(picked, gate_weights[None, :, :top_count], 0.0), axis=2)
    shadow_weight = gate_weights[:, top_count] * shadow_mask.astype(jnp.float32)
    table = jnp.concatenate([table, jnp.broadcast_to(shadow_weight[None], table.shape)], axis=1)
    table = jnp.concatenate(split_parts(table), axis=1)
    spare = -table.shape[1] % (16 * block_width)
    table_rows = (table.shape[1] + spare) // block_width
    table = jnp.pad(table, ((0, 0), (0, spare))).reshape(ep_count, table_rows, block_width)
    shadow_blocks = jnp.concatenate(
        [
            s_gate.T.reshape(ep_count, shadow_part, block_width),
            s_up.T.reshape(ep_count, shadow_part, block_width),
            s_down.reshape(ep_count, shadow_part, block_width),
            table,
        ],
        axis=1,
    )
    (shadow_blocks,) = after([shadow_blocks], dy_z[0])
    shadow_pieces = exchange_chips(*exchange_cores(shadow_blocks))
    x_own = join_plane(tp_index, x_piece, *x_plane, *x_diagonal, earlier=[dy_piece])
    x_other = swap_cores(x_own)
    dy_plane = after(dy_plane, x_own)

    x_far = [(x_own, 0, later), (x_other, 0, later)]
    x_groups = [x_far[0], x_near[0], x_far[1], x_near[1]]
    dy_diagonal = send_diagonal(*dy_plane)
    hidden_far, slope_far, act_far = forward_rows(x_far, w_both, 2 * tile)
    dy_own = join_plane(tp_index, dy_piece, *dy_plane, *dy_diagonal, earlier=[hidden_far])
    dy_other = swap_cores(dy_own)
    dy_groups = [(dy_own, 0, later), (near_own, 1, tok_count), (dy_other, 0, later), (near_other, 1, tok_count)]

    shadow_rows = exchange_end(after(shadow_pieces, hidden_far))
    table = shadow_rows[:, 3 * shadow_part :].reshape(ep_count, -1)[:, : 4 * tok_count].astype(jnp.float32)
    table = table[:, : 2 * tok_count] + table[:, 2 * tok_count :]
    shadow_rows = shadow_rows[:, : 3 * shadow_part].reshape(ep_count, 3, shadow_part, block_width)
    shadow_rows = shadow_rows.transpose(1, 2, 0, 3).reshape(3, shadow_part, width)
    shadow_rows = jnp.pad(shadow_rows, ((0, 0), (0, -shadow_part % 128), (0, 0)))
    shadow_in = shadow_rows[:2].reshape(-1, width)
    hidden_s, slope_s, act_s = forward_rows(x_groups, shadow_in, 2 * tile, transposed=True)
    order = [(ep_index - 2 * s) % ep_count for s in list(range(1, steps)) + [0]]
    table = [lax.dynamic_index_in_dim(table, index, 0) for index in order + [index ^ 1 for index in order]]
    table = jnp.concatenate(table, axis=0)
    w_rows, w_shadow = table[:, :tok_count].reshape(-1, 1), table[:, tok_count:].reshape(-1, 1)

    down = jnp.concatenate([w_down[0], shadow_rows[2]], axis=0)
    hidden = jnp.concatenate(
        [hidden_far[:later], hidden_near[:tok_count], hidden_far[later:], hidden_near[tok_count:]], axis=0
    )
    weighted = jnp.concatenate(
        [
            (hidden.astype(jnp.float32) * w_rows).astype(jnp.bfloat16),
            (hidden_s.astype(jnp.float32) * w_shadow).astype(jnp.bfloat16),
        ],
        axis=1,
    )
    parts = 2 if steps % 2 == 0 else 1
    sent = output_other(weighted, down, tp_index, parts, quarter)
    got = [swap_cores(array) for array in sent]

    segments = [
        (slope_far, act_far, 0),
        (slope_near, act_near, 0),
        (slope_far, act_far, later),
        (slope_near, act_near, tok_count),
    ]
    pre, pre_s = backward_rows(
        dy_groups, down, segments, slope_s, act_s, w_rows, w_shadow, tile, earlier=sent
    )
    owns = output_own(weighted, got, down, tp_index, quarter, earlier=[pre])
    diagonals = [
        (lax.ppermute(own[3], "tp", along), lax.ppermute(own[4], "tp", across)) for own in owns
    ]
    grad_s = shadow_grads(x_groups, dy_groups, pre_s, weighted, shadow_part, tile, earlier=[own[3] for own in owns])
    sums = []
    for (own, to_x, to_y, _, _), diagonal in zip(owns, diagonals):
        half = own.shape[0] // 2
        top, low = after(diagonal, grad_s)
        to_y = jnp.concatenate(
            [(to_y[:half].astype(jnp.float32) + top.astype(jnp.float32)).astype(jnp.bfloat16), to_y[half:]], axis=0
        )
        to_x = jnp.concatenate(
            [to_x[:half], (to_x[half:].astype(jnp.float32) + low.astype(jnp.float32)).astype(jnp.bfloat16)], axis=0
        )
        sums.append([own, lax.ppermute(to_x, "tp", along), lax.ppermute(to_y, "tp", across), to_x, to_y])
    grad_s = grad_s.reshape(3 * shadow_part, ep_count, block_width).transpose(1, 0, 2)
    grad_kept, grad_taken = exchange_cores(grad_s)
    (grad_taken,) = after([grad_taken], *[array for group in sums for array in group[3:]])
    grad_s = exchange_chips(grad_kept, grad_taken)
    grad_gate, grad_up = input_grads(x_groups, pre, tile, earlier=[grad_taken])
    sums[0][1:3] = after(sums[0][1:3], grad_gate)

    def slot_rows(i):
        own, from_x, from_y = sums[i * parts // steps][:3]
        part = slice(i % (steps // parts) * tok_count, (i % (steps // parts) + 1) * tok_count)
        return own[part] + from_x[part].astype(jnp.float32) + from_y[part].astype(jnp.float32)

    first = [slot_rows(i).astype(jnp.bfloat16) for i in range(steps // parts)]
    grad_down = down_grad(dy_groups, weighted, hidden_part, tile, earlier=first)
    if parts > 1:
        sums[-1][1:3] = after(sums[-1][1:3], grad_down)
    total = slot_rows(steps - 1)
    for s in range(1, steps):
        piece = first[s - 1] if s <= len(first) else slot_rows(s - 1).astype(jnp.bfloat16)
        total = total + lax.ppermute(piece, "ep", ring_pairs(ep_count, -2 * s)).astype(jnp.float32)
    mixed = total.astype(jnp.bfloat16)

    grad_s = exchange_end(after(grad_s, grad_down))
    grad_s_gate = grad_s[:, :shadow_part].reshape(hidden_part, block_width).T
    grad_s_up = grad_s[:, shadow_part : 2 * shadow_part].reshape(hidden_part, block_width).T
    grad_s_down = grad_s[:, 2 * shadow_part :].reshape(hidden_part, block_width)
    return (
        mixed,
        grad_gate[None],
        grad_up[None],
        grad_down[None],
        grad_s_gate,
        grad_s_up,
        grad_s_down,
    )


def solution(mesh):
    tp_count, ep_count = mesh.shape["tp"], mesh.shape["ep"]
    dense = tp_count == 4 and ep_count % 2 == 0 and ep_count <= 8
    return jax.shard_map(
        dense_shards if dense else shards,
        mesh=mesh,
        in_specs=(
            P("ep", "tp"),
            P("ep", "tp"),
            P("ep", None),
            P("ep", None),
            P("ep"),
            P("ep", None, "tp"),
            P("ep", None, "tp"),
            P("ep", "tp", None),
            P("ep", "tp"),
            P("ep", "tp"),
            P("tp", "ep"),
        ),
        out_specs=(
            P("ep", "tp"),
            P("ep", None, "tp"),
            P("ep", None, "tp"),
            P("ep", "tp", None),
            P("ep", "tp"),
            P("ep", "tp"),
            P("tp", "ep"),
        ),
        check_vma=False,
    )
```

```python
import functools
import math

import jax
import jax.numpy as jnp
from jax import lax
from jax.experimental import pallas as pl
from jax.experimental.pallas import tpu as pltpu
from jax.sharding import PartitionSpec as P


def contract_rows(left, right):
    return lax.dot_general(
        left, right, (((0,), (0,)), ((), ())), preferred_element_type=jnp.float32
    )


def split_parts(values):
    upper_part = values.astype(jnp.bfloat16)
    lower_part = (values - upper_part.astype(jnp.float32)).astype(jnp.bfloat16)
    return (upper_part, lower_part)


def weigh_rows(weight_table, rows):
    weight_upper, weight_lower = split_parts(weight_table)
    return jnp.dot(weight_upper, rows, preferred_element_type=jnp.float32) + jnp.dot(
        weight_lower, rows, preferred_element_type=jnp.float32
    )


def expert_pass(rows_x, rows_dout, weight_gate, weight_up, weight_down):
    pre_gate = jnp.dot(rows_x, weight_gate, preferred_element_type=jnp.float32)
    pre_up = jnp.dot(rows_x, weight_up, preferred_element_type=jnp.float32)
    sigmoid_gate = jax.nn.sigmoid(pre_gate)
    activated = pre_gate * sigmoid_gate
    hidden = (activated * pre_up).astype(jnp.bfloat16)
    partial_out = jnp.dot(hidden, weight_down, preferred_element_type=jnp.float32).astype(
        jnp.bfloat16
    )
    hidden_grad = lax.dot_general(
        rows_dout, weight_down, (((1,), (1,)), ((), ())), preferred_element_type=jnp.float32
    )
    grad_pre_gate = (
        hidden_grad * pre_up * sigmoid_gate * (1.0 + pre_gate * (1.0 - sigmoid_gate))
    ).astype(jnp.bfloat16)
    grad_pre_up = (hidden_grad * activated).astype(jnp.bfloat16)
    return (partial_out, hidden, grad_pre_gate, grad_pre_up)


def shards(
    tokens,
    cotangent,
    expert_ids,
    gate_weights,
    shadow_mask,
    w_gate,
    w_up,
    w_down,
    s_gate,
    s_up,
    s_down,
):
    ep_count = lax.axis_size("ep")
    tok_count, top_count = expert_ids.shape
    quarter_width = tokens.shape[1]
    width = quarter_width * lax.axis_size("tp")
    expert_count = w_gate.shape[0] * ep_count
    capacity = (5 * tok_count * top_count + 4 * expert_count - 1) // (4 * expert_count)
    slot_count = expert_count * capacity
    picks_flat = expert_ids.reshape(-1)
    onehot = (picks_flat[:, None] == jnp.arange(expert_count, dtype=jnp.int32)[None, :]).astype(
        jnp.int32
    )
    slot_rank = jnp.sum((jnp.cumsum(onehot, axis=0) - onehot) * onehot, axis=1)
    slot_index = (picks_flat * capacity + slot_rank).reshape(tok_count, top_count)
    matches = jnp.arange(slot_count, dtype=jnp.int32)[:, None, None] == slot_index[None, :, :]
    dispatch = jnp.any(matches, axis=2).astype(jnp.bfloat16)
    weighting = jnp.sum(jnp.where(matches, gate_weights[None, :, :top_count], 0.0), axis=2)
    slot_gate = jnp.sum(weighting, axis=1)
    shadow_weight = gate_weights[:, top_count] * shadow_mask.astype(jnp.float32)
    x_full, dy_full = (
        lax.all_gather(tokens, "tp", axis=1, tiled=True),
        lax.all_gather(cotangent, "tp", axis=1, tiled=True),
    )
    rows_x = jnp.dot(dispatch, tokens, preferred_element_type=jnp.float32).astype(jnp.bfloat16)
    rows_dy = jnp.dot(dispatch, cotangent, preferred_element_type=jnp.float32)
    rows_dout = (slot_gate[:, None] * rows_dy).astype(jnp.bfloat16)
    recv_x, recv_dout = (
        lax.all_to_all(
            rows_x.reshape(ep_count, -1, quarter_width),
            "ep",
            split_axis=0,
            concat_axis=0,
            tiled=True,
        ),
        lax.all_to_all(
            rows_dout.reshape(ep_count, -1, quarter_width),
            "ep",
            split_axis=0,
            concat_axis=0,
            tiled=True,
        ),
    )
    expert_x, expert_dout = (
        lax.all_gather(recv_x.reshape(-1, quarter_width), "tp", axis=1, tiled=True),
        lax.all_gather(recv_dout.reshape(-1, quarter_width), "tp", axis=1, tiled=True),
    )
    partial_out, hidden, grad_pre_gate, grad_pre_up = expert_pass(
        expert_x, expert_dout, w_gate[0], w_up[0], w_down[0]
    )
    grad_gate = contract_rows(expert_x, grad_pre_gate).astype(jnp.bfloat16)[None]
    grad_up = contract_rows(expert_x, grad_pre_up).astype(jnp.bfloat16)[None]
    grad_down = contract_rows(hidden, expert_dout).astype(jnp.bfloat16)[None]
    full_gate, full_up, full_down = (
        lax.all_gather(s_gate, "ep", axis=0, tiled=True),
        lax.all_gather(s_up, "ep", axis=0, tiled=True),
        lax.all_gather(s_down, "ep", axis=1, tiled=True),
    )
    shadow_dout = (shadow_weight[:, None] * dy_full.astype(jnp.float32)).astype(jnp.bfloat16)
    shadow_out, shadow_hidden, shadow_gate_pre, shadow_up_pre = expert_pass(
        x_full, shadow_dout, full_gate, full_up, full_down
    )
    shadow_sums = lax.psum_scatter(
        jnp.concatenate(
            [
                contract_rows(x_full, shadow_gate_pre),
                contract_rows(x_full, shadow_up_pre),
                contract_rows(shadow_dout, shadow_hidden),
            ],
            axis=1,
        ).astype(jnp.bfloat16),
        "ep",
        scatter_dimension=0,
        tiled=True,
    ).astype(jnp.float32)
    hidden_part = s_gate.shape[1]
    grad_s_gate = shadow_sums[:, :hidden_part].astype(jnp.bfloat16)
    grad_s_up = shadow_sums[:, hidden_part : 2 * hidden_part].astype(jnp.bfloat16)
    grad_s_down = shadow_sums[:, 2 * hidden_part :].T.astype(jnp.bfloat16)
    back_rows = lax.all_to_all(
        partial_out.reshape(ep_count, -1, width), "ep", split_axis=0, concat_axis=0, tiled=True
    ).reshape(-1, width)
    term = weigh_rows(weighting.T, back_rows)
    term = term + shadow_weight[:, None] * shadow_out.astype(jnp.float32)
    mixed = lax.psum_scatter(term.astype(jnp.bfloat16), "tp", scatter_dimension=1, tiled=True)
    return (mixed, grad_gate, grad_up, grad_down, grad_s_gate, grad_s_up, grad_s_down)


ANY = pl.BlockSpec(memory_space=pl.ANY)
VMEM_LIMIT = 60 * 1024 * 1024
SHORT = pl.CostEstimate(flops=1, bytes_accessed=1, transcendentals=0)


def swap_pairs(count, bit):
    return [(i, i ^ bit) for i in range(count)]


def ring_pairs(count, shift):
    return [(i, (i + shift) % count) for i in range(count)]


def dot32(left, right):
    return jnp.dot(left, right, preferred_element_type=jnp.float32)


def contract_last(left, right):
    return lax.dot_general(
        left, right, (((1,), (1,)), ((), ())), preferred_element_type=jnp.float32
    )


def shape_of(*dims, dtype=jnp.bfloat16):
    return jax.ShapeDtypeStruct(dims, dtype)


def after(arrays, *earlier):
    def nothing(*refs):
        del refs

    count = len(arrays)
    return pl.pallas_call(
        nothing,
        out_shape=[jax.ShapeDtypeStruct(a.shape, a.dtype) for a in arrays],
        in_specs=[ANY] * (count + len(earlier)),
        out_specs=[ANY] * count,
        input_output_aliases={i: i for i in range(count)},
        compiler_params=pltpu.CompilerParams(vmem_limit_bytes=VMEM_LIMIT),
        cost_estimate=SHORT,
        name="after",
    )(*arrays, *earlier)


def kernel_call(body, grid, in_specs, out_specs, out_shape, operands, scratch, name, column=None, earlier=()):
    count = len(operands)

    def run(column_ref, *refs):
        del column_ref
        body(*refs[:count], *refs[count + len(earlier) :])

    column = jnp.zeros((1,), jnp.int32) if column is None else column.reshape(1).astype(jnp.int32)
    return pl.pallas_call(
        run,
        out_shape=out_shape,
        grid_spec=pltpu.PrefetchScalarGridSpec(
            num_scalar_prefetch=1,
            grid=grid,
            in_specs=list(in_specs) + [ANY] * len(earlier),
            out_specs=out_specs,
            scratch_shapes=scratch,
        ),
        compiler_params=pltpu.CompilerParams(vmem_limit_bytes=VMEM_LIMIT),
        cost_estimate=SHORT,
        name=name,
    )(column, *operands, *earlier)


def whole(array):
    return pl.BlockSpec(array.shape, lambda *_: (0,) * len(array.shape))


def join_plane(column, *pieces, earlier=()):
    rows, quarter = pieces[0].shape
    count = len(pieces)
    chunk = rows // 4

    def body(*refs):
        column_ref, sources, out = refs[0], refs[1 : 1 + count], refs[-1]
        for own_column in range(count):

            @pl.when(column_ref[0] == own_column)
            def _():
                for bit, source in enumerate(sources):
                    place = own_column ^ bit
                    out[:, place * quarter : (place + 1) * quarter] = source[...]

    return pl.pallas_call(
        body,
        out_shape=shape_of(rows, count * quarter),
        grid_spec=pltpu.PrefetchScalarGridSpec(
            num_scalar_prefetch=1,
            grid=(4,),
            in_specs=[pl.BlockSpec((chunk, quarter), lambda i, *_: (i, 0))] * count + [ANY] * len(earlier),
            out_specs=pl.BlockSpec((chunk, count * quarter), lambda i, *_: (i, 0)),
        ),
        compiler_params=pltpu.CompilerParams(vmem_limit_bytes=VMEM_LIMIT),
        cost_estimate=SHORT,
        name="join_plane",
    )(column.reshape(1).astype(jnp.int32), *pieces, *earlier)


def stack_pieces(pieces, earlier=()):
    rows, columns = pieces[0].shape
    count = len(pieces)

    def body(*refs):
        for i, ref in enumerate(refs[:count]):

            @pl.when(pl.program_id(0) == i)
            def _():
                refs[-1][...] = ref[...]

    return pl.pallas_call(
        body,
        out_shape=shape_of(count * rows, columns),
        grid=(count,),
        in_specs=[pl.BlockSpec((rows, columns), lambda i: (0, 0))] * count + [ANY] * len(earlier),
        out_specs=pl.BlockSpec((rows, columns), lambda i: (i, 0)),
        compiler_params=pltpu.CompilerParams(vmem_limit_bytes=VMEM_LIMIT),
        cost_estimate=SHORT,
        name="stack_pieces",
    )(*pieces, *earlier)


def piece_specs(pieces):
    return [pl.BlockSpec((1, 1) + p.shape[2:], lambda e, *_: (0, lax.rem(e, 2), 0, 0)) for p in pieces]


def on_piece(chip_ref, refs, use):
    shift = lax.rem(chip_ref[0] - pl.program_id(0) // 2 + len(refs), len(refs))
    for i, ref in enumerate(refs):
        pl.when(shift == i)(functools.partial(use, ref))


def lay_out_shadow(pieces, w_down, units, chip, earlier=()):
    count = len(pieces)
    ep_count = 2 * count
    block_width = pieces[0].shape[3]
    apart = units + -units % 128
    hidden, width = w_down.shape

    def body(chip_ref, *refs):
        down_ref, shadow_ref, out = refs[count], refs[-2], refs[-1]

        def use(ref):
            shadow_ref[...] = jnp.zeros_like(shadow_ref)
            shadow_ref[:units, :] = ref[0, 0, :units, :]
            shadow_ref[apart : apart + units, :] = ref[0, 0, units : 2 * units, :]
            out[:hidden, :] = down_ref[...]
            out[hidden + units :, :] = jnp.zeros((apart - units, block_width), jnp.bfloat16)
            out[hidden : hidden + units, :] = ref[0, 0, 2 * units : 3 * units, :]

        on_piece(chip_ref, refs[:count], use)

    return pl.pallas_call(
        body,
        out_shape=[shape_of(2 * apart, width), shape_of(hidden + apart, width)],
        grid_spec=pltpu.PrefetchScalarGridSpec(
            num_scalar_prefetch=1,
            grid=(ep_count,),
            in_specs=piece_specs(pieces)
            + [pl.BlockSpec((hidden, block_width), lambda e, *_: (0, e))]
            + [ANY] * len(earlier),
            out_specs=[
                pl.BlockSpec((2 * apart, block_width), lambda e, *_: (0, e)),
                pl.BlockSpec((hidden + apart, block_width), lambda e, *_: (0, e)),
            ],
        ),
        compiler_params=pltpu.CompilerParams(vmem_limit_bytes=VMEM_LIMIT),
        cost_estimate=SHORT,
        name="lay_out_shadow",
    )(chip.reshape(1).astype(jnp.int32), *pieces, w_down, *earlier)


def lay_out_grads(pieces, units, chip, earlier=()):
    count = len(pieces)
    ep_count = 2 * count
    block_width = pieces[0].shape[3]
    hidden = ep_count * units

    def body(chip_ref, *refs):
        gate_ref, up_ref, down_ref, gate_t, up_t = refs[-5:]
        place = pl.ds(pl.multiple_of(pl.program_id(0) * units, 16), units)

        def use(ref):
            gate_t[place, :] = ref[0, 0, :units, :]
            up_t[place, :] = ref[0, 0, units : 2 * units, :]
            down_ref[place, :] = ref[0, 0, 2 * units :, :]

        on_piece(chip_ref, refs[:count], use)

        @pl.when(pl.program_id(0) == ep_count - 1)
        def _():
            gate_ref[...] = gate_t[...].T
            up_ref[...] = up_t[...].T

    return pl.pallas_call(
        body,
        out_shape=[shape_of(block_width, hidden), shape_of(block_width, hidden), shape_of(hidden, block_width)],
        grid_spec=pltpu.PrefetchScalarGridSpec(
            num_scalar_prefetch=1,
            grid=(ep_count,),
            in_specs=piece_specs(pieces) + [ANY] * len(earlier),
            out_specs=[pl.BlockSpec((block_width, hidden), lambda *_: (0, 0))] * 2
            + [pl.BlockSpec((hidden, block_width), lambda *_: (0, 0))],
            scratch_shapes=[pltpu.VMEM((hidden, block_width), jnp.bfloat16)] * 2,
        ),
        compiler_params=pltpu.CompilerParams(vmem_limit_bytes=VMEM_LIMIT),
        cost_estimate=SHORT,
        name="lay_out_grads",
    )(chip.reshape(1).astype(jnp.int32), *pieces, *earlier)


def row_specs(groups, tile):
    def spec(index, rows):
        return pl.BlockSpec((rows, tile), lambda k, *_: (index, k))

    return [spec(index, rows) for _, index, rows in groups]


def apply_gate(pre_gate, pre_up):
    sigmoid_gate = jax.nn.sigmoid(pre_gate)
    activated = pre_gate * sigmoid_gate
    hidden = (activated * pre_up).astype(jnp.bfloat16)
    return hidden, pre_up * sigmoid_gate * (1.0 + pre_gate * (1.0 - sigmoid_gate)), activated


def clear_first(acc):
    @pl.when(pl.program_id(0) == 0)
    def _():
        acc[...] = jnp.zeros_like(acc)


def forward_rows(groups, w_both, tile, transposed=False, earlier=()):
    rows = sum(g[2] for g in groups)
    if transposed:
        units, width = w_both.shape[0] // 2, w_both.shape[1]
        tile_spec = pl.BlockSpec((2 * units, tile), lambda k, *_: (0, k))
    else:
        width, units = w_both.shape[0], w_both.shape[1] // 2
        tile_spec = pl.BlockSpec((tile, 2 * units), lambda k, *_: (k, 0))
    steps = width // tile

    def body(*refs):
        n = len(groups)
        both_ref, hidden_ref, slope_ref, act_ref, acc = refs[n:]
        clear_first(acc)
        start = 0
        for ref, (_, _, count) in zip(refs[:n], groups):
            part = pl.ds(start, count)
            if transposed:
                acc[part, :] += contract_last(ref[...], both_ref[...])
            else:
                acc[part, :] += dot32(ref[...], both_ref[...])
            start += count

        @pl.when(pl.program_id(0) == steps - 1)
        def _():
            chunk = 64

            @pl.loop(0, rows // chunk)
            def _(i):
                part = pl.ds(pl.multiple_of(i * chunk, chunk), chunk)
                hidden, slope, act = apply_gate(acc[part, :units], acc[part, units:])
                hidden_ref[part, :] = hidden
                slope_ref[part, :] = slope
                act_ref[part, :] = act

    out_spec = pl.BlockSpec((rows, units), lambda *_: (0, 0))
    return kernel_call(
        body,
        (steps,),
        row_specs(groups, tile) + [tile_spec],
        [out_spec] * 3,
        [shape_of(rows, units), shape_of(rows, units, dtype=jnp.float32), shape_of(rows, units, dtype=jnp.float32)],
        [g[0] for g in groups] + [w_both],
        [pltpu.VMEM((rows, 2 * units), jnp.float32)],
        "forward_rows",
        earlier=earlier,
    )


def output_other(weighted, down, column, parts, quarter, earlier=()):
    rows, units = weighted.shape
    count = rows // 2 // parts

    def body(weighted_ref, down_ref, *outs):
        for i, out in enumerate(outs):
            out[...] = dot32(weighted_ref[i * count : (i + 1) * count, :], down_ref[...]).astype(jnp.bfloat16)

    return kernel_call(
        body,
        (4,),
        [
            pl.BlockSpec((rows // 2, units), lambda *_: (1, 0)),
            pl.BlockSpec((units, quarter), lambda q, column_ref: (0, column_ref[0] ^ q)),
        ],
        [pl.BlockSpec((count, quarter), lambda q, *_: (0, q))] * parts,
        [shape_of(count, 4 * quarter)] * parts,
        [weighted, down],
        [],
        "output_other",
        column=column,
        earlier=earlier,
    )


def output_own(weighted, got, down, column, quarter, earlier=()):
    count, units = got[0].shape[0], weighted.shape[1]
    parts = len(got)

    def body(weighted_ref, down_ref, *refs):
        for i in range(parts):
            value = dot32(weighted_ref[i * count : (i + 1) * count, :], down_ref[...])
            value = value + refs[i][...].astype(jnp.float32)
            for j, out in enumerate(refs[parts + 4 * i : parts + 4 * i + 4]):

                @pl.when(pl.program_id(0) == 3 - j)
                def _(out=out, value=value):
                    out[...] = value.astype(out.dtype)

    full = pl.BlockSpec((count, quarter), lambda *_: (0, 0))
    out = kernel_call(
        body,
        (4,),
        [
            pl.BlockSpec((parts * count, units), lambda *_: (0, 0)),
            pl.BlockSpec((units, quarter), lambda q, column_ref: (0, column_ref[0] ^ 3 ^ q)),
        ]
        + [pl.BlockSpec((count, quarter), lambda q, *_: (0, 3 - q))] * parts,
        [full] * (4 * parts),
        ([shape_of(count, quarter, dtype=jnp.float32)] + [shape_of(count, quarter)] * 3) * parts,
        [weighted, down] + list(got),
        [],
        "output_own",
        column=column,
        earlier=earlier,
    )
    return [out[4 * i : 4 * i + 4] for i in range(parts)]


def backward_rows(groups, down, parts, slope_s, act_s, w_rows, w_shadow, tile, earlier=()):
    rows = sum(g[2] for g in groups)
    units_all, width = down.shape
    units_s = slope_s.shape[1]
    units = units_all - units_s
    steps = width // tile
    arrays = list({id(a): a for part in parts for a in part[:2]}.values())
    places = [[next(i for i, a in enumerate(arrays) if a is b) for b in part[:2]] for part in parts]

    def body(*refs):
        n, m = len(groups), len(arrays)
        down_ref = refs[n]
        array_refs = refs[n + 1 : n + 1 + m]
        slope_s_ref, act_s_ref, w_ref, w_s_ref, pre_ref, pre_s_ref, acc = refs[n + 1 + m :]
        clear_first(acc)
        start = 0
        for ref, (_, _, count) in zip(refs[:n], groups):
            acc[pl.ds(start, count), :] += contract_last(ref[...], down_ref[...])
            start += count

        @pl.when(pl.program_id(0) == steps - 1)
        def _():
            chunk = 64
            start = 0
            for (_, _, count), (_, _, first), (slope_at, act_at) in zip(groups, parts, places):

                @pl.loop(0, count // chunk)
                def _(i, start=start, first=first, slope_ref=array_refs[slope_at], act_ref=array_refs[act_at]):
                    source = pl.ds(pl.multiple_of(first + i * chunk, chunk), chunk)
                    part = pl.ds(pl.multiple_of(start + i * chunk, chunk), chunk)
                    grad = acc[part, :units] * w_ref[part, :]
                    pre_ref[part, :units] = (grad * slope_ref[source, :]).astype(jnp.bfloat16)
                    pre_ref[part, units:] = (grad * act_ref[source, :]).astype(jnp.bfloat16)
                    grad = acc[part, units:] * w_s_ref[part, :]
                    pre_s_ref[part, :units_s] = (grad * slope_s_ref[part, :]).astype(jnp.bfloat16)
                    pre_s_ref[part, units_s:] = (grad * act_s_ref[part, :]).astype(jnp.bfloat16)

                start += count

    extra = arrays + [slope_s, act_s, w_rows, w_shadow]
    return kernel_call(
        body,
        (steps,),
        row_specs(groups, tile) + [pl.BlockSpec((units_all, tile), lambda k, *_: (0, k))] + [whole(a) for a in extra],
        [pl.BlockSpec((rows, 2 * units), lambda *_: (0, 0)), pl.BlockSpec((rows, 2 * units_s), lambda *_: (0, 0))],
        [shape_of(rows, 2 * units), shape_of(rows, 2 * units_s)],
        [g[0] for g in groups] + [down] + extra,
        [pltpu.VMEM((rows, units_all), jnp.float32)],
        "backward_rows",
        earlier=earlier,
    )


def stage_rows(refs, groups, held):
    start = 0
    for ref, (_, _, count) in zip(refs, groups):
        held[pl.ds(start, count), :] = ref[...]
        start += count
    return held[...]


def shadow_grads(x_groups, dy_groups, pre_s, weighted, units, tile, earlier=()):
    rows, wide = pre_s.shape
    apart = wide // 2
    width = x_groups[0][0].shape[1]

    def body(*refs):
        n = len(x_groups)
        pre_ref, hidden_ref, out, held, pre_t, hidden_t = refs[2 * n :]

        @pl.when(pl.program_id(0) == 0)
        def _():
            pre_t[...] = pre_ref[...].T
            hidden_t[...] = hidden_ref[...].T

        value = dot32(pre_t[...], stage_rows(refs[:n], x_groups, held))
        out[:units, :] = value[:units].astype(jnp.bfloat16)
        out[units : 2 * units, :] = value[apart : apart + units].astype(jnp.bfloat16)
        value = dot32(hidden_t[...], stage_rows(refs[n : 2 * n], dy_groups, held))
        out[2 * units :, :] = value[:units].astype(jnp.bfloat16)

    (out,) = kernel_call(
        body,
        (width // tile,),
        row_specs(x_groups, tile)
        + row_specs(dy_groups, tile)
        + [whole(pre_s), pl.BlockSpec((rows, apart), lambda *_: (0, weighted.shape[1] // apart - 1))],
        [pl.BlockSpec((3 * units, tile), lambda k, *_: (0, k))],
        [shape_of(3 * units, width)],
        [g[0] for g in x_groups + dy_groups] + [pre_s, weighted],
        [
            pltpu.VMEM((rows, tile), jnp.bfloat16),
            pltpu.VMEM((wide, rows), jnp.bfloat16),
            pltpu.VMEM((apart, rows), jnp.bfloat16),
        ],
        "shadow_grads",
        earlier=earlier,
    )
    return out


def input_grads(groups, pre, tile, earlier=()):
    rows, both = pre.shape
    units = both // 2
    width = groups[0][0].shape[1]

    def body(*refs):
        n = len(groups)
        pre_ref, gate_ref, up_ref, held = refs[n:]
        value = contract_rows(stage_rows(refs[:n], groups, held), pre_ref[...])
        gate_ref[...] = value[:, :units].astype(jnp.bfloat16)
        up_ref[...] = value[:, units:].astype(jnp.bfloat16)

    return kernel_call(
        body,
        (width // tile,),
        row_specs(groups, tile) + [whole(pre)],
        [pl.BlockSpec((tile, units), lambda k, *_: (k, 0))] * 2,
        [shape_of(width, units)] * 2,
        [g[0] for g in groups] + [pre],
        [pltpu.VMEM((rows, tile), jnp.bfloat16)],
        "input_grads",
        earlier=earlier,
    )


def down_grad(groups, weighted, units, tile, earlier=()):
    rows = weighted.shape[0]
    width = groups[0][0].shape[1]

    def body(*refs):
        n = len(groups)
        hidden_ref, out, held, hidden_t = refs[n:]

        @pl.when(pl.program_id(0) == 0)
        def _():
            hidden_t[...] = hidden_ref[...].T

        out[...] = dot32(hidden_t[...], stage_rows(refs[:n], groups, held)).astype(jnp.bfloat16)

    (out,) = kernel_call(
        body,
        (width // tile,),
        row_specs(groups, tile) + [pl.BlockSpec((rows, units), lambda *_: (0, 0))],
        [pl.BlockSpec((units, tile), lambda k, *_: (0, k))],
        [shape_of(units, width)],
        [g[0] for g in groups] + [weighted],
        [pltpu.VMEM((rows, tile), jnp.bfloat16), pltpu.VMEM((units, rows), jnp.bfloat16)],
        "down_grad",
        earlier=earlier,
    )
    return out


def send_along_z(own):
    ep_count = lax.axis_size("ep")
    return [lax.ppermute(own, "ep", ring_pairs(ep_count, 2 * s)) for s in range(1, ep_count // 2)]


def swap_cores(block):
    return lax.ppermute(block, "ep", swap_pairs(lax.axis_size("ep"), 1))


def send_plane(*pieces):
    pieces = pieces * (3 // len(pieces))
    return [lax.ppermute(p, "tp", swap_pairs(lax.axis_size("tp"), bit)) for p, bit in zip(pieces, (1, 2, 3))]


def exchange_cores(blocks):
    ep_count, core = lax.axis_size("ep"), lax.axis_index("ep") % 2
    pairs = blocks.reshape(ep_count // 2, 2, *blocks.shape[1:])
    kept = jnp.where(core == 0, pairs[:, 0], pairs[:, 1])
    given = jnp.where(core == 0, pairs[:, 1], pairs[:, 0])
    return kept, swap_cores(given)


def exchange_chips(kept, taken, in_turn=False, earlier=()):
    ep_count, me = lax.axis_size("ep"), lax.axis_index("ep")
    chips, chip, core = ep_count // 2, me // 2, me % 2
    both = jnp.stack([jnp.where(core == 0, kept, taken), jnp.where(core == 0, taken, kept)], axis=1)
    pieces = [lax.dynamic_index_in_dim(both, (chip + shift) % chips, 0) for shift in range(chips)]
    if earlier:
        pieces = after(pieces, *earlier)
    result = [pieces[0]]
    for shift in range(1, chips):
        piece = pieces[shift]
        if in_turn and shift > 1:
            (piece,) = after([piece], result[-1])
        result.append(lax.ppermute(piece, "ep", ring_pairs(ep_count, 2 * shift)))
    return result


def dense_shards(
    tokens,
    cotangent,
    expert_ids,
    gate_weights,
    shadow_mask,
    w_gate,
    w_up,
    w_down,
    s_gate,
    s_up,
    s_down,
):
    ep_count, tp_count = lax.axis_size("ep"), lax.axis_size("tp")
    ep_index, tp_index = lax.axis_index("ep"), lax.axis_index("tp")
    tok_count, top_count = expert_ids.shape
    quarter = tokens.shape[1]
    width = quarter * tp_count
    hidden_part = w_gate.shape[2]
    shadow_part = hidden_part // ep_count
    block_width = s_gate.shape[0]
    steps = ep_count // 2
    later = (steps - 1) * tok_count
    tile = width // 8
    along, across = swap_pairs(tp_count, 1), swap_pairs(tp_count, 2)

    picked = expert_ids[None, :, :] == jnp.arange(ep_count, dtype=jnp.int32)[:, None, None]
    table = jnp.sum(jnp.where(picked, gate_weights[None, :, :top_count], 0.0), axis=2)
    shadow_weight = gate_weights[:, top_count] * shadow_mask.astype(jnp.float32)
    table = jnp.concatenate([table, jnp.broadcast_to(shadow_weight[None], table.shape)], axis=1)
    table = jnp.concatenate(split_parts(table), axis=1)
    spare = -table.shape[1] % (16 * block_width)
    table_rows = (table.shape[1] + spare) // block_width
    table = jnp.pad(table, ((0, 0), (0, spare))).reshape(ep_count, table_rows, block_width)
    shadow_blocks = jnp.concatenate(
        [
            s_gate.T.reshape(ep_count, shadow_part, block_width),
            s_up.T.reshape(ep_count, shadow_part, block_width),
            s_down.reshape(ep_count, shadow_part, block_width),
            table,
        ],
        axis=1,
    )

    x_z = send_along_z(tokens)
    near = stack_pieces([tokens, cotangent])
    near_late = stack_pieces([tokens, cotangent], earlier=[x_z[0]])
    near_plane = send_plane(near, near, near_late)
    w_both = jnp.concatenate([w_gate[0], w_up[0]], axis=1)
    *x_z, near_x, near_y, near_d = after(x_z + near_plane, w_both, shadow_blocks)

    x_piece = stack_pieces(x_z)
    x_plane = send_plane(x_piece)
    (dy_first,) = after([cotangent], x_z[0])
    dy_z = send_along_z(dy_first)
    near_own = join_plane(tp_index, near, near_x, near_y, near_d, earlier=[dy_z[0]])
    near_other = swap_cores(near_own)
    x_near = [(near_own, 0, tok_count), (near_other, 0, tok_count)]
    hidden_near, slope_near, act_near = forward_rows(x_near, w_both, 2 * tile)
    *x_plane, dy_z1, dy_z2, dy_z3 = after([*x_plane, *dy_z], hidden_near)
    dy_z = [dy_z1, dy_z2, dy_z3]

    dy_piece = stack_pieces(dy_z)
    dy_plane = send_plane(dy_piece)
    (shadow_blocks,) = after([shadow_blocks], dy_z[0])
    shadow_pieces = exchange_chips(*exchange_cores(shadow_blocks), in_turn=True)
    x_own = join_plane(tp_index, x_piece, *x_plane, earlier=[dy_piece])
    x_other = swap_cores(x_own)
    x_far = [(x_own, 0, later), (x_other, 0, later)]
    x_groups = [x_far[0], x_near[0], x_far[1], x_near[1]]
    hidden_far, slope_far, act_far = forward_rows(x_far, w_both, 2 * tile)
    chip = ep_index // 2
    shadow_in, down = lay_out_shadow(shadow_pieces, w_down[0], shadow_part, chip, earlier=[hidden_far])
    hidden_s, slope_s, act_s = forward_rows(x_groups, shadow_in, 2 * tile, transposed=True)

    table = jnp.stack([piece[0, :, 3 * shadow_part :].reshape(2, -1) for piece in shadow_pieces])
    table = table[..., : 4 * tok_count].astype(jnp.float32)
    table = table[..., : 2 * tok_count] + table[..., 2 * tok_count :]
    table = jnp.where(ep_index % 2 == 0, table, table[:, ::-1])
    table = jnp.concatenate([table[1:], table[:1]], axis=0).transpose(1, 0, 2)
    w_rows, w_shadow = table[..., :tok_count].reshape(-1, 1), table[..., tok_count:].reshape(-1, 1)

    hidden = jnp.concatenate(
        [hidden_far[:later], hidden_near[:tok_count], hidden_far[later:], hidden_near[tok_count:]], axis=0
    )
    weighted = jnp.concatenate(
        [
            (hidden.astype(jnp.float32) * w_rows).astype(jnp.bfloat16),
            (hidden_s.astype(jnp.float32) * w_shadow).astype(jnp.bfloat16),
        ],
        axis=1,
    )
    parts = 2 if steps % 2 == 0 else 1
    sent = output_other(weighted, down, tp_index, parts, quarter)
    got = [swap_cores(array) for array in sent]
    dy_plane = after(dy_plane, *sent)

    dy_own = join_plane(tp_index, dy_piece, *dy_plane)
    dy_other = swap_cores(dy_own)
    dy_groups = [(dy_own, 0, later), (near_own, 1, tok_count), (dy_other, 0, later), (near_other, 1, tok_count)]
    owns = output_own(weighted, got, down, tp_index, quarter, earlier=[dy_own])
    sums = [send_plane(*own[1:]) for own in owns]
    segments = [
        (slope_far, act_far, 0),
        (slope_near, act_near, 0),
        (slope_far, act_far, later),
        (slope_near, act_near, tok_count),
    ]
    pre, pre_s = backward_rows(
        dy_groups, down, segments, slope_s, act_s, w_rows, w_shadow, tile, earlier=[own[1] for own in owns]
    )
    grad_s = shadow_grads(x_groups, dy_groups, pre_s, weighted, shadow_part, tile)
    blocks = grad_s.reshape(3 * shadow_part, ep_count, block_width).transpose(1, 0, 2)
    grad_kept, grad_taken = exchange_cores(blocks)
    sums[0] = after(sums[0], grad_s)

    def slot_rows(i):
        part = slice(i % (steps // parts) * tok_count, (i % (steps // parts) + 1) * tok_count)
        total = owns[i * parts // steps][0][part]
        for array in sums[i * parts // steps]:
            total = total + array[part].astype(jnp.float32)
        return total

    first = [slot_rows(i).astype(jnp.bfloat16) for i in range(steps // parts)]
    grad_pieces = exchange_chips(grad_kept, grad_taken, earlier=first)
    grad_gate, grad_up = input_grads(x_groups, pre, tile, earlier=[grad_pieces[0]])
    if parts > 1:
        sums[-1] = after(sums[-1], grad_gate)
    total = slot_rows(steps - 1)
    pieces = first + [slot_rows(i).astype(jnp.bfloat16) for i in range(len(first), steps - 1)]
    grad_down = down_grad(dy_groups, weighted, hidden_part, tile, earlier=[pieces[-1], grad_gate])
    for s in range(1, steps):
        total = total + lax.ppermute(pieces[s - 1], "ep", ring_pairs(ep_count, -2 * s)).astype(jnp.float32)
    mixed = total.astype(jnp.bfloat16)

    grads_s = lay_out_grads(grad_pieces, shadow_part, chip, earlier=[grad_down])
    return (mixed, grad_gate[None], grad_up[None], grad_down[None], *grads_s)


def solution(mesh):
    tp_count, ep_count = mesh.shape["tp"], mesh.shape["ep"]
    dense = tp_count == 4 and ep_count % 2 == 0 and ep_count <= 8
    return jax.shard_map(
        dense_shards if dense else shards,
        mesh=mesh,
        in_specs=(
            P("ep", "tp"),
            P("ep", "tp"),
            P("ep", None),
            P("ep", None),
            P("ep"),
            P("ep", None, "tp"),
            P("ep", None, "tp"),
            P("ep", "tp", None),
            P("ep", "tp"),
            P("ep", "tp"),
            P("tp", "ep"),
        ),
        out_specs=(
            P("ep", "tp"),
            P("ep", None, "tp"),
            P("ep", None, "tp"),
            P("ep", "tp", None),
            P("ep", "tp"),
            P("ep", "tp"),
            P("tp", "ep"),
        ),
        check_vma=False,
    )
```

```python
import functools

import jax
import jax.numpy as jnp
from jax import lax
from jax.experimental import pallas as pl
from jax.experimental.pallas import tpu as pltpu
from jax.sharding import PartitionSpec as P


def contract_rows(left, right):
    return lax.dot_general(
        left, right, (((0,), (0,)), ((), ())), preferred_element_type=jnp.float32
    )


def split_parts(values):
    upper_part = values.astype(jnp.bfloat16)
    lower_part = (values - upper_part.astype(jnp.float32)).astype(jnp.bfloat16)
    return (upper_part, lower_part)


def weigh_rows(weight_table, rows):
    weight_upper, weight_lower = split_parts(weight_table)
    return jnp.dot(weight_upper, rows, preferred_element_type=jnp.float32) + jnp.dot(
        weight_lower, rows, preferred_element_type=jnp.float32
    )


def expert_pass(rows_x, rows_dout, weight_gate, weight_up, weight_down):
    pre_gate = jnp.dot(rows_x, weight_gate, preferred_element_type=jnp.float32)
    pre_up = jnp.dot(rows_x, weight_up, preferred_element_type=jnp.float32)
    sigmoid_gate = jax.nn.sigmoid(pre_gate)
    activated = pre_gate * sigmoid_gate
    hidden = (activated * pre_up).astype(jnp.bfloat16)
    partial_out = jnp.dot(hidden, weight_down, preferred_element_type=jnp.float32).astype(
        jnp.bfloat16
    )
    hidden_grad = lax.dot_general(
        rows_dout, weight_down, (((1,), (1,)), ((), ())), preferred_element_type=jnp.float32
    )
    grad_pre_gate = (
        hidden_grad * pre_up * sigmoid_gate * (1.0 + pre_gate * (1.0 - sigmoid_gate))
    ).astype(jnp.bfloat16)
    grad_pre_up = (hidden_grad * activated).astype(jnp.bfloat16)
    return (partial_out, hidden, grad_pre_gate, grad_pre_up)


def routed_shards(
    tokens,
    cotangent,
    expert_ids,
    gate_weights,
    shadow_mask,
    w_gate,
    w_up,
    w_down,
    s_gate,
    s_up,
    s_down,
):
    ep_count = lax.axis_size("ep")
    tok_count, top_count = expert_ids.shape
    quarter_width = tokens.shape[1]
    width = quarter_width * lax.axis_size("tp")
    expert_count = w_gate.shape[0] * ep_count
    capacity = (5 * tok_count * top_count + 4 * expert_count - 1) // (4 * expert_count)
    slot_count = expert_count * capacity
    picks_flat = expert_ids.reshape(-1)
    onehot = (picks_flat[:, None] == jnp.arange(expert_count, dtype=jnp.int32)[None, :]).astype(
        jnp.int32
    )
    slot_rank = jnp.sum((jnp.cumsum(onehot, axis=0) - onehot) * onehot, axis=1)
    slot_index = (picks_flat * capacity + slot_rank).reshape(tok_count, top_count)
    matches = jnp.arange(slot_count, dtype=jnp.int32)[:, None, None] == slot_index[None, :, :]
    dispatch = jnp.any(matches, axis=2).astype(jnp.bfloat16)
    weighting = jnp.sum(jnp.where(matches, gate_weights[None, :, :top_count], 0.0), axis=2)
    slot_gate = jnp.sum(weighting, axis=1)
    shadow_weight = gate_weights[:, top_count] * shadow_mask.astype(jnp.float32)
    x_full, dy_full = (
        lax.all_gather(tokens, "tp", axis=1, tiled=True),
        lax.all_gather(cotangent, "tp", axis=1, tiled=True),
    )
    rows_x = jnp.dot(dispatch, tokens, preferred_element_type=jnp.float32).astype(jnp.bfloat16)
    rows_dy = jnp.dot(dispatch, cotangent, preferred_element_type=jnp.float32)
    rows_dout = (slot_gate[:, None] * rows_dy).astype(jnp.bfloat16)
    recv_x, recv_dout = (
        lax.all_to_all(
            rows_x.reshape(ep_count, -1, quarter_width),
            "ep",
            split_axis=0,
            concat_axis=0,
            tiled=True,
        ),
        lax.all_to_all(
            rows_dout.reshape(ep_count, -1, quarter_width),
            "ep",
            split_axis=0,
            concat_axis=0,
            tiled=True,
        ),
    )
    expert_x, expert_dout = (
        lax.all_gather(recv_x.reshape(-1, quarter_width), "tp", axis=1, tiled=True),
        lax.all_gather(recv_dout.reshape(-1, quarter_width), "tp", axis=1, tiled=True),
    )
    partial_out, hidden, grad_pre_gate, grad_pre_up = expert_pass(
        expert_x, expert_dout, w_gate[0], w_up[0], w_down[0]
    )
    grad_gate = contract_rows(expert_x, grad_pre_gate).astype(jnp.bfloat16)[None]
    grad_up = contract_rows(expert_x, grad_pre_up).astype(jnp.bfloat16)[None]
    grad_down = contract_rows(hidden, expert_dout).astype(jnp.bfloat16)[None]
    full_gate, full_up, full_down = (
        lax.all_gather(s_gate, "ep", axis=0, tiled=True),
        lax.all_gather(s_up, "ep", axis=0, tiled=True),
        lax.all_gather(s_down, "ep", axis=1, tiled=True),
    )
    shadow_dout = (shadow_weight[:, None] * dy_full.astype(jnp.float32)).astype(jnp.bfloat16)
    shadow_out, shadow_hidden, shadow_gate_pre, shadow_up_pre = expert_pass(
        x_full, shadow_dout, full_gate, full_up, full_down
    )
    shadow_sums = lax.psum_scatter(
        jnp.concatenate(
            [
                contract_rows(x_full, shadow_gate_pre),
                contract_rows(x_full, shadow_up_pre),
                contract_rows(shadow_dout, shadow_hidden),
            ],
            axis=1,
        ).astype(jnp.bfloat16),
        "ep",
        scatter_dimension=0,
        tiled=True,
    ).astype(jnp.float32)
    hidden_part = s_gate.shape[1]
    grad_s_gate = shadow_sums[:, :hidden_part].astype(jnp.bfloat16)
    grad_s_up = shadow_sums[:, hidden_part : 2 * hidden_part].astype(jnp.bfloat16)
    grad_s_down = shadow_sums[:, 2 * hidden_part :].T.astype(jnp.bfloat16)
    back_rows = lax.all_to_all(
        partial_out.reshape(ep_count, -1, width), "ep", split_axis=0, concat_axis=0, tiled=True
    ).reshape(-1, width)
    term = weigh_rows(weighting.T, back_rows)
    term = term + shadow_weight[:, None] * shadow_out.astype(jnp.float32)
    mixed = lax.psum_scatter(term.astype(jnp.bfloat16), "tp", scatter_dimension=1, tiled=True)
    return (mixed, grad_gate, grad_up, grad_down, grad_s_gate, grad_s_up, grad_s_down)


ANY = pl.BlockSpec(memory_space=pl.ANY)
VMEM_LIMIT = 60 * 1024 * 1024
SHORT = pl.CostEstimate(flops=1, bytes_accessed=1, transcendentals=0)


def swap_pairs(count, bit):
    return [(i, i ^ bit) for i in range(count)]


def ring_pairs(count, shift):
    return [(i, (i + shift) % count) for i in range(count)]


def dot32(left, right):
    return jnp.dot(left, right, preferred_element_type=jnp.float32)


def contract_last(left, right):
    return lax.dot_general(
        left, right, (((1,), (1,)), ((), ())), preferred_element_type=jnp.float32
    )


def shape_of(*dims, dtype=jnp.bfloat16):
    return jax.ShapeDtypeStruct(dims, dtype)


def after(arrays, *earlier):
    def nothing(*refs):
        del refs

    count = len(arrays)
    return pl.pallas_call(
        nothing,
        out_shape=[jax.ShapeDtypeStruct(a.shape, a.dtype) for a in arrays],
        in_specs=[ANY] * (count + len(earlier)),
        out_specs=[ANY] * count,
        input_output_aliases={i: i for i in range(count)},
        compiler_params=pltpu.CompilerParams(vmem_limit_bytes=VMEM_LIMIT),
        cost_estimate=SHORT,
        name="after",
    )(*arrays, *earlier)


def kernel_call(body, grid, in_specs, out_specs, out_shape, operands, scratch, name, column=None, earlier=()):
    count = len(operands)

    def run(column_ref, *refs):
        del column_ref
        body(*refs[:count], *refs[count + len(earlier) :])

    column = jnp.zeros((1,), jnp.int32) if column is None else column.reshape(1).astype(jnp.int32)
    return pl.pallas_call(
        run,
        out_shape=out_shape,
        grid_spec=pltpu.PrefetchScalarGridSpec(
            num_scalar_prefetch=1,
            grid=grid,
            in_specs=list(in_specs) + [ANY] * len(earlier),
            out_specs=out_specs,
            scratch_shapes=scratch,
        ),
        compiler_params=pltpu.CompilerParams(vmem_limit_bytes=VMEM_LIMIT),
        cost_estimate=SHORT,
        name=name,
    )(column, *operands, *earlier)


def whole(array):
    return pl.BlockSpec(array.shape, lambda *_: (0,) * len(array.shape))


def join_plane(column, *pieces, earlier=()):
    rows, quarter = pieces[0].shape
    count = len(pieces)
    chunk = rows // 4

    def body(*refs):
        column_ref, sources, out = refs[0], refs[1 : 1 + count], refs[-1]
        for own_column in range(count):

            @pl.when(column_ref[0] == own_column)
            def _():
                for bit, source in enumerate(sources):
                    place = own_column ^ bit
                    out[:, place * quarter : (place + 1) * quarter] = source[...]

    return pl.pallas_call(
        body,
        out_shape=shape_of(rows, count * quarter),
        grid_spec=pltpu.PrefetchScalarGridSpec(
            num_scalar_prefetch=1,
            grid=(4,),
            in_specs=[pl.BlockSpec((chunk, quarter), lambda i, *_: (i, 0))] * count + [ANY] * len(earlier),
            out_specs=pl.BlockSpec((chunk, count * quarter), lambda i, *_: (i, 0)),
        ),
        compiler_params=pltpu.CompilerParams(vmem_limit_bytes=VMEM_LIMIT),
        cost_estimate=SHORT,
        name="join_plane",
    )(column.reshape(1).astype(jnp.int32), *pieces, *earlier)


def stack_pieces(pieces, earlier=()):
    rows, columns = pieces[0].shape
    count = len(pieces)

    def body(*refs):
        for i, ref in enumerate(refs[:count]):

            @pl.when(pl.program_id(0) == i)
            def _():
                refs[-1][...] = ref[...]

    return pl.pallas_call(
        body,
        out_shape=shape_of(count * rows, columns),
        grid=(count,),
        in_specs=[pl.BlockSpec((rows, columns), lambda i: (0, 0))] * count + [ANY] * len(earlier),
        out_specs=pl.BlockSpec((rows, columns), lambda i: (i, 0)),
        compiler_params=pltpu.CompilerParams(vmem_limit_bytes=VMEM_LIMIT),
        cost_estimate=SHORT,
        name="stack_pieces",
    )(*pieces, *earlier)


def on_piece(chip_ref, refs, use):
    step = pl.program_id(0)
    shift = lax.rem(chip_ref[0] - step // 2 + len(refs), len(refs))
    for i, ref in enumerate(refs):
        for core in range(2):

            @pl.when((shift == i) & (lax.rem(step, 2) == core))
            def _(ref=ref, core=core):
                use(ref.at[0, core])


def lay_out_shadow(pieces, w_down, units, chip, earlier=()):
    count = len(pieces)
    ep_count = 2 * count
    block_width = pieces[0].shape[3]
    apart = units + -units % 128
    hidden, width = w_down.shape

    def body(chip_ref, *refs):
        down_ref, shadow_ref, out = refs[count], refs[-2], refs[-1]

        def use(ref):
            shadow_ref[...] = jnp.zeros_like(shadow_ref)
            shadow_ref[:units, :] = ref[:units, :]
            shadow_ref[apart : apart + units, :] = ref[units : 2 * units, :]
            out[:hidden, :] = down_ref[...]
            out[hidden + units :, :] = jnp.zeros((apart - units, block_width), jnp.bfloat16)
            out[hidden : hidden + units, :] = ref[2 * units : 3 * units, :]

        on_piece(chip_ref, refs[:count], use)

    return pl.pallas_call(
        body,
        out_shape=[shape_of(2 * apart, width), shape_of(hidden + apart, width)],
        grid_spec=pltpu.PrefetchScalarGridSpec(
            num_scalar_prefetch=1,
            grid=(ep_count,),
            in_specs=[whole(p) for p in pieces]
            + [pl.BlockSpec((hidden, block_width), lambda e, *_: (0, e))]
            + [ANY] * len(earlier),
            out_specs=[
                pl.BlockSpec((2 * apart, block_width), lambda e, *_: (0, e)),
                pl.BlockSpec((hidden + apart, block_width), lambda e, *_: (0, e)),
            ],
        ),
        compiler_params=pltpu.CompilerParams(vmem_limit_bytes=VMEM_LIMIT),
        cost_estimate=SHORT,
        name="lay_out_shadow",
    )(chip.reshape(1).astype(jnp.int32), *pieces, w_down, *earlier)


def lay_out_grads(pieces, units, chip, earlier=()):
    count = len(pieces)
    ep_count = 2 * count
    block_width = pieces[0].shape[3]
    hidden = ep_count * units

    def body(chip_ref, *refs):
        gate_ref, up_ref, down_ref, gate_t, up_t = refs[-5:]
        place = pl.ds(pl.multiple_of(pl.program_id(0) * units, 16), units)

        def use(ref):
            gate_t[place, :] = ref[:units, :]
            up_t[place, :] = ref[units : 2 * units, :]
            down_ref[place, :] = ref[2 * units :, :]

        on_piece(chip_ref, refs[:count], use)

        @pl.when(pl.program_id(0) == ep_count - 1)
        def _():
            gate_ref[...] = gate_t[...].T
            up_ref[...] = up_t[...].T

    return pl.pallas_call(
        body,
        out_shape=[shape_of(block_width, hidden), shape_of(block_width, hidden), shape_of(hidden, block_width)],
        grid_spec=pltpu.PrefetchScalarGridSpec(
            num_scalar_prefetch=1,
            grid=(ep_count,),
            in_specs=[whole(p) for p in pieces] + [ANY] * len(earlier),
            out_specs=[pl.BlockSpec((block_width, hidden), lambda *_: (0, 0))] * 2
            + [pl.BlockSpec((hidden, block_width), lambda *_: (0, 0))],
            scratch_shapes=[pltpu.VMEM((hidden, block_width), jnp.bfloat16)] * 2,
        ),
        compiler_params=pltpu.CompilerParams(vmem_limit_bytes=VMEM_LIMIT),
        cost_estimate=SHORT,
        name="lay_out_grads",
    )(chip.reshape(1).astype(jnp.int32), *pieces, *earlier)


def row_specs(groups, tile):
    def spec(index, rows):
        return pl.BlockSpec((rows, tile), lambda k, *_: (index, k))

    return [spec(index, rows) for _, index, rows in groups]


def apply_gate(pre_gate, pre_up):
    sigmoid_gate = jax.nn.sigmoid(pre_gate)
    activated = pre_gate * sigmoid_gate
    hidden = (activated * pre_up).astype(jnp.bfloat16)
    return hidden, pre_up * sigmoid_gate * (1.0 + pre_gate * (1.0 - sigmoid_gate)), activated


def clear_first(acc):
    @pl.when(pl.program_id(0) == 0)
    def _():
        acc[...] = jnp.zeros_like(acc)


def forward_rows(groups, w_both, tile, transposed=False, earlier=()):
    rows = sum(g[2] for g in groups)
    if transposed:
        units, width = w_both.shape[0] // 2, w_both.shape[1]
        tile_spec = pl.BlockSpec((2 * units, tile), lambda k, *_: (0, k))
    else:
        width, units = w_both.shape[0], w_both.shape[1] // 2
        tile_spec = pl.BlockSpec((tile, 2 * units), lambda k, *_: (k, 0))
    steps = width // tile

    def body(*refs):
        n = len(groups)
        both_ref, hidden_ref, slope_ref, act_ref, acc = refs[n:]
        clear_first(acc)
        start = 0
        for ref, (_, _, count) in zip(refs[:n], groups):
            part = pl.ds(start, count)
            if transposed:
                acc[part, :] += contract_last(ref[...], both_ref[...])
            else:
                acc[part, :] += dot32(ref[...], both_ref[...])
            start += count

        @pl.when(pl.program_id(0) == steps - 1)
        def _():
            chunk = 64

            @pl.loop(0, rows // chunk)
            def _(i):
                part = pl.ds(pl.multiple_of(i * chunk, chunk), chunk)
                hidden, slope, act = apply_gate(acc[part, :units], acc[part, units:])
                hidden_ref[part, :] = hidden
                slope_ref[part, :] = slope
                act_ref[part, :] = act

    out_spec = pl.BlockSpec((rows, units), lambda *_: (0, 0))
    return kernel_call(
        body,
        (steps,),
        row_specs(groups, tile) + [tile_spec],
        [out_spec] * 3,
        [shape_of(rows, units), shape_of(rows, units, dtype=jnp.float32), shape_of(rows, units, dtype=jnp.float32)],
        [g[0] for g in groups] + [w_both],
        [pltpu.VMEM((rows, 2 * units), jnp.float32)],
        "forward_rows",
        earlier=earlier,
    )


def weigh_hidden(hidden_near, hidden_far, hidden_s, pieces, first_row, slot_rows, core, earlier=()):
    count = len(pieces)
    rows, units_s = hidden_s.shape
    units = hidden_near.shape[1]
    slots = [(s, 0) for s in list(range(1, count)) + [0]] + [(s, 1) for s in range(count)]

    def body(core_ref, *refs):
        near_ref, far_ref, s_ref, *piece_refs = refs[: 3 + count]
        out, w_ref, w_s_ref = refs[-3:]
        near, far = 0, 0
        for i, (slot, other) in enumerate(slots):
            part = pl.ds(i * slot_rows, slot_rows)
            table = piece_refs[slot][0, core_ref[0] ^ other, first_row : first_row + 16, :][:1].astype(jnp.float32)

            def column(j):
                both = table[:, j * slot_rows : (j + 1) * slot_rows]
                both = both + table[:, (j + 2) * slot_rows : (j + 3) * slot_rows]
                return jnp.broadcast_to(both, (slot_rows, slot_rows)).T[:, :1]

            weight, weight_s = column(0), column(1)
            w_ref[part, :] = weight
            w_s_ref[part, :] = weight_s
            if slot == 0:
                hidden = near_ref[near : near + slot_rows, :]
                near += slot_rows
            else:
                hidden = far_ref[far : far + slot_rows, :]
                far += slot_rows
            out[part, :units] = (hidden.astype(jnp.float32) * weight).astype(jnp.bfloat16)
            out[part, units:] = (s_ref[part, :].astype(jnp.float32) * weight_s).astype(jnp.bfloat16)

    return pl.pallas_call(
        body,
        out_shape=[
            shape_of(rows, units + units_s),
            shape_of(rows, 1, dtype=jnp.float32),
            shape_of(rows, 1, dtype=jnp.float32),
        ],
        grid_spec=pltpu.PrefetchScalarGridSpec(
            num_scalar_prefetch=1,
            grid=(1,),
            in_specs=[whole(a) for a in (hidden_near, hidden_far, hidden_s, *pieces)] + [ANY] * len(earlier),
            out_specs=[
                pl.BlockSpec((rows, units + units_s), lambda *_: (0, 0)),
                pl.BlockSpec((rows, 1), lambda *_: (0, 0)),
                pl.BlockSpec((rows, 1), lambda *_: (0, 0)),
            ],
        ),
        compiler_params=pltpu.CompilerParams(vmem_limit_bytes=VMEM_LIMIT),
        cost_estimate=SHORT,
        name="weigh_hidden",
    )(core.reshape(1).astype(jnp.int32), hidden_near, hidden_far, hidden_s, *pieces, *earlier)


def output_other(weighted, down, column, parts, slot_rows, quarter, earlier=()):
    rows, units = weighted.shape
    count = rows // 2 // parts

    def body(weighted_ref, down_ref, *outs):
        for i, out in enumerate(outs):
            first, last = slot_rows + i * count, slot_rows + (i + 1) * count
            kept = min(last, rows // 2) - first
            value = dot32(weighted_ref[first : first + kept, :], down_ref[...])
            out[:kept, :] = value.astype(jnp.bfloat16)
            if kept < count:
                value = dot32(weighted_ref[: count - kept, :], down_ref[...])
                out[kept:, :] = value.astype(jnp.bfloat16)

    return kernel_call(
        body,
        (4,),
        [
            pl.BlockSpec((rows // 2, units), lambda *_: (1, 0)),
            pl.BlockSpec((units, quarter), lambda q, column_ref: (0, column_ref[0] ^ q)),
        ],
        [pl.BlockSpec((count, quarter), lambda q, *_: (0, q))] * parts,
        [shape_of(count, 4 * quarter)] * parts,
        [weighted, down],
        [],
        "output_other",
        column=column,
        earlier=earlier,
    )


def output_own(weighted, got, down, column, quarter, earlier=()):
    count, units = got[0].shape[0], weighted.shape[1]
    parts = len(got)

    def body(weighted_ref, down_ref, *refs):
        for i in range(parts):
            value = dot32(weighted_ref[i * count : (i + 1) * count, :], down_ref[...])
            value = value + refs[i][...].astype(jnp.float32)
            for j, out in enumerate(refs[parts + 4 * i : parts + 4 * i + 4]):

                @pl.when(pl.program_id(0) == 3 - j)
                def _(out=out, value=value):
                    out[...] = value.astype(out.dtype)

    full = pl.BlockSpec((count, quarter), lambda *_: (0, 0))
    out = kernel_call(
        body,
        (4,),
        [
            pl.BlockSpec((parts * count, units), lambda *_: (0, 0)),
            pl.BlockSpec((units, quarter), lambda q, column_ref: (0, column_ref[0] ^ 3 ^ q)),
        ]
        + [pl.BlockSpec((count, quarter), lambda q, *_: (0, 3 - q))] * parts,
        [full] * (4 * parts),
        ([shape_of(count, quarter, dtype=jnp.float32)] + [shape_of(count, quarter)] * 3) * parts,
        [weighted, down] + list(got),
        [],
        "output_own",
        column=column,
        earlier=earlier,
    )
    return [out[4 * i : 4 * i + 4] for i in range(parts)]


def backward_rows(groups, down, parts, per_row, first_row, tile, earlier=()):
    slope_s, act_s, w_rows, w_shadow = per_row
    rows = sum(g[2] for g in groups)
    units_all, width = down.shape
    units_s = slope_s.shape[1]
    units = units_all - units_s
    steps = width // tile
    arrays = list({id(a): a for part in parts for a in part[:2]}.values())
    places = [[next(i for i, a in enumerate(arrays) if a is b) for b in part[:2]] for part in parts]

    def body(*refs):
        n, m = len(groups), len(arrays)
        down_ref = refs[n]
        array_refs = refs[n + 1 : n + 1 + m]
        slope_s_ref, act_s_ref, w_ref, w_s_ref, pre_ref, pre_s_ref, acc = refs[n + 1 + m :]
        clear_first(acc)
        start = 0
        for ref, (_, _, count) in zip(refs[:n], groups):
            acc[pl.ds(start, count), :] += contract_last(ref[...], down_ref[...])
            start += count

        @pl.when(pl.program_id(0) == steps - 1)
        def _():
            chunk = 64
            start = 0
            for (_, _, count), (_, _, first), (slope_at, act_at) in zip(groups, parts, places):

                @pl.loop(0, count // chunk)
                def _(i, start=start, first=first, slope_ref=array_refs[slope_at], act_ref=array_refs[act_at]):
                    source = pl.ds(pl.multiple_of(first + i * chunk, chunk), chunk)
                    part = pl.ds(pl.multiple_of(start + i * chunk, chunk), chunk)
                    whole_part = pl.ds(pl.multiple_of(first_row + start + i * chunk, chunk), chunk)
                    grad = acc[part, :units] * w_ref[whole_part, :]
                    pre_ref[part, :units] = (grad * slope_ref[source, :]).astype(jnp.bfloat16)
                    pre_ref[part, units:] = (grad * act_ref[source, :]).astype(jnp.bfloat16)
                    grad = acc[part, units:] * w_s_ref[whole_part, :]
                    pre_s_ref[part, :units_s] = (grad * slope_s_ref[whole_part, :]).astype(jnp.bfloat16)
                    pre_s_ref[part, units_s:] = (grad * act_s_ref[whole_part, :]).astype(jnp.bfloat16)

                start += count

    extra = arrays + [slope_s, act_s, w_rows, w_shadow]
    return kernel_call(
        body,
        (steps,),
        row_specs(groups, tile) + [pl.BlockSpec((units_all, tile), lambda k, *_: (0, k))] + [whole(a) for a in extra],
        [pl.BlockSpec((rows, 2 * units), lambda *_: (0, 0)), pl.BlockSpec((rows, 2 * units_s), lambda *_: (0, 0))],
        [shape_of(rows, 2 * units), shape_of(rows, 2 * units_s)],
        [g[0] for g in groups] + [down] + extra,
        [pltpu.VMEM((rows, units_all), jnp.float32)],
        "backward_rows",
        earlier=earlier,
    )


def stage_rows(refs, groups, held):
    start = 0
    for ref, (_, _, count) in zip(refs, groups):
        held[pl.ds(start, count), :] = ref[...]
        start += count
    return held[...]


def shadow_grads(x_groups, dy_groups, pre_s, weighted, units, tile, earlier=()):
    rows, wide = weighted.shape[0], pre_s[0].shape[1]
    apart = wide // 2
    width = x_groups[0][0].shape[1]
    m = len(pre_s)

    def body(*refs):
        n = len(x_groups)
        pre_refs = refs[2 * n : 2 * n + m]
        hidden_ref, out, held, pre_t, hidden_t = refs[2 * n + m :]

        @pl.when(pl.program_id(0) == 0)
        def _():
            start = 0
            for ref in pre_refs:
                pre_t[:, start : start + ref.shape[0]] = ref[...].T
                start += ref.shape[0]
            hidden_t[...] = hidden_ref[...].T

        value = dot32(pre_t[...], stage_rows(refs[:n], x_groups, held))
        out[:units, :] = value[:units].astype(jnp.bfloat16)
        out[units : 2 * units, :] = value[apart : apart + units].astype(jnp.bfloat16)
        value = dot32(hidden_t[...], stage_rows(refs[n : 2 * n], dy_groups, held))
        out[2 * units :, :] = value[:units].astype(jnp.bfloat16)

    (out,) = kernel_call(
        body,
        (width // tile,),
        row_specs(x_groups, tile)
        + row_specs(dy_groups, tile)
        + [whole(p) for p in pre_s]
        + [pl.BlockSpec((rows, apart), lambda *_: (0, weighted.shape[1] // apart - 1))],
        [pl.BlockSpec((3 * units, tile), lambda k, *_: (0, k))],
        [shape_of(3 * units, width)],
        [g[0] for g in x_groups + dy_groups] + list(pre_s) + [weighted],
        [
            pltpu.VMEM((rows, tile), jnp.bfloat16),
            pltpu.VMEM((wide, rows), jnp.bfloat16),
            pltpu.VMEM((apart, rows), jnp.bfloat16),
        ],
        "shadow_grads",
        earlier=earlier,
    )
    return out


def input_grads(groups, pre, tile, earlier=()):
    both = pre[0].shape[1]
    rows = sum(p.shape[0] for p in pre)
    units = both // 2
    width = groups[0][0].shape[1]
    m = len(pre)

    def body(*refs):
        n = len(groups)
        gate_ref, up_ref, held, pre_held = refs[n + m :]

        @pl.when(pl.program_id(0) == 0)
        def _():
            start = 0
            for ref in refs[n : n + m]:
                pre_held[start : start + ref.shape[0], :] = ref[...]
                start += ref.shape[0]

        value = contract_rows(stage_rows(refs[:n], groups, held), pre_held[...])
        gate_ref[...] = value[:, :units].astype(jnp.bfloat16)
        up_ref[...] = value[:, units:].astype(jnp.bfloat16)

    return kernel_call(
        body,
        (width // tile,),
        row_specs(groups, tile) + [whole(p) for p in pre],
        [pl.BlockSpec((tile, units), lambda k, *_: (k, 0))] * 2,
        [shape_of(width, units)] * 2,
        [g[0] for g in groups] + list(pre),
        [pltpu.VMEM((rows, tile), jnp.bfloat16), pltpu.VMEM((rows, both), jnp.bfloat16)],
        "input_grads",
        earlier=earlier,
    )


def down_grad(groups, weighted, units, tile, earlier=()):
    rows = weighted.shape[0]
    width = groups[0][0].shape[1]

    def body(*refs):
        n = len(groups)
        hidden_ref, out, held, hidden_t = refs[n:]

        @pl.when(pl.program_id(0) == 0)
        def _():
            hidden_t[...] = hidden_ref[...].T

        out[...] = dot32(hidden_t[...], stage_rows(refs[:n], groups, held)).astype(jnp.bfloat16)

    (out,) = kernel_call(
        body,
        (width // tile,),
        row_specs(groups, tile) + [pl.BlockSpec((rows, units), lambda *_: (0, 0))],
        [pl.BlockSpec((units, tile), lambda k, *_: (0, k))],
        [shape_of(units, width)],
        [g[0] for g in groups] + [weighted],
        [pltpu.VMEM((rows, tile), jnp.bfloat16), pltpu.VMEM((units, rows), jnp.bfloat16)],
        "down_grad",
        earlier=earlier,
    )
    return out


def send_along_z(own):
    ep_count = lax.axis_size("ep")
    return [lax.ppermute(own, "ep", ring_pairs(ep_count, 2 * s)) for s in range(1, ep_count // 2)]


def swap_cores(block):
    return lax.ppermute(block, "ep", swap_pairs(lax.axis_size("ep"), 1))


def send_plane(*pieces):
    pieces = pieces * (3 // len(pieces))
    return [lax.ppermute(p, "tp", swap_pairs(lax.axis_size("tp"), bit)) for p, bit in zip(pieces, (1, 2, 3))]


def exchange_cores(blocks):
    ep_count, core = lax.axis_size("ep"), lax.axis_index("ep") % 2
    pairs = blocks.reshape(ep_count // 2, 2, *blocks.shape[1:])
    kept = jnp.where(core == 0, pairs[:, 0], pairs[:, 1])
    given = jnp.where(core == 0, pairs[:, 1], pairs[:, 0])
    return kept, swap_cores(given)


def exchange_chips(kept, taken, in_turn=False, earlier=()):
    ep_count, me = lax.axis_size("ep"), lax.axis_index("ep")
    chips, chip, core = ep_count // 2, me // 2, me % 2
    both = jnp.stack([jnp.where(core == 0, kept, taken), jnp.where(core == 0, taken, kept)], axis=1)
    pieces = [lax.dynamic_index_in_dim(both, (chip + shift) % chips, 0) for shift in range(chips)]
    if earlier:
        pieces = after(pieces, *earlier)
    result = [pieces[0]]
    for shift in range(1, chips):
        piece = pieces[shift]
        if in_turn and shift > 1:
            (piece,) = after([piece], result[-1])
        result.append(lax.ppermute(piece, "ep", ring_pairs(ep_count, 2 * shift)))
    return result


def dense_shards(
    tokens,
    cotangent,
    expert_ids,
    gate_weights,
    shadow_mask,
    w_gate,
    w_up,
    w_down,
    s_gate,
    s_up,
    s_down,
):
    ep_count, tp_count = lax.axis_size("ep"), lax.axis_size("tp")
    ep_index, tp_index = lax.axis_index("ep"), lax.axis_index("tp")
    tok_count, top_count = expert_ids.shape
    quarter = tokens.shape[1]
    width = quarter * tp_count
    hidden_part = w_gate.shape[2]
    shadow_part = hidden_part // ep_count
    block_width = s_gate.shape[0]
    steps = ep_count // 2
    later = (steps - 1) * tok_count
    tile = width // 8
    along, across = swap_pairs(tp_count, 1), swap_pairs(tp_count, 2)

    picked = expert_ids[None, :, :] == jnp.arange(ep_count, dtype=jnp.int32)[:, None, None]
    table = jnp.sum(jnp.where(picked, gate_weights[None, :, :top_count], 0.0), axis=2)
    shadow_weight = gate_weights[:, top_count] * shadow_mask.astype(jnp.float32)
    table = jnp.concatenate([table, jnp.broadcast_to(shadow_weight[None], table.shape)], axis=1)
    table = jnp.concatenate(split_parts(table), axis=1)
    table = jnp.pad(table[:, None, :], ((0, 0), (0, 15), (0, block_width - table.shape[1])))
    shadow_blocks = jnp.concatenate(
        [
            s_gate.T.reshape(ep_count, shadow_part, block_width),
            s_up.T.reshape(ep_count, shadow_part, block_width),
            s_down.reshape(ep_count, shadow_part, block_width),
            table,
        ],
        axis=1,
    )

    x_z = send_along_z(tokens)
    near = stack_pieces([tokens, cotangent])
    near_late = stack_pieces([tokens, cotangent], earlier=[x_z[0]])
    near_plane = send_plane(near, near, near_late)
    w_both = jnp.concatenate([w_gate[0], w_up[0]], axis=1)
    *x_z, near_x, near_y, near_d = after(x_z + near_plane, w_both, shadow_blocks)

    x_piece = stack_pieces(x_z)
    x_plane = send_plane(x_piece)
    (dy_first,) = after([cotangent], x_z[0])
    dy_z = send_along_z(dy_first)
    near_own = join_plane(tp_index, near, near_x, near_y, near_d)
    near_other = swap_cores(near_own)
    x_near = [(near_own, 0, tok_count), (near_other, 0, tok_count)]
    hidden_near, slope_near, act_near = forward_rows(x_near, w_both, 2 * tile)
    (shadow_blocks,) = after([shadow_blocks], x_z[0])
    shadow_kept, shadow_taken = exchange_cores(shadow_blocks)
    fenced = after([*x_plane, *dy_z, shadow_taken], hidden_near)
    x_plane, dy_z, shadow_taken = fenced[:3], fenced[3:-1], fenced[-1]

    dy_piece = stack_pieces(dy_z)
    dy_plane = send_plane(dy_piece)
    shadow_pieces = exchange_chips(shadow_kept, shadow_taken)
    x_own = join_plane(tp_index, x_piece, *x_plane, earlier=[dy_piece])
    x_other = swap_cores(x_own)
    x_far = [(x_own, 0, later), (x_other, 0, later)]
    x_groups = [x_far[0], x_near[0], x_near[1], x_far[1]]
    hidden_far, slope_far, act_far = forward_rows(x_far, w_both, 2 * tile)
    chip = ep_index // 2
    shadow_in, down = lay_out_shadow(shadow_pieces, w_down[0], shadow_part, chip, earlier=[hidden_far])
    hidden_s, slope_s, act_s = forward_rows(x_groups, shadow_in, 2 * tile, transposed=True)

    weighted, w_rows, w_shadow = weigh_hidden(
        hidden_near, hidden_far, hidden_s, shadow_pieces, 3 * shadow_part, tok_count, ep_index % 2
    )

    parts = 2 if steps % 2 == 0 else 1
    sent = output_other(weighted, down, tp_index, parts, tok_count, quarter)
    got = [swap_cores(array) for array in sent]
    dy_plane = after(dy_plane, *sent)

    dy_own = join_plane(tp_index, dy_piece, *dy_plane)
    dy_other = swap_cores(dy_own)
    dy_groups = [(dy_own, 0, later), (near_own, 1, tok_count), (near_other, 1, tok_count), (dy_other, 0, later)]
    segments = [
        (slope_far, act_far, 0),
        (slope_near, act_near, 0),
        (slope_near, act_near, tok_count),
        (slope_far, act_far, later),
    ]
    per_row = (slope_s, act_s, w_rows, w_shadow)
    pre_first, pre_s_first = backward_rows(dy_groups[:3], down, segments[:3], per_row, 0, tile)
    owns = output_own(weighted, got, down, tp_index, quarter, earlier=[pre_first])
    sums = [send_plane(*own[1:]) for own in owns]
    first_rows = sum(g[2] for g in dy_groups[:3])
    pre_last, pre_s_last = backward_rows(
        dy_groups[3:], down, segments[3:], per_row, first_rows, tile, earlier=[own[1] for own in owns]
    )
    pre, pre_s = [pre_first, pre_last], [pre_s_first, pre_s_last]
    grad_s = shadow_grads(x_groups, dy_groups, pre_s, weighted, shadow_part, tile)
    blocks = grad_s.reshape(3 * shadow_part, ep_count, block_width).transpose(1, 0, 2)
    grad_kept, grad_taken = exchange_cores(blocks)
    sums[0] = after(sums[0], grad_s)

    def slot_rows(i):
        part = slice(i % (steps // parts) * tok_count, (i % (steps // parts) + 1) * tok_count)
        total = owns[i * parts // steps][0][part]
        for array in sums[i * parts // steps]:
            total = total + array[part].astype(jnp.float32)
        return total

    first = [slot_rows(i).astype(jnp.bfloat16) for i in range(steps // parts)]
    grad_pieces = exchange_chips(grad_kept, grad_taken, earlier=first)
    grad_gate, grad_up = input_grads(x_groups, pre, tile, earlier=[grad_pieces[0]])
    if parts > 1:
        sums[-1] = after(sums[-1], grad_gate)
    total = slot_rows(steps - 1)
    pieces = first + [slot_rows(i).astype(jnp.bfloat16) for i in range(len(first), steps - 1)]
    grad_down = down_grad(dy_groups, weighted, hidden_part, tile, earlier=[pieces[-1], grad_gate])
    for s in range(1, steps):
        total = total + lax.ppermute(pieces[s - 1], "ep", ring_pairs(ep_count, -2 * s)).astype(jnp.float32)
    mixed = total.astype(jnp.bfloat16)

    grads_s = lay_out_grads(grad_pieces, shadow_part, chip, earlier=[grad_down])
    return (mixed, grad_gate[None], grad_up[None], grad_down[None], *grads_s)


def shards(tokens, cotangent, expert_ids, *others):
    tp_count, ep_count = lax.axis_size("tp"), lax.axis_size("ep")
    tok_count, top_count = expert_ids.shape
    rows = (5 * tok_count * top_count) // 4
    fits = tp_count == 4 and ep_count % 2 == 0 and tok_count % 128 == 0
    dense = fits and ep_count * tok_count <= 3 * rows
    return (dense_shards if dense else routed_shards)(tokens, cotangent, expert_ids, *others)


def solution(mesh):
    return jax.shard_map(
        shards,
        mesh=mesh,
        in_specs=(
            P("ep", "tp"),
            P("ep", "tp"),
            P("ep", None),
            P("ep", None),
            P("ep"),
            P("ep", None, "tp"),
            P("ep", None, "tp"),
            P("ep", "tp", None),
            P("ep", "tp"),
            P("ep", "tp"),
            P("tp", "ep"),
        ),
        out_specs=(
            P("ep", "tp"),
            P("ep", None, "tp"),
            P("ep", None, "tp"),
            P("ep", "tp", None),
            P("ep", "tp"),
            P("ep", "tp"),
            P("tp", "ep"),
        ),
        check_vma=False,
    )
```

```python
import functools

import jax
import jax.numpy as jnp
from jax import lax
from jax.experimental import pallas as pl
from jax.experimental.pallas import tpu as pltpu
from jax.sharding import PartitionSpec as P


def contract_rows(left, right):
    return lax.dot_general(
        left, right, (((0,), (0,)), ((), ())), preferred_element_type=jnp.float32
    )


def split_parts(values):
    upper_part = values.astype(jnp.bfloat16)
    lower_part = (values - upper_part.astype(jnp.float32)).astype(jnp.bfloat16)
    return (upper_part, lower_part)


def weigh_rows(weight_table, rows):
    weight_upper, weight_lower = split_parts(weight_table)
    return jnp.dot(weight_upper, rows, preferred_element_type=jnp.float32) + jnp.dot(
        weight_lower, rows, preferred_element_type=jnp.float32
    )


def expert_pass(rows_x, rows_dout, weight_gate, weight_up, weight_down):
    pre_gate = jnp.dot(rows_x, weight_gate, preferred_element_type=jnp.float32)
    pre_up = jnp.dot(rows_x, weight_up, preferred_element_type=jnp.float32)
    sigmoid_gate = jax.nn.sigmoid(pre_gate)
    activated = pre_gate * sigmoid_gate
    hidden = (activated * pre_up).astype(jnp.bfloat16)
    partial_out = jnp.dot(hidden, weight_down, preferred_element_type=jnp.float32).astype(
        jnp.bfloat16
    )
    hidden_grad = lax.dot_general(
        rows_dout, weight_down, (((1,), (1,)), ((), ())), preferred_element_type=jnp.float32
    )
    grad_pre_gate = (
        hidden_grad * pre_up * sigmoid_gate * (1.0 + pre_gate * (1.0 - sigmoid_gate))
    ).astype(jnp.bfloat16)
    grad_pre_up = (hidden_grad * activated).astype(jnp.bfloat16)
    return (partial_out, hidden, grad_pre_gate, grad_pre_up)


def routed_shards(
    tokens,
    cotangent,
    expert_ids,
    gate_weights,
    shadow_mask,
    w_gate,
    w_up,
    w_down,
    s_gate,
    s_up,
    s_down,
):
    ep_count = lax.axis_size("ep")
    tok_count, top_count = expert_ids.shape
    quarter_width = tokens.shape[1]
    width = quarter_width * lax.axis_size("tp")
    expert_count = w_gate.shape[0] * ep_count
    capacity = (5 * tok_count * top_count + 4 * expert_count - 1) // (4 * expert_count)
    slot_count = expert_count * capacity
    picks_flat = expert_ids.reshape(-1)
    onehot = (picks_flat[:, None] == jnp.arange(expert_count, dtype=jnp.int32)[None, :]).astype(
        jnp.int32
    )
    slot_rank = jnp.sum((jnp.cumsum(onehot, axis=0) - onehot) * onehot, axis=1)
    slot_index = (picks_flat * capacity + slot_rank).reshape(tok_count, top_count)
    matches = jnp.arange(slot_count, dtype=jnp.int32)[:, None, None] == slot_index[None, :, :]
    dispatch = jnp.any(matches, axis=2).astype(jnp.bfloat16)
    weighting = jnp.sum(jnp.where(matches, gate_weights[None, :, :top_count], 0.0), axis=2)
    slot_gate = jnp.sum(weighting, axis=1)
    shadow_weight = gate_weights[:, top_count] * shadow_mask.astype(jnp.float32)
    x_full, dy_full = (
        lax.all_gather(tokens, "tp", axis=1, tiled=True),
        lax.all_gather(cotangent, "tp", axis=1, tiled=True),
    )
    rows_x = jnp.dot(dispatch, tokens, preferred_element_type=jnp.float32).astype(jnp.bfloat16)
    rows_dy = jnp.dot(dispatch, cotangent, preferred_element_type=jnp.float32)
    rows_dout = (slot_gate[:, None] * rows_dy).astype(jnp.bfloat16)
    recv_x, recv_dout = (
        lax.all_to_all(
            rows_x.reshape(ep_count, -1, quarter_width),
            "ep",
            split_axis=0,
            concat_axis=0,
            tiled=True,
        ),
        lax.all_to_all(
            rows_dout.reshape(ep_count, -1, quarter_width),
            "ep",
            split_axis=0,
            concat_axis=0,
            tiled=True,
        ),
    )
    expert_x, expert_dout = (
        lax.all_gather(recv_x.reshape(-1, quarter_width), "tp", axis=1, tiled=True),
        lax.all_gather(recv_dout.reshape(-1, quarter_width), "tp", axis=1, tiled=True),
    )
    partial_out, hidden, grad_pre_gate, grad_pre_up = expert_pass(
        expert_x, expert_dout, w_gate[0], w_up[0], w_down[0]
    )
    grad_gate = contract_rows(expert_x, grad_pre_gate).astype(jnp.bfloat16)[None]
    grad_up = contract_rows(expert_x, grad_pre_up).astype(jnp.bfloat16)[None]
    grad_down = contract_rows(hidden, expert_dout).astype(jnp.bfloat16)[None]
    full_gate, full_up, full_down = (
        lax.all_gather(s_gate, "ep", axis=0, tiled=True),
        lax.all_gather(s_up, "ep", axis=0, tiled=True),
        lax.all_gather(s_down, "ep", axis=1, tiled=True),
    )
    shadow_dout = (shadow_weight[:, None] * dy_full.astype(jnp.float32)).astype(jnp.bfloat16)
    shadow_out, shadow_hidden, shadow_gate_pre, shadow_up_pre = expert_pass(
        x_full, shadow_dout, full_gate, full_up, full_down
    )
    shadow_sums = lax.psum_scatter(
        jnp.concatenate(
            [
                contract_rows(x_full, shadow_gate_pre),
                contract_rows(x_full, shadow_up_pre),
                contract_rows(shadow_dout, shadow_hidden),
            ],
            axis=1,
        ).astype(jnp.bfloat16),
        "ep",
        scatter_dimension=0,
        tiled=True,
    ).astype(jnp.float32)
    hidden_part = s_gate.shape[1]
    grad_s_gate = shadow_sums[:, :hidden_part].astype(jnp.bfloat16)
    grad_s_up = shadow_sums[:, hidden_part : 2 * hidden_part].astype(jnp.bfloat16)
    grad_s_down = shadow_sums[:, 2 * hidden_part :].T.astype(jnp.bfloat16)
    back_rows = lax.all_to_all(
        partial_out.reshape(ep_count, -1, width), "ep", split_axis=0, concat_axis=0, tiled=True
    ).reshape(-1, width)
    term = weigh_rows(weighting.T, back_rows)
    term = term + shadow_weight[:, None] * shadow_out.astype(jnp.float32)
    mixed = lax.psum_scatter(term.astype(jnp.bfloat16), "tp", scatter_dimension=1, tiled=True)
    return (mixed, grad_gate, grad_up, grad_down, grad_s_gate, grad_s_up, grad_s_down)


ANY = pl.BlockSpec(memory_space=pl.ANY)
VMEM_LIMIT = 60 * 1024 * 1024
SHORT = pl.CostEstimate(flops=1, bytes_accessed=1, transcendentals=0)


def swap_pairs(count, bit):
    return [(i, i ^ bit) for i in range(count)]


def dot32(left, right):
    return jnp.dot(left, right, preferred_element_type=jnp.float32)


def contract_last(left, right):
    return lax.dot_general(
        left, right, (((1,), (1,)), ((), ())), preferred_element_type=jnp.float32
    )


def shape_of(*dims, dtype=jnp.bfloat16):
    return jax.ShapeDtypeStruct(dims, dtype)


def after(arrays, *earlier):
    def nothing(*refs):
        del refs

    count = len(arrays)
    return pl.pallas_call(
        nothing,
        out_shape=[jax.ShapeDtypeStruct(a.shape, a.dtype) for a in arrays],
        in_specs=[ANY] * (count + len(earlier)),
        out_specs=[ANY] * count,
        input_output_aliases={i: i for i in range(count)},
        compiler_params=pltpu.CompilerParams(vmem_limit_bytes=VMEM_LIMIT),
        cost_estimate=SHORT,
        name="after",
    )(*arrays, *earlier)


def kernel_call(body, grid, in_specs, out_specs, out_shape, operands, scratch, name, column=None, earlier=()):
    count = len(operands)

    def run(column_ref, *refs):
        del column_ref
        body(*refs[:count], *refs[count + len(earlier) :])

    column = jnp.zeros((1,), jnp.int32) if column is None else column.reshape(1).astype(jnp.int32)
    return pl.pallas_call(
        run,
        out_shape=out_shape,
        grid_spec=pltpu.PrefetchScalarGridSpec(
            num_scalar_prefetch=1,
            grid=grid,
            in_specs=list(in_specs) + [ANY] * len(earlier),
            out_specs=out_specs,
            scratch_shapes=scratch,
        ),
        compiler_params=pltpu.CompilerParams(vmem_limit_bytes=VMEM_LIMIT),
        cost_estimate=SHORT,
        name=name,
    )(column, *operands, *earlier)


def whole(array):
    return pl.BlockSpec(array.shape, lambda *_: (0,) * len(array.shape))


def join_plane(column, *pieces, earlier=()):
    rows, quarter = pieces[0].shape
    count = len(pieces)
    chunk = rows // 4

    def body(*refs):
        column_ref, sources, out = refs[0], refs[1 : 1 + count], refs[-1]
        for own_column in range(count):

            @pl.when(column_ref[0] == own_column)
            def _():
                for bit, source in enumerate(sources):
                    place = own_column ^ bit
                    out[:, place * quarter : (place + 1) * quarter] = source[...]

    return pl.pallas_call(
        body,
        out_shape=shape_of(rows, count * quarter),
        grid_spec=pltpu.PrefetchScalarGridSpec(
            num_scalar_prefetch=1,
            grid=(4,),
            in_specs=[pl.BlockSpec((chunk, quarter), lambda i, *_: (i, 0))] * count + [ANY] * len(earlier),
            out_specs=pl.BlockSpec((chunk, count * quarter), lambda i, *_: (i, 0)),
        ),
        compiler_params=pltpu.CompilerParams(vmem_limit_bytes=VMEM_LIMIT),
        cost_estimate=SHORT,
        name="join_plane",
    )(column.reshape(1).astype(jnp.int32), *pieces, *earlier)


def stack_pieces(pieces, earlier=()):
    rows, columns = pieces[0].shape
    count = len(pieces)

    def body(*refs):
        for i, ref in enumerate(refs[:count]):

            @pl.when(pl.program_id(0) == i)
            def _():
                refs[-1][...] = ref[...]

    return pl.pallas_call(
        body,
        out_shape=shape_of(count * rows, columns),
        grid=(count,),
        in_specs=[pl.BlockSpec((rows, columns), lambda i: (0, 0))] * count + [ANY] * len(earlier),
        out_specs=pl.BlockSpec((rows, columns), lambda i: (i, 0)),
        compiler_params=pltpu.CompilerParams(vmem_limit_bytes=VMEM_LIMIT),
        cost_estimate=SHORT,
        name="stack_pieces",
    )(*pieces, *earlier)


def on_piece(chip_ref, refs, use):
    step = pl.program_id(0)
    shift = chip_ref[0] ^ (step // 2)
    for i, ref in enumerate(refs):
        for core in range(2):

            @pl.when((shift == i) & (lax.rem(step, 2) == core))
            def _(ref=ref, core=core):
                use(ref.at[0, core])


def lay_out_shadow(pieces, down, units, chip, earlier=()):
    count = len(pieces)
    ep_count = 2 * count
    block_width = pieces[0].shape[3]
    apart = units + -units % 128
    all_units, width = down.shape

    def body(chip_ref, *refs):
        shadow_ref, out = refs[-2:]

        def use(ref):
            shadow_ref[...] = jnp.zeros_like(shadow_ref)
            shadow_ref[:units, :] = ref[:units, :]
            shadow_ref[apart : apart + units, :] = ref[units : 2 * units, :]
            out[units:, :] = jnp.zeros((apart - units, block_width), jnp.bfloat16)
            out[:units, :] = ref[2 * units : 3 * units, :]

        on_piece(chip_ref, refs[:count], use)

    return pl.pallas_call(
        body,
        out_shape=[shape_of(2 * apart, width), shape_of(all_units, width)],
        grid_spec=pltpu.PrefetchScalarGridSpec(
            num_scalar_prefetch=1,
            grid=(ep_count,),
            in_specs=[whole(p) for p in pieces] + [ANY] * (1 + len(earlier)),
            out_specs=[
                pl.BlockSpec((2 * apart, block_width), lambda e, *_: (0, e)),
                pl.BlockSpec((apart, block_width), lambda e, *_: (all_units // apart - 1, e)),
            ],
        ),
        input_output_aliases={1 + count: 1},
        compiler_params=pltpu.CompilerParams(vmem_limit_bytes=VMEM_LIMIT),
        cost_estimate=SHORT,
        name="lay_out_shadow",
    )(chip.reshape(1).astype(jnp.int32), *pieces, down, *earlier)


def lay_out_grads(pieces, units, chip, earlier=()):
    count = len(pieces)
    ep_count = 2 * count
    block_width = pieces[0].shape[3]
    hidden = ep_count * units

    def body(chip_ref, *refs):
        gate_ref, up_ref, down_ref, gate_t, up_t = refs[-5:]
        place = pl.ds(pl.multiple_of(pl.program_id(0) * units, 16), units)

        def use(ref):
            gate_t[place, :] = ref[:units, :]
            up_t[place, :] = ref[units : 2 * units, :]
            down_ref[place, :] = ref[2 * units :, :]

        on_piece(chip_ref, refs[:count], use)

        @pl.when(pl.program_id(0) == ep_count - 1)
        def _():
            gate_ref[...] = gate_t[...].T
            up_ref[...] = up_t[...].T

    return pl.pallas_call(
        body,
        out_shape=[shape_of(block_width, hidden), shape_of(block_width, hidden), shape_of(hidden, block_width)],
        grid_spec=pltpu.PrefetchScalarGridSpec(
            num_scalar_prefetch=1,
            grid=(ep_count,),
            in_specs=[whole(p) for p in pieces] + [ANY] * len(earlier),
            out_specs=[pl.BlockSpec((block_width, hidden), lambda *_: (0, 0))] * 2
            + [pl.BlockSpec((hidden, block_width), lambda *_: (0, 0))],
            scratch_shapes=[pltpu.VMEM((hidden, block_width), jnp.bfloat16)] * 2,
        ),
        compiler_params=pltpu.CompilerParams(vmem_limit_bytes=VMEM_LIMIT),
        cost_estimate=SHORT,
        name="lay_out_grads",
    )(chip.reshape(1).astype(jnp.int32), *pieces, *earlier)


def row_specs(groups, tile):
    def spec(index, rows):
        return pl.BlockSpec((rows, tile), lambda k, *_: (index, k))

    return [spec(index, rows) for _, index, rows in groups]


def apply_gate(pre_gate, pre_up):
    sigmoid_gate = jax.nn.sigmoid(pre_gate)
    activated = pre_gate * sigmoid_gate
    hidden = (activated * pre_up).astype(jnp.bfloat16)
    return hidden, pre_up * sigmoid_gate * (1.0 + pre_gate * (1.0 - sigmoid_gate)), activated


def clear_first(acc):
    @pl.when(pl.program_id(0) == 0)
    def _():
        acc[...] = jnp.zeros_like(acc)


def rows_operand(refs, groups, held):
    if len(groups) == 1:
        return refs[0][...]
    return stage_rows(refs, groups, held)


def forward_rows(groups, w_both, tile, transposed=False, earlier=()):
    rows = sum(g[2] for g in groups)
    if transposed:
        units, width = w_both.shape[0] // 2, w_both.shape[1]
        tile_spec = pl.BlockSpec((2 * units, tile), lambda k, *_: (0, k))
    else:
        width, units = w_both.shape[0], w_both.shape[1] // 2
        tile_spec = pl.BlockSpec((tile, 2 * units), lambda k, *_: (k, 0))
    steps = width // tile

    def body(*refs):
        n = len(groups)
        both_ref, hidden_ref, slope_ref, act_ref, acc, held = refs[n:]
        clear_first(acc)
        operand = rows_operand(refs[:n], groups, held)
        acc[...] += contract_last(operand, both_ref[...]) if transposed else dot32(operand, both_ref[...])

        @pl.when(pl.program_id(0) == steps - 1)
        def _():
            chunk = 128

            @pl.loop(0, rows // chunk)
            def _(i):
                part = pl.ds(pl.multiple_of(i * chunk, chunk), chunk)
                hidden, slope, act = apply_gate(acc[part, :units], acc[part, units:])
                hidden_ref[part, :] = hidden
                slope_ref[part, :] = slope.astype(jnp.bfloat16)
                act_ref[part, :] = act.astype(jnp.bfloat16)

    out_spec = pl.BlockSpec((rows, units), lambda *_: (0, 0))
    return kernel_call(
        body,
        (steps,),
        row_specs(groups, tile) + [tile_spec],
        [out_spec] * 3,
        [shape_of(rows, units)] * 3,
        [g[0] for g in groups] + [w_both],
        [pltpu.VMEM((rows, 2 * units), jnp.float32), pltpu.VMEM((rows, tile), jnp.bfloat16)],
        "forward_rows",
        earlier=earlier,
    )


def weigh_hidden(hidden_near, hidden_far, hidden_s, pieces, first_row, slot_rows, core, earlier=()):
    count = len(pieces)
    rows, units_s = hidden_s.shape
    units = hidden_near.shape[1]
    slots = [(s, 0) for s in list(range(1, count)) + [0]] + [(s, 1) for s in range(count)]

    def body(core_ref, *refs):
        near_ref, far_ref, s_ref, *piece_refs = refs[: 3 + count]
        out, w_ref, w_s_ref = refs[-3:]
        near, far = 0, 0
        for i, (slot, other) in enumerate(slots):
            part = pl.ds(i * slot_rows, slot_rows)
            table = piece_refs[slot][0, core_ref[0] ^ other, first_row : first_row + 16, :][:1].astype(jnp.float32)

            def column(j):
                both = table[:, j * slot_rows : (j + 1) * slot_rows]
                both = both + table[:, (j + 2) * slot_rows : (j + 3) * slot_rows]
                return jnp.broadcast_to(both, (slot_rows, slot_rows)).T[:, :1]

            weight, weight_s = column(0), column(1)
            w_ref[part, :] = weight
            w_s_ref[part, :] = weight_s
            if slot == 0:
                hidden = near_ref[near : near + slot_rows, :]
                near += slot_rows
            else:
                hidden = far_ref[far : far + slot_rows, :]
                far += slot_rows
            out[part, :units] = (hidden.astype(jnp.float32) * weight).astype(jnp.bfloat16)
            out[part, units:] = (s_ref[part, :].astype(jnp.float32) * weight_s).astype(jnp.bfloat16)

    return pl.pallas_call(
        body,
        out_shape=[
            shape_of(rows, units + units_s),
            shape_of(rows, 1, dtype=jnp.float32),
            shape_of(rows, 1, dtype=jnp.float32),
        ],
        grid_spec=pltpu.PrefetchScalarGridSpec(
            num_scalar_prefetch=1,
            grid=(1,),
            in_specs=[whole(a) for a in (hidden_near, hidden_far, hidden_s, *pieces)] + [ANY] * len(earlier),
            out_specs=[
                pl.BlockSpec((rows, units + units_s), lambda *_: (0, 0)),
                pl.BlockSpec((rows, 1), lambda *_: (0, 0)),
                pl.BlockSpec((rows, 1), lambda *_: (0, 0)),
            ],
        ),
        compiler_params=pltpu.CompilerParams(vmem_limit_bytes=VMEM_LIMIT),
        cost_estimate=SHORT,
        name="weigh_hidden",
    )(core.reshape(1).astype(jnp.int32), hidden_near, hidden_far, hidden_s, *pieces, *earlier)


def output_other(weighted, down, column, parts, slot_rows, quarter, earlier=()):
    rows, units = weighted.shape
    count = rows // 2 // parts

    def body(weighted_ref, down_ref, *outs):
        for i, out in enumerate(outs):
            first, last = slot_rows + i * count, slot_rows + (i + 1) * count
            kept = min(last, rows // 2) - first
            value = dot32(weighted_ref[first : first + kept, :], down_ref[...])
            out[:kept, :] = value.astype(jnp.bfloat16)
            if kept < count:
                value = dot32(weighted_ref[: count - kept, :], down_ref[...])
                out[kept:, :] = value.astype(jnp.bfloat16)

    return kernel_call(
        body,
        (4,),
        [
            pl.BlockSpec((rows // 2, units), lambda *_: (1, 0)),
            pl.BlockSpec((units, quarter), lambda q, column_ref: (0, column_ref[0] ^ q)),
        ],
        [pl.BlockSpec((count, quarter), lambda q, *_: (0, q))] * parts,
        [shape_of(count, 4 * quarter)] * parts,
        [weighted, down],
        [],
        "output_other",
        column=column,
        earlier=earlier,
    )


def output_own(weighted, got, down, column, quarter, earlier=()):
    count, units = got[0].shape[0], weighted.shape[1]
    parts = len(got)

    def body(weighted_ref, down_ref, *refs):
        for i in range(parts):
            value = dot32(weighted_ref[i * count : (i + 1) * count, :], down_ref[...])
            value = value + refs[i][...].astype(jnp.float32)
            for j, out in enumerate(refs[parts + 4 * i : parts + 4 * i + 4]):

                @pl.when(pl.program_id(0) == 3 - j)
                def _(out=out, value=value):
                    out[...] = value.astype(out.dtype)

    full = pl.BlockSpec((count, quarter), lambda *_: (0, 0))
    out = kernel_call(
        body,
        (4,),
        [
            pl.BlockSpec((parts * count, units), lambda *_: (0, 0)),
            pl.BlockSpec((units, quarter), lambda q, column_ref: (0, column_ref[0] ^ 3 ^ q)),
        ]
        + [pl.BlockSpec((count, quarter), lambda q, *_: (0, 3 - q))] * parts,
        [full] * (4 * parts),
        ([shape_of(count, quarter, dtype=jnp.float32)] + [shape_of(count, quarter)] * 3) * parts,
        [weighted, down] + list(got),
        [],
        "output_own",
        column=column,
        earlier=earlier,
    )
    return [out[4 * i : 4 * i + 4] for i in range(parts)]


def backward_rows(groups, down, parts, per_row, first_row, tile, earlier=()):
    slope_s, act_s, w_rows, w_shadow = per_row
    rows = sum(g[2] for g in groups)
    units_all, width = down.shape
    units_s = slope_s.shape[1]
    units = units_all - units_s
    steps = width // tile
    arrays = list({id(a): a for part in parts for a in part[:2]}.values())
    places = [[next(i for i, a in enumerate(arrays) if a is b) for b in part[:2]] for part in parts]

    def body(*refs):
        n, m = len(groups), len(arrays)
        down_ref = refs[n]
        array_refs = refs[n + 1 : n + 1 + m]
        slope_s_ref, act_s_ref, w_ref, w_s_ref, pre_ref, pre_s_ref, acc, held = refs[n + 1 + m :]
        clear_first(acc)
        acc[...] += contract_last(rows_operand(refs[:n], groups, held), down_ref[...])

        @pl.when(pl.program_id(0) == steps - 1)
        def _():
            chunk = 128
            start = 0
            for (_, _, count), (_, _, first), (slope_at, act_at) in zip(groups, parts, places):

                @pl.loop(0, count // chunk)
                def _(i, start=start, first=first, slope_ref=array_refs[slope_at], act_ref=array_refs[act_at]):
                    source = pl.ds(pl.multiple_of(first + i * chunk, chunk), chunk)
                    part = pl.ds(pl.multiple_of(start + i * chunk, chunk), chunk)
                    whole_part = pl.ds(pl.multiple_of(first_row + start + i * chunk, chunk), chunk)
                    grad = acc[part, :units] * w_ref[whole_part, :]
                    pre_ref[part, :units] = (grad * slope_ref[source, :]).astype(jnp.bfloat16)
                    pre_ref[part, units:] = (grad * act_ref[source, :]).astype(jnp.bfloat16)
                    grad = acc[part, units:] * w_s_ref[whole_part, :]
                    pre_s_ref[part, :units_s] = (grad * slope_s_ref[whole_part, :]).astype(jnp.bfloat16)
                    pre_s_ref[part, units_s:] = (grad * act_s_ref[whole_part, :]).astype(jnp.bfloat16)

                start += count

    extra = arrays + [slope_s, act_s, w_rows, w_shadow]
    return kernel_call(
        body,
        (steps,),
        row_specs(groups, tile) + [pl.BlockSpec((units_all, tile), lambda k, *_: (0, k))] + [whole(a) for a in extra],
        [pl.BlockSpec((rows, 2 * units), lambda *_: (0, 0)), pl.BlockSpec((rows, 2 * units_s), lambda *_: (0, 0))],
        [shape_of(rows, 2 * units), shape_of(rows, 2 * units_s)],
        [g[0] for g in groups] + [down] + extra,
        [pltpu.VMEM((rows, units_all), jnp.float32), pltpu.VMEM((rows, tile), jnp.bfloat16)],
        "backward_rows",
        earlier=earlier,
    )


def stage_rows(refs, groups, held):
    start = 0
    for ref, (_, _, count) in zip(refs, groups):
        held[pl.ds(start, count), :] = ref[...]
        start += count
    return held[...]


def shadow_grads(x_groups, dy_groups, pre_s, weighted, units, tile, earlier=()):
    rows, wide = weighted.shape[0], pre_s[0].shape[1]
    apart = wide // 2
    width = x_groups[0][0].shape[1]
    m = len(pre_s)

    def body(*refs):
        n = len(x_groups)
        pre_refs = refs[2 * n : 2 * n + m]
        hidden_ref, out, held, pre_t, hidden_t = refs[2 * n + m :]

        @pl.when(pl.program_id(0) == 0)
        def _():
            start = 0
            for ref in pre_refs:
                pre_t[:, start : start + ref.shape[0]] = ref[...].T
                start += ref.shape[0]
            hidden_t[...] = hidden_ref[...].T

        value = dot32(pre_t[...], stage_rows(refs[:n], x_groups, held))
        out[:units, :] = value[:units].astype(jnp.bfloat16)
        out[units : 2 * units, :] = value[apart : apart + units].astype(jnp.bfloat16)
        value = dot32(hidden_t[...], stage_rows(refs[n : 2 * n], dy_groups, held))
        out[2 * units :, :] = value[:units].astype(jnp.bfloat16)

    (out,) = kernel_call(
        body,
        (width // tile,),
        row_specs(x_groups, tile)
        + row_specs(dy_groups, tile)
        + [whole(p) for p in pre_s]
        + [pl.BlockSpec((rows, apart), lambda *_: (0, weighted.shape[1] // apart - 1))],
        [pl.BlockSpec((3 * units, tile), lambda k, *_: (0, k))],
        [shape_of(3 * units, width)],
        [g[0] for g in x_groups + dy_groups] + list(pre_s) + [weighted],
        [
            pltpu.VMEM((rows, tile), jnp.bfloat16),
            pltpu.VMEM((wide, rows), jnp.bfloat16),
            pltpu.VMEM((apart, rows), jnp.bfloat16),
        ],
        "shadow_grads",
        earlier=earlier,
    )
    return out


def input_grads(groups, pre, tile, earlier=()):
    both = pre[0].shape[1]
    rows = sum(p.shape[0] for p in pre)
    units = both // 2
    width = groups[0][0].shape[1]
    m = len(pre)

    def body(*refs):
        n = len(groups)
        gate_ref, up_ref, held, pre_held = refs[n + m :]

        @pl.when(pl.program_id(0) == 0)
        def _():
            start = 0
            for ref in refs[n : n + m]:
                pre_held[start : start + ref.shape[0], :] = ref[...]
                start += ref.shape[0]

        value = contract_rows(stage_rows(refs[:n], groups, held), pre_held[...])
        gate_ref[...] = value[:, :units].astype(jnp.bfloat16)
        up_ref[...] = value[:, units:].astype(jnp.bfloat16)

    return kernel_call(
        body,
        (width // tile,),
        row_specs(groups, tile) + [whole(p) for p in pre],
        [pl.BlockSpec((tile, units), lambda k, *_: (k, 0))] * 2,
        [shape_of(width, units)] * 2,
        [g[0] for g in groups] + list(pre),
        [pltpu.VMEM((rows, tile), jnp.bfloat16), pltpu.VMEM((rows, both), jnp.bfloat16)],
        "input_grads",
        earlier=earlier,
    )


def down_grad(groups, weighted, units, tile, earlier=()):
    rows = weighted.shape[0]
    width = groups[0][0].shape[1]

    def body(*refs):
        n = len(groups)
        hidden_ref, out, held, hidden_t = refs[n:]

        @pl.when(pl.program_id(0) == 0)
        def _():
            hidden_t[...] = hidden_ref[...].T

        out[...] = dot32(hidden_t[...], stage_rows(refs[:n], groups, held)).astype(jnp.bfloat16)

    (out,) = kernel_call(
        body,
        (width // tile,),
        row_specs(groups, tile) + [pl.BlockSpec((rows, units), lambda *_: (0, 0))],
        [pl.BlockSpec((units, tile), lambda k, *_: (0, k))],
        [shape_of(units, width)],
        [g[0] for g in groups] + [weighted],
        [pltpu.VMEM((rows, tile), jnp.bfloat16), pltpu.VMEM((units, rows), jnp.bfloat16)],
        "down_grad",
        earlier=earlier,
    )
    return out


def send_along_z(own):
    ep_count = lax.axis_size("ep")
    return [lax.ppermute(own, "ep", swap_pairs(ep_count, 2 * s)) for s in range(1, ep_count // 2)]


def swap_cores(block):
    return lax.ppermute(block, "ep", swap_pairs(lax.axis_size("ep"), 1))


def send_plane(*pieces):
    pieces = pieces * 3 if len(pieces) == 1 else pieces
    return [lax.ppermute(p, "tp", swap_pairs(lax.axis_size("tp"), bit)) for p, bit in zip(pieces, (1, 2, 3))]


def exchange_cores(blocks):
    ep_count, core = lax.axis_size("ep"), lax.axis_index("ep") % 2
    pairs = blocks.reshape(ep_count // 2, 2, *blocks.shape[1:])
    kept = jnp.where(core == 0, pairs[:, 0], pairs[:, 1])
    given = jnp.where(core == 0, pairs[:, 1], pairs[:, 0])
    return kept, swap_cores(given)


def exchange_chips(kept, taken, late=(), earlier=()):
    ep_count, me = lax.axis_size("ep"), lax.axis_index("ep")
    chips, chip, core = ep_count // 2, me // 2, me % 2
    both = jnp.stack([jnp.where(core == 0, kept, taken), jnp.where(core == 0, taken, kept)], axis=1)
    pieces = [lax.dynamic_index_in_dim(both, chip ^ shift, 0) for shift in range(chips)]
    if earlier:
        pieces = list(after(pieces, *earlier))
    if late:
        pieces[-1:] = after(pieces[-1:], *late)
    return pieces[:1] + [
        lax.ppermute(pieces[shift], "ep", swap_pairs(ep_count, 2 * shift)) for shift in range(1, chips)
    ]


def dense_shards(
    tokens,
    cotangent,
    expert_ids,
    gate_weights,
    shadow_mask,
    w_gate,
    w_up,
    w_down,
    s_gate,
    s_up,
    s_down,
):
    ep_count, tp_count = lax.axis_size("ep"), lax.axis_size("tp")
    ep_index, tp_index = lax.axis_index("ep"), lax.axis_index("tp")
    tok_count, top_count = expert_ids.shape
    quarter = tokens.shape[1]
    width = quarter * tp_count
    hidden_part = w_gate.shape[2]
    shadow_part = hidden_part // ep_count
    block_width = s_gate.shape[0]
    steps = ep_count // 2
    later = (steps - 1) * tok_count
    tile = width // 8
    along, across = swap_pairs(tp_count, 1), swap_pairs(tp_count, 2)

    picked = expert_ids[None, :, :] == jnp.arange(ep_count, dtype=jnp.int32)[:, None, None]
    table = jnp.sum(jnp.where(picked, gate_weights[None, :, :top_count], 0.0), axis=2)
    shadow_weight = gate_weights[:, top_count] * shadow_mask.astype(jnp.float32)
    table = jnp.concatenate([table, jnp.broadcast_to(shadow_weight[None], table.shape)], axis=1)
    table = jnp.concatenate(split_parts(table), axis=1)
    table = jnp.pad(table[:, None, :], ((0, 0), (0, 15), (0, block_width - table.shape[1])))
    shadow_blocks = jnp.concatenate(
        [
            s_gate.T.reshape(ep_count, shadow_part, block_width),
            s_up.T.reshape(ep_count, shadow_part, block_width),
            s_down.reshape(ep_count, shadow_part, block_width),
            table,
        ],
        axis=1,
    )

    x_z = send_along_z(tokens)
    near = stack_pieces([tokens, cotangent])
    near_x, near_y = send_plane(near, near)
    near_late = stack_pieces([tokens, cotangent], earlier=[near_x, near_y])
    near_d = lax.ppermute(near_late, "tp", swap_pairs(tp_count, 3))
    w_both = jnp.concatenate([w_gate[0], w_up[0]], axis=1)
    (shadow_blocks,) = after([shadow_blocks], near_x, near_y)
    shadow_kept, shadow_taken = exchange_cores(shadow_blocks)
    *x_z, near_d, shadow_taken = after(x_z + [near_d, shadow_taken], w_both)

    x_piece = stack_pieces(x_z)
    x_plane = send_plane(x_piece)
    dy_z = send_along_z(cotangent)
    near_own = join_plane(tp_index, near, near_x, near_y, near_d)
    near_other = swap_cores(near_own)
    x_near = [(near_own, 0, tok_count), (near_other, 0, tok_count)]
    hidden_near, slope_near, act_near = forward_rows(x_near, w_both, 2 * tile)
    spare_rows = -shadow_part % 128 + shadow_part
    down = jnp.pad(w_down[0], ((0, spare_rows), (0, 0)))
    fenced = after([*x_plane, *dy_z, down], hidden_near)
    x_plane, dy_z, down = fenced[:3], fenced[3:-1], fenced[-1]

    dy_piece = stack_pieces(dy_z)
    dy_plane = send_plane(dy_piece)
    x_own = join_plane(tp_index, x_piece, *x_plane, earlier=[dy_piece])
    x_other = swap_cores(x_own)
    x_far = [(x_own, 0, later), (x_other, 0, later)]
    x_groups = [x_far[0], x_near[0], x_near[1], x_far[1]]
    hidden_far, slope_far, act_far = forward_rows(x_far, w_both, 2 * tile)
    shadow_pieces = exchange_chips(shadow_kept, shadow_taken, late=[hidden_far])
    chip = ep_index // 2
    shadow_in, down = lay_out_shadow(shadow_pieces, down, shadow_part, chip, earlier=[hidden_far])
    hidden_s, slope_s, act_s = forward_rows(x_groups, shadow_in, 2 * tile, transposed=True)

    weighted, w_rows, w_shadow = weigh_hidden(
        hidden_near, hidden_far, hidden_s, shadow_pieces, 3 * shadow_part, tok_count, ep_index % 2
    )

    parts = 2 if steps % 2 == 0 else 1
    sent = output_other(weighted, down, tp_index, parts, tok_count, quarter)
    got = [swap_cores(array) for array in sent]
    dy_plane = after(dy_plane, *sent)

    dy_own = join_plane(tp_index, dy_piece, *dy_plane)
    dy_other = swap_cores(dy_own)
    dy_groups = [(dy_own, 0, later), (near_own, 1, tok_count), (near_other, 1, tok_count), (dy_other, 0, later)]
    segments = [
        (slope_far, act_far, 0),
        (slope_near, act_near, 0),
        (slope_near, act_near, tok_count),
        (slope_far, act_far, later),
    ]
    per_row = (slope_s, act_s, w_rows, w_shadow)
    pre_first, pre_s_first = backward_rows(dy_groups[:3], down, segments[:3], per_row, 0, 2 * tile)
    owns = output_own(weighted, got, down, tp_index, quarter, earlier=[pre_first])
    sums = [send_plane(*own[1:]) for own in owns]
    first_rows = sum(g[2] for g in dy_groups[:3])
    pre_last, pre_s_last = backward_rows(
        dy_groups[3:], down, segments[3:], per_row, first_rows, 2 * tile, earlier=[own[1] for own in owns]
    )
    pre, pre_s = [pre_first, pre_last], [pre_s_first, pre_s_last]
    grad_s = shadow_grads(x_groups, dy_groups, pre_s, weighted, shadow_part, tile)
    blocks = grad_s.reshape(3 * shadow_part, ep_count, block_width).transpose(1, 0, 2)
    grad_kept, grad_taken = exchange_cores(blocks)
    sums[0] = after(sums[0], grad_s)

    def slot_rows(i):
        part = slice(i % (steps // parts) * tok_count, (i % (steps // parts) + 1) * tok_count)
        total = owns[i * parts // steps][0][part]
        for array in sums[i * parts // steps]:
            total = total + array[part].astype(jnp.float32)
        return total

    first = [slot_rows(i).astype(jnp.bfloat16) for i in range(steps // parts)]
    grad_pieces = exchange_chips(grad_kept, grad_taken, earlier=first)
    grad_gate, grad_up = input_grads(x_groups, pre, tile, earlier=[grad_pieces[0]])
    if parts > 1:
        sums[-1] = after(sums[-1], grad_gate)
    total = slot_rows(steps - 1)
    pieces = first + [slot_rows(i).astype(jnp.bfloat16) for i in range(len(first), steps - 1)]
    grad_down = down_grad(dy_groups, weighted, hidden_part, tile, earlier=[pieces[-1], grad_gate])
    for s in range(1, steps):
        total = total + lax.ppermute(pieces[s - 1], "ep", swap_pairs(ep_count, 2 * s)).astype(jnp.float32)
    mixed = total.astype(jnp.bfloat16)

    grads_s = lay_out_grads(grad_pieces, shadow_part, chip, earlier=[grad_down])
    return (mixed, grad_gate[None], grad_up[None], grad_down[None], *grads_s)


def shards(tokens, cotangent, expert_ids, *others):
    tp_count, ep_count = lax.axis_size("tp"), lax.axis_size("ep")
    tok_count, top_count = expert_ids.shape
    rows = (5 * tok_count * top_count) // 4
    chips = ep_count // 2
    fits = tp_count == 4 and ep_count == 2 * chips and chips & (chips - 1) == 0 and tok_count % 128 == 0
    dense = fits and ep_count * tok_count <= 3 * rows
    return (dense_shards if dense else routed_shards)(tokens, cotangent, expert_ids, *others)


def solution(mesh):
    return jax.shard_map(
        shards,
        mesh=mesh,
        in_specs=(
            P("ep", "tp"),
            P("ep", "tp"),
            P("ep", None),
            P("ep", None),
            P("ep"),
            P("ep", None, "tp"),
            P("ep", None, "tp"),
            P("ep", "tp", None),
            P("ep", "tp"),
            P("ep", "tp"),
            P("tp", "ep"),
        ),
        out_specs=(
            P("ep", "tp"),
            P("ep", None, "tp"),
            P("ep", None, "tp"),
            P("ep", "tp", None),
            P("ep", "tp"),
            P("ep", "tp"),
            P("tp", "ep"),
        ),
        check_vma=False,
    )
```

```python
import functools

import jax
import jax.numpy as jnp
from jax import lax
from jax.experimental import pallas as pl
from jax.experimental.pallas import tpu as pltpu
from jax.sharding import PartitionSpec as P


def contract_rows(left, right):
    return lax.dot_general(
        left, right, (((0,), (0,)), ((), ())), preferred_element_type=jnp.float32
    )


def split_parts(values):
    upper_part = values.astype(jnp.bfloat16)
    lower_part = (values - upper_part.astype(jnp.float32)).astype(jnp.bfloat16)
    return (upper_part, lower_part)


def weigh_rows(weight_table, rows):
    weight_upper, weight_lower = split_parts(weight_table)
    return jnp.dot(weight_upper, rows, preferred_element_type=jnp.float32) + jnp.dot(
        weight_lower, rows, preferred_element_type=jnp.float32
    )


def expert_pass(rows_x, rows_dout, weight_gate, weight_up, weight_down):
    pre_gate = jnp.dot(rows_x, weight_gate, preferred_element_type=jnp.float32)
    pre_up = jnp.dot(rows_x, weight_up, preferred_element_type=jnp.float32)
    sigmoid_gate = jax.nn.sigmoid(pre_gate)
    activated = pre_gate * sigmoid_gate
    hidden = (activated * pre_up).astype(jnp.bfloat16)
    partial_out = jnp.dot(hidden, weight_down, preferred_element_type=jnp.float32).astype(
        jnp.bfloat16
    )
    hidden_grad = lax.dot_general(
        rows_dout, weight_down, (((1,), (1,)), ((), ())), preferred_element_type=jnp.float32
    )
    grad_pre_gate = (
        hidden_grad * pre_up * sigmoid_gate * (1.0 + pre_gate * (1.0 - sigmoid_gate))
    ).astype(jnp.bfloat16)
    grad_pre_up = (hidden_grad * activated).astype(jnp.bfloat16)
    return (partial_out, hidden, grad_pre_gate, grad_pre_up)


def routed_shards(
    tokens,
    cotangent,
    expert_ids,
    gate_weights,
    shadow_mask,
    w_gate,
    w_up,
    w_down,
    s_gate,
    s_up,
    s_down,
):
    ep_count = lax.axis_size("ep")
    tok_count, top_count = expert_ids.shape
    quarter_width = tokens.shape[1]
    width = quarter_width * lax.axis_size("tp")
    expert_count = w_gate.shape[0] * ep_count
    capacity = (5 * tok_count * top_count + 4 * expert_count - 1) // (4 * expert_count)
    slot_count = expert_count * capacity
    picks_flat = expert_ids.reshape(-1)
    onehot = (picks_flat[:, None] == jnp.arange(expert_count, dtype=jnp.int32)[None, :]).astype(
        jnp.int32
    )
    slot_rank = jnp.sum((jnp.cumsum(onehot, axis=0) - onehot) * onehot, axis=1)
    slot_index = (picks_flat * capacity + slot_rank).reshape(tok_count, top_count)
    matches = jnp.arange(slot_count, dtype=jnp.int32)[:, None, None] == slot_index[None, :, :]
    dispatch = jnp.any(matches, axis=2).astype(jnp.bfloat16)
    weighting = jnp.sum(jnp.where(matches, gate_weights[None, :, :top_count], 0.0), axis=2)
    slot_gate = jnp.sum(weighting, axis=1)
    shadow_weight = gate_weights[:, top_count] * shadow_mask.astype(jnp.float32)
    x_full, dy_full = (
        lax.all_gather(tokens, "tp", axis=1, tiled=True),
        lax.all_gather(cotangent, "tp", axis=1, tiled=True),
    )
    rows_x = jnp.dot(dispatch, tokens, preferred_element_type=jnp.float32).astype(jnp.bfloat16)
    rows_dy = jnp.dot(dispatch, cotangent, preferred_element_type=jnp.float32)
    rows_dout = (slot_gate[:, None] * rows_dy).astype(jnp.bfloat16)
    recv_x, recv_dout = (
        lax.all_to_all(
            rows_x.reshape(ep_count, -1, quarter_width),
            "ep",
            split_axis=0,
            concat_axis=0,
            tiled=True,
        ),
        lax.all_to_all(
            rows_dout.reshape(ep_count, -1, quarter_width),
            "ep",
            split_axis=0,
            concat_axis=0,
            tiled=True,
        ),
    )
    expert_x, expert_dout = (
        lax.all_gather(recv_x.reshape(-1, quarter_width), "tp", axis=1, tiled=True),
        lax.all_gather(recv_dout.reshape(-1, quarter_width), "tp", axis=1, tiled=True),
    )
    partial_out, hidden, grad_pre_gate, grad_pre_up = expert_pass(
        expert_x, expert_dout, w_gate[0], w_up[0], w_down[0]
    )
    grad_gate = contract_rows(expert_x, grad_pre_gate).astype(jnp.bfloat16)[None]
    grad_up = contract_rows(expert_x, grad_pre_up).astype(jnp.bfloat16)[None]
    grad_down = contract_rows(hidden, expert_dout).astype(jnp.bfloat16)[None]
    full_gate, full_up, full_down = (
        lax.all_gather(s_gate, "ep", axis=0, tiled=True),
        lax.all_gather(s_up, "ep", axis=0, tiled=True),
        lax.all_gather(s_down, "ep", axis=1, tiled=True),
    )
    shadow_dout = (shadow_weight[:, None] * dy_full.astype(jnp.float32)).astype(jnp.bfloat16)
    shadow_out, shadow_hidden, shadow_gate_pre, shadow_up_pre = expert_pass(
        x_full, shadow_dout, full_gate, full_up, full_down
    )
    shadow_sums = lax.psum_scatter(
        jnp.concatenate(
            [
                contract_rows(x_full, shadow_gate_pre),
                contract_rows(x_full, shadow_up_pre),
                contract_rows(shadow_dout, shadow_hidden),
            ],
            axis=1,
        ).astype(jnp.bfloat16),
        "ep",
        scatter_dimension=0,
        tiled=True,
    ).astype(jnp.float32)
    hidden_part = s_gate.shape[1]
    grad_s_gate = shadow_sums[:, :hidden_part].astype(jnp.bfloat16)
    grad_s_up = shadow_sums[:, hidden_part : 2 * hidden_part].astype(jnp.bfloat16)
    grad_s_down = shadow_sums[:, 2 * hidden_part :].T.astype(jnp.bfloat16)
    back_rows = lax.all_to_all(
        partial_out.reshape(ep_count, -1, width), "ep", split_axis=0, concat_axis=0, tiled=True
    ).reshape(-1, width)
    term = weigh_rows(weighting.T, back_rows)
    term = term + shadow_weight[:, None] * shadow_out.astype(jnp.float32)
    mixed = lax.psum_scatter(term.astype(jnp.bfloat16), "tp", scatter_dimension=1, tiled=True)
    return (mixed, grad_gate, grad_up, grad_down, grad_s_gate, grad_s_up, grad_s_down)


ANY = pl.BlockSpec(memory_space=pl.ANY)
VMEM_LIMIT = 60 * 1024 * 1024
SHORT = pl.CostEstimate(flops=1, bytes_accessed=1, transcendentals=0)


def swap_pairs(count, bit):
    return [(i, i ^ bit) for i in range(count)]


def dot32(left, right):
    return jnp.dot(left, right, preferred_element_type=jnp.float32)


def contract_last(left, right):
    return lax.dot_general(
        left, right, (((1,), (1,)), ((), ())), preferred_element_type=jnp.float32
    )


def shape_of(*dims, dtype=jnp.bfloat16):
    return jax.ShapeDtypeStruct(dims, dtype)


def after(arrays, *earlier):
    def nothing(*refs):
        del refs

    count = len(arrays)
    return pl.pallas_call(
        nothing,
        out_shape=[jax.ShapeDtypeStruct(a.shape, a.dtype) for a in arrays],
        in_specs=[ANY] * (count + len(earlier)),
        out_specs=[ANY] * count,
        input_output_aliases={i: i for i in range(count)},
        compiler_params=pltpu.CompilerParams(vmem_limit_bytes=VMEM_LIMIT),
        cost_estimate=SHORT,
        name="after",
    )(*arrays, *earlier)


def kernel_call(body, grid, in_specs, out_specs, out_shape, operands, scratch, name, column=None, earlier=()):
    count = len(operands)

    def run(column_ref, *refs):
        del column_ref
        body(*refs[:count], *refs[count + len(earlier) :])

    column = jnp.zeros((1,), jnp.int32) if column is None else column.reshape(1).astype(jnp.int32)
    return pl.pallas_call(
        run,
        out_shape=out_shape,
        grid_spec=pltpu.PrefetchScalarGridSpec(
            num_scalar_prefetch=1,
            grid=grid,
            in_specs=list(in_specs) + [ANY] * len(earlier),
            out_specs=out_specs,
            scratch_shapes=scratch,
        ),
        compiler_params=pltpu.CompilerParams(vmem_limit_bytes=VMEM_LIMIT),
        cost_estimate=SHORT,
        name=name,
    )(column, *operands, *earlier)


def whole(array):
    return pl.BlockSpec(array.shape, lambda *_: (0,) * len(array.shape))


def join_plane(column, *pieces, earlier=()):
    rows, quarter = pieces[0].shape
    count = len(pieces)
    chunk = rows // 4

    def body(*refs):
        column_ref, sources, out = refs[0], refs[1 : 1 + count], refs[-1]
        for own_column in range(count):

            @pl.when(column_ref[0] == own_column)
            def _():
                for bit, source in enumerate(sources):
                    place = own_column ^ bit
                    out[:, place * quarter : (place + 1) * quarter] = source[...]

    return pl.pallas_call(
        body,
        out_shape=shape_of(rows, count * quarter),
        grid_spec=pltpu.PrefetchScalarGridSpec(
            num_scalar_prefetch=1,
            grid=(4,),
            in_specs=[pl.BlockSpec((chunk, quarter), lambda i, *_: (i, 0))] * count + [ANY] * len(earlier),
            out_specs=pl.BlockSpec((chunk, count * quarter), lambda i, *_: (i, 0)),
        ),
        compiler_params=pltpu.CompilerParams(vmem_limit_bytes=VMEM_LIMIT),
        cost_estimate=SHORT,
        name="join_plane",
    )(column.reshape(1).astype(jnp.int32), *pieces, *earlier)


def stack_pieces(pieces, earlier=()):
    rows, columns = pieces[0].shape
    count = len(pieces)

    def body(*refs):
        for i, ref in enumerate(refs[:count]):

            @pl.when(pl.program_id(0) == i)
            def _():
                refs[-1][...] = ref[...]

    return pl.pallas_call(
        body,
        out_shape=shape_of(count * rows, columns),
        grid=(count,),
        in_specs=[pl.BlockSpec((rows, columns), lambda i: (0, 0))] * count + [ANY] * len(earlier),
        out_specs=pl.BlockSpec((rows, columns), lambda i: (i, 0)),
        compiler_params=pltpu.CompilerParams(vmem_limit_bytes=VMEM_LIMIT),
        cost_estimate=SHORT,
        name="stack_pieces",
    )(*pieces, *earlier)


def other_chips(gathered, chips, chip, earlier=()):
    rows, columns = gathered.shape[0] // chips, gathered.shape[1]

    def body(chip_ref, source, *refs):
        del chip_ref
        refs[-1][...] = source[...]

    return pl.pallas_call(
        body,
        out_shape=shape_of((chips - 1) * rows, columns),
        grid_spec=pltpu.PrefetchScalarGridSpec(
            num_scalar_prefetch=1,
            grid=(chips - 1,),
            in_specs=[pl.BlockSpec((rows, columns), lambda i, chip_ref: (chip_ref[0] ^ (i + 1), 0))]
            + [ANY] * len(earlier),
            out_specs=pl.BlockSpec((rows, columns), lambda i, *_: (i, 0)),
        ),
        compiler_params=pltpu.CompilerParams(vmem_limit_bytes=VMEM_LIMIT),
        cost_estimate=SHORT,
        name="other_chips",
    )(chip.reshape(1).astype(jnp.int32), gathered, *earlier)


def on_piece(chip_ref, refs, use):
    step = pl.program_id(0)
    shift = chip_ref[0] ^ (step // 2)
    for i, ref in enumerate(refs):
        for core in range(2):

            @pl.when((shift == i) & (lax.rem(step, 2) == core))
            def _(ref=ref, core=core):
                use(ref.at[0, core])


def lay_out_shadow(pieces, down, units, chip, earlier=()):
    count = len(pieces)
    ep_count = 2 * count
    block_width = pieces[0].shape[3]
    apart = units + -units % 128
    all_units, width = down.shape

    def body(chip_ref, *refs):
        shadow_ref, out = refs[-2:]

        def use(ref):
            shadow_ref[...] = jnp.zeros_like(shadow_ref)
            shadow_ref[:units, :] = ref[:units, :]
            shadow_ref[apart : apart + units, :] = ref[units : 2 * units, :]
            out[units:, :] = jnp.zeros((apart - units, block_width), jnp.bfloat16)
            out[:units, :] = ref[2 * units : 3 * units, :]

        on_piece(chip_ref, refs[:count], use)

    return pl.pallas_call(
        body,
        out_shape=[shape_of(2 * apart, width), shape_of(all_units, width)],
        grid_spec=pltpu.PrefetchScalarGridSpec(
            num_scalar_prefetch=1,
            grid=(ep_count,),
            in_specs=[whole(p) for p in pieces] + [ANY] * (1 + len(earlier)),
            out_specs=[
                pl.BlockSpec((2 * apart, block_width), lambda e, *_: (0, e)),
                pl.BlockSpec((apart, block_width), lambda e, *_: (all_units // apart - 1, e)),
            ],
        ),
        input_output_aliases={1 + count: 1},
        compiler_params=pltpu.CompilerParams(vmem_limit_bytes=VMEM_LIMIT),
        cost_estimate=SHORT,
        name="lay_out_shadow",
    )(chip.reshape(1).astype(jnp.int32), *pieces, down, *earlier)


def lay_out_grads(pieces, units, chip, earlier=()):
    count = len(pieces)
    ep_count = 2 * count
    block_width = pieces[0].shape[3]
    hidden = ep_count * units

    def body(chip_ref, *refs):
        gate_ref, up_ref, down_ref, gate_t, up_t = refs[-5:]
        place = pl.ds(pl.multiple_of(pl.program_id(0) * units, 16), units)

        def use(ref):
            gate_t[place, :] = ref[:units, :]
            up_t[place, :] = ref[units : 2 * units, :]
            down_ref[place, :] = ref[2 * units :, :]

        on_piece(chip_ref, refs[:count], use)

        @pl.when(pl.program_id(0) == ep_count - 1)
        def _():
            gate_ref[...] = gate_t[...].T
            up_ref[...] = up_t[...].T

    return pl.pallas_call(
        body,
        out_shape=[shape_of(block_width, hidden), shape_of(block_width, hidden), shape_of(hidden, block_width)],
        grid_spec=pltpu.PrefetchScalarGridSpec(
            num_scalar_prefetch=1,
            grid=(ep_count,),
            in_specs=[whole(p) for p in pieces] + [ANY] * len(earlier),
            out_specs=[pl.BlockSpec((block_width, hidden), lambda *_: (0, 0))] * 2
            + [pl.BlockSpec((hidden, block_width), lambda *_: (0, 0))],
            scratch_shapes=[pltpu.VMEM((hidden, block_width), jnp.bfloat16)] * 2,
        ),
        compiler_params=pltpu.CompilerParams(vmem_limit_bytes=VMEM_LIMIT),
        cost_estimate=SHORT,
        name="lay_out_grads",
    )(chip.reshape(1).astype(jnp.int32), *pieces, *earlier)


def row_specs(groups, tile):
    def spec(index, rows):
        return pl.BlockSpec((rows, tile), lambda k, *_: (index, k))

    return [spec(index, rows) for _, index, rows in groups]


def apply_gate(pre_gate, pre_up):
    sigmoid_gate = jax.nn.sigmoid(pre_gate)
    activated = pre_gate * sigmoid_gate
    hidden = (activated * pre_up).astype(jnp.bfloat16)
    return hidden, pre_up * sigmoid_gate * (1.0 + pre_gate * (1.0 - sigmoid_gate)), activated


def clear_first(acc):
    @pl.when(pl.program_id(0) == 0)
    def _():
        acc[...] = jnp.zeros_like(acc)


def rows_operand(refs, groups, held):
    if len(groups) == 1:
        return refs[0][...]
    return stage_rows(refs, groups, held)


def forward_rows(groups, w_both, tile, transposed=False, earlier=()):
    rows = sum(g[2] for g in groups)
    if transposed:
        units, width = w_both.shape[0] // 2, w_both.shape[1]
        tile_spec = pl.BlockSpec((2 * units, tile), lambda k, *_: (0, k))
    else:
        width, units = w_both.shape[0], w_both.shape[1] // 2
        tile_spec = pl.BlockSpec((tile, 2 * units), lambda k, *_: (k, 0))
    steps = width // tile

    def body(*refs):
        n = len(groups)
        both_ref, hidden_ref, slope_ref, act_ref, acc, held = refs[n:]
        clear_first(acc)
        operand = rows_operand(refs[:n], groups, held)
        acc[...] += contract_last(operand, both_ref[...]) if transposed else dot32(operand, both_ref[...])

        @pl.when(pl.program_id(0) == steps - 1)
        def _():
            chunk = 128

            @pl.loop(0, rows // chunk)
            def _(i):
                part = pl.ds(pl.multiple_of(i * chunk, chunk), chunk)
                hidden, slope, act = apply_gate(acc[part, :units], acc[part, units:])
                hidden_ref[part, :] = hidden
                slope_ref[part, :] = slope.astype(jnp.bfloat16)
                act_ref[part, :] = act.astype(jnp.bfloat16)

    out_spec = pl.BlockSpec((rows, units), lambda *_: (0, 0))
    return kernel_call(
        body,
        (steps,),
        row_specs(groups, tile) + [tile_spec],
        [out_spec] * 3,
        [shape_of(rows, units)] * 3,
        [g[0] for g in groups] + [w_both],
        [pltpu.VMEM((rows, 2 * units), jnp.float32), pltpu.VMEM((rows, tile), jnp.bfloat16)],
        "forward_rows",
        earlier=earlier,
    )


def weigh_hidden(hidden_near, hidden_far, hidden_s, pieces, first_row, slot_rows, core, earlier=()):
    count = len(pieces)
    rows, units_s = hidden_s.shape
    units = hidden_near.shape[1]
    slots = [(s, 0) for s in list(range(1, count)) + [0]] + [(s, 1) for s in range(count)]

    def body(core_ref, *refs):
        near_ref, far_ref, s_ref, *piece_refs = refs[: 3 + count]
        out, w_ref, w_s_ref = refs[-3:]
        near, far = 0, 0
        for i, (slot, other) in enumerate(slots):
            part = pl.ds(i * slot_rows, slot_rows)
            table = piece_refs[slot][0, core_ref[0] ^ other, first_row : first_row + 16, :][:1].astype(jnp.float32)

            def column(j):
                both = table[:, j * slot_rows : (j + 1) * slot_rows]
                both = both + table[:, (j + 2) * slot_rows : (j + 3) * slot_rows]
                return jnp.broadcast_to(both, (slot_rows, slot_rows)).T[:, :1]

            weight, weight_s = column(0), column(1)
            w_ref[part, :] = weight
            w_s_ref[part, :] = weight_s
            if slot == 0:
                hidden = near_ref[near : near + slot_rows, :]
                near += slot_rows
            else:
                hidden = far_ref[far : far + slot_rows, :]
                far += slot_rows
            out[part, :units] = (hidden.astype(jnp.float32) * weight).astype(jnp.bfloat16)
            out[part, units:] = (s_ref[part, :].astype(jnp.float32) * weight_s).astype(jnp.bfloat16)

    return pl.pallas_call(
        body,
        out_shape=[
            shape_of(rows, units + units_s),
            shape_of(rows, 1, dtype=jnp.float32),
            shape_of(rows, 1, dtype=jnp.float32),
        ],
        grid_spec=pltpu.PrefetchScalarGridSpec(
            num_scalar_prefetch=1,
            grid=(1,),
            in_specs=[whole(a) for a in (hidden_near, hidden_far, hidden_s, *pieces)] + [ANY] * len(earlier),
            out_specs=[
                pl.BlockSpec((rows, units + units_s), lambda *_: (0, 0)),
                pl.BlockSpec((rows, 1), lambda *_: (0, 0)),
                pl.BlockSpec((rows, 1), lambda *_: (0, 0)),
            ],
        ),
        compiler_params=pltpu.CompilerParams(vmem_limit_bytes=VMEM_LIMIT),
        cost_estimate=SHORT,
        name="weigh_hidden",
    )(core.reshape(1).astype(jnp.int32), hidden_near, hidden_far, hidden_s, *pieces, *earlier)


def output_other(weighted, down, column, parts, slot_rows, quarter, earlier=()):
    rows, units = weighted.shape
    count = rows // 2 // parts

    def body(weighted_ref, down_ref, *outs):
        for i, out in enumerate(outs):
            first, last = slot_rows + i * count, slot_rows + (i + 1) * count
            kept = min(last, rows // 2) - first
            value = dot32(weighted_ref[first : first + kept, :], down_ref[...])
            out[:kept, :] = value.astype(jnp.bfloat16)
            if kept < count:
                value = dot32(weighted_ref[: count - kept, :], down_ref[...])
                out[kept:, :] = value.astype(jnp.bfloat16)

    return kernel_call(
        body,
        (4,),
        [
            pl.BlockSpec((rows // 2, units), lambda *_: (1, 0)),
            pl.BlockSpec((units, quarter), lambda q, column_ref: (0, column_ref[0] ^ q)),
        ],
        [pl.BlockSpec((count, quarter), lambda q, *_: (0, q))] * parts,
        [shape_of(count, 4 * quarter)] * parts,
        [weighted, down],
        [],
        "output_other",
        column=column,
        earlier=earlier,
    )


def output_own(weighted, got, down, column, quarter, earlier=()):
    count, units = got[0].shape[0], weighted.shape[1]
    parts = len(got)

    def body(weighted_ref, down_ref, *refs):
        for i in range(parts):
            value = dot32(weighted_ref[i * count : (i + 1) * count, :], down_ref[...])
            value = value + refs[i][...].astype(jnp.float32)
            for j, out in enumerate(refs[parts + 4 * i : parts + 4 * i + 4]):

                @pl.when(pl.program_id(0) == 3 - j)
                def _(out=out, value=value):
                    out[...] = value.astype(out.dtype)

    full = pl.BlockSpec((count, quarter), lambda *_: (0, 0))
    out = kernel_call(
        body,
        (4,),
        [
            pl.BlockSpec((parts * count, units), lambda *_: (0, 0)),
            pl.BlockSpec((units, quarter), lambda q, column_ref: (0, column_ref[0] ^ 3 ^ q)),
        ]
        + [pl.BlockSpec((count, quarter), lambda q, *_: (0, 3 - q))] * parts,
        [full] * (4 * parts),
        ([shape_of(count, quarter, dtype=jnp.float32)] + [shape_of(count, quarter)] * 3) * parts,
        [weighted, down] + list(got),
        [],
        "output_own",
        column=column,
        earlier=earlier,
    )
    return [out[4 * i : 4 * i + 4] for i in range(parts)]


def backward_rows(groups, down, parts, per_row, first_row, tile, earlier=()):
    slope_s, act_s, w_rows, w_shadow = per_row
    rows = sum(g[2] for g in groups)
    units_all, width = down.shape
    units_s = slope_s.shape[1]
    units = units_all - units_s
    steps = width // tile
    arrays = list({id(a): a for part in parts for a in part[:2]}.values())
    places = [[next(i for i, a in enumerate(arrays) if a is b) for b in part[:2]] for part in parts]

    def body(*refs):
        n, m = len(groups), len(arrays)
        down_ref = refs[n]
        array_refs = refs[n + 1 : n + 1 + m]
        slope_s_ref, act_s_ref, w_ref, w_s_ref, pre_ref, pre_s_ref, acc, held = refs[n + 1 + m :]
        clear_first(acc)
        acc[...] += contract_last(rows_operand(refs[:n], groups, held), down_ref[...])

        @pl.when(pl.program_id(0) == steps - 1)
        def _():
            chunk = 128
            start = 0
            for (_, _, count), (_, _, first), (slope_at, act_at) in zip(groups, parts, places):

                @pl.loop(0, count // chunk)
                def _(i, start=start, first=first, slope_ref=array_refs[slope_at], act_ref=array_refs[act_at]):
                    source = pl.ds(pl.multiple_of(first + i * chunk, chunk), chunk)
                    part = pl.ds(pl.multiple_of(start + i * chunk, chunk), chunk)
                    whole_part = pl.ds(pl.multiple_of(first_row + start + i * chunk, chunk), chunk)
                    grad = acc[part, :units] * w_ref[whole_part, :]
                    pre_ref[part, :units] = (grad * slope_ref[source, :]).astype(jnp.bfloat16)
                    pre_ref[part, units:] = (grad * act_ref[source, :]).astype(jnp.bfloat16)
                    grad = acc[part, units:] * w_s_ref[whole_part, :]
                    pre_s_ref[part, :units_s] = (grad * slope_s_ref[whole_part, :]).astype(jnp.bfloat16)
                    pre_s_ref[part, units_s:] = (grad * act_s_ref[whole_part, :]).astype(jnp.bfloat16)

                start += count

    extra = arrays + [slope_s, act_s, w_rows, w_shadow]
    return kernel_call(
        body,
        (steps,),
        row_specs(groups, tile) + [pl.BlockSpec((units_all, tile), lambda k, *_: (0, k))] + [whole(a) for a in extra],
        [pl.BlockSpec((rows, 2 * units), lambda *_: (0, 0)), pl.BlockSpec((rows, 2 * units_s), lambda *_: (0, 0))],
        [shape_of(rows, 2 * units), shape_of(rows, 2 * units_s)],
        [g[0] for g in groups] + [down] + extra,
        [pltpu.VMEM((rows, units_all), jnp.float32), pltpu.VMEM((rows, tile), jnp.bfloat16)],
        "backward_rows",
        earlier=earlier,
    )


def stage_rows(refs, groups, held):
    start = 0
    for ref, (_, _, count) in zip(refs, groups):
        held[pl.ds(start, count), :] = ref[...]
        start += count
    return held[...]


def shadow_grads(x_groups, dy_groups, pre_s, weighted, units, tile, earlier=()):
    rows, wide = weighted.shape[0], pre_s[0].shape[1]
    apart = wide // 2
    width = x_groups[0][0].shape[1]
    m = len(pre_s)

    def body(*refs):
        n = len(x_groups)
        pre_refs = refs[2 * n : 2 * n + m]
        hidden_ref, out, held, pre_t, hidden_t = refs[2 * n + m :]

        @pl.when(pl.program_id(0) == 0)
        def _():
            start = 0
            for ref in pre_refs:
                pre_t[:, start : start + ref.shape[0]] = ref[...].T
                start += ref.shape[0]
            hidden_t[...] = hidden_ref[...].T

        value = dot32(pre_t[...], stage_rows(refs[:n], x_groups, held))
        out[:units, :] = value[:units].astype(jnp.bfloat16)
        out[units : 2 * units, :] = value[apart : apart + units].astype(jnp.bfloat16)
        value = dot32(hidden_t[...], stage_rows(refs[n : 2 * n], dy_groups, held))
        out[2 * units :, :] = value[:units].astype(jnp.bfloat16)

    (out,) = kernel_call(
        body,
        (width // tile,),
        row_specs(x_groups, tile)
        + row_specs(dy_groups, tile)
        + [whole(p) for p in pre_s]
        + [pl.BlockSpec((rows, apart), lambda *_: (0, weighted.shape[1] // apart - 1))],
        [pl.BlockSpec((3 * units, tile), lambda k, *_: (0, k))],
        [shape_of(3 * units, width)],
        [g[0] for g in x_groups + dy_groups] + list(pre_s) + [weighted],
        [
            pltpu.VMEM((rows, tile), jnp.bfloat16),
            pltpu.VMEM((wide, rows), jnp.bfloat16),
            pltpu.VMEM((apart, rows), jnp.bfloat16),
        ],
        "shadow_grads",
        earlier=earlier,
    )
    return out


def input_grads(groups, pre, tile, earlier=()):
    both = pre[0].shape[1]
    rows = sum(p.shape[0] for p in pre)
    units = both // 2
    width = groups[0][0].shape[1]
    m = len(pre)

    def body(*refs):
        n = len(groups)
        gate_ref, up_ref, held, pre_held = refs[n + m :]

        @pl.when(pl.program_id(0) == 0)
        def _():
            start = 0
            for ref in refs[n : n + m]:
                pre_held[start : start + ref.shape[0], :] = ref[...]
                start += ref.shape[0]

        value = contract_rows(stage_rows(refs[:n], groups, held), pre_held[...])
        gate_ref[...] = value[:, :units].astype(jnp.bfloat16)
        up_ref[...] = value[:, units:].astype(jnp.bfloat16)

    return kernel_call(
        body,
        (width // tile,),
        row_specs(groups, tile) + [whole(p) for p in pre],
        [pl.BlockSpec((tile, units), lambda k, *_: (k, 0))] * 2,
        [shape_of(width, units)] * 2,
        [g[0] for g in groups] + list(pre),
        [pltpu.VMEM((rows, tile), jnp.bfloat16), pltpu.VMEM((rows, both), jnp.bfloat16)],
        "input_grads",
        earlier=earlier,
    )


def down_grad(groups, weighted, units, tile, earlier=()):
    rows = weighted.shape[0]
    width = groups[0][0].shape[1]

    def body(*refs):
        n = len(groups)
        hidden_ref, out, held, hidden_t = refs[n:]

        @pl.when(pl.program_id(0) == 0)
        def _():
            hidden_t[...] = hidden_ref[...].T

        out[...] = dot32(hidden_t[...], stage_rows(refs[:n], groups, held)).astype(jnp.bfloat16)

    (out,) = kernel_call(
        body,
        (width // tile,),
        row_specs(groups, tile) + [pl.BlockSpec((rows, units), lambda *_: (0, 0))],
        [pl.BlockSpec((units, tile), lambda k, *_: (0, k))],
        [shape_of(units, width)],
        [g[0] for g in groups] + [weighted],
        [pltpu.VMEM((rows, tile), jnp.bfloat16), pltpu.VMEM((units, rows), jnp.bfloat16)],
        "down_grad",
        earlier=earlier,
    )
    return out


def gather_along_z(own):
    ep_count = lax.axis_size("ep")
    groups = [list(range(core, ep_count, 2)) for core in range(2)]
    return lax.all_gather(own, "ep", axis_index_groups=groups, axis=0, tiled=True)


def swap_cores(block):
    return lax.ppermute(block, "ep", swap_pairs(lax.axis_size("ep"), 1))


def send_plane(*pieces):
    pieces = pieces * 3 if len(pieces) == 1 else pieces
    return [lax.ppermute(p, "tp", swap_pairs(lax.axis_size("tp"), bit)) for p, bit in zip(pieces, (1, 2, 3))]


def exchange_cores(blocks):
    ep_count, core = lax.axis_size("ep"), lax.axis_index("ep") % 2
    pairs = blocks.reshape(ep_count // 2, 2, *blocks.shape[1:])
    kept = jnp.where(core == 0, pairs[:, 0], pairs[:, 1])
    given = jnp.where(core == 0, pairs[:, 1], pairs[:, 0])
    return kept, swap_cores(given)


def exchange_chips(kept, taken, late=(), earlier=()):
    ep_count, me = lax.axis_size("ep"), lax.axis_index("ep")
    chips, chip, core = ep_count // 2, me // 2, me % 2
    both = jnp.stack([jnp.where(core == 0, kept, taken), jnp.where(core == 0, taken, kept)], axis=1)
    pieces = [lax.dynamic_index_in_dim(both, chip ^ shift, 0) for shift in range(chips)]
    if earlier:
        pieces = list(after(pieces, *earlier))
    if late:
        pieces[-1:] = after(pieces[-1:], *late)
    return pieces[:1] + [
        lax.ppermute(pieces[shift], "ep", swap_pairs(ep_count, 2 * shift)) for shift in range(1, chips)
    ]


def dense_shards(
    tokens,
    cotangent,
    expert_ids,
    gate_weights,
    shadow_mask,
    w_gate,
    w_up,
    w_down,
    s_gate,
    s_up,
    s_down,
):
    ep_count, tp_count = lax.axis_size("ep"), lax.axis_size("tp")
    ep_index, tp_index = lax.axis_index("ep"), lax.axis_index("tp")
    tok_count, top_count = expert_ids.shape
    quarter = tokens.shape[1]
    width = quarter * tp_count
    hidden_part = w_gate.shape[2]
    shadow_part = hidden_part // ep_count
    block_width = s_gate.shape[0]
    steps = ep_count // 2
    later = (steps - 1) * tok_count
    tile = width // 8
    along, across = swap_pairs(tp_count, 1), swap_pairs(tp_count, 2)

    picked = expert_ids[None, :, :] == jnp.arange(ep_count, dtype=jnp.int32)[:, None, None]
    table = jnp.sum(jnp.where(picked, gate_weights[None, :, :top_count], 0.0), axis=2)
    shadow_weight = gate_weights[:, top_count] * shadow_mask.astype(jnp.float32)
    table = jnp.concatenate([table, jnp.broadcast_to(shadow_weight[None], table.shape)], axis=1)
    table = jnp.concatenate(split_parts(table), axis=1)
    table = jnp.pad(table[:, None, :], ((0, 0), (0, 15), (0, block_width - table.shape[1])))
    shadow_blocks = jnp.concatenate(
        [
            s_gate.T.reshape(ep_count, shadow_part, block_width),
            s_up.T.reshape(ep_count, shadow_part, block_width),
            s_down.reshape(ep_count, shadow_part, block_width),
            table,
        ],
        axis=1,
    )

    chip = ep_index // 2
    x_z = gather_along_z(tokens)
    dy_z = gather_along_z(cotangent)
    near = stack_pieces([tokens, cotangent])
    near_plane = send_plane(near)
    w_both = jnp.concatenate([w_gate[0], w_up[0]], axis=1)
    shadow_kept, shadow_taken = exchange_cores(shadow_blocks)
    x_z, near_x, near_y, near_d, shadow_taken = after([x_z, *near_plane, shadow_taken], w_both)

    x_piece = other_chips(x_z, steps, chip)
    x_plane = send_plane(x_piece)
    shadow_pieces = exchange_chips(shadow_kept, shadow_taken)
    near_own = join_plane(tp_index, near, near_x, near_y, near_d)
    near_other = swap_cores(near_own)
    x_near = [(near_own, 0, tok_count), (near_other, 0, tok_count)]
    hidden_near, slope_near, act_near = forward_rows(x_near, w_both, 2 * tile)
    spare_rows = -shadow_part % 128 + shadow_part
    down = jnp.pad(w_down[0], ((0, spare_rows), (0, 0)))
    fenced = after([*x_plane, dy_z, down, *shadow_pieces], hidden_near)
    x_plane, dy_z, down, shadow_pieces = fenced[:3], fenced[3], fenced[4], fenced[5:]

    dy_piece = other_chips(dy_z, steps, chip)
    dy_plane = send_plane(dy_piece)
    x_own = join_plane(tp_index, x_piece, *x_plane, earlier=[dy_piece])
    x_other = swap_cores(x_own)
    x_far = [(x_own, 0, later), (x_other, 0, later)]
    x_groups = [x_far[0], x_near[0], x_near[1], x_far[1]]
    hidden_far, slope_far, act_far = forward_rows(x_far, w_both, 2 * tile)
    shadow_in, down = lay_out_shadow(shadow_pieces, down, shadow_part, chip, earlier=[x_own])
    hidden_s, slope_s, act_s = forward_rows(x_groups, shadow_in, 2 * tile, transposed=True)

    weighted, w_rows, w_shadow = weigh_hidden(
        hidden_near, hidden_far, hidden_s, shadow_pieces, 3 * shadow_part, tok_count, ep_index % 2
    )

    parts = 2 if steps % 2 == 0 else 1
    sent = output_other(weighted, down, tp_index, parts, tok_count, quarter)
    got = [swap_cores(array) for array in sent]
    dy_plane = after(dy_plane, *sent)

    dy_own = join_plane(tp_index, dy_piece, *dy_plane)
    dy_other = swap_cores(dy_own)
    dy_groups = [(dy_own, 0, later), (near_own, 1, tok_count), (near_other, 1, tok_count), (dy_other, 0, later)]
    segments = [
        (slope_far, act_far, 0),
        (slope_near, act_near, 0),
        (slope_near, act_near, tok_count),
        (slope_far, act_far, later),
    ]
    per_row = (slope_s, act_s, w_rows, w_shadow)
    pre_first, pre_s_first = backward_rows(dy_groups[:3], down, segments[:3], per_row, 0, 2 * tile)
    owns = output_own(weighted, got, down, tp_index, quarter, earlier=[pre_first])
    sums = [send_plane(*own[1:]) for own in owns]
    first_rows = sum(g[2] for g in dy_groups[:3])
    pre_last, pre_s_last = backward_rows(
        dy_groups[3:], down, segments[3:], per_row, first_rows, 2 * tile, earlier=[own[1] for own in owns]
    )
    pre, pre_s = [pre_first, pre_last], [pre_s_first, pre_s_last]
    grad_s = shadow_grads(x_groups, dy_groups, pre_s, weighted, shadow_part, tile)
    blocks = grad_s.reshape(3 * shadow_part, ep_count, block_width).transpose(1, 0, 2)
    grad_kept, grad_taken = exchange_cores(blocks)
    sums[0] = after(sums[0], grad_s)

    def slot_rows(i):
        part = slice(i % (steps // parts) * tok_count, (i % (steps // parts) + 1) * tok_count)
        total = owns[i * parts // steps][0][part]
        for array in sums[i * parts // steps]:
            total = total + array[part].astype(jnp.float32)
        return total

    first = [slot_rows(i).astype(jnp.bfloat16) for i in range(steps // parts)]
    grad_pieces = exchange_chips(grad_kept, grad_taken, earlier=first)
    grad_gate, grad_up = input_grads(x_groups, pre, tile, earlier=[grad_pieces[0]])
    if parts > 1:
        sums[-1] = after(sums[-1], grad_gate)
    total = slot_rows(steps - 1)
    pieces = first + [slot_rows(i).astype(jnp.bfloat16) for i in range(len(first), steps - 1)]
    grad_down = down_grad(dy_groups, weighted, hidden_part, tile, earlier=[pieces[-1], grad_gate])
    for s in range(1, steps):
        total = total + lax.ppermute(pieces[s - 1], "ep", swap_pairs(ep_count, 2 * s)).astype(jnp.float32)
    mixed = total.astype(jnp.bfloat16)

    grads_s = lay_out_grads(grad_pieces, shadow_part, chip, earlier=[grad_down])
    return (mixed, grad_gate[None], grad_up[None], grad_down[None], *grads_s)


def shards(tokens, cotangent, expert_ids, *others):
    tp_count, ep_count = lax.axis_size("tp"), lax.axis_size("ep")
    tok_count, top_count = expert_ids.shape
    rows = (5 * tok_count * top_count) // 4
    chips = ep_count // 2
    fits = tp_count == 4 and ep_count == 2 * chips and chips & (chips - 1) == 0 and tok_count % 128 == 0
    dense = fits and ep_count * tok_count <= 3 * rows
    return (dense_shards if dense else routed_shards)(tokens, cotangent, expert_ids, *others)


def solution(mesh):
    return jax.shard_map(
        shards,
        mesh=mesh,
        in_specs=(
            P("ep", "tp"),
            P("ep", "tp"),
            P("ep", None),
            P("ep", None),
            P("ep"),
            P("ep", None, "tp"),
            P("ep", None, "tp"),
            P("ep", "tp", None),
            P("ep", "tp"),
            P("ep", "tp"),
            P("tp", "ep"),
        ),
        out_specs=(
            P("ep", "tp"),
            P("ep", None, "tp"),
            P("ep", None, "tp"),
            P("ep", "tp", None),
            P("ep", "tp"),
            P("ep", "tp"),
            P("tp", "ep"),
        ),
        check_vma=False,
    )
```

```python
import functools

import jax
import jax.numpy as jnp
from jax import lax
from jax.experimental import pallas as pl
from jax.experimental.pallas import tpu as pltpu
from jax.sharding import PartitionSpec as P


def contract_rows(left, right):
    return lax.dot_general(
        left, right, (((0,), (0,)), ((), ())), preferred_element_type=jnp.float32
    )


def split_parts(values):
    upper_part = values.astype(jnp.bfloat16)
    lower_part = (values - upper_part.astype(jnp.float32)).astype(jnp.bfloat16)
    return (upper_part, lower_part)


def weigh_rows(weight_table, rows):
    weight_upper, weight_lower = split_parts(weight_table)
    return jnp.dot(weight_upper, rows, preferred_element_type=jnp.float32) + jnp.dot(
        weight_lower, rows, preferred_element_type=jnp.float32
    )


def expert_pass(rows_x, rows_dout, weight_gate, weight_up, weight_down):
    pre_gate = jnp.dot(rows_x, weight_gate, preferred_element_type=jnp.float32)
    pre_up = jnp.dot(rows_x, weight_up, preferred_element_type=jnp.float32)
    sigmoid_gate = jax.nn.sigmoid(pre_gate)
    activated = pre_gate * sigmoid_gate
    hidden = (activated * pre_up).astype(jnp.bfloat16)
    partial_out = jnp.dot(hidden, weight_down, preferred_element_type=jnp.float32).astype(
        jnp.bfloat16
    )
    hidden_grad = lax.dot_general(
        rows_dout, weight_down, (((1,), (1,)), ((), ())), preferred_element_type=jnp.float32
    )
    grad_pre_gate = (
        hidden_grad * pre_up * sigmoid_gate * (1.0 + pre_gate * (1.0 - sigmoid_gate))
    ).astype(jnp.bfloat16)
    grad_pre_up = (hidden_grad * activated).astype(jnp.bfloat16)
    return (partial_out, hidden, grad_pre_gate, grad_pre_up)


def routed_shards(
    tokens,
    cotangent,
    expert_ids,
    gate_weights,
    shadow_mask,
    w_gate,
    w_up,
    w_down,
    s_gate,
    s_up,
    s_down,
):
    ep_count = lax.axis_size("ep")
    tok_count, top_count = expert_ids.shape
    quarter_width = tokens.shape[1]
    width = quarter_width * lax.axis_size("tp")
    expert_count = w_gate.shape[0] * ep_count
    capacity = (5 * tok_count * top_count + 4 * expert_count - 1) // (4 * expert_count)
    slot_count = expert_count * capacity
    picks_flat = expert_ids.reshape(-1)
    onehot = (picks_flat[:, None] == jnp.arange(expert_count, dtype=jnp.int32)[None, :]).astype(
        jnp.int32
    )
    slot_rank = jnp.sum((jnp.cumsum(onehot, axis=0) - onehot) * onehot, axis=1)
    slot_index = (picks_flat * capacity + slot_rank).reshape(tok_count, top_count)
    matches = jnp.arange(slot_count, dtype=jnp.int32)[:, None, None] == slot_index[None, :, :]
    dispatch = jnp.any(matches, axis=2).astype(jnp.bfloat16)
    weighting = jnp.sum(jnp.where(matches, gate_weights[None, :, :top_count], 0.0), axis=2)
    slot_gate = jnp.sum(weighting, axis=1)
    shadow_weight = gate_weights[:, top_count] * shadow_mask.astype(jnp.float32)
    x_full, dy_full = (
        lax.all_gather(tokens, "tp", axis=1, tiled=True),
        lax.all_gather(cotangent, "tp", axis=1, tiled=True),
    )
    rows_x = jnp.dot(dispatch, tokens, preferred_element_type=jnp.float32).astype(jnp.bfloat16)
    rows_dy = jnp.dot(dispatch, cotangent, preferred_element_type=jnp.float32)
    rows_dout = (slot_gate[:, None] * rows_dy).astype(jnp.bfloat16)
    recv_x, recv_dout = (
        lax.all_to_all(
            rows_x.reshape(ep_count, -1, quarter_width),
            "ep",
            split_axis=0,
            concat_axis=0,
            tiled=True,
        ),
        lax.all_to_all(
            rows_dout.reshape(ep_count, -1, quarter_width),
            "ep",
            split_axis=0,
            concat_axis=0,
            tiled=True,
        ),
    )
    expert_x, expert_dout = (
        lax.all_gather(recv_x.reshape(-1, quarter_width), "tp", axis=1, tiled=True),
        lax.all_gather(recv_dout.reshape(-1, quarter_width), "tp", axis=1, tiled=True),
    )
    partial_out, hidden, grad_pre_gate, grad_pre_up = expert_pass(
        expert_x, expert_dout, w_gate[0], w_up[0], w_down[0]
    )
    grad_gate = contract_rows(expert_x, grad_pre_gate).astype(jnp.bfloat16)[None]
    grad_up = contract_rows(expert_x, grad_pre_up).astype(jnp.bfloat16)[None]
    grad_down = contract_rows(hidden, expert_dout).astype(jnp.bfloat16)[None]
    full_gate, full_up, full_down = (
        lax.all_gather(s_gate, "ep", axis=0, tiled=True),
        lax.all_gather(s_up, "ep", axis=0, tiled=True),
        lax.all_gather(s_down, "ep", axis=1, tiled=True),
    )
    shadow_dout = (shadow_weight[:, None] * dy_full.astype(jnp.float32)).astype(jnp.bfloat16)
    shadow_out, shadow_hidden, shadow_gate_pre, shadow_up_pre = expert_pass(
        x_full, shadow_dout, full_gate, full_up, full_down
    )
    shadow_sums = lax.psum_scatter(
        jnp.concatenate(
            [
                contract_rows(x_full, shadow_gate_pre),
                contract_rows(x_full, shadow_up_pre),
                contract_rows(shadow_dout, shadow_hidden),
            ],
            axis=1,
        ).astype(jnp.bfloat16),
        "ep",
        scatter_dimension=0,
        tiled=True,
    ).astype(jnp.float32)
    hidden_part = s_gate.shape[1]
    grad_s_gate = shadow_sums[:, :hidden_part].astype(jnp.bfloat16)
    grad_s_up = shadow_sums[:, hidden_part : 2 * hidden_part].astype(jnp.bfloat16)
    grad_s_down = shadow_sums[:, 2 * hidden_part :].T.astype(jnp.bfloat16)
    back_rows = lax.all_to_all(
        partial_out.reshape(ep_count, -1, width), "ep", split_axis=0, concat_axis=0, tiled=True
    ).reshape(-1, width)
    term = weigh_rows(weighting.T, back_rows)
    term = term + shadow_weight[:, None] * shadow_out.astype(jnp.float32)
    mixed = lax.psum_scatter(term.astype(jnp.bfloat16), "tp", scatter_dimension=1, tiled=True)
    return (mixed, grad_gate, grad_up, grad_down, grad_s_gate, grad_s_up, grad_s_down)


ANY = pl.BlockSpec(memory_space=pl.ANY)
VMEM_LIMIT = 60 * 1024 * 1024
SHORT = pl.CostEstimate(flops=1, bytes_accessed=1, transcendentals=0)


def swap_pairs(count, bit):
    return [(i, i ^ bit) for i in range(count)]


def dot32(left, right):
    return jnp.dot(left, right, preferred_element_type=jnp.float32)


def contract_last(left, right):
    return lax.dot_general(
        left, right, (((1,), (1,)), ((), ())), preferred_element_type=jnp.float32
    )


def shape_of(*dims, dtype=jnp.bfloat16):
    return jax.ShapeDtypeStruct(dims, dtype)


def after(arrays, *earlier):
    def nothing(*refs):
        del refs

    count = len(arrays)
    return pl.pallas_call(
        nothing,
        out_shape=[jax.ShapeDtypeStruct(a.shape, a.dtype) for a in arrays],
        in_specs=[ANY] * (count + len(earlier)),
        out_specs=[ANY] * count,
        input_output_aliases={i: i for i in range(count)},
        compiler_params=pltpu.CompilerParams(vmem_limit_bytes=VMEM_LIMIT),
        cost_estimate=SHORT,
        name="after",
    )(*arrays, *earlier)


def kernel_call(body, grid, in_specs, out_specs, out_shape, operands, scratch, name, column=None, earlier=()):
    count = len(operands)

    def run(column_ref, *refs):
        del column_ref
        body(*refs[:count], *refs[count + len(earlier) :])

    column = jnp.zeros((1,), jnp.int32) if column is None else column.reshape(1).astype(jnp.int32)
    return pl.pallas_call(
        run,
        out_shape=out_shape,
        grid_spec=pltpu.PrefetchScalarGridSpec(
            num_scalar_prefetch=1,
            grid=grid,
            in_specs=list(in_specs) + [ANY] * len(earlier),
            out_specs=out_specs,
            scratch_shapes=scratch,
        ),
        compiler_params=pltpu.CompilerParams(vmem_limit_bytes=VMEM_LIMIT),
        cost_estimate=SHORT,
        name=name,
    )(column, *operands, *earlier)


def whole(array):
    return pl.BlockSpec(array.shape, lambda *_: (0,) * len(array.shape))


def join_plane(column, *pieces, earlier=()):
    rows, quarter = pieces[0].shape
    count = len(pieces)
    chunk = rows // 4

    def body(*refs):
        column_ref, sources, out = refs[0], refs[1 : 1 + count], refs[-1]
        for own_column in range(count):

            @pl.when(column_ref[0] == own_column)
            def _():
                for bit, source in enumerate(sources):
                    place = own_column ^ bit
                    out[:, place * quarter : (place + 1) * quarter] = source[...]

    return pl.pallas_call(
        body,
        out_shape=shape_of(rows, count * quarter),
        grid_spec=pltpu.PrefetchScalarGridSpec(
            num_scalar_prefetch=1,
            grid=(4,),
            in_specs=[pl.BlockSpec((chunk, quarter), lambda i, *_: (i, 0))] * count + [ANY] * len(earlier),
            out_specs=pl.BlockSpec((chunk, count * quarter), lambda i, *_: (i, 0)),
        ),
        compiler_params=pltpu.CompilerParams(vmem_limit_bytes=VMEM_LIMIT),
        cost_estimate=SHORT,
        name="join_plane",
    )(column.reshape(1).astype(jnp.int32), *pieces, *earlier)


def stack_pieces(pieces, earlier=()):
    rows, columns = pieces[0].shape
    count = len(pieces)

    def body(*refs):
        for i, ref in enumerate(refs[:count]):

            @pl.when(pl.program_id(0) == i)
            def _():
                refs[-1][...] = ref[...]

    return pl.pallas_call(
        body,
        out_shape=shape_of(count * rows, columns),
        grid=(count,),
        in_specs=[pl.BlockSpec((rows, columns), lambda i: (0, 0))] * count + [ANY] * len(earlier),
        out_specs=pl.BlockSpec((rows, columns), lambda i: (i, 0)),
        compiler_params=pltpu.CompilerParams(vmem_limit_bytes=VMEM_LIMIT),
        cost_estimate=SHORT,
        name="stack_pieces",
    )(*pieces, *earlier)


def on_piece(chip_ref, refs, use):
    step = pl.program_id(0)
    shift = chip_ref[0] ^ (step // 2)
    for i, ref in enumerate(refs):
        for core in range(2):

            @pl.when((shift == i) & (lax.rem(step, 2) == core))
            def _(ref=ref, core=core):
                use(ref.at[0, core])


def lay_out_shadow(pieces, down, units, chip, earlier=()):
    count = len(pieces)
    ep_count = 2 * count
    block_width = pieces[0].shape[3]
    apart = units + -units % 128
    all_units, width = down.shape

    def body(chip_ref, *refs):
        shadow_ref, out = refs[-2:]

        def use(ref):
            shadow_ref[...] = jnp.zeros_like(shadow_ref)
            shadow_ref[:units, :] = ref[:units, :]
            shadow_ref[apart : apart + units, :] = ref[units : 2 * units, :]
            out[units:, :] = jnp.zeros((apart - units, block_width), jnp.bfloat16)
            out[:units, :] = ref[2 * units : 3 * units, :]

        on_piece(chip_ref, refs[:count], use)

    return pl.pallas_call(
        body,
        out_shape=[shape_of(2 * apart, width), shape_of(all_units, width)],
        grid_spec=pltpu.PrefetchScalarGridSpec(
            num_scalar_prefetch=1,
            grid=(ep_count,),
            in_specs=[whole(p) for p in pieces] + [ANY] * (1 + len(earlier)),
            out_specs=[
                pl.BlockSpec((2 * apart, block_width), lambda e, *_: (0, e)),
                pl.BlockSpec((apart, block_width), lambda e, *_: (all_units // apart - 1, e)),
            ],
        ),
        input_output_aliases={1 + count: 1},
        compiler_params=pltpu.CompilerParams(vmem_limit_bytes=VMEM_LIMIT),
        cost_estimate=SHORT,
        name="lay_out_shadow",
    )(chip.reshape(1).astype(jnp.int32), *pieces, down, *earlier)


def lay_out_grads(pieces, units, chip, earlier=()):
    count = len(pieces)
    ep_count = 2 * count
    block_width = pieces[0].shape[3]
    hidden = ep_count * units

    def body(chip_ref, *refs):
        gate_ref, up_ref, down_ref, gate_t, up_t = refs[-5:]
        place = pl.ds(pl.multiple_of(pl.program_id(0) * units, 16), units)

        def use(ref):
            gate_t[place, :] = ref[:units, :]
            up_t[place, :] = ref[units : 2 * units, :]
            down_ref[place, :] = ref[2 * units :, :]

        on_piece(chip_ref, refs[:count], use)

        @pl.when(pl.program_id(0) == ep_count - 1)
        def _():
            gate_ref[...] = gate_t[...].T
            up_ref[...] = up_t[...].T

    return pl.pallas_call(
        body,
        out_shape=[shape_of(block_width, hidden), shape_of(block_width, hidden), shape_of(hidden, block_width)],
        grid_spec=pltpu.PrefetchScalarGridSpec(
            num_scalar_prefetch=1,
            grid=(ep_count,),
            in_specs=[whole(p) for p in pieces] + [ANY] * len(earlier),
            out_specs=[pl.BlockSpec((block_width, hidden), lambda *_: (0, 0))] * 2
            + [pl.BlockSpec((hidden, block_width), lambda *_: (0, 0))],
            scratch_shapes=[pltpu.VMEM((hidden, block_width), jnp.bfloat16)] * 2,
        ),
        compiler_params=pltpu.CompilerParams(vmem_limit_bytes=VMEM_LIMIT),
        cost_estimate=SHORT,
        name="lay_out_grads",
    )(chip.reshape(1).astype(jnp.int32), *pieces, *earlier)


def row_specs(groups, tile):
    def spec(index, rows):
        return pl.BlockSpec((rows, tile), lambda k, *_: (index, k))

    return [spec(index, rows) for _, index, rows in groups]


def apply_gate(pre_gate, pre_up):
    sigmoid_gate = jax.nn.sigmoid(pre_gate)
    activated = pre_gate * sigmoid_gate
    hidden = (activated * pre_up).astype(jnp.bfloat16)
    return hidden, pre_up * sigmoid_gate * (1.0 + pre_gate * (1.0 - sigmoid_gate)), activated


def clear_first(acc):
    @pl.when(pl.program_id(0) == 0)
    def _():
        acc[...] = jnp.zeros_like(acc)


def rows_operand(refs, groups, held):
    if len(groups) == 1:
        return refs[0][...]
    return stage_rows(refs, groups, held)


def forward_rows(groups, w_both, tile, transposed=False, earlier=()):
    rows = sum(g[2] for g in groups)
    if transposed:
        units, width = w_both.shape[0] // 2, w_both.shape[1]
        tile_spec = pl.BlockSpec((2 * units, tile), lambda k, *_: (0, k))
    else:
        width, units = w_both.shape[0], w_both.shape[1] // 2
        tile_spec = pl.BlockSpec((tile, 2 * units), lambda k, *_: (k, 0))
    steps = width // tile

    def body(*refs):
        n = len(groups)
        both_ref, hidden_ref, slope_ref, act_ref, acc, held = refs[n:]
        clear_first(acc)
        operand = rows_operand(refs[:n], groups, held)
        acc[...] += contract_last(operand, both_ref[...]) if transposed else dot32(operand, both_ref[...])

        @pl.when(pl.program_id(0) == steps - 1)
        def _():
            chunk = 128

            @pl.loop(0, rows // chunk)
            def _(i):
                part = pl.ds(pl.multiple_of(i * chunk, chunk), chunk)
                hidden, slope, act = apply_gate(acc[part, :units], acc[part, units:])
                hidden_ref[part, :] = hidden
                slope_ref[part, :] = slope.astype(jnp.bfloat16)
                act_ref[part, :] = act.astype(jnp.bfloat16)

    out_spec = pl.BlockSpec((rows, units), lambda *_: (0, 0))
    return kernel_call(
        body,
        (steps,),
        row_specs(groups, tile) + [tile_spec],
        [out_spec] * 3,
        [shape_of(rows, units)] * 3,
        [g[0] for g in groups] + [w_both],
        [pltpu.VMEM((rows, 2 * units), jnp.float32), pltpu.VMEM((rows, tile), jnp.bfloat16)],
        "forward_rows",
        earlier=earlier,
    )


def weigh_hidden(hidden_near, hidden_far, hidden_s, pieces, first_row, slot_rows, core, earlier=()):
    count = len(pieces)
    rows, units_s = hidden_s.shape
    units = hidden_near.shape[1]
    slots = [(s, 0) for s in list(range(1, count)) + [0]] + [(s, 1) for s in range(count)]

    def body(core_ref, *refs):
        near_ref, far_ref, s_ref, *piece_refs = refs[: 3 + count]
        out, w_ref, w_s_ref = refs[-3:]
        near, far = 0, 0
        for i, (slot, other) in enumerate(slots):
            part = pl.ds(i * slot_rows, slot_rows)
            table = piece_refs[slot][0, core_ref[0] ^ other, first_row : first_row + 16, :][:1].astype(jnp.float32)

            def column(j):
                both = table[:, j * slot_rows : (j + 1) * slot_rows]
                both = both + table[:, (j + 2) * slot_rows : (j + 3) * slot_rows]
                return jnp.broadcast_to(both, (slot_rows, slot_rows)).T[:, :1]

            weight, weight_s = column(0), column(1)
            w_ref[part, :] = weight
            w_s_ref[part, :] = weight_s
            if slot == 0:
                hidden = near_ref[near : near + slot_rows, :]
                near += slot_rows
            else:
                hidden = far_ref[far : far + slot_rows, :]
                far += slot_rows
            out[part, :units] = (hidden.astype(jnp.float32) * weight).astype(jnp.bfloat16)
            out[part, units:] = (s_ref[part, :].astype(jnp.float32) * weight_s).astype(jnp.bfloat16)

    return pl.pallas_call(
        body,
        out_shape=[
            shape_of(rows, units + units_s),
            shape_of(rows, 1, dtype=jnp.float32),
            shape_of(rows, 1, dtype=jnp.float32),
        ],
        grid_spec=pltpu.PrefetchScalarGridSpec(
            num_scalar_prefetch=1,
            grid=(1,),
            in_specs=[whole(a) for a in (hidden_near, hidden_far, hidden_s, *pieces)] + [ANY] * len(earlier),
            out_specs=[
                pl.BlockSpec((rows, units + units_s), lambda *_: (0, 0)),
                pl.BlockSpec((rows, 1), lambda *_: (0, 0)),
                pl.BlockSpec((rows, 1), lambda *_: (0, 0)),
            ],
        ),
        compiler_params=pltpu.CompilerParams(vmem_limit_bytes=VMEM_LIMIT),
        cost_estimate=SHORT,
        name="weigh_hidden",
    )(core.reshape(1).astype(jnp.int32), hidden_near, hidden_far, hidden_s, *pieces, *earlier)


def output_other(weighted, down, column, parts, slot_rows, quarter, earlier=()):
    rows, units = weighted.shape
    count = rows // 2 // parts

    def body(weighted_ref, down_ref, *outs):
        for i, out in enumerate(outs):
            first, last = slot_rows + i * count, slot_rows + (i + 1) * count
            kept = min(last, rows // 2) - first
            value = dot32(weighted_ref[first : first + kept, :], down_ref[...])
            out[:kept, :] = value.astype(jnp.bfloat16)
            if kept < count:
                value = dot32(weighted_ref[: count - kept, :], down_ref[...])
                out[kept:, :] = value.astype(jnp.bfloat16)

    return kernel_call(
        body,
        (4,),
        [
            pl.BlockSpec((rows // 2, units), lambda *_: (1, 0)),
            pl.BlockSpec((units, quarter), lambda q, column_ref: (0, column_ref[0] ^ q)),
        ],
        [pl.BlockSpec((count, quarter), lambda q, *_: (0, q))] * parts,
        [shape_of(count, 4 * quarter)] * parts,
        [weighted, down],
        [],
        "output_other",
        column=column,
        earlier=earlier,
    )


def output_own(weighted, got, down, column, quarter, earlier=()):
    count, units = got[0].shape[0], weighted.shape[1]
    parts = len(got)
    rows = parts * count

    def body(weighted_ref, down_ref, *refs):
        for i in range(parts):
            part = slice(i * count, (i + 1) * count)
            value = dot32(weighted_ref[part, :], down_ref[...]) + refs[i][...].astype(jnp.float32)
            for j, out in enumerate(refs[parts:]):

                @pl.when(pl.program_id(0) == 3 - j)
                def _(out=out, part=part, value=value):
                    out[part, :] = value.astype(out.dtype)

    full = pl.BlockSpec((rows, quarter), lambda *_: (0, 0))
    return kernel_call(
        body,
        (4,),
        [
            pl.BlockSpec((rows, units), lambda *_: (0, 0)),
            pl.BlockSpec((units, quarter), lambda q, column_ref: (0, column_ref[0] ^ 3 ^ q)),
        ]
        + [pl.BlockSpec((count, quarter), lambda q, *_: (0, 3 - q))] * parts,
        [full] * 4,
        [shape_of(rows, quarter, dtype=jnp.float32)] + [shape_of(rows, quarter)] * 3,
        [weighted, down] + list(got),
        [],
        "output_own",
        column=column,
        earlier=earlier,
    )


def backward_rows(groups, down, parts, per_row, first_row, tile, earlier=()):
    slope_s, act_s, w_rows, w_shadow = per_row
    rows = sum(g[2] for g in groups)
    units_all, width = down.shape
    units_s = slope_s.shape[1]
    units = units_all - units_s
    steps = width // tile
    arrays = list({id(a): a for part in parts for a in part[:2]}.values())
    places = [[next(i for i, a in enumerate(arrays) if a is b) for b in part[:2]] for part in parts]

    def body(*refs):
        n, m = len(groups), len(arrays)
        down_ref = refs[n]
        array_refs = refs[n + 1 : n + 1 + m]
        slope_s_ref, act_s_ref, w_ref, w_s_ref, pre_ref, pre_s_ref, acc, held = refs[n + 1 + m :]
        clear_first(acc)
        acc[...] += contract_last(rows_operand(refs[:n], groups, held), down_ref[...])

        @pl.when(pl.program_id(0) == steps - 1)
        def _():
            chunk = 128
            start = 0
            for (_, _, count), (_, _, first), (slope_at, act_at) in zip(groups, parts, places):

                @pl.loop(0, count // chunk)
                def _(i, start=start, first=first, slope_ref=array_refs[slope_at], act_ref=array_refs[act_at]):
                    source = pl.ds(pl.multiple_of(first + i * chunk, chunk), chunk)
                    part = pl.ds(pl.multiple_of(start + i * chunk, chunk), chunk)
                    whole_part = pl.ds(pl.multiple_of(first_row + start + i * chunk, chunk), chunk)
                    grad = acc[part, :units] * w_ref[whole_part, :]
                    pre_ref[part, :units] = (grad * slope_ref[source, :]).astype(jnp.bfloat16)
                    pre_ref[part, units:] = (grad * act_ref[source, :]).astype(jnp.bfloat16)
                    grad = acc[part, units:] * w_s_ref[whole_part, :]
                    pre_s_ref[part, :units_s] = (grad * slope_s_ref[whole_part, :]).astype(jnp.bfloat16)
                    pre_s_ref[part, units_s:] = (grad * act_s_ref[whole_part, :]).astype(jnp.bfloat16)

                start += count

    extra = arrays + [slope_s, act_s, w_rows, w_shadow]
    return kernel_call(
        body,
        (steps,),
        row_specs(groups, tile) + [pl.BlockSpec((units_all, tile), lambda k, *_: (0, k))] + [whole(a) for a in extra],
        [pl.BlockSpec((rows, 2 * units), lambda *_: (0, 0)), pl.BlockSpec((rows, 2 * units_s), lambda *_: (0, 0))],
        [shape_of(rows, 2 * units), shape_of(rows, 2 * units_s)],
        [g[0] for g in groups] + [down] + extra,
        [pltpu.VMEM((rows, units_all), jnp.float32), pltpu.VMEM((rows, tile), jnp.bfloat16)],
        "backward_rows",
        earlier=earlier,
    )


def stage_rows(refs, groups, held):
    start = 0
    for ref, (_, _, count) in zip(refs, groups):
        held[pl.ds(start, count), :] = ref[...]
        start += count
    return held[...]


def shadow_grads(x_groups, dy_groups, pre_s, weighted, units, tile, earlier=()):
    rows, wide = weighted.shape[0], pre_s[0].shape[1]
    apart = wide // 2
    width = x_groups[0][0].shape[1]
    m = len(pre_s)

    def body(*refs):
        n = len(x_groups)
        pre_refs = refs[2 * n : 2 * n + m]
        hidden_ref, out, held, pre_t, hidden_t = refs[2 * n + m :]

        @pl.when(pl.program_id(0) == 0)
        def _():
            start = 0
            for ref in pre_refs:
                pre_t[:, start : start + ref.shape[0]] = ref[...].T
                start += ref.shape[0]
            hidden_t[...] = hidden_ref[...].T

        value = dot32(pre_t[...], stage_rows(refs[:n], x_groups, held))
        out[:units, :] = value[:units].astype(jnp.bfloat16)
        out[units : 2 * units, :] = value[apart : apart + units].astype(jnp.bfloat16)
        value = dot32(hidden_t[...], stage_rows(refs[n : 2 * n], dy_groups, held))
        out[2 * units :, :] = value[:units].astype(jnp.bfloat16)

    (out,) = kernel_call(
        body,
        (width // tile,),
        row_specs(x_groups, tile)
        + row_specs(dy_groups, tile)
        + [whole(p) for p in pre_s]
        + [pl.BlockSpec((rows, apart), lambda *_: (0, weighted.shape[1] // apart - 1))],
        [pl.BlockSpec((3 * units, tile), lambda k, *_: (0, k))],
        [shape_of(3 * units, width)],
        [g[0] for g in x_groups + dy_groups] + list(pre_s) + [weighted],
        [
            pltpu.VMEM((rows, tile), jnp.bfloat16),
            pltpu.VMEM((wide, rows), jnp.bfloat16),
            pltpu.VMEM((apart, rows), jnp.bfloat16),
        ],
        "shadow_grads",
        earlier=earlier,
    )
    return out


def input_grads(groups, pre, tile, earlier=()):
    both = pre[0].shape[1]
    rows = sum(p.shape[0] for p in pre)
    units = both // 2
    width = groups[0][0].shape[1]
    m = len(pre)

    def body(*refs):
        n = len(groups)
        gate_ref, up_ref, held, pre_held = refs[n + m :]

        @pl.when(pl.program_id(0) == 0)
        def _():
            start = 0
            for ref in refs[n : n + m]:
                pre_held[start : start + ref.shape[0], :] = ref[...]
                start += ref.shape[0]

        value = contract_rows(stage_rows(refs[:n], groups, held), pre_held[...])
        gate_ref[...] = value[:, :units].astype(jnp.bfloat16)
        up_ref[...] = value[:, units:].astype(jnp.bfloat16)

    return kernel_call(
        body,
        (width // tile,),
        row_specs(groups, tile) + [whole(p) for p in pre],
        [pl.BlockSpec((tile, units), lambda k, *_: (k, 0))] * 2,
        [shape_of(width, units)] * 2,
        [g[0] for g in groups] + list(pre),
        [pltpu.VMEM((rows, tile), jnp.bfloat16), pltpu.VMEM((rows, both), jnp.bfloat16)],
        "input_grads",
        earlier=earlier,
    )


def down_grad(groups, weighted, units, tile, earlier=()):
    rows = weighted.shape[0]
    width = groups[0][0].shape[1]

    def body(*refs):
        n = len(groups)
        hidden_ref, out, held, hidden_t = refs[n:]

        @pl.when(pl.program_id(0) == 0)
        def _():
            hidden_t[...] = hidden_ref[...].T

        out[...] = dot32(hidden_t[...], stage_rows(refs[:n], groups, held)).astype(jnp.bfloat16)

    (out,) = kernel_call(
        body,
        (width // tile,),
        row_specs(groups, tile) + [pl.BlockSpec((rows, units), lambda *_: (0, 0))],
        [pl.BlockSpec((units, tile), lambda k, *_: (0, k))],
        [shape_of(units, width)],
        [g[0] for g in groups] + [weighted],
        [pltpu.VMEM((rows, tile), jnp.bfloat16), pltpu.VMEM((units, rows), jnp.bfloat16)],
        "down_grad",
        earlier=earlier,
    )
    return out


def send_along_z(own):
    ep_count = lax.axis_size("ep")
    return [lax.ppermute(own, "ep", swap_pairs(ep_count, 2 * s)) for s in range(1, ep_count // 2)]


def swap_cores(block):
    return lax.ppermute(block, "ep", swap_pairs(lax.axis_size("ep"), 1))


def send_plane(*pieces):
    pieces = pieces * 3 if len(pieces) == 1 else pieces
    return [lax.ppermute(p, "tp", swap_pairs(lax.axis_size("tp"), bit)) for p, bit in zip(pieces, (1, 2, 3))]


def exchange_cores(blocks):
    ep_count, core = lax.axis_size("ep"), lax.axis_index("ep") % 2
    pairs = blocks.reshape(ep_count // 2, 2, *blocks.shape[1:])
    kept = jnp.where(core == 0, pairs[:, 0], pairs[:, 1])
    given = jnp.where(core == 0, pairs[:, 1], pairs[:, 0])
    return kept, swap_cores(given)


def exchange_chips(kept, taken, late=(), earlier=()):
    ep_count, me = lax.axis_size("ep"), lax.axis_index("ep")
    chips, chip, core = ep_count // 2, me // 2, me % 2
    both = jnp.stack([jnp.where(core == 0, kept, taken), jnp.where(core == 0, taken, kept)], axis=1)
    pieces = [lax.dynamic_index_in_dim(both, chip ^ shift, 0) for shift in range(chips)]
    if earlier:
        pieces = list(after(pieces, *earlier))
    if late:
        pieces[-1:] = after(pieces[-1:], *late)
    return pieces[:1] + [
        lax.ppermute(pieces[shift], "ep", swap_pairs(ep_count, 2 * shift)) for shift in range(1, chips)
    ]


def dense_shards(
    tokens,
    cotangent,
    expert_ids,
    gate_weights,
    shadow_mask,
    w_gate,
    w_up,
    w_down,
    s_gate,
    s_up,
    s_down,
):
    ep_count, tp_count = lax.axis_size("ep"), lax.axis_size("tp")
    ep_index, tp_index = lax.axis_index("ep"), lax.axis_index("tp")
    tok_count, top_count = expert_ids.shape
    quarter = tokens.shape[1]
    width = quarter * tp_count
    hidden_part = w_gate.shape[2]
    shadow_part = hidden_part // ep_count
    block_width = s_gate.shape[0]
    steps = ep_count // 2
    later = (steps - 1) * tok_count
    tile = width // 8
    along, across = swap_pairs(tp_count, 1), swap_pairs(tp_count, 2)

    picked = expert_ids[None, :, :] == jnp.arange(ep_count, dtype=jnp.int32)[:, None, None]
    table = jnp.sum(jnp.where(picked, gate_weights[None, :, :top_count], 0.0), axis=2)
    shadow_weight = gate_weights[:, top_count] * shadow_mask.astype(jnp.float32)
    table = jnp.concatenate([table, jnp.broadcast_to(shadow_weight[None], table.shape)], axis=1)
    table = jnp.concatenate(split_parts(table), axis=1)
    table = jnp.pad(table[:, None, :], ((0, 0), (0, 15), (0, block_width - table.shape[1])))
    shadow_blocks = jnp.concatenate(
        [
            s_gate.T.reshape(ep_count, shadow_part, block_width),
            s_up.T.reshape(ep_count, shadow_part, block_width),
            s_down.reshape(ep_count, shadow_part, block_width),
            table,
        ],
        axis=1,
    )

    x_z = send_along_z(tokens)
    near = stack_pieces([tokens, cotangent])
    near_x, near_y = send_plane(near, near)
    near_late = stack_pieces([tokens, cotangent], earlier=[*x_z[:2], near_x, near_y])
    near_d = lax.ppermute(near_late, "tp", swap_pairs(tp_count, 3))
    w_both = jnp.concatenate([w_gate[0], w_up[0]], axis=1)
    (shadow_blocks,) = after([shadow_blocks], *x_z[:2], near_x, near_y)
    shadow_kept, shadow_taken = exchange_cores(shadow_blocks)
    *x_z, near_x, near_y, near_d, shadow_taken = after(x_z + [near_x, near_y, near_d, shadow_taken], w_both)

    x_piece = stack_pieces(x_z)
    x_plane = send_plane(x_piece)
    dy_z = send_along_z(cotangent)
    near_own = join_plane(tp_index, near, near_x, near_y, near_d)
    near_other = swap_cores(near_own)
    x_near = [(near_own, 0, tok_count), (near_other, 0, tok_count)]
    hidden_near, slope_near, act_near = forward_rows(x_near, w_both, 2 * tile)
    spare_rows = -shadow_part % 128 + shadow_part
    down = jnp.pad(w_down[0], ((0, spare_rows), (0, 0)))
    fenced = after([*x_plane, *dy_z, down], hidden_near)
    x_plane, dy_z, down = fenced[:3], fenced[3:-1], fenced[-1]

    dy_piece = stack_pieces(dy_z)
    dy_plane = send_plane(dy_piece)
    x_own = join_plane(tp_index, x_piece, *x_plane, earlier=[dy_piece])
    x_other = swap_cores(x_own)
    x_far = [(x_own, 0, later), (x_other, 0, later)]
    x_groups = [x_far[0], x_near[0], x_near[1], x_far[1]]
    hidden_far, slope_far, act_far = forward_rows(x_far, w_both, 2 * tile)
    shadow_pieces = exchange_chips(shadow_kept, shadow_taken, late=[hidden_far])
    chip = ep_index // 2
    shadow_in, down = lay_out_shadow(shadow_pieces, down, shadow_part, chip, earlier=[hidden_far])
    hidden_s, slope_s, act_s = forward_rows(x_groups, shadow_in, 2 * tile, transposed=True)

    weighted, w_rows, w_shadow = weigh_hidden(
        hidden_near, hidden_far, hidden_s, shadow_pieces, 3 * shadow_part, tok_count, ep_index % 2
    )

    parts = 2 if steps % 2 == 0 else 1
    sent = output_other(weighted, down, tp_index, parts, tok_count, quarter)
    got = [swap_cores(array) for array in sent]
    dy_plane = after(dy_plane, *sent)

    dy_own = join_plane(tp_index, dy_piece, *dy_plane)
    dy_other = swap_cores(dy_own)
    dy_groups = [(dy_own, 0, later), (near_own, 1, tok_count), (near_other, 1, tok_count), (dy_other, 0, later)]
    segments = [
        (slope_far, act_far, 0),
        (slope_near, act_near, 0),
        (slope_near, act_near, tok_count),
        (slope_far, act_far, later),
    ]
    per_row = (slope_s, act_s, w_rows, w_shadow)
    pre_first, pre_s_first = backward_rows(dy_groups[:3], down, segments[:3], per_row, 0, 2 * tile)
    owns = output_own(weighted, got, down, tp_index, quarter, earlier=[pre_first])
    sums = send_plane(*owns[1:])
    first_rows = sum(g[2] for g in dy_groups[:3])
    pre_last, pre_s_last = backward_rows(
        dy_groups[3:], down, segments[3:], per_row, first_rows, 2 * tile, earlier=owns[1:]
    )
    pre, pre_s = [pre_first, pre_last], [pre_s_first, pre_s_last]
    grad_s = shadow_grads(x_groups, dy_groups, pre_s, weighted, shadow_part, tile)
    blocks = grad_s.reshape(3 * shadow_part, ep_count, block_width).transpose(1, 0, 2)
    grad_kept, grad_taken = exchange_cores(blocks)
    grad_pieces = exchange_chips(grad_kept, grad_taken)
    grad_gate, grad_up = input_grads(x_groups, pre, tile, earlier=[grad_pieces[0]])
    sums = after(sums, grad_gate)

    def slot_rows(i):
        part = slice(i * tok_count, (i + 1) * tok_count)
        total = owns[0][part]
        for array in sums:
            total = total + array[part].astype(jnp.float32)
        return total

    pieces = [slot_rows(i).astype(jnp.bfloat16) for i in range(steps - 1)]
    grad_down = down_grad(dy_groups, weighted, hidden_part, tile, earlier=[*pieces, grad_gate])
    total = slot_rows(steps - 1)
    for s in range(1, steps):
        total = total + lax.ppermute(pieces[s - 1], "ep", swap_pairs(ep_count, 2 * s)).astype(jnp.float32)
    mixed = total.astype(jnp.bfloat16)

    grads_s = lay_out_grads(grad_pieces, shadow_part, chip, earlier=[grad_down])
    return (mixed, grad_gate[None], grad_up[None], grad_down[None], *grads_s)


def shards(tokens, cotangent, expert_ids, *others):
    tp_count, ep_count = lax.axis_size("tp"), lax.axis_size("ep")
    tok_count, top_count = expert_ids.shape
    rows = (5 * tok_count * top_count) // 4
    chips = ep_count // 2
    fits = tp_count == 4 and ep_count == 2 * chips and chips & (chips - 1) == 0 and tok_count % 128 == 0
    dense = fits and ep_count * tok_count <= 3 * rows
    return (dense_shards if dense else routed_shards)(tokens, cotangent, expert_ids, *others)


def solution(mesh):
    return jax.shard_map(
        shards,
        mesh=mesh,
        in_specs=(
            P("ep", "tp"),
            P("ep", "tp"),
            P("ep", None),
            P("ep", None),
            P("ep"),
            P("ep", None, "tp"),
            P("ep", None, "tp"),
            P("ep", "tp", None),
            P("ep", "tp"),
            P("ep", "tp"),
            P("tp", "ep"),
        ),
        out_specs=(
            P("ep", "tp"),
            P("ep", None, "tp"),
            P("ep", None, "tp"),
            P("ep", "tp", None),
            P("ep", "tp"),
            P("ep", "tp"),
            P("tp", "ep"),
        ),
        check_vma=False,
    )
```

```python
import functools

import jax
import jax.numpy as jnp
from jax import lax
from jax.experimental import pallas as pl
from jax.experimental.pallas import tpu as pltpu
from jax.sharding import PartitionSpec as P


def contract_rows(left, right):
    return lax.dot_general(
        left, right, (((0,), (0,)), ((), ())), preferred_element_type=jnp.float32
    )


def split_parts(values):
    upper_part = values.astype(jnp.bfloat16)
    lower_part = (values - upper_part.astype(jnp.float32)).astype(jnp.bfloat16)
    return (upper_part, lower_part)


def weigh_rows(weight_table, rows):
    weight_upper, weight_lower = split_parts(weight_table)
    return jnp.dot(weight_upper, rows, preferred_element_type=jnp.float32) + jnp.dot(
        weight_lower, rows, preferred_element_type=jnp.float32
    )


def expert_pass(rows_x, rows_dout, weight_gate, weight_up, weight_down):
    pre_gate = jnp.dot(rows_x, weight_gate, preferred_element_type=jnp.float32)
    pre_up = jnp.dot(rows_x, weight_up, preferred_element_type=jnp.float32)
    sigmoid_gate = jax.nn.sigmoid(pre_gate)
    activated = pre_gate * sigmoid_gate
    hidden = (activated * pre_up).astype(jnp.bfloat16)
    partial_out = jnp.dot(hidden, weight_down, preferred_element_type=jnp.float32).astype(
        jnp.bfloat16
    )
    hidden_grad = lax.dot_general(
        rows_dout, weight_down, (((1,), (1,)), ((), ())), preferred_element_type=jnp.float32
    )
    grad_pre_gate = (
        hidden_grad * pre_up * sigmoid_gate * (1.0 + pre_gate * (1.0 - sigmoid_gate))
    ).astype(jnp.bfloat16)
    grad_pre_up = (hidden_grad * activated).astype(jnp.bfloat16)
    return (partial_out, hidden, grad_pre_gate, grad_pre_up)


def routed_shards(
    tokens,
    cotangent,
    expert_ids,
    gate_weights,
    shadow_mask,
    w_gate,
    w_up,
    w_down,
    s_gate,
    s_up,
    s_down,
):
    ep_count = lax.axis_size("ep")
    tok_count, top_count = expert_ids.shape
    quarter_width = tokens.shape[1]
    width = quarter_width * lax.axis_size("tp")
    expert_count = w_gate.shape[0] * ep_count
    capacity = (5 * tok_count * top_count + 4 * expert_count - 1) // (4 * expert_count)
    slot_count = expert_count * capacity
    picks_flat = expert_ids.reshape(-1)
    onehot = (picks_flat[:, None] == jnp.arange(expert_count, dtype=jnp.int32)[None, :]).astype(
        jnp.int32
    )
    slot_rank = jnp.sum((jnp.cumsum(onehot, axis=0) - onehot) * onehot, axis=1)
    slot_index = (picks_flat * capacity + slot_rank).reshape(tok_count, top_count)
    matches = jnp.arange(slot_count, dtype=jnp.int32)[:, None, None] == slot_index[None, :, :]
    dispatch = jnp.any(matches, axis=2).astype(jnp.bfloat16)
    weighting = jnp.sum(jnp.where(matches, gate_weights[None, :, :top_count], 0.0), axis=2)
    slot_gate = jnp.sum(weighting, axis=1)
    shadow_weight = gate_weights[:, top_count] * shadow_mask.astype(jnp.float32)
    x_full, dy_full = (
        lax.all_gather(tokens, "tp", axis=1, tiled=True),
        lax.all_gather(cotangent, "tp", axis=1, tiled=True),
    )
    rows_x = jnp.dot(dispatch, tokens, preferred_element_type=jnp.float32).astype(jnp.bfloat16)
    rows_dy = jnp.dot(dispatch, cotangent, preferred_element_type=jnp.float32)
    rows_dout = (slot_gate[:, None] * rows_dy).astype(jnp.bfloat16)
    recv_x, recv_dout = (
        lax.all_to_all(
            rows_x.reshape(ep_count, -1, quarter_width),
            "ep",
            split_axis=0,
            concat_axis=0,
            tiled=True,
        ),
        lax.all_to_all(
            rows_dout.reshape(ep_count, -1, quarter_width),
            "ep",
            split_axis=0,
            concat_axis=0,
            tiled=True,
        ),
    )
    expert_x, expert_dout = (
        lax.all_gather(recv_x.reshape(-1, quarter_width), "tp", axis=1, tiled=True),
        lax.all_gather(recv_dout.reshape(-1, quarter_width), "tp", axis=1, tiled=True),
    )
    partial_out, hidden, grad_pre_gate, grad_pre_up = expert_pass(
        expert_x, expert_dout, w_gate[0], w_up[0], w_down[0]
    )
    grad_gate = contract_rows(expert_x, grad_pre_gate).astype(jnp.bfloat16)[None]
    grad_up = contract_rows(expert_x, grad_pre_up).astype(jnp.bfloat16)[None]
    grad_down = contract_rows(hidden, expert_dout).astype(jnp.bfloat16)[None]
    full_gate, full_up, full_down = (
        lax.all_gather(s_gate, "ep", axis=0, tiled=True),
        lax.all_gather(s_up, "ep", axis=0, tiled=True),
        lax.all_gather(s_down, "ep", axis=1, tiled=True),
    )
    shadow_dout = (shadow_weight[:, None] * dy_full.astype(jnp.float32)).astype(jnp.bfloat16)
    shadow_out, shadow_hidden, shadow_gate_pre, shadow_up_pre = expert_pass(
        x_full, shadow_dout, full_gate, full_up, full_down
    )
    shadow_sums = lax.psum_scatter(
        jnp.concatenate(
            [
                contract_rows(x_full, shadow_gate_pre),
                contract_rows(x_full, shadow_up_pre),
                contract_rows(shadow_dout, shadow_hidden),
            ],
            axis=1,
        ).astype(jnp.bfloat16),
        "ep",
        scatter_dimension=0,
        tiled=True,
    ).astype(jnp.float32)
    hidden_part = s_gate.shape[1]
    grad_s_gate = shadow_sums[:, :hidden_part].astype(jnp.bfloat16)
    grad_s_up = shadow_sums[:, hidden_part : 2 * hidden_part].astype(jnp.bfloat16)
    grad_s_down = shadow_sums[:, 2 * hidden_part :].T.astype(jnp.bfloat16)
    back_rows = lax.all_to_all(
        partial_out.reshape(ep_count, -1, width), "ep", split_axis=0, concat_axis=0, tiled=True
    ).reshape(-1, width)
    term = weigh_rows(weighting.T, back_rows)
    term = term + shadow_weight[:, None] * shadow_out.astype(jnp.float32)
    mixed = lax.psum_scatter(term.astype(jnp.bfloat16), "tp", scatter_dimension=1, tiled=True)
    return (mixed, grad_gate, grad_up, grad_down, grad_s_gate, grad_s_up, grad_s_down)


ANY = pl.BlockSpec(memory_space=pl.ANY)
VMEM_LIMIT = 60 * 1024 * 1024
SHORT = pl.CostEstimate(flops=1, bytes_accessed=1, transcendentals=0)


def swap_pairs(count, bit):
    return [(i, i ^ bit) for i in range(count)]


def dot32(left, right):
    return jnp.dot(left, right, preferred_element_type=jnp.float32)


def contract_last(left, right):
    return lax.dot_general(
        left, right, (((1,), (1,)), ((), ())), preferred_element_type=jnp.float32
    )


def shape_of(*dims, dtype=jnp.bfloat16):
    return jax.ShapeDtypeStruct(dims, dtype)


def after(arrays, *earlier):
    def nothing(*refs):
        del refs

    count = len(arrays)
    return pl.pallas_call(
        nothing,
        out_shape=[jax.ShapeDtypeStruct(a.shape, a.dtype) for a in arrays],
        in_specs=[ANY] * (count + len(earlier)),
        out_specs=[ANY] * count,
        input_output_aliases={i: i for i in range(count)},
        compiler_params=pltpu.CompilerParams(vmem_limit_bytes=VMEM_LIMIT),
        cost_estimate=SHORT,
        name="after",
    )(*arrays, *earlier)


def kernel_call(body, grid, in_specs, out_specs, out_shape, operands, scratch, name, column=None, earlier=()):
    count = len(operands)

    def run(column_ref, *refs):
        del column_ref
        body(*refs[:count], *refs[count + len(earlier) :])

    column = jnp.zeros((1,), jnp.int32) if column is None else column.reshape(1).astype(jnp.int32)
    return pl.pallas_call(
        run,
        out_shape=out_shape,
        grid_spec=pltpu.PrefetchScalarGridSpec(
            num_scalar_prefetch=1,
            grid=grid,
            in_specs=list(in_specs) + [ANY] * len(earlier),
            out_specs=out_specs,
            scratch_shapes=scratch,
        ),
        compiler_params=pltpu.CompilerParams(vmem_limit_bytes=VMEM_LIMIT),
        cost_estimate=SHORT,
        name=name,
    )(column, *operands, *earlier)


def whole(array):
    return pl.BlockSpec(array.shape, lambda *_: (0,) * len(array.shape))


def join_plane(column, *pieces, earlier=()):
    rows, quarter = pieces[0].shape
    count = len(pieces)
    chunk = rows // 4

    def body(*refs):
        column_ref, sources, out = refs[0], refs[1 : 1 + count], refs[-1]
        for own_column in range(count):

            @pl.when(column_ref[0] == own_column)
            def _():
                for bit, source in enumerate(sources):
                    place = own_column ^ bit
                    out[:, place * quarter : (place + 1) * quarter] = source[...]

    return pl.pallas_call(
        body,
        out_shape=shape_of(rows, count * quarter),
        grid_spec=pltpu.PrefetchScalarGridSpec(
            num_scalar_prefetch=1,
            grid=(4,),
            in_specs=[pl.BlockSpec((chunk, quarter), lambda i, *_: (i, 0))] * count + [ANY] * len(earlier),
            out_specs=pl.BlockSpec((chunk, count * quarter), lambda i, *_: (i, 0)),
        ),
        compiler_params=pltpu.CompilerParams(vmem_limit_bytes=VMEM_LIMIT),
        cost_estimate=SHORT,
        name="join_plane",
    )(column.reshape(1).astype(jnp.int32), *pieces, *earlier)


def stack_pieces(pieces, earlier=()):
    rows, columns = pieces[0].shape
    count = len(pieces)

    def body(*refs):
        for i, ref in enumerate(refs[:count]):

            @pl.when(pl.program_id(0) == i)
            def _():
                refs[-1][...] = ref[...]

    return pl.pallas_call(
        body,
        out_shape=shape_of(count * rows, columns),
        grid=(count,),
        in_specs=[pl.BlockSpec((rows, columns), lambda i: (0, 0))] * count + [ANY] * len(earlier),
        out_specs=pl.BlockSpec((rows, columns), lambda i: (i, 0)),
        compiler_params=pltpu.CompilerParams(vmem_limit_bytes=VMEM_LIMIT),
        cost_estimate=SHORT,
        name="stack_pieces",
    )(*pieces, *earlier)


def on_piece(chip_ref, refs, use):
    step = pl.program_id(0)
    shift = chip_ref[0] ^ (step // 2)
    for i, ref in enumerate(refs):
        for core in range(2):

            @pl.when((shift == i) & (lax.rem(step, 2) == core))
            def _(ref=ref, core=core):
                use(ref.at[0, core])


def lay_out_shadow(pieces, down, units, chip, earlier=()):
    count = len(pieces)
    ep_count = 2 * count
    block_width = pieces[0].shape[3]
    apart = units + -units % 128
    all_units, width = down.shape

    def body(chip_ref, *refs):
        shadow_ref, out = refs[-2:]

        def use(ref):
            shadow_ref[...] = jnp.zeros_like(shadow_ref)
            shadow_ref[:units, :] = ref[:units, :]
            shadow_ref[apart : apart + units, :] = ref[units : 2 * units, :]
            out[units:, :] = jnp.zeros((apart - units, block_width), jnp.bfloat16)
            out[:units, :] = ref[2 * units : 3 * units, :]

        on_piece(chip_ref, refs[:count], use)

    return pl.pallas_call(
        body,
        out_shape=[shape_of(2 * apart, width), shape_of(all_units, width)],
        grid_spec=pltpu.PrefetchScalarGridSpec(
            num_scalar_prefetch=1,
            grid=(ep_count,),
            in_specs=[whole(p) for p in pieces] + [ANY] * (1 + len(earlier)),
            out_specs=[
                pl.BlockSpec((2 * apart, block_width), lambda e, *_: (0, e)),
                pl.BlockSpec((apart, block_width), lambda e, *_: (all_units // apart - 1, e)),
            ],
        ),
        input_output_aliases={1 + count: 1},
        compiler_params=pltpu.CompilerParams(vmem_limit_bytes=VMEM_LIMIT),
        cost_estimate=SHORT,
        name="lay_out_shadow",
    )(chip.reshape(1).astype(jnp.int32), *pieces, down, *earlier)


def lay_out_grads(pieces, units, chip, earlier=()):
    count = len(pieces)
    ep_count = 2 * count
    block_width = pieces[0].shape[3]
    hidden = ep_count * units

    def body(chip_ref, *refs):
        gate_ref, up_ref, down_ref, gate_t, up_t = refs[-5:]
        place = pl.ds(pl.multiple_of(pl.program_id(0) * units, 16), units)

        def use(ref):
            gate_t[place, :] = ref[:units, :]
            up_t[place, :] = ref[units : 2 * units, :]
            down_ref[place, :] = ref[2 * units :, :]

        on_piece(chip_ref, refs[:count], use)

        @pl.when(pl.program_id(0) == ep_count - 1)
        def _():
            gate_ref[...] = gate_t[...].T
            up_ref[...] = up_t[...].T

    return pl.pallas_call(
        body,
        out_shape=[shape_of(block_width, hidden), shape_of(block_width, hidden), shape_of(hidden, block_width)],
        grid_spec=pltpu.PrefetchScalarGridSpec(
            num_scalar_prefetch=1,
            grid=(ep_count,),
            in_specs=[whole(p) for p in pieces] + [ANY] * len(earlier),
            out_specs=[pl.BlockSpec((block_width, hidden), lambda *_: (0, 0))] * 2
            + [pl.BlockSpec((hidden, block_width), lambda *_: (0, 0))],
            scratch_shapes=[pltpu.VMEM((hidden, block_width), jnp.bfloat16)] * 2,
        ),
        compiler_params=pltpu.CompilerParams(vmem_limit_bytes=VMEM_LIMIT),
        cost_estimate=SHORT,
        name="lay_out_grads",
    )(chip.reshape(1).astype(jnp.int32), *pieces, *earlier)


def row_specs(groups, tile):
    def spec(index, rows):
        return pl.BlockSpec((rows, tile), lambda k, *_: (index, k))

    return [spec(index, rows) for _, index, rows in groups]


def apply_gate(pre_gate, pre_up):
    sigmoid_gate = jax.nn.sigmoid(pre_gate)
    activated = pre_gate * sigmoid_gate
    hidden = (activated * pre_up).astype(jnp.bfloat16)
    return hidden, pre_up * sigmoid_gate * (1.0 + pre_gate * (1.0 - sigmoid_gate)), activated


def clear_first(acc):
    @pl.when(pl.program_id(0) == 0)
    def _():
        acc[...] = jnp.zeros_like(acc)


def rows_operand(refs, groups, held):
    if len(groups) == 1:
        return refs[0][...]
    return stage_rows(refs, groups, held)


def forward_rows(groups, w_both, tile, transposed=False, earlier=()):
    rows = sum(g[2] for g in groups)
    if transposed:
        units, width = w_both.shape[0] // 2, w_both.shape[1]
        tile_spec = pl.BlockSpec((2 * units, tile), lambda k, *_: (0, k))
    else:
        width, units = w_both.shape[0], w_both.shape[1] // 2
        tile_spec = pl.BlockSpec((tile, 2 * units), lambda k, *_: (k, 0))
    steps = width // tile

    def body(*refs):
        n = len(groups)
        both_ref, hidden_ref, slope_ref, act_ref, acc, held = refs[n:]
        clear_first(acc)
        operand = rows_operand(refs[:n], groups, held)
        acc[...] += contract_last(operand, both_ref[...]) if transposed else dot32(operand, both_ref[...])

        @pl.when(pl.program_id(0) == steps - 1)
        def _():
            chunk = 128

            @pl.loop(0, rows // chunk)
            def _(i):
                part = pl.ds(pl.multiple_of(i * chunk, chunk), chunk)
                hidden, slope, act = apply_gate(acc[part, :units], acc[part, units:])
                hidden_ref[part, :] = hidden
                slope_ref[part, :] = slope.astype(jnp.bfloat16)
                act_ref[part, :] = act.astype(jnp.bfloat16)

    out_spec = pl.BlockSpec((rows, units), lambda *_: (0, 0))
    return kernel_call(
        body,
        (steps,),
        row_specs(groups, tile) + [tile_spec],
        [out_spec] * 3,
        [shape_of(rows, units)] * 3,
        [g[0] for g in groups] + [w_both],
        [pltpu.VMEM((rows, 2 * units), jnp.float32), pltpu.VMEM((rows, tile), jnp.bfloat16)],
        "forward_rows",
        earlier=earlier,
    )


def weigh_hidden(hidden_near, hidden_far, hidden_s, pieces, first_row, slot_rows, core, earlier=()):
    count = len(pieces)
    rows, units_s = hidden_s.shape
    units = hidden_near.shape[1]
    slots = [(s, 0) for s in list(range(1, count)) + [0]] + [(s, 1) for s in range(count)]

    def body(core_ref, *refs):
        near_ref, far_ref, s_ref, *piece_refs = refs[: 3 + count]
        out, w_ref, w_s_ref = refs[-3:]
        near, far = 0, 0
        for i, (slot, other) in enumerate(slots):
            part = pl.ds(i * slot_rows, slot_rows)
            table = piece_refs[slot][0, core_ref[0] ^ other, first_row : first_row + 16, :][:1].astype(jnp.float32)

            def column(j):
                both = table[:, j * slot_rows : (j + 1) * slot_rows]
                both = both + table[:, (j + 2) * slot_rows : (j + 3) * slot_rows]
                return jnp.broadcast_to(both, (slot_rows, slot_rows)).T[:, :1]

            weight, weight_s = column(0), column(1)
            w_ref[part, :] = weight
            w_s_ref[part, :] = weight_s
            if slot == 0:
                hidden = near_ref[near : near + slot_rows, :]
                near += slot_rows
            else:
                hidden = far_ref[far : far + slot_rows, :]
                far += slot_rows
            out[part, :units] = (hidden.astype(jnp.float32) * weight).astype(jnp.bfloat16)
            out[part, units:] = (s_ref[part, :].astype(jnp.float32) * weight_s).astype(jnp.bfloat16)

    return pl.pallas_call(
        body,
        out_shape=[
            shape_of(rows, units + units_s),
            shape_of(rows, 1, dtype=jnp.float32),
            shape_of(rows, 1, dtype=jnp.float32),
        ],
        grid_spec=pltpu.PrefetchScalarGridSpec(
            num_scalar_prefetch=1,
            grid=(1,),
            in_specs=[whole(a) for a in (hidden_near, hidden_far, hidden_s, *pieces)] + [ANY] * len(earlier),
            out_specs=[
                pl.BlockSpec((rows, units + units_s), lambda *_: (0, 0)),
                pl.BlockSpec((rows, 1), lambda *_: (0, 0)),
                pl.BlockSpec((rows, 1), lambda *_: (0, 0)),
            ],
        ),
        compiler_params=pltpu.CompilerParams(vmem_limit_bytes=VMEM_LIMIT),
        cost_estimate=SHORT,
        name="weigh_hidden",
    )(core.reshape(1).astype(jnp.int32), hidden_near, hidden_far, hidden_s, *pieces, *earlier)


def output_other(weighted, down, column, parts, slot_rows, quarter, earlier=()):
    rows, units = weighted.shape
    count = rows // 2 // parts

    def body(weighted_ref, down_ref, *outs):
        for i, out in enumerate(outs):
            first, last = slot_rows + i * count, slot_rows + (i + 1) * count
            kept = min(last, rows // 2) - first
            value = dot32(weighted_ref[first : first + kept, :], down_ref[...])
            out[:kept, :] = value.astype(jnp.bfloat16)
            if kept < count:
                value = dot32(weighted_ref[: count - kept, :], down_ref[...])
                out[kept:, :] = value.astype(jnp.bfloat16)

    return kernel_call(
        body,
        (4,),
        [
            pl.BlockSpec((rows // 2, units), lambda *_: (1, 0)),
            pl.BlockSpec((units, quarter), lambda q, column_ref: (0, column_ref[0] ^ q)),
        ],
        [pl.BlockSpec((count, quarter), lambda q, *_: (0, q))] * parts,
        [shape_of(count, 4 * quarter)] * parts,
        [weighted, down],
        [],
        "output_other",
        column=column,
        earlier=earlier,
    )


def output_own(weighted, got, down, column, quarter, earlier=()):
    count, units = got[0].shape[0], weighted.shape[1]
    parts = len(got)

    def body(weighted_ref, down_ref, *refs):
        for i in range(parts):
            value = dot32(weighted_ref[i * count : (i + 1) * count, :], down_ref[...])
            value = value + refs[i][...].astype(jnp.float32)
            for j, out in enumerate(refs[parts + 4 * i : parts + 4 * i + 4]):

                @pl.when(pl.program_id(0) == 3 - j)
                def _(out=out, value=value):
                    out[...] = value.astype(out.dtype)

    full = pl.BlockSpec((count, quarter), lambda *_: (0, 0))
    out = kernel_call(
        body,
        (4,),
        [
            pl.BlockSpec((parts * count, units), lambda *_: (0, 0)),
            pl.BlockSpec((units, quarter), lambda q, column_ref: (0, column_ref[0] ^ 3 ^ q)),
        ]
        + [pl.BlockSpec((count, quarter), lambda q, *_: (0, 3 - q))] * parts,
        [full] * (4 * parts),
        ([shape_of(count, quarter, dtype=jnp.float32)] + [shape_of(count, quarter)] * 3) * parts,
        [weighted, down] + list(got),
        [],
        "output_own",
        column=column,
        earlier=earlier,
    )
    return [out[4 * i : 4 * i + 4] for i in range(parts)]


def backward_rows(groups, down, parts, per_row, first_row, tile, earlier=()):
    slope_s, act_s, w_rows, w_shadow = per_row
    rows = sum(g[2] for g in groups)
    units_all, width = down.shape
    units_s = slope_s.shape[1]
    units = units_all - units_s
    steps = width // tile
    arrays = list({id(a): a for part in parts for a in part[:2]}.values())
    places = [[next(i for i, a in enumerate(arrays) if a is b) for b in part[:2]] for part in parts]

    def body(*refs):
        n, m = len(groups), len(arrays)
        down_ref = refs[n]
        array_refs = refs[n + 1 : n + 1 + m]
        slope_s_ref, act_s_ref, w_ref, w_s_ref, pre_ref, pre_s_ref, acc, held = refs[n + 1 + m :]
        clear_first(acc)
        acc[...] += contract_last(rows_operand(refs[:n], groups, held), down_ref[...])

        @pl.when(pl.program_id(0) == steps - 1)
        def _():
            chunk = 128
            start = 0
            for (_, _, count), (_, _, first), (slope_at, act_at) in zip(groups, parts, places):

                @pl.loop(0, count // chunk)
                def _(i, start=start, first=first, slope_ref=array_refs[slope_at], act_ref=array_refs[act_at]):
                    source = pl.ds(pl.multiple_of(first + i * chunk, chunk), chunk)
                    part = pl.ds(pl.multiple_of(start + i * chunk, chunk), chunk)
                    whole_part = pl.ds(pl.multiple_of(first_row + start + i * chunk, chunk), chunk)
                    grad = acc[part, :units] * w_ref[whole_part, :]
                    pre_ref[part, :units] = (grad * slope_ref[source, :]).astype(jnp.bfloat16)
                    pre_ref[part, units:] = (grad * act_ref[source, :]).astype(jnp.bfloat16)
                    grad = acc[part, units:] * w_s_ref[whole_part, :]
                    pre_s_ref[part, :units_s] = (grad * slope_s_ref[whole_part, :]).astype(jnp.bfloat16)
                    pre_s_ref[part, units_s:] = (grad * act_s_ref[whole_part, :]).astype(jnp.bfloat16)

                start += count

    extra = arrays + [slope_s, act_s, w_rows, w_shadow]
    return kernel_call(
        body,
        (steps,),
        row_specs(groups, tile) + [pl.BlockSpec((units_all, tile), lambda k, *_: (0, k))] + [whole(a) for a in extra],
        [pl.BlockSpec((rows, 2 * units), lambda *_: (0, 0)), pl.BlockSpec((rows, 2 * units_s), lambda *_: (0, 0))],
        [shape_of(rows, 2 * units), shape_of(rows, 2 * units_s)],
        [g[0] for g in groups] + [down] + extra,
        [pltpu.VMEM((rows, units_all), jnp.float32), pltpu.VMEM((rows, tile), jnp.bfloat16)],
        "backward_rows",
        earlier=earlier,
    )


def stage_rows(refs, groups, held):
    start = 0
    for ref, (_, _, count) in zip(refs, groups):
        held[pl.ds(start, count), :] = ref[...]
        start += count
    return held[...]


def shadow_grads(x_groups, dy_groups, pre_s, weighted, units, tile, earlier=()):
    rows, wide = weighted.shape[0], pre_s[0].shape[1]
    apart = wide // 2
    width = x_groups[0][0].shape[1]
    m = len(pre_s)

    def body(*refs):
        n = len(x_groups)
        pre_refs = refs[2 * n : 2 * n + m]
        hidden_ref, out, held, pre_t, hidden_t = refs[2 * n + m :]

        @pl.when(pl.program_id(0) == 0)
        def _():
            start = 0
            for ref in pre_refs:
                pre_t[:, start : start + ref.shape[0]] = ref[...].T
                start += ref.shape[0]
            hidden_t[...] = hidden_ref[...].T

        value = dot32(pre_t[...], stage_rows(refs[:n], x_groups, held))
        out[:units, :] = value[:units].astype(jnp.bfloat16)
        out[units : 2 * units, :] = value[apart : apart + units].astype(jnp.bfloat16)
        value = dot32(hidden_t[...], stage_rows(refs[n : 2 * n], dy_groups, held))
        out[2 * units :, :] = value[:units].astype(jnp.bfloat16)

    (out,) = kernel_call(
        body,
        (width // tile,),
        row_specs(x_groups, tile)
        + row_specs(dy_groups, tile)
        + [whole(p) for p in pre_s]
        + [pl.BlockSpec((rows, apart), lambda *_: (0, weighted.shape[1] // apart - 1))],
        [pl.BlockSpec((3 * units, tile), lambda k, *_: (0, k))],
        [shape_of(3 * units, width)],
        [g[0] for g in x_groups + dy_groups] + list(pre_s) + [weighted],
        [
            pltpu.VMEM((rows, tile), jnp.bfloat16),
            pltpu.VMEM((wide, rows), jnp.bfloat16),
            pltpu.VMEM((apart, rows), jnp.bfloat16),
        ],
        "shadow_grads",
        earlier=earlier,
    )
    return out


def input_grads(groups, pre, tile, earlier=()):
    both = pre[0].shape[1]
    rows = sum(p.shape[0] for p in pre)
    units = both // 2
    width = groups[0][0].shape[1]
    m = len(pre)

    def body(*refs):
        n = len(groups)
        gate_ref, up_ref, held, pre_held = refs[n + m :]

        @pl.when(pl.program_id(0) == 0)
        def _():
            start = 0
            for ref in refs[n : n + m]:
                pre_held[start : start + ref.shape[0], :] = ref[...]
                start += ref.shape[0]

        value = contract_rows(stage_rows(refs[:n], groups, held), pre_held[...])
        gate_ref[...] = value[:, :units].astype(jnp.bfloat16)
        up_ref[...] = value[:, units:].astype(jnp.bfloat16)

    return kernel_call(
        body,
        (width // tile,),
        row_specs(groups, tile) + [whole(p) for p in pre],
        [pl.BlockSpec((tile, units), lambda k, *_: (k, 0))] * 2,
        [shape_of(width, units)] * 2,
        [g[0] for g in groups] + list(pre),
        [pltpu.VMEM((rows, tile), jnp.bfloat16), pltpu.VMEM((rows, both), jnp.bfloat16)],
        "input_grads",
        earlier=earlier,
    )


def down_grad(groups, weighted, units, tile, earlier=()):
    rows = weighted.shape[0]
    width = groups[0][0].shape[1]

    def body(*refs):
        n = len(groups)
        hidden_ref, out, held, hidden_t = refs[n:]

        @pl.when(pl.program_id(0) == 0)
        def _():
            hidden_t[...] = hidden_ref[...].T

        out[...] = dot32(hidden_t[...], stage_rows(refs[:n], groups, held)).astype(jnp.bfloat16)

    (out,) = kernel_call(
        body,
        (width // tile,),
        row_specs(groups, tile) + [pl.BlockSpec((rows, units), lambda *_: (0, 0))],
        [pl.BlockSpec((units, tile), lambda k, *_: (0, k))],
        [shape_of(units, width)],
        [g[0] for g in groups] + [weighted],
        [pltpu.VMEM((rows, tile), jnp.bfloat16), pltpu.VMEM((units, rows), jnp.bfloat16)],
        "down_grad",
        earlier=earlier,
    )
    return out


def send_along_z(own):
    ep_count = lax.axis_size("ep")
    return [lax.ppermute(own, "ep", swap_pairs(ep_count, 2 * s)) for s in range(1, ep_count // 2)]


def swap_cores(block):
    return lax.ppermute(block, "ep", swap_pairs(lax.axis_size("ep"), 1))


def send_plane(*pieces):
    pieces = pieces * 3 if len(pieces) == 1 else pieces
    return [lax.ppermute(p, "tp", swap_pairs(lax.axis_size("tp"), bit)) for p, bit in zip(pieces, (1, 2, 3))]


def exchange_cores(blocks, cuts=1):
    ep_count, core = lax.axis_size("ep"), lax.axis_index("ep") % 2
    pairs = blocks.reshape(ep_count // 2, 2, *blocks.shape[1:])
    kept = jnp.where(core == 0, pairs[:, 0], pairs[:, 1])
    given = jnp.where(core == 0, pairs[:, 1], pairs[:, 0])
    return kept, [swap_cores(part) for part in jnp.split(given, cuts)]


def chip_pieces(kept, taken):
    ep_count, me = lax.axis_size("ep"), lax.axis_index("ep")
    chips, chip, core = ep_count // 2, me // 2, me % 2
    taken = jnp.concatenate(taken, axis=0)
    both = jnp.stack([jnp.where(core == 0, kept, taken), jnp.where(core == 0, taken, kept)], axis=1)
    return [lax.dynamic_index_in_dim(both, chip ^ shift, 0) for shift in range(chips)]


def send_piece(piece, shift):
    return lax.ppermute(piece, "ep", swap_pairs(lax.axis_size("ep"), 2 * shift))


def dense_shards(
    tokens,
    cotangent,
    expert_ids,
    gate_weights,
    shadow_mask,
    w_gate,
    w_up,
    w_down,
    s_gate,
    s_up,
    s_down,
):
    ep_count, tp_count = lax.axis_size("ep"), lax.axis_size("tp")
    ep_index, tp_index = lax.axis_index("ep"), lax.axis_index("tp")
    tok_count, top_count = expert_ids.shape
    quarter = tokens.shape[1]
    width = quarter * tp_count
    hidden_part = w_gate.shape[2]
    shadow_part = hidden_part // ep_count
    block_width = s_gate.shape[0]
    steps = ep_count // 2
    later = (steps - 1) * tok_count
    tile = width // 8
    along, across = swap_pairs(tp_count, 1), swap_pairs(tp_count, 2)

    picked = expert_ids[None, :, :] == jnp.arange(ep_count, dtype=jnp.int32)[:, None, None]
    table = jnp.sum(jnp.where(picked, gate_weights[None, :, :top_count], 0.0), axis=2)
    shadow_weight = gate_weights[:, top_count] * shadow_mask.astype(jnp.float32)
    table = jnp.concatenate([table, jnp.broadcast_to(shadow_weight[None], table.shape)], axis=1)
    table = jnp.concatenate(split_parts(table), axis=1)
    table = jnp.pad(table[:, None, :], ((0, 0), (0, 15), (0, block_width - table.shape[1])))
    shadow_blocks = jnp.concatenate(
        [
            s_gate.T.reshape(ep_count, shadow_part, block_width),
            s_up.T.reshape(ep_count, shadow_part, block_width),
            s_down.reshape(ep_count, shadow_part, block_width),
            table,
        ],
        axis=1,
    )

    x_z = send_along_z(tokens)
    near = stack_pieces([tokens, cotangent])
    near_x, near_y = send_plane(near, near)
    near_late = stack_pieces([tokens, cotangent], earlier=[x_z[0]])
    near_d = lax.ppermute(near_late, "tp", swap_pairs(tp_count, 3))
    w_both = jnp.concatenate([w_gate[0], w_up[0]], axis=1)
    near_x, near_y, near_d, *x_z = after([near_x, near_y, near_d, *x_z], w_both, shadow_blocks)

    x_piece = stack_pieces(x_z)
    x_plane = send_plane(x_piece)
    dy_z = send_along_z(cotangent)
    near_own = join_plane(tp_index, near, near_x, near_y, near_d)
    near_other = swap_cores(near_own)
    x_near = [(near_own, 0, tok_count), (near_other, 0, tok_count)]
    hidden_near, slope_near, act_near = forward_rows(x_near, w_both, 2 * tile)
    spare_rows = -shadow_part % 128 + shadow_part
    down = jnp.pad(w_down[0], ((0, spare_rows), (0, 0)))
    (shadow_blocks,) = after([shadow_blocks], x_z[0])
    shadow_kept, shadow_taken = exchange_cores(shadow_blocks)
    fenced = after([*x_plane, down, *shadow_taken, *dy_z], hidden_near)
    x_plane, down, shadow_taken, dy_z = fenced[:3], fenced[3], fenced[4:5], fenced[5:]

    dy_piece = stack_pieces(dy_z)
    dy_plane = send_plane(dy_piece)
    shadow_pieces = chip_pieces(shadow_kept, shadow_taken)
    for shift in range(1, steps - 1):
        shadow_pieces[shift] = send_piece(shadow_pieces[shift], shift)
    x_own = join_plane(tp_index, x_piece, *x_plane, earlier=[dy_piece])
    x_other = swap_cores(x_own)
    x_far = [(x_own, 0, later), (x_other, 0, later)]
    x_groups = [x_far[0], x_near[0], x_near[1], x_far[1]]
    hidden_far, slope_far, act_far = forward_rows(x_far, w_both, 2 * tile)
    shadow_pieces[-1:] = after(shadow_pieces[-1:], hidden_far)
    shadow_pieces[-1] = send_piece(shadow_pieces[-1], steps - 1)
    chip = ep_index // 2
    shadow_in, down = lay_out_shadow(shadow_pieces, down, shadow_part, chip, earlier=[hidden_far])
    hidden_s, slope_s, act_s = forward_rows(x_groups, shadow_in, 2 * tile, transposed=True)

    weighted, w_rows, w_shadow = weigh_hidden(
        hidden_near, hidden_far, hidden_s, shadow_pieces, 3 * shadow_part, tok_count, ep_index % 2
    )

    parts = 2 if steps % 2 == 0 else 1
    sent = output_other(weighted, down, tp_index, parts, tok_count, quarter)
    got = [swap_cores(array) for array in sent]
    dy_plane = after(dy_plane, *sent)

    dy_own = join_plane(tp_index, dy_piece, *dy_plane)
    dy_other = swap_cores(dy_own)
    dy_groups = [(dy_own, 0, later), (near_own, 1, tok_count), (near_other, 1, tok_count), (dy_other, 0, later)]
    segments = [
        (slope_far, act_far, 0),
        (slope_near, act_near, 0),
        (slope_near, act_near, tok_count),
        (slope_far, act_far, later),
    ]
    per_row = (slope_s, act_s, w_rows, w_shadow)
    pre_first, pre_s_first = backward_rows(dy_groups[:3], down, segments[:3], per_row, 0, 2 * tile)
    owns = output_own(weighted, got, down, tp_index, quarter, earlier=[pre_first])
    sums = [send_plane(*own[1:]) for own in owns]
    first_rows = sum(g[2] for g in dy_groups[:3])
    pre_last, pre_s_last = backward_rows(
        dy_groups[3:], down, segments[3:], per_row, first_rows, 2 * tile, earlier=[own[1] for own in owns]
    )
    pre, pre_s = [pre_first, pre_last], [pre_s_first, pre_s_last]
    grad_s = shadow_grads(x_groups, dy_groups, pre_s, weighted, shadow_part, tile)
    blocks = grad_s.reshape(3 * shadow_part, ep_count, block_width).transpose(1, 0, 2)
    grad_pieces = chip_pieces(*exchange_cores(blocks))

    def slot_rows(i):
        part = slice(i % (steps // parts) * tok_count, (i % (steps // parts) + 1) * tok_count)
        total = owns[i * parts // steps][0][part]
        for array in sums[i * parts // steps]:
            total = total + array[part].astype(jnp.float32)
        return total

    def send_rows(piece, i):
        return lax.ppermute(piece, "ep", swap_pairs(ep_count, 2 * (i + 1)))

    early = steps // parts if parts > 1 else 0
    sums[0] = after(sums[0], grad_s)
    rows = [slot_rows(i).astype(jnp.bfloat16) for i in range(early)]
    grad_down = down_grad(dy_groups, weighted, hidden_part, tile, earlier=[*rows, grad_pieces[0]])
    rows = [send_rows(piece, i) for i, piece in enumerate(rows)]
    fenced = after([*rows, *grad_pieces[1:]], grad_down)
    rows, grad_pieces[1:] = list(fenced[:early]), fenced[early:]
    grad_gate, grad_up = input_grads(x_groups, pre, tile, earlier=[grad_pieces[1]])
    for shift in range(1, steps - 1):
        grad_pieces[shift] = send_piece(grad_pieces[shift], shift)
    fenced = after([*sums[-1], *grad_pieces[1:]], grad_gate)
    sums[-1], grad_pieces[1:] = fenced[:3], fenced[3:]
    grad_pieces[-1] = send_piece(grad_pieces[-1], steps - 1)
    rows += [send_rows(slot_rows(i).astype(jnp.bfloat16), i) for i in range(early, steps - 1)]
    total = slot_rows(steps - 1)
    for piece in rows:
        total = total + piece.astype(jnp.float32)
    mixed = total.astype(jnp.bfloat16)

    grads_s = lay_out_grads(grad_pieces, shadow_part, chip)
    return (mixed, grad_gate[None], grad_up[None], grad_down[None], *grads_s)


def shards(tokens, cotangent, expert_ids, *others):
    tp_count, ep_count = lax.axis_size("tp"), lax.axis_size("ep")
    tok_count, top_count = expert_ids.shape
    rows = (5 * tok_count * top_count) // 4
    chips = ep_count // 2
    fits = tp_count == 4 and ep_count == 2 * chips and chips & (chips - 1) == 0 and tok_count % 128 == 0
    dense = fits and ep_count * tok_count <= 3 * rows
    return (dense_shards if dense else routed_shards)(tokens, cotangent, expert_ids, *others)


def solution(mesh):
    return jax.shard_map(
        shards,
        mesh=mesh,
        in_specs=(
            P("ep", "tp"),
            P("ep", "tp"),
            P("ep", None),
            P("ep", None),
            P("ep"),
            P("ep", None, "tp"),
            P("ep", None, "tp"),
            P("ep", "tp", None),
            P("ep", "tp"),
            P("ep", "tp"),
            P("tp", "ep"),
        ),
        out_specs=(
            P("ep", "tp"),
            P("ep", None, "tp"),
            P("ep", None, "tp"),
            P("ep", "tp", None),
            P("ep", "tp"),
            P("ep", "tp"),
            P("tp", "ep"),
        ),
        check_vma=False,
    )
```

```python
import functools

import jax
import jax.numpy as jnp
from jax import lax
from jax.experimental import pallas as pl
from jax.experimental.pallas import tpu as pltpu
from jax.sharding import PartitionSpec as P


def contract_rows(left, right):
    return lax.dot_general(
        left, right, (((0,), (0,)), ((), ())), preferred_element_type=jnp.float32
    )


def split_parts(values):
    upper_part = values.astype(jnp.bfloat16)
    lower_part = (values - upper_part.astype(jnp.float32)).astype(jnp.bfloat16)
    return (upper_part, lower_part)


def weigh_rows(weight_table, rows):
    weight_upper, weight_lower = split_parts(weight_table)
    return jnp.dot(weight_upper, rows, preferred_element_type=jnp.float32) + jnp.dot(
        weight_lower, rows, preferred_element_type=jnp.float32
    )


def expert_pass(rows_x, rows_dout, weight_gate, weight_up, weight_down):
    pre_gate = jnp.dot(rows_x, weight_gate, preferred_element_type=jnp.float32)
    pre_up = jnp.dot(rows_x, weight_up, preferred_element_type=jnp.float32)
    sigmoid_gate = jax.nn.sigmoid(pre_gate)
    activated = pre_gate * sigmoid_gate
    hidden = (activated * pre_up).astype(jnp.bfloat16)
    partial_out = jnp.dot(hidden, weight_down, preferred_element_type=jnp.float32).astype(
        jnp.bfloat16
    )
    hidden_grad = lax.dot_general(
        rows_dout, weight_down, (((1,), (1,)), ((), ())), preferred_element_type=jnp.float32
    )
    grad_pre_gate = (
        hidden_grad * pre_up * sigmoid_gate * (1.0 + pre_gate * (1.0 - sigmoid_gate))
    ).astype(jnp.bfloat16)
    grad_pre_up = (hidden_grad * activated).astype(jnp.bfloat16)
    return (partial_out, hidden, grad_pre_gate, grad_pre_up)


def routed_shards(
    tokens,
    cotangent,
    expert_ids,
    gate_weights,
    shadow_mask,
    w_gate,
    w_up,
    w_down,
    s_gate,
    s_up,
    s_down,
):
    ep_count = lax.axis_size("ep")
    tok_count, top_count = expert_ids.shape
    quarter_width = tokens.shape[1]
    width = quarter_width * lax.axis_size("tp")
    expert_count = w_gate.shape[0] * ep_count
    capacity = (5 * tok_count * top_count + 4 * expert_count - 1) // (4 * expert_count)
    slot_count = expert_count * capacity
    picks_flat = expert_ids.reshape(-1)
    onehot = (picks_flat[:, None] == jnp.arange(expert_count, dtype=jnp.int32)[None, :]).astype(
        jnp.int32
    )
    slot_rank = jnp.sum((jnp.cumsum(onehot, axis=0) - onehot) * onehot, axis=1)
    slot_index = (picks_flat * capacity + slot_rank).reshape(tok_count, top_count)
    matches = jnp.arange(slot_count, dtype=jnp.int32)[:, None, None] == slot_index[None, :, :]
    dispatch = jnp.any(matches, axis=2).astype(jnp.bfloat16)
    weighting = jnp.sum(jnp.where(matches, gate_weights[None, :, :top_count], 0.0), axis=2)
    slot_gate = jnp.sum(weighting, axis=1)
    shadow_weight = gate_weights[:, top_count] * shadow_mask.astype(jnp.float32)
    x_full, dy_full = (
        lax.all_gather(tokens, "tp", axis=1, tiled=True),
        lax.all_gather(cotangent, "tp", axis=1, tiled=True),
    )
    rows_x = jnp.dot(dispatch, tokens, preferred_element_type=jnp.float32).astype(jnp.bfloat16)
    rows_dy = jnp.dot(dispatch, cotangent, preferred_element_type=jnp.float32)
    rows_dout = (slot_gate[:, None] * rows_dy).astype(jnp.bfloat16)
    recv_x, recv_dout = (
        lax.all_to_all(
            rows_x.reshape(ep_count, -1, quarter_width),
            "ep",
            split_axis=0,
            concat_axis=0,
            tiled=True,
        ),
        lax.all_to_all(
            rows_dout.reshape(ep_count, -1, quarter_width),
            "ep",
            split_axis=0,
            concat_axis=0,
            tiled=True,
        ),
    )
    expert_x, expert_dout = (
        lax.all_gather(recv_x.reshape(-1, quarter_width), "tp", axis=1, tiled=True),
        lax.all_gather(recv_dout.reshape(-1, quarter_width), "tp", axis=1, tiled=True),
    )
    partial_out, hidden, grad_pre_gate, grad_pre_up = expert_pass(
        expert_x, expert_dout, w_gate[0], w_up[0], w_down[0]
    )
    grad_gate = contract_rows(expert_x, grad_pre_gate).astype(jnp.bfloat16)[None]
    grad_up = contract_rows(expert_x, grad_pre_up).astype(jnp.bfloat16)[None]
    grad_down = contract_rows(hidden, expert_dout).astype(jnp.bfloat16)[None]
    full_gate, full_up, full_down = (
        lax.all_gather(s_gate, "ep", axis=0, tiled=True),
        lax.all_gather(s_up, "ep", axis=0, tiled=True),
        lax.all_gather(s_down, "ep", axis=1, tiled=True),
    )
    shadow_dout = (shadow_weight[:, None] * dy_full.astype(jnp.float32)).astype(jnp.bfloat16)
    shadow_out, shadow_hidden, shadow_gate_pre, shadow_up_pre = expert_pass(
        x_full, shadow_dout, full_gate, full_up, full_down
    )
    shadow_sums = lax.psum_scatter(
        jnp.concatenate(
            [
                contract_rows(x_full, shadow_gate_pre),
                contract_rows(x_full, shadow_up_pre),
                contract_rows(shadow_dout, shadow_hidden),
            ],
            axis=1,
        ).astype(jnp.bfloat16),
        "ep",
        scatter_dimension=0,
        tiled=True,
    ).astype(jnp.float32)
    hidden_part = s_gate.shape[1]
    grad_s_gate = shadow_sums[:, :hidden_part].astype(jnp.bfloat16)
    grad_s_up = shadow_sums[:, hidden_part : 2 * hidden_part].astype(jnp.bfloat16)
    grad_s_down = shadow_sums[:, 2 * hidden_part :].T.astype(jnp.bfloat16)
    back_rows = lax.all_to_all(
        partial_out.reshape(ep_count, -1, width), "ep", split_axis=0, concat_axis=0, tiled=True
    ).reshape(-1, width)
    term = weigh_rows(weighting.T, back_rows)
    term = term + shadow_weight[:, None] * shadow_out.astype(jnp.float32)
    mixed = lax.psum_scatter(term.astype(jnp.bfloat16), "tp", scatter_dimension=1, tiled=True)
    return (mixed, grad_gate, grad_up, grad_down, grad_s_gate, grad_s_up, grad_s_down)


ANY = pl.BlockSpec(memory_space=pl.ANY)
VMEM_LIMIT = 60 * 1024 * 1024
SHORT = pl.CostEstimate(flops=1, bytes_accessed=1, transcendentals=0)


def swap_pairs(count, bit):
    return [(i, i ^ bit) for i in range(count)]


def dot32(left, right):
    return jnp.dot(left, right, preferred_element_type=jnp.float32)


def contract_last(left, right):
    return lax.dot_general(
        left, right, (((1,), (1,)), ((), ())), preferred_element_type=jnp.float32
    )


def shape_of(*dims, dtype=jnp.bfloat16):
    return jax.ShapeDtypeStruct(dims, dtype)


def after(arrays, *earlier):
    def nothing(*refs):
        del refs

    count = len(arrays)
    return pl.pallas_call(
        nothing,
        out_shape=[jax.ShapeDtypeStruct(a.shape, a.dtype) for a in arrays],
        in_specs=[ANY] * (count + len(earlier)),
        out_specs=[ANY] * count,
        input_output_aliases={i: i for i in range(count)},
        compiler_params=pltpu.CompilerParams(vmem_limit_bytes=VMEM_LIMIT),
        cost_estimate=SHORT,
        name="after",
    )(*arrays, *earlier)


def kernel_call(body, grid, in_specs, out_specs, out_shape, operands, scratch, name, column=None, earlier=()):
    count = len(operands)

    def run(column_ref, *refs):
        del column_ref
        body(*refs[:count], *refs[count + len(earlier) :])

    column = jnp.zeros((1,), jnp.int32) if column is None else column.reshape(1).astype(jnp.int32)
    return pl.pallas_call(
        run,
        out_shape=out_shape,
        grid_spec=pltpu.PrefetchScalarGridSpec(
            num_scalar_prefetch=1,
            grid=grid,
            in_specs=list(in_specs) + [ANY] * len(earlier),
            out_specs=out_specs,
            scratch_shapes=scratch,
        ),
        compiler_params=pltpu.CompilerParams(vmem_limit_bytes=VMEM_LIMIT),
        cost_estimate=SHORT,
        name=name,
    )(column, *operands, *earlier)


def whole(array):
    return pl.BlockSpec(array.shape, lambda *_: (0,) * len(array.shape))


def join_plane(column, *pieces, earlier=()):
    rows, quarter = pieces[0].shape
    count = len(pieces)
    chunk = rows // 4

    def body(*refs):
        column_ref, sources, out = refs[0], refs[1 : 1 + count], refs[-1]
        for own_column in range(count):

            @pl.when(column_ref[0] == own_column)
            def _():
                for bit, source in enumerate(sources):
                    place = own_column ^ bit
                    out[:, place * quarter : (place + 1) * quarter] = source[...]

    return pl.pallas_call(
        body,
        out_shape=shape_of(rows, count * quarter),
        grid_spec=pltpu.PrefetchScalarGridSpec(
            num_scalar_prefetch=1,
            grid=(4,),
            in_specs=[pl.BlockSpec((chunk, quarter), lambda i, *_: (i, 0))] * count + [ANY] * len(earlier),
            out_specs=pl.BlockSpec((chunk, count * quarter), lambda i, *_: (i, 0)),
        ),
        compiler_params=pltpu.CompilerParams(vmem_limit_bytes=VMEM_LIMIT),
        cost_estimate=SHORT,
        name="join_plane",
    )(column.reshape(1).astype(jnp.int32), *pieces, *earlier)


def stack_pieces(pieces, earlier=()):
    rows, columns = pieces[0].shape
    count = len(pieces)

    def body(*refs):
        for i, ref in enumerate(refs[:count]):

            @pl.when(pl.program_id(0) == i)
            def _():
                refs[-1][...] = ref[...]

    return pl.pallas_call(
        body,
        out_shape=shape_of(count * rows, columns),
        grid=(count,),
        in_specs=[pl.BlockSpec((rows, columns), lambda i: (0, 0))] * count + [ANY] * len(earlier),
        out_specs=pl.BlockSpec((rows, columns), lambda i: (i, 0)),
        compiler_params=pltpu.CompilerParams(vmem_limit_bytes=VMEM_LIMIT),
        cost_estimate=SHORT,
        name="stack_pieces",
    )(*pieces, *earlier)


def on_piece(chip_ref, refs, use):
    step = pl.program_id(0)
    shift = chip_ref[0] ^ (step // 2)
    for i, ref in enumerate(refs):
        for core in range(2):

            @pl.when((shift == i) & (lax.rem(step, 2) == core))
            def _(ref=ref, core=core):
                use(ref.at[0, core])


def lay_out_shadow(pieces, down, units, chip, earlier=()):
    count = len(pieces)
    ep_count = 2 * count
    block_width = pieces[0].shape[3]
    apart = units + -units % 128
    all_units, width = down.shape

    def body(chip_ref, *refs):
        shadow_ref, out = refs[-2:]

        def use(ref):
            shadow_ref[...] = jnp.zeros_like(shadow_ref)
            shadow_ref[:units, :] = ref[:units, :]
            shadow_ref[apart : apart + units, :] = ref[units : 2 * units, :]
            out[units:, :] = jnp.zeros((apart - units, block_width), jnp.bfloat16)
            out[:units, :] = ref[2 * units : 3 * units, :]

        on_piece(chip_ref, refs[:count], use)

    return pl.pallas_call(
        body,
        out_shape=[shape_of(2 * apart, width), shape_of(all_units, width)],
        grid_spec=pltpu.PrefetchScalarGridSpec(
            num_scalar_prefetch=1,
            grid=(ep_count,),
            in_specs=[whole(p) for p in pieces] + [ANY] * (1 + len(earlier)),
            out_specs=[
                pl.BlockSpec((2 * apart, block_width), lambda e, *_: (0, e)),
                pl.BlockSpec((apart, block_width), lambda e, *_: (all_units // apart - 1, e)),
            ],
        ),
        input_output_aliases={1 + count: 1},
        compiler_params=pltpu.CompilerParams(vmem_limit_bytes=VMEM_LIMIT),
        cost_estimate=SHORT,
        name="lay_out_shadow",
    )(chip.reshape(1).astype(jnp.int32), *pieces, down, *earlier)


def lay_out_grads(pieces, units, chip, earlier=()):
    count = len(pieces)
    ep_count = 2 * count
    block_width = pieces[0].shape[3]
    hidden = ep_count * units

    def body(chip_ref, *refs):
        gate_ref, up_ref, down_ref, gate_t, up_t = refs[-5:]
        place = pl.ds(pl.multiple_of(pl.program_id(0) * units, 16), units)

        def use(ref):
            gate_t[place, :] = ref[:units, :]
            up_t[place, :] = ref[units : 2 * units, :]
            down_ref[place, :] = ref[2 * units :, :]

        on_piece(chip_ref, refs[:count], use)

        @pl.when(pl.program_id(0) == ep_count - 1)
        def _():
            gate_ref[...] = gate_t[...].T
            up_ref[...] = up_t[...].T

    return pl.pallas_call(
        body,
        out_shape=[shape_of(block_width, hidden), shape_of(block_width, hidden), shape_of(hidden, block_width)],
        grid_spec=pltpu.PrefetchScalarGridSpec(
            num_scalar_prefetch=1,
            grid=(ep_count,),
            in_specs=[whole(p) for p in pieces] + [ANY] * len(earlier),
            out_specs=[pl.BlockSpec((block_width, hidden), lambda *_: (0, 0))] * 2
            + [pl.BlockSpec((hidden, block_width), lambda *_: (0, 0))],
            scratch_shapes=[pltpu.VMEM((hidden, block_width), jnp.bfloat16)] * 2,
        ),
        compiler_params=pltpu.CompilerParams(vmem_limit_bytes=VMEM_LIMIT),
        cost_estimate=SHORT,
        name="lay_out_grads",
    )(chip.reshape(1).astype(jnp.int32), *pieces, *earlier)


def row_specs(groups, tile):
    def spec(index, rows):
        return pl.BlockSpec((rows, tile), lambda k, *_: (index, k))

    return [spec(index, rows) for _, index, rows in groups]


def apply_gate(pre_gate, pre_up):
    sigmoid_gate = jax.nn.sigmoid(pre_gate)
    activated = pre_gate * sigmoid_gate
    hidden = (activated * pre_up).astype(jnp.bfloat16)
    return hidden, pre_up * sigmoid_gate * (1.0 + pre_gate * (1.0 - sigmoid_gate)), activated


def clear_first(acc):
    @pl.when(pl.program_id(0) == 0)
    def _():
        acc[...] = jnp.zeros_like(acc)


def rows_operand(refs, groups, held):
    if len(groups) == 1:
        return refs[0][...]
    return stage_rows(refs, groups, held)


def forward_rows(groups, w_both, tile, transposed=False, earlier=()):
    rows = sum(g[2] for g in groups)
    if transposed:
        units, width = w_both.shape[0] // 2, w_both.shape[1]
        tile_spec = pl.BlockSpec((2 * units, tile), lambda k, *_: (0, k))
    else:
        width, units = w_both.shape[0], w_both.shape[1] // 2
        tile_spec = pl.BlockSpec((tile, 2 * units), lambda k, *_: (k, 0))
    steps = width // tile

    def body(*refs):
        n = len(groups)
        both_ref, hidden_ref, slope_ref, act_ref, acc, held = refs[n:]
        clear_first(acc)
        operand = rows_operand(refs[:n], groups, held)
        acc[...] += contract_last(operand, both_ref[...]) if transposed else dot32(operand, both_ref[...])

        @pl.when(pl.program_id(0) == steps - 1)
        def _():
            chunk = 128

            @pl.loop(0, rows // chunk)
            def _(i):
                part = pl.ds(pl.multiple_of(i * chunk, chunk), chunk)
                hidden, slope, act = apply_gate(acc[part, :units], acc[part, units:])
                hidden_ref[part, :] = hidden
                slope_ref[part, :] = slope.astype(jnp.bfloat16)
                act_ref[part, :] = act.astype(jnp.bfloat16)

    out_spec = pl.BlockSpec((rows, units), lambda *_: (0, 0))
    return kernel_call(
        body,
        (steps,),
        row_specs(groups, tile) + [tile_spec],
        [out_spec] * 3,
        [shape_of(rows, units)] * 3,
        [g[0] for g in groups] + [w_both],
        [pltpu.VMEM((rows, 2 * units), jnp.float32), pltpu.VMEM((rows, tile), jnp.bfloat16)],
        "forward_rows",
        earlier=earlier,
    )


def weigh_hidden(hidden_near, hidden_far, hidden_s, pieces, first_row, slot_rows, core, earlier=()):
    count = len(pieces)
    rows, units_s = hidden_s.shape
    units = hidden_near.shape[1]
    slots = [(s, 0) for s in list(range(1, count)) + [0]] + [(s, 1) for s in range(count)]

    def body(core_ref, *refs):
        near_ref, far_ref, s_ref, *piece_refs = refs[: 3 + count]
        out, w_ref, w_s_ref = refs[-3:]
        near, far = 0, 0
        for i, (slot, other) in enumerate(slots):
            part = pl.ds(i * slot_rows, slot_rows)
            table = piece_refs[slot][0, core_ref[0] ^ other, first_row : first_row + 16, :][:1].astype(jnp.float32)

            def column(j):
                both = table[:, j * slot_rows : (j + 1) * slot_rows]
                both = both + table[:, (j + 2) * slot_rows : (j + 3) * slot_rows]
                return jnp.broadcast_to(both, (slot_rows, slot_rows)).T[:, :1]

            weight, weight_s = column(0), column(1)
            w_ref[part, :] = weight
            w_s_ref[part, :] = weight_s
            if slot == 0:
                hidden = near_ref[near : near + slot_rows, :]
                near += slot_rows
            else:
                hidden = far_ref[far : far + slot_rows, :]
                far += slot_rows
            out[part, :units] = (hidden.astype(jnp.float32) * weight).astype(jnp.bfloat16)
            out[part, units:] = (s_ref[part, :].astype(jnp.float32) * weight_s).astype(jnp.bfloat16)

    return pl.pallas_call(
        body,
        out_shape=[
            shape_of(rows, units + units_s),
            shape_of(rows, 1, dtype=jnp.float32),
            shape_of(rows, 1, dtype=jnp.float32),
        ],
        grid_spec=pltpu.PrefetchScalarGridSpec(
            num_scalar_prefetch=1,
            grid=(1,),
            in_specs=[whole(a) for a in (hidden_near, hidden_far, hidden_s, *pieces)] + [ANY] * len(earlier),
            out_specs=[
                pl.BlockSpec((rows, units + units_s), lambda *_: (0, 0)),
                pl.BlockSpec((rows, 1), lambda *_: (0, 0)),
                pl.BlockSpec((rows, 1), lambda *_: (0, 0)),
            ],
        ),
        compiler_params=pltpu.CompilerParams(vmem_limit_bytes=VMEM_LIMIT),
        cost_estimate=SHORT,
        name="weigh_hidden",
    )(core.reshape(1).astype(jnp.int32), hidden_near, hidden_far, hidden_s, *pieces, *earlier)


def output_other(weighted, down, column, parts, slot_rows, quarter, earlier=()):
    rows, units = weighted.shape
    count = rows // 2 // parts

    def body(weighted_ref, down_ref, *outs):
        value = dot32(weighted_ref[...], down_ref[...]).astype(jnp.bfloat16)
        for i, out in enumerate(outs):
            first, last = slot_rows + i * count, slot_rows + (i + 1) * count
            kept = min(last, rows // 2) - first
            out[:kept, :] = value[first : first + kept]
            if kept < count:
                out[kept:, :] = value[: count - kept]

    return kernel_call(
        body,
        (4,),
        [
            pl.BlockSpec((rows // 2, units), lambda *_: (1, 0)),
            pl.BlockSpec((units, quarter), lambda q, column_ref: (0, column_ref[0] ^ q)),
        ],
        [pl.BlockSpec((count, quarter), lambda q, *_: (0, q))] * parts,
        [shape_of(count, 4 * quarter)] * parts,
        [weighted, down],
        [],
        "output_other",
        column=column,
        earlier=earlier,
    )


def output_own(weighted, got, down, column, quarter, earlier=()):
    count, units = got[0].shape[0], weighted.shape[1]
    parts = len(got)

    def body(weighted_ref, down_ref, *refs):
        product = dot32(weighted_ref[...], down_ref[...])
        for i in range(parts):
            value = product[i * count : (i + 1) * count] + refs[i][...].astype(jnp.float32)
            for j, out in enumerate(refs[parts + 4 * i : parts + 4 * i + 4]):

                @pl.when(pl.program_id(0) == 3 - j)
                def _(out=out, value=value):
                    out[...] = value.astype(out.dtype)

    full = pl.BlockSpec((count, quarter), lambda *_: (0, 0))
    out = kernel_call(
        body,
        (4,),
        [
            pl.BlockSpec((parts * count, units), lambda *_: (0, 0)),
            pl.BlockSpec((units, quarter), lambda q, column_ref: (0, column_ref[0] ^ 3 ^ q)),
        ]
        + [pl.BlockSpec((count, quarter), lambda q, *_: (0, 3 - q))] * parts,
        [full] * (4 * parts),
        ([shape_of(count, quarter, dtype=jnp.float32)] + [shape_of(count, quarter)] * 3) * parts,
        [weighted, down] + list(got),
        [],
        "output_own",
        column=column,
        earlier=earlier,
    )
    return [out[4 * i : 4 * i + 4] for i in range(parts)]


def backward_rows(groups, down, parts, per_row, first_row, tile, earlier=()):
    slope_s, act_s, w_rows, w_shadow = per_row
    rows = sum(g[2] for g in groups)
    units_all, width = down.shape
    units_s = slope_s.shape[1]
    units = units_all - units_s
    steps = width // tile
    arrays = list({id(a): a for part in parts for a in part[:2]}.values())
    places = [[next(i for i, a in enumerate(arrays) if a is b) for b in part[:2]] for part in parts]

    def body(*refs):
        n, m = len(groups), len(arrays)
        down_ref = refs[n]
        array_refs = refs[n + 1 : n + 1 + m]
        slope_s_ref, act_s_ref, w_ref, w_s_ref, pre_ref, pre_s_ref, acc, held = refs[n + 1 + m :]
        clear_first(acc)
        acc[...] += contract_last(rows_operand(refs[:n], groups, held), down_ref[...])

        @pl.when(pl.program_id(0) == steps - 1)
        def _():
            chunk = 128
            start = 0
            for (_, _, count), (_, _, first), (slope_at, act_at) in zip(groups, parts, places):

                @pl.loop(0, count // chunk)
                def _(i, start=start, first=first, slope_ref=array_refs[slope_at], act_ref=array_refs[act_at]):
                    source = pl.ds(pl.multiple_of(first + i * chunk, chunk), chunk)
                    part = pl.ds(pl.multiple_of(start + i * chunk, chunk), chunk)
                    whole_part = pl.ds(pl.multiple_of(first_row + start + i * chunk, chunk), chunk)
                    grad = acc[part, :units] * w_ref[whole_part, :]
                    pre_ref[part, :units] = (grad * slope_ref[source, :]).astype(jnp.bfloat16)
                    pre_ref[part, units:] = (grad * act_ref[source, :]).astype(jnp.bfloat16)
                    grad = acc[part, units:] * w_s_ref[whole_part, :]
                    pre_s_ref[part, :units_s] = (grad * slope_s_ref[whole_part, :]).astype(jnp.bfloat16)
                    pre_s_ref[part, units_s:] = (grad * act_s_ref[whole_part, :]).astype(jnp.bfloat16)

                start += count

    extra = arrays + [slope_s, act_s, w_rows, w_shadow]
    return kernel_call(
        body,
        (steps,),
        row_specs(groups, tile) + [pl.BlockSpec((units_all, tile), lambda k, *_: (0, k))] + [whole(a) for a in extra],
        [pl.BlockSpec((rows, 2 * units), lambda *_: (0, 0)), pl.BlockSpec((rows, 2 * units_s), lambda *_: (0, 0))],
        [shape_of(rows, 2 * units), shape_of(rows, 2 * units_s)],
        [g[0] for g in groups] + [down] + extra,
        [pltpu.VMEM((rows, units_all), jnp.float32), pltpu.VMEM((rows, tile), jnp.bfloat16)],
        "backward_rows",
        earlier=earlier,
    )


def stage_rows(refs, groups, held):
    start = 0
    for ref, (_, _, count) in zip(refs, groups):
        held[pl.ds(start, count), :] = ref[...]
        start += count
    return held[...]


def shadow_grads(x_groups, dy_groups, pre_s, weighted, units, block, tile, earlier=()):
    rows, wide = weighted.shape[0], pre_s[0].shape[1]
    apart = wide // 2
    width = x_groups[0][0].shape[1]
    m = len(pre_s)

    def body(*refs):
        n = len(x_groups)
        pre_refs = refs[2 * n : 2 * n + m]
        hidden_ref, out, held, pre_t, hidden_t = refs[2 * n + m :]

        @pl.when(pl.program_id(0) == 0)
        def _():
            start = 0
            for ref in pre_refs:
                pre_t[:, start : start + ref.shape[0]] = ref[...].T
                start += ref.shape[0]
            hidden_t[...] = hidden_ref[...].T

        value = dot32(pre_t[...], stage_rows(refs[:n], x_groups, held)).astype(jnp.bfloat16)
        for i in range(tile // block):
            part = slice(i * block, (i + 1) * block)
            out[i, :units, :] = value[:units, part]
            out[i, units : 2 * units, :] = value[apart : apart + units, part]
        value = dot32(hidden_t[...], stage_rows(refs[n : 2 * n], dy_groups, held)).astype(jnp.bfloat16)
        for i in range(tile // block):
            out[i, 2 * units :, :] = value[:units, i * block : (i + 1) * block]

    (out,) = kernel_call(
        body,
        (width // tile,),
        row_specs(x_groups, tile)
        + row_specs(dy_groups, tile)
        + [whole(p) for p in pre_s]
        + [pl.BlockSpec((rows, apart), lambda *_: (0, weighted.shape[1] // apart - 1))],
        [pl.BlockSpec((tile // block, 3 * units, block), lambda k, *_: (k, 0, 0))],
        [shape_of(width // block, 3 * units, block)],
        [g[0] for g in x_groups + dy_groups] + list(pre_s) + [weighted],
        [
            pltpu.VMEM((rows, tile), jnp.bfloat16),
            pltpu.VMEM((wide, rows), jnp.bfloat16),
            pltpu.VMEM((apart, rows), jnp.bfloat16),
        ],
        "shadow_grads",
        earlier=earlier,
    )
    return out


def input_grads(groups, pre, tile, earlier=()):
    both = pre[0].shape[1]
    rows = sum(p.shape[0] for p in pre)
    units = both // 2
    width = groups[0][0].shape[1]
    m = len(pre)

    def body(*refs):
        n = len(groups)
        gate_ref, up_ref, held, pre_held = refs[n + m :]

        @pl.when(pl.program_id(0) == 0)
        def _():
            start = 0
            for ref in refs[n : n + m]:
                pre_held[start : start + ref.shape[0], :] = ref[...]
                start += ref.shape[0]

        value = contract_rows(stage_rows(refs[:n], groups, held), pre_held[...])
        gate_ref[...] = value[:, :units].astype(jnp.bfloat16)
        up_ref[...] = value[:, units:].astype(jnp.bfloat16)

    return kernel_call(
        body,
        (width // tile,),
        row_specs(groups, tile) + [whole(p) for p in pre],
        [pl.BlockSpec((tile, units), lambda k, *_: (k, 0))] * 2,
        [shape_of(width, units)] * 2,
        [g[0] for g in groups] + list(pre),
        [pltpu.VMEM((rows, tile), jnp.bfloat16), pltpu.VMEM((rows, both), jnp.bfloat16)],
        "input_grads",
        earlier=earlier,
    )


def down_grad(groups, weighted, units, tile, earlier=()):
    rows = weighted.shape[0]
    width = groups[0][0].shape[1]

    def body(*refs):
        n = len(groups)
        hidden_ref, out, held, hidden_t = refs[n:]

        @pl.when(pl.program_id(0) == 0)
        def _():
            hidden_t[...] = hidden_ref[...].T

        out[...] = dot32(hidden_t[...], stage_rows(refs[:n], groups, held)).astype(jnp.bfloat16)

    (out,) = kernel_call(
        body,
        (width // tile,),
        row_specs(groups, tile) + [pl.BlockSpec((rows, units), lambda *_: (0, 0))],
        [pl.BlockSpec((units, tile), lambda k, *_: (0, k))],
        [shape_of(units, width)],
        [g[0] for g in groups] + [weighted],
        [pltpu.VMEM((rows, tile), jnp.bfloat16), pltpu.VMEM((units, rows), jnp.bfloat16)],
        "down_grad",
        earlier=earlier,
    )
    return out


def send_along_z(own):
    ep_count = lax.axis_size("ep")
    return [lax.ppermute(own, "ep", swap_pairs(ep_count, 2 * s)) for s in range(1, ep_count // 2)]


def swap_cores(block):
    return lax.ppermute(block, "ep", swap_pairs(lax.axis_size("ep"), 1))


def send_plane(*pieces):
    pieces = pieces * 3 if len(pieces) == 1 else pieces
    return [lax.ppermute(p, "tp", swap_pairs(lax.axis_size("tp"), bit)) for p, bit in zip(pieces, (1, 2, 3))]


def exchange_cores(blocks, cuts=1):
    ep_count, core = lax.axis_size("ep"), lax.axis_index("ep") % 2
    pairs = blocks.reshape(ep_count // 2, 2, *blocks.shape[1:])
    kept = jnp.where(core == 0, pairs[:, 0], pairs[:, 1])
    given = jnp.where(core == 0, pairs[:, 1], pairs[:, 0])
    return kept, [swap_cores(part) for part in jnp.split(given, cuts)]


def chip_pieces(kept, taken):
    ep_count, me = lax.axis_size("ep"), lax.axis_index("ep")
    chips, chip, core = ep_count // 2, me // 2, me % 2
    taken = jnp.concatenate(taken, axis=0)
    both = jnp.stack([jnp.where(core == 0, kept, taken), jnp.where(core == 0, taken, kept)], axis=1)
    return [lax.dynamic_index_in_dim(both, chip ^ shift, 0) for shift in range(chips)]


def send_piece(piece, shift):
    return lax.ppermute(piece, "ep", swap_pairs(lax.axis_size("ep"), 2 * shift))


def dense_shards(
    tokens,
    cotangent,
    expert_ids,
    gate_weights,
    shadow_mask,
    w_gate,
    w_up,
    w_down,
    s_gate,
    s_up,
    s_down,
):
    ep_count, tp_count = lax.axis_size("ep"), lax.axis_size("tp")
    ep_index, tp_index = lax.axis_index("ep"), lax.axis_index("tp")
    tok_count, top_count = expert_ids.shape
    quarter = tokens.shape[1]
    width = quarter * tp_count
    hidden_part = w_gate.shape[2]
    shadow_part = hidden_part // ep_count
    block_width = s_gate.shape[0]
    steps = ep_count // 2
    later = (steps - 1) * tok_count
    tile = width // 8
    along, across = swap_pairs(tp_count, 1), swap_pairs(tp_count, 2)

    picked = expert_ids[None, :, :] == jnp.arange(ep_count, dtype=jnp.int32)[:, None, None]
    table = jnp.sum(jnp.where(picked, gate_weights[None, :, :top_count], 0.0), axis=2)
    shadow_weight = gate_weights[:, top_count] * shadow_mask.astype(jnp.float32)
    table = jnp.concatenate([table, jnp.broadcast_to(shadow_weight[None], table.shape)], axis=1)
    table = jnp.concatenate(split_parts(table), axis=1)
    table = jnp.pad(table[:, None, :], ((0, 0), (0, 15), (0, block_width - table.shape[1])))
    shadow_blocks = jnp.concatenate(
        [
            s_gate.T.reshape(ep_count, shadow_part, block_width),
            s_up.T.reshape(ep_count, shadow_part, block_width),
            s_down.reshape(ep_count, shadow_part, block_width),
            table,
        ],
        axis=1,
    )

    x_z = send_along_z(tokens)
    near = stack_pieces([tokens, cotangent])
    near_x, near_y = send_plane(near, near)
    near_late = stack_pieces([tokens, cotangent], earlier=[x_z[0]])
    near_d = lax.ppermute(near_late, "tp", swap_pairs(tp_count, 3))
    w_both = jnp.concatenate([w_gate[0], w_up[0]], axis=1)
    near_x, near_y, near_d, *x_z = after([near_x, near_y, near_d, *x_z], w_both, shadow_blocks)

    x_piece = stack_pieces(x_z)
    x_plane = send_plane(x_piece)
    dy_z = send_along_z(cotangent)
    near_own = join_plane(tp_index, near, near_x, near_y, near_d)
    near_other = swap_cores(near_own)
    x_near = [(near_own, 0, tok_count), (near_other, 0, tok_count)]
    hidden_near, slope_near, act_near = forward_rows(x_near, w_both, 2 * tile)
    spare_rows = -shadow_part % 128 + shadow_part
    down = jnp.pad(w_down[0], ((0, spare_rows), (0, 0)))
    (shadow_blocks,) = after([shadow_blocks], x_z[0])
    shadow_kept, shadow_taken = exchange_cores(shadow_blocks)
    fenced = after([*x_plane, down, *shadow_taken, *dy_z], hidden_near)
    x_plane, down, shadow_taken, dy_z = fenced[:3], fenced[3], fenced[4:5], fenced[5:]

    dy_piece = stack_pieces(dy_z)
    dy_plane = send_plane(dy_piece)
    shadow_pieces = chip_pieces(shadow_kept, shadow_taken)
    for shift in range(1, steps - 1):
        shadow_pieces[shift] = send_piece(shadow_pieces[shift], shift)
    x_own = join_plane(tp_index, x_piece, *x_plane, earlier=[dy_piece])
    x_other = swap_cores(x_own)
    x_far = [(x_own, 0, later), (x_other, 0, later)]
    x_groups = [x_far[0], x_near[0], x_near[1], x_far[1]]
    hidden_far, slope_far, act_far = forward_rows(x_far, w_both, 2 * tile)
    shadow_pieces[-1:] = after(shadow_pieces[-1:], hidden_far)
    shadow_pieces[-1] = send_piece(shadow_pieces[-1], steps - 1)
    chip = ep_index // 2
    shadow_in, down = lay_out_shadow(shadow_pieces, down, shadow_part, chip, earlier=[hidden_far])
    hidden_s, slope_s, act_s = forward_rows(x_groups, shadow_in, 2 * tile, transposed=True)

    weighted, w_rows, w_shadow = weigh_hidden(
        hidden_near, hidden_far, hidden_s, shadow_pieces, 3 * shadow_part, tok_count, ep_index % 2
    )

    parts = 2 if steps % 2 == 0 else 1
    sent = output_other(weighted, down, tp_index, parts, tok_count, quarter)
    got = [swap_cores(array) for array in sent]
    dy_plane = after(dy_plane, *sent)

    dy_own = join_plane(tp_index, dy_piece, *dy_plane)
    dy_other = swap_cores(dy_own)
    dy_groups = [(dy_own, 0, later), (near_own, 1, tok_count), (near_other, 1, tok_count), (dy_other, 0, later)]
    segments = [
        (slope_far, act_far, 0),
        (slope_near, act_near, 0),
        (slope_near, act_near, tok_count),
        (slope_far, act_far, later),
    ]
    per_row = (slope_s, act_s, w_rows, w_shadow)
    pre_first, pre_s_first = backward_rows(dy_groups[:3], down, segments[:3], per_row, 0, 2 * tile)
    owns = output_own(weighted, got, down, tp_index, quarter, earlier=[pre_first])
    sums = [send_plane(*own[1:]) for own in owns]
    first_rows = sum(g[2] for g in dy_groups[:3])
    pre_last, pre_s_last = backward_rows(
        dy_groups[3:], down, segments[3:], per_row, first_rows, 2 * tile, earlier=[own[1] for own in owns]
    )
    pre, pre_s = [pre_first, pre_last], [pre_s_first, pre_s_last]
    grad_s = shadow_grads(x_groups, dy_groups, pre_s, weighted, shadow_part, block_width, 2 * tile)
    grad_pieces = chip_pieces(*exchange_cores(grad_s))

    def slot_rows(i):
        part = slice(i % (steps // parts) * tok_count, (i % (steps // parts) + 1) * tok_count)
        total = owns[i * parts // steps][0][part]
        for array in sums[i * parts // steps]:
            total = total + array[part].astype(jnp.float32)
        return total

    def send_rows(piece, i):
        return lax.ppermute(piece, "ep", swap_pairs(ep_count, 2 * (i + 1)))

    early = steps // parts if parts > 1 else 0
    sums[0] = after(sums[0], grad_s)
    rows = [slot_rows(i).astype(jnp.bfloat16) for i in range(early)]
    grad_down = down_grad(dy_groups, weighted, hidden_part, 2 * tile, earlier=[*rows, grad_pieces[0]])
    rows = [send_rows(piece, i) for i, piece in enumerate(rows)]
    fenced = after([*rows, *grad_pieces[1:]], grad_down)
    rows, grad_pieces[1:] = list(fenced[:early]), fenced[early:]
    grad_gate, grad_up = input_grads(x_groups, pre, 2 * tile, earlier=[grad_pieces[1]])
    for shift in range(1, steps - 1):
        grad_pieces[shift] = send_piece(grad_pieces[shift], shift)
    fenced = after([*sums[-1], *grad_pieces[1:]], grad_gate)
    sums[-1], grad_pieces[1:] = fenced[:3], fenced[3:]
    grad_pieces[-1] = send_piece(grad_pieces[-1], steps - 1)
    rows += [send_rows(slot_rows(i).astype(jnp.bfloat16), i) for i in range(early, steps - 1)]
    total = slot_rows(steps - 1)
    for piece in rows:
        total = total + piece.astype(jnp.float32)
    mixed = total.astype(jnp.bfloat16)

    grads_s = lay_out_grads(grad_pieces, shadow_part, chip)
    return (mixed, grad_gate[None], grad_up[None], grad_down[None], *grads_s)


def shards(tokens, cotangent, expert_ids, *others):
    tp_count, ep_count = lax.axis_size("tp"), lax.axis_size("ep")
    tok_count, top_count = expert_ids.shape
    rows = (5 * tok_count * top_count) // 4
    chips = ep_count // 2
    fits = tp_count == 4 and ep_count == 2 * chips and chips & (chips - 1) == 0 and tok_count % 128 == 0
    dense = fits and ep_count * tok_count <= 3 * rows
    return (dense_shards if dense else routed_shards)(tokens, cotangent, expert_ids, *others)


def solution(mesh):
    return jax.shard_map(
        shards,
        mesh=mesh,
        in_specs=(
            P("ep", "tp"),
            P("ep", "tp"),
            P("ep", None),
            P("ep", None),
            P("ep"),
            P("ep", None, "tp"),
            P("ep", None, "tp"),
            P("ep", "tp", None),
            P("ep", "tp"),
            P("ep", "tp"),
            P("tp", "ep"),
        ),
        out_specs=(
            P("ep", "tp"),
            P("ep", None, "tp"),
            P("ep", None, "tp"),
            P("ep", "tp", None),
            P("ep", "tp"),
            P("ep", "tp"),
            P("tp", "ep"),
        ),
        check_vma=False,
    )
```

```python
import functools

import jax
import jax.numpy as jnp
from jax import lax
from jax.experimental import pallas as pl
from jax.experimental.pallas import tpu as pltpu
from jax.sharding import PartitionSpec as P


def contract_rows(left, right):
    return lax.dot_general(
        left, right, (((0,), (0,)), ((), ())), preferred_element_type=jnp.float32
    )


def split_parts(values):
    upper_part = values.astype(jnp.bfloat16)
    lower_part = (values - upper_part.astype(jnp.float32)).astype(jnp.bfloat16)
    return (upper_part, lower_part)


def weigh_rows(weight_table, rows):
    weight_upper, weight_lower = split_parts(weight_table)
    return jnp.dot(weight_upper, rows, preferred_element_type=jnp.float32) + jnp.dot(
        weight_lower, rows, preferred_element_type=jnp.float32
    )


def expert_pass(rows_x, rows_dout, weight_gate, weight_up, weight_down):
    pre_gate = jnp.dot(rows_x, weight_gate, preferred_element_type=jnp.float32)
    pre_up = jnp.dot(rows_x, weight_up, preferred_element_type=jnp.float32)
    sigmoid_gate = jax.nn.sigmoid(pre_gate)
    activated = pre_gate * sigmoid_gate
    hidden = (activated * pre_up).astype(jnp.bfloat16)
    partial_out = jnp.dot(hidden, weight_down, preferred_element_type=jnp.float32).astype(
        jnp.bfloat16
    )
    hidden_grad = lax.dot_general(
        rows_dout, weight_down, (((1,), (1,)), ((), ())), preferred_element_type=jnp.float32
    )
    grad_pre_gate = (
        hidden_grad * pre_up * sigmoid_gate * (1.0 + pre_gate * (1.0 - sigmoid_gate))
    ).astype(jnp.bfloat16)
    grad_pre_up = (hidden_grad * activated).astype(jnp.bfloat16)
    return (partial_out, hidden, grad_pre_gate, grad_pre_up)


def routed_shards(
    tokens,
    cotangent,
    expert_ids,
    gate_weights,
    shadow_mask,
    w_gate,
    w_up,
    w_down,
    s_gate,
    s_up,
    s_down,
):
    ep_count = lax.axis_size("ep")
    tok_count, top_count = expert_ids.shape
    quarter_width = tokens.shape[1]
    width = quarter_width * lax.axis_size("tp")
    expert_count = w_gate.shape[0] * ep_count
    capacity = (5 * tok_count * top_count + 4 * expert_count - 1) // (4 * expert_count)
    slot_count = expert_count * capacity
    picks_flat = expert_ids.reshape(-1)
    onehot = (picks_flat[:, None] == jnp.arange(expert_count, dtype=jnp.int32)[None, :]).astype(
        jnp.int32
    )
    slot_rank = jnp.sum((jnp.cumsum(onehot, axis=0) - onehot) * onehot, axis=1)
    slot_index = (picks_flat * capacity + slot_rank).reshape(tok_count, top_count)
    matches = jnp.arange(slot_count, dtype=jnp.int32)[:, None, None] == slot_index[None, :, :]
    dispatch = jnp.any(matches, axis=2).astype(jnp.bfloat16)
    weighting = jnp.sum(jnp.where(matches, gate_weights[None, :, :top_count], 0.0), axis=2)
    slot_gate = jnp.sum(weighting, axis=1)
    shadow_weight = gate_weights[:, top_count] * shadow_mask.astype(jnp.float32)
    x_full, dy_full = (
        lax.all_gather(tokens, "tp", axis=1, tiled=True),
        lax.all_gather(cotangent, "tp", axis=1, tiled=True),
    )
    rows_x = jnp.dot(dispatch, tokens, preferred_element_type=jnp.float32).astype(jnp.bfloat16)
    rows_dy = jnp.dot(dispatch, cotangent, preferred_element_type=jnp.float32)
    rows_dout = (slot_gate[:, None] * rows_dy).astype(jnp.bfloat16)
    recv_x, recv_dout = (
        lax.all_to_all(
            rows_x.reshape(ep_count, -1, quarter_width),
            "ep",
            split_axis=0,
            concat_axis=0,
            tiled=True,
        ),
        lax.all_to_all(
            rows_dout.reshape(ep_count, -1, quarter_width),
            "ep",
            split_axis=0,
            concat_axis=0,
            tiled=True,
        ),
    )
    expert_x, expert_dout = (
        lax.all_gather(recv_x.reshape(-1, quarter_width), "tp", axis=1, tiled=True),
        lax.all_gather(recv_dout.reshape(-1, quarter_width), "tp", axis=1, tiled=True),
    )
    partial_out, hidden, grad_pre_gate, grad_pre_up = expert_pass(
        expert_x, expert_dout, w_gate[0], w_up[0], w_down[0]
    )
    grad_gate = contract_rows(expert_x, grad_pre_gate).astype(jnp.bfloat16)[None]
    grad_up = contract_rows(expert_x, grad_pre_up).astype(jnp.bfloat16)[None]
    grad_down = contract_rows(hidden, expert_dout).astype(jnp.bfloat16)[None]
    full_gate, full_up, full_down = (
        lax.all_gather(s_gate, "ep", axis=0, tiled=True),
        lax.all_gather(s_up, "ep", axis=0, tiled=True),
        lax.all_gather(s_down, "ep", axis=1, tiled=True),
    )
    shadow_dout = (shadow_weight[:, None] * dy_full.astype(jnp.float32)).astype(jnp.bfloat16)
    shadow_out, shadow_hidden, shadow_gate_pre, shadow_up_pre = expert_pass(
        x_full, shadow_dout, full_gate, full_up, full_down
    )
    shadow_sums = lax.psum_scatter(
        jnp.concatenate(
            [
                contract_rows(x_full, shadow_gate_pre),
                contract_rows(x_full, shadow_up_pre),
                contract_rows(shadow_dout, shadow_hidden),
            ],
            axis=1,
        ).astype(jnp.bfloat16),
        "ep",
        scatter_dimension=0,
        tiled=True,
    ).astype(jnp.float32)
    hidden_part = s_gate.shape[1]
    grad_s_gate = shadow_sums[:, :hidden_part].astype(jnp.bfloat16)
    grad_s_up = shadow_sums[:, hidden_part : 2 * hidden_part].astype(jnp.bfloat16)
    grad_s_down = shadow_sums[:, 2 * hidden_part :].T.astype(jnp.bfloat16)
    back_rows = lax.all_to_all(
        partial_out.reshape(ep_count, -1, width), "ep", split_axis=0, concat_axis=0, tiled=True
    ).reshape(-1, width)
    term = weigh_rows(weighting.T, back_rows)
    term = term + shadow_weight[:, None] * shadow_out.astype(jnp.float32)
    mixed = lax.psum_scatter(term.astype(jnp.bfloat16), "tp", scatter_dimension=1, tiled=True)
    return (mixed, grad_gate, grad_up, grad_down, grad_s_gate, grad_s_up, grad_s_down)


ANY = pl.BlockSpec(memory_space=pl.ANY)
VMEM_LIMIT = 60 * 1024 * 1024
SHORT = pl.CostEstimate(flops=1, bytes_accessed=1, transcendentals=0)


def swap_pairs(count, bit):
    return [(i, i ^ bit) for i in range(count)]


def dot32(left, right):
    return jnp.dot(left, right, preferred_element_type=jnp.float32)


def contract_last(left, right):
    return lax.dot_general(
        left, right, (((1,), (1,)), ((), ())), preferred_element_type=jnp.float32
    )


def shape_of(*dims, dtype=jnp.bfloat16):
    return jax.ShapeDtypeStruct(dims, dtype)


def after(arrays, *earlier):
    def nothing(*refs):
        del refs

    count = len(arrays)
    return pl.pallas_call(
        nothing,
        out_shape=[jax.ShapeDtypeStruct(a.shape, a.dtype) for a in arrays],
        in_specs=[ANY] * (count + len(earlier)),
        out_specs=[ANY] * count,
        input_output_aliases={i: i for i in range(count)},
        compiler_params=pltpu.CompilerParams(vmem_limit_bytes=VMEM_LIMIT),
        cost_estimate=SHORT,
        name="after",
    )(*arrays, *earlier)


def kernel_call(body, grid, in_specs, out_specs, out_shape, operands, scratch, name, column=None, earlier=()):
    count = len(operands)

    def run(column_ref, *refs):
        del column_ref
        body(*refs[:count], *refs[count + len(earlier) :])

    column = jnp.zeros((1,), jnp.int32) if column is None else column.reshape(1).astype(jnp.int32)
    return pl.pallas_call(
        run,
        out_shape=out_shape,
        grid_spec=pltpu.PrefetchScalarGridSpec(
            num_scalar_prefetch=1,
            grid=grid,
            in_specs=list(in_specs) + [ANY] * len(earlier),
            out_specs=out_specs,
            scratch_shapes=scratch,
        ),
        compiler_params=pltpu.CompilerParams(vmem_limit_bytes=VMEM_LIMIT),
        cost_estimate=SHORT,
        name=name,
    )(column, *operands, *earlier)


def whole(array):
    return pl.BlockSpec(array.shape, lambda *_: (0,) * len(array.shape))


def join_plane(column, *pieces, earlier=()):
    rows, quarter = pieces[0].shape
    count, halves = 4, len(pieces) - 3
    chunk = rows // 4
    per = 4 // halves

    def body(column_ref, *refs):
        out = refs[-1]
        for own_column in range(count):
            for j, from_diagonal in enumerate(refs[3 : 3 + halves]):

                @pl.when((column_ref[0] == own_column) & (pl.program_id(0) // per == j))
                def _(from_diagonal=from_diagonal, own_column=own_column):
                    for bit, source in enumerate(refs[:3] + (from_diagonal,)):
                        place = own_column ^ bit
                        out[:, place * quarter : (place + 1) * quarter] = source[...]

    def diagonal_spec(j):
        return pl.BlockSpec((chunk, quarter), lambda i, *_: (jnp.clip(i - j * per, 0, per - 1), 0))

    return pl.pallas_call(
        body,
        out_shape=shape_of(rows, count * quarter),
        grid_spec=pltpu.PrefetchScalarGridSpec(
            num_scalar_prefetch=1,
            grid=(4,),
            in_specs=[pl.BlockSpec((chunk, quarter), lambda i, *_: (i, 0))] * 3
            + [diagonal_spec(j) for j in range(halves)]
            + [ANY] * len(earlier),
            out_specs=pl.BlockSpec((chunk, count * quarter), lambda i, *_: (i, 0)),
        ),
        compiler_params=pltpu.CompilerParams(vmem_limit_bytes=VMEM_LIMIT),
        cost_estimate=SHORT,
        name="join_plane",
    )(column.reshape(1).astype(jnp.int32), *pieces, *earlier)


def stack_pieces(pieces, earlier=()):
    rows, columns = pieces[0].shape
    count = len(pieces)

    def body(*refs):
        for i, ref in enumerate(refs[:count]):

            @pl.when(pl.program_id(0) == i)
            def _():
                refs[-1][...] = ref[...]

    return pl.pallas_call(
        body,
        out_shape=shape_of(count * rows, columns),
        grid=(count,),
        in_specs=[pl.BlockSpec((rows, columns), lambda i: (0, 0))] * count + [ANY] * len(earlier),
        out_specs=pl.BlockSpec((rows, columns), lambda i: (i, 0)),
        compiler_params=pltpu.CompilerParams(vmem_limit_bytes=VMEM_LIMIT),
        cost_estimate=SHORT,
        name="stack_pieces",
    )(*pieces, *earlier)


def on_piece(chip_ref, refs, use):
    step = pl.program_id(0)
    shift = chip_ref[0] ^ (step // 2)
    for i, ref in enumerate(refs):
        for core in range(2):

            @pl.when((shift == i) & (lax.rem(step, 2) == core))
            def _(ref=ref, core=core):
                use(ref.at[0, core])


def lay_out_shadow(pieces, down, units, chip, earlier=()):
    count = len(pieces)
    ep_count = 2 * count
    block_width = pieces[0].shape[3]
    apart = units + -units % 128
    all_units, width = down.shape

    def body(chip_ref, *refs):
        shadow_ref, out = refs[-2:]

        def use(ref):
            shadow_ref[...] = jnp.zeros_like(shadow_ref)
            shadow_ref[:units, :] = ref[:units, :]
            shadow_ref[apart : apart + units, :] = ref[units : 2 * units, :]
            out[units:, :] = jnp.zeros((apart - units, block_width), jnp.bfloat16)
            out[:units, :] = ref[2 * units : 3 * units, :]

        on_piece(chip_ref, refs[:count], use)

    return pl.pallas_call(
        body,
        out_shape=[shape_of(2 * apart, width), shape_of(all_units, width)],
        grid_spec=pltpu.PrefetchScalarGridSpec(
            num_scalar_prefetch=1,
            grid=(ep_count,),
            in_specs=[whole(p) for p in pieces] + [ANY] * (1 + len(earlier)),
            out_specs=[
                pl.BlockSpec((2 * apart, block_width), lambda e, *_: (0, e)),
                pl.BlockSpec((apart, block_width), lambda e, *_: (all_units // apart - 1, e)),
            ],
        ),
        input_output_aliases={1 + count: 1},
        compiler_params=pltpu.CompilerParams(vmem_limit_bytes=VMEM_LIMIT),
        cost_estimate=SHORT,
        name="lay_out_shadow",
    )(chip.reshape(1).astype(jnp.int32), *pieces, down, *earlier)


def lay_out_grads(pieces, units, chip, earlier=()):
    count = len(pieces)
    ep_count = 2 * count
    block_width = pieces[0].shape[3]
    hidden = ep_count * units

    def body(chip_ref, *refs):
        gate_ref, up_ref, down_ref, gate_t, up_t = refs[-5:]
        place = pl.ds(pl.multiple_of(pl.program_id(0) * units, 16), units)

        def use(ref):
            gate_t[place, :] = ref[:units, :]
            up_t[place, :] = ref[units : 2 * units, :]
            down_ref[place, :] = ref[2 * units :, :]

        on_piece(chip_ref, refs[:count], use)

        @pl.when(pl.program_id(0) == ep_count - 1)
        def _():
            gate_ref[...] = gate_t[...].T
            up_ref[...] = up_t[...].T

    return pl.pallas_call(
        body,
        out_shape=[shape_of(block_width, hidden), shape_of(block_width, hidden), shape_of(hidden, block_width)],
        grid_spec=pltpu.PrefetchScalarGridSpec(
            num_scalar_prefetch=1,
            grid=(ep_count,),
            in_specs=[whole(p) for p in pieces] + [ANY] * len(earlier),
            out_specs=[pl.BlockSpec((block_width, hidden), lambda *_: (0, 0))] * 2
            + [pl.BlockSpec((hidden, block_width), lambda *_: (0, 0))],
            scratch_shapes=[pltpu.VMEM((hidden, block_width), jnp.bfloat16)] * 2,
        ),
        compiler_params=pltpu.CompilerParams(vmem_limit_bytes=VMEM_LIMIT),
        cost_estimate=SHORT,
        name="lay_out_grads",
    )(chip.reshape(1).astype(jnp.int32), *pieces, *earlier)


def row_specs(groups, tile):
    def spec(index, rows):
        return pl.BlockSpec((rows, tile), lambda k, *_: (index, k))

    return [spec(index, rows) for _, index, rows in groups]


def apply_gate(pre_gate, pre_up):
    sigmoid_gate = jax.nn.sigmoid(pre_gate)
    activated = pre_gate * sigmoid_gate
    hidden = (activated * pre_up).astype(jnp.bfloat16)
    return hidden, pre_up * sigmoid_gate * (1.0 + pre_gate * (1.0 - sigmoid_gate)), activated


def clear_first(acc):
    @pl.when(pl.program_id(0) == 0)
    def _():
        acc[...] = jnp.zeros_like(acc)


def rows_operand(refs, groups, held):
    if len(groups) == 1:
        return refs[0][...]
    return stage_rows(refs, groups, held)


def forward_rows(groups, w_both, tile, transposed=False, earlier=()):
    rows = sum(g[2] for g in groups)
    if transposed:
        units, width = w_both.shape[0] // 2, w_both.shape[1]
        tile_spec = pl.BlockSpec((2 * units, tile), lambda k, *_: (0, k))
    else:
        width, units = w_both.shape[0], w_both.shape[1] // 2
        tile_spec = pl.BlockSpec((tile, 2 * units), lambda k, *_: (k, 0))
    steps = width // tile

    def body(*refs):
        n = len(groups)
        both_ref, hidden_ref, slope_ref, act_ref, acc, held = refs[n:]
        clear_first(acc)
        operand = rows_operand(refs[:n], groups, held)
        acc[...] += contract_last(operand, both_ref[...]) if transposed else dot32(operand, both_ref[...])

        @pl.when(pl.program_id(0) == steps - 1)
        def _():
            chunk = 128

            @pl.loop(0, rows // chunk)
            def _(i):
                part = pl.ds(pl.multiple_of(i * chunk, chunk), chunk)
                hidden, slope, act = apply_gate(acc[part, :units], acc[part, units:])
                hidden_ref[part, :] = hidden
                slope_ref[part, :] = slope.astype(jnp.bfloat16)
                act_ref[part, :] = act.astype(jnp.bfloat16)

    out_spec = pl.BlockSpec((rows, units), lambda *_: (0, 0))
    return kernel_call(
        body,
        (steps,),
        row_specs(groups, tile) + [tile_spec],
        [out_spec] * 3,
        [shape_of(rows, units)] * 3,
        [g[0] for g in groups] + [w_both],
        [pltpu.VMEM((rows, 2 * units), jnp.float32), pltpu.VMEM((rows, tile), jnp.bfloat16)],
        "forward_rows",
        earlier=earlier,
    )


def weigh_hidden(hidden_near, hidden_far, hidden_s, pieces, first_row, slot_rows, core, earlier=()):
    count = len(pieces)
    rows, units_s = hidden_s.shape
    units = hidden_near.shape[1]
    slots = [(s, 0) for s in list(range(1, count)) + [0]] + [(s, 1) for s in range(count)]

    def body(core_ref, *refs):
        near_ref, far_ref, s_ref, *piece_refs = refs[: 3 + count]
        out, w_ref, w_s_ref = refs[-3:]
        near, far = 0, 0
        for i, (slot, other) in enumerate(slots):
            part = pl.ds(i * slot_rows, slot_rows)
            table = piece_refs[slot][0, core_ref[0] ^ other, first_row : first_row + 16, :][:1].astype(jnp.float32)

            def column(j):
                both = table[:, j * slot_rows : (j + 1) * slot_rows]
                both = both + table[:, (j + 2) * slot_rows : (j + 3) * slot_rows]
                return jnp.broadcast_to(both, (slot_rows, slot_rows)).T[:, :1]

            weight, weight_s = column(0), column(1)
            w_ref[part, :] = weight
            w_s_ref[part, :] = weight_s
            if slot == 0:
                hidden = near_ref[near : near + slot_rows, :]
                near += slot_rows
            else:
                hidden = far_ref[far : far + slot_rows, :]
                far += slot_rows
            out[part, :units] = (hidden.astype(jnp.float32) * weight).astype(jnp.bfloat16)
            out[part, units:] = (s_ref[part, :].astype(jnp.float32) * weight_s).astype(jnp.bfloat16)

    return pl.pallas_call(
        body,
        out_shape=[
            shape_of(rows, units + units_s),
            shape_of(rows, 1, dtype=jnp.float32),
            shape_of(rows, 1, dtype=jnp.float32),
        ],
        grid_spec=pltpu.PrefetchScalarGridSpec(
            num_scalar_prefetch=1,
            grid=(1,),
            in_specs=[whole(a) for a in (hidden_near, hidden_far, hidden_s, *pieces)] + [ANY] * len(earlier),
            out_specs=[
                pl.BlockSpec((rows, units + units_s), lambda *_: (0, 0)),
                pl.BlockSpec((rows, 1), lambda *_: (0, 0)),
                pl.BlockSpec((rows, 1), lambda *_: (0, 0)),
            ],
        ),
        compiler_params=pltpu.CompilerParams(vmem_limit_bytes=VMEM_LIMIT),
        cost_estimate=SHORT,
        name="weigh_hidden",
    )(core.reshape(1).astype(jnp.int32), hidden_near, hidden_far, hidden_s, *pieces, *earlier)


def output_other(weighted, down, column, parts, slot_rows, quarter, earlier=()):
    rows, units = weighted.shape
    count = rows // 2 // parts

    def body(weighted_ref, down_ref, *outs):
        value = dot32(weighted_ref[...], down_ref[...]).astype(jnp.bfloat16)
        for i, out in enumerate(outs):
            first, last = slot_rows + i * count, slot_rows + (i + 1) * count
            kept = min(last, rows // 2) - first
            out[:kept, :] = value[first : first + kept]
            if kept < count:
                out[kept:, :] = value[: count - kept]

    return kernel_call(
        body,
        (4,),
        [
            pl.BlockSpec((rows // 2, units), lambda *_: (1, 0)),
            pl.BlockSpec((units, quarter), lambda q, column_ref: (0, column_ref[0] ^ q)),
        ],
        [pl.BlockSpec((count, quarter), lambda q, *_: (0, q))] * parts,
        [shape_of(count, 4 * quarter)] * parts,
        [weighted, down],
        [],
        "output_other",
        column=column,
        earlier=earlier,
    )


def output_own(weighted, got, down, column, quarter, earlier=()):
    count, units = got[0].shape[0], weighted.shape[1]
    parts = len(got)

    def body(weighted_ref, down_ref, *refs):
        product = dot32(weighted_ref[...], down_ref[...])
        for i in range(parts):
            value = product[i * count : (i + 1) * count] + refs[i][...].astype(jnp.float32)
            for j, out in enumerate(refs[parts + 4 * i : parts + 4 * i + 4]):

                @pl.when(pl.program_id(0) == 3 - j)
                def _(out=out, value=value):
                    out[...] = value.astype(out.dtype)

    full = pl.BlockSpec((count, quarter), lambda *_: (0, 0))
    out = kernel_call(
        body,
        (4,),
        [
            pl.BlockSpec((parts * count, units), lambda *_: (0, 0)),
            pl.BlockSpec((units, quarter), lambda q, column_ref: (0, column_ref[0] ^ 3 ^ q)),
        ]
        + [pl.BlockSpec((count, quarter), lambda q, *_: (0, 3 - q))] * parts,
        [full] * (4 * parts),
        ([shape_of(count, quarter, dtype=jnp.float32)] + [shape_of(count, quarter)] * 3) * parts,
        [weighted, down] + list(got),
        [],
        "output_own",
        column=column,
        earlier=earlier,
    )
    return [out[4 * i : 4 * i + 4] for i in range(parts)]


def backward_rows(groups, down, parts, per_row, first_row, tile, earlier=()):
    slope_s, act_s, w_rows, w_shadow = per_row
    rows = sum(g[2] for g in groups)
    units_all, width = down.shape
    units_s = slope_s.shape[1]
    units = units_all - units_s
    steps = width // tile
    arrays = list({id(a): a for part in parts for a in part[:2]}.values())
    places = [[next(i for i, a in enumerate(arrays) if a is b) for b in part[:2]] for part in parts]

    def body(*refs):
        n, m = len(groups), len(arrays)
        down_ref = refs[n]
        array_refs = refs[n + 1 : n + 1 + m]
        slope_s_ref, act_s_ref, w_ref, w_s_ref, pre_ref, pre_s_ref, acc, held = refs[n + 1 + m :]
        clear_first(acc)
        acc[...] += contract_last(rows_operand(refs[:n], groups, held), down_ref[...])

        @pl.when(pl.program_id(0) == steps - 1)
        def _():
            chunk = 128
            start = 0
            for (_, _, count), (_, _, first), (slope_at, act_at) in zip(groups, parts, places):

                @pl.loop(0, count // chunk)
                def _(i, start=start, first=first, slope_ref=array_refs[slope_at], act_ref=array_refs[act_at]):
                    source = pl.ds(pl.multiple_of(first + i * chunk, chunk), chunk)
                    part = pl.ds(pl.multiple_of(start + i * chunk, chunk), chunk)
                    whole_part = pl.ds(pl.multiple_of(first_row + start + i * chunk, chunk), chunk)
                    grad = acc[part, :units] * w_ref[whole_part, :]
                    pre_ref[part, :units] = (grad * slope_ref[source, :]).astype(jnp.bfloat16)
                    pre_ref[part, units:] = (grad * act_ref[source, :]).astype(jnp.bfloat16)
                    grad = acc[part, units:] * w_s_ref[whole_part, :]
                    pre_s_ref[part, :units_s] = (grad * slope_s_ref[whole_part, :]).astype(jnp.bfloat16)
                    pre_s_ref[part, units_s:] = (grad * act_s_ref[whole_part, :]).astype(jnp.bfloat16)

                start += count

    extra = arrays + [slope_s, act_s, w_rows, w_shadow]
    return kernel_call(
        body,
        (steps,),
        row_specs(groups, tile) + [pl.BlockSpec((units_all, tile), lambda k, *_: (0, k))] + [whole(a) for a in extra],
        [pl.BlockSpec((rows, 2 * units), lambda *_: (0, 0)), pl.BlockSpec((rows, 2 * units_s), lambda *_: (0, 0))],
        [shape_of(rows, 2 * units), shape_of(rows, 2 * units_s)],
        [g[0] for g in groups] + [down] + extra,
        [pltpu.VMEM((rows, units_all), jnp.float32), pltpu.VMEM((rows, tile), jnp.bfloat16)],
        "backward_rows",
        earlier=earlier,
    )


def stage_rows(refs, groups, held):
    start = 0
    for ref, (_, _, count) in zip(refs, groups):
        held[pl.ds(start, count), :] = ref[...]
        start += count
    return held[...]


def shadow_grads(x_groups, dy_groups, pre_s, weighted, units, block, tile, earlier=()):
    rows, wide = weighted.shape[0], pre_s[0].shape[1]
    apart = wide // 2
    width = x_groups[0][0].shape[1]
    m = len(pre_s)

    def body(*refs):
        n = len(x_groups)
        pre_refs = refs[2 * n : 2 * n + m]
        hidden_ref, out, held, pre_t, hidden_t = refs[2 * n + m :]

        @pl.when(pl.program_id(0) == 0)
        def _():
            start = 0
            for ref in pre_refs:
                pre_t[:, start : start + ref.shape[0]] = ref[...].T
                start += ref.shape[0]
            hidden_t[...] = hidden_ref[...].T

        value = dot32(pre_t[...], stage_rows(refs[:n], x_groups, held)).astype(jnp.bfloat16)
        for i in range(tile // block):
            part = slice(i * block, (i + 1) * block)
            out[i, :units, :] = value[:units, part]
            out[i, units : 2 * units, :] = value[apart : apart + units, part]
        value = dot32(hidden_t[...], stage_rows(refs[n : 2 * n], dy_groups, held)).astype(jnp.bfloat16)
        for i in range(tile // block):
            out[i, 2 * units :, :] = value[:units, i * block : (i + 1) * block]

    (out,) = kernel_call(
        body,
        (width // tile,),
        row_specs(x_groups, tile)
        + row_specs(dy_groups, tile)
        + [whole(p) for p in pre_s]
        + [pl.BlockSpec((rows, apart), lambda *_: (0, weighted.shape[1] // apart - 1))],
        [pl.BlockSpec((tile // block, 3 * units, block), lambda k, *_: (k, 0, 0))],
        [shape_of(width // block, 3 * units, block)],
        [g[0] for g in x_groups + dy_groups] + list(pre_s) + [weighted],
        [
            pltpu.VMEM((rows, tile), jnp.bfloat16),
            pltpu.VMEM((wide, rows), jnp.bfloat16),
            pltpu.VMEM((apart, rows), jnp.bfloat16),
        ],
        "shadow_grads",
        earlier=earlier,
    )
    return out


def input_grads(groups, pre, tile, earlier=()):
    both = pre[0].shape[1]
    rows = sum(p.shape[0] for p in pre)
    units = both // 2
    width = groups[0][0].shape[1]
    m = len(pre)

    def body(*refs):
        n = len(groups)
        gate_ref, up_ref, held, pre_held = refs[n + m :]

        @pl.when(pl.program_id(0) == 0)
        def _():
            start = 0
            for ref in refs[n : n + m]:
                pre_held[start : start + ref.shape[0], :] = ref[...]
                start += ref.shape[0]

        value = contract_rows(stage_rows(refs[:n], groups, held), pre_held[...])
        gate_ref[...] = value[:, :units].astype(jnp.bfloat16)
        up_ref[...] = value[:, units:].astype(jnp.bfloat16)

    return kernel_call(
        body,
        (width // tile,),
        row_specs(groups, tile) + [whole(p) for p in pre],
        [pl.BlockSpec((tile, units), lambda k, *_: (k, 0))] * 2,
        [shape_of(width, units)] * 2,
        [g[0] for g in groups] + list(pre),
        [pltpu.VMEM((rows, tile), jnp.bfloat16), pltpu.VMEM((rows, both), jnp.bfloat16)],
        "input_grads",
        earlier=earlier,
    )


def down_grad(groups, weighted, units, tile, earlier=()):
    rows = weighted.shape[0]
    width = groups[0][0].shape[1]

    def body(*refs):
        n = len(groups)
        hidden_ref, out, held, hidden_t = refs[n:]

        @pl.when(pl.program_id(0) == 0)
        def _():
            hidden_t[...] = hidden_ref[...].T

        out[...] = dot32(hidden_t[...], stage_rows(refs[:n], groups, held)).astype(jnp.bfloat16)

    (out,) = kernel_call(
        body,
        (width // tile,),
        row_specs(groups, tile) + [pl.BlockSpec((rows, units), lambda *_: (0, 0))],
        [pl.BlockSpec((units, tile), lambda k, *_: (0, k))],
        [shape_of(units, width)],
        [g[0] for g in groups] + [weighted],
        [pltpu.VMEM((rows, tile), jnp.bfloat16), pltpu.VMEM((units, rows), jnp.bfloat16)],
        "down_grad",
        earlier=earlier,
    )
    return out


def send_along_z(own):
    ep_count = lax.axis_size("ep")
    return [lax.ppermute(own, "ep", swap_pairs(ep_count, 2 * s)) for s in range(1, ep_count // 2)]


def swap_cores(block):
    return lax.ppermute(block, "ep", swap_pairs(lax.axis_size("ep"), 1))


def send_plane(*pieces):
    pieces = pieces * 3 if len(pieces) == 1 else pieces
    return [lax.ppermute(p, "tp", swap_pairs(lax.axis_size("tp"), bit)) for p, bit in zip(pieces, (1, 2, 3))]


def send_diagonal(from_x, from_y):
    along, across = [swap_pairs(lax.axis_size("tp"), bit) for bit in (1, 2)]
    half = from_x.shape[0] // 2
    return [lax.ppermute(from_x[:half], "tp", across), lax.ppermute(from_y[half:], "tp", along)]


def exchange_cores(blocks, cuts=1):
    ep_count, core = lax.axis_size("ep"), lax.axis_index("ep") % 2
    pairs = blocks.reshape(ep_count // 2, 2, *blocks.shape[1:])
    kept = jnp.where(core == 0, pairs[:, 0], pairs[:, 1])
    given = jnp.where(core == 0, pairs[:, 1], pairs[:, 0])
    return kept, [swap_cores(part) for part in jnp.split(given, cuts)]


def chip_pieces(kept, taken):
    ep_count, me = lax.axis_size("ep"), lax.axis_index("ep")
    chips, chip, core = ep_count // 2, me // 2, me % 2
    taken = jnp.concatenate(taken, axis=0)
    both = jnp.stack([jnp.where(core == 0, kept, taken), jnp.where(core == 0, taken, kept)], axis=1)
    return [lax.dynamic_index_in_dim(both, chip ^ shift, 0) for shift in range(chips)]


def send_piece(piece, shift):
    return lax.ppermute(piece, "ep", swap_pairs(lax.axis_size("ep"), 2 * shift))


def dense_shards(
    tokens,
    cotangent,
    expert_ids,
    gate_weights,
    shadow_mask,
    w_gate,
    w_up,
    w_down,
    s_gate,
    s_up,
    s_down,
):
    ep_count, tp_count = lax.axis_size("ep"), lax.axis_size("tp")
    ep_index, tp_index = lax.axis_index("ep"), lax.axis_index("tp")
    tok_count, top_count = expert_ids.shape
    quarter = tokens.shape[1]
    width = quarter * tp_count
    hidden_part = w_gate.shape[2]
    shadow_part = hidden_part // ep_count
    block_width = s_gate.shape[0]
    steps = ep_count // 2
    later = (steps - 1) * tok_count
    tile = width // 8
    along, across = swap_pairs(tp_count, 1), swap_pairs(tp_count, 2)

    picked = expert_ids[None, :, :] == jnp.arange(ep_count, dtype=jnp.int32)[:, None, None]
    table = jnp.sum(jnp.where(picked, gate_weights[None, :, :top_count], 0.0), axis=2)
    shadow_weight = gate_weights[:, top_count] * shadow_mask.astype(jnp.float32)
    table = jnp.concatenate([table, jnp.broadcast_to(shadow_weight[None], table.shape)], axis=1)
    table = jnp.concatenate(split_parts(table), axis=1)
    table = jnp.pad(table[:, None, :], ((0, 0), (0, 15), (0, block_width - table.shape[1])))
    shadow_blocks = jnp.concatenate(
        [
            s_gate.T.reshape(ep_count, shadow_part, block_width),
            s_up.T.reshape(ep_count, shadow_part, block_width),
            s_down.reshape(ep_count, shadow_part, block_width),
            table,
        ],
        axis=1,
    )

    x_z = send_along_z(tokens)
    near = stack_pieces([tokens, cotangent])
    near_x, near_y = send_plane(near, near)
    near_x, near_y = after([near_x, near_y], x_z[0])
    near_d = send_diagonal(near_x, near_y)
    w_both = jnp.concatenate([w_gate[0], w_up[0]], axis=1)
    fenced = after([*near_d, *x_z], w_both, shadow_blocks)
    near_d, x_z = fenced[:2], fenced[2:]

    x_piece = stack_pieces(x_z)
    x_plane = send_plane(x_piece, x_piece)
    dy_z = send_along_z(cotangent)
    x_plane = after(x_plane, *dy_z[:2])
    x_plane = [*x_plane, *send_diagonal(*x_plane)]
    near_own = join_plane(tp_index, near, near_x, near_y, *near_d)
    near_other = swap_cores(near_own)
    x_near = [(near_own, 0, tok_count), (near_other, 0, tok_count)]
    hidden_near, slope_near, act_near = forward_rows(x_near, w_both, 2 * tile)
    spare_rows = -shadow_part % 128 + shadow_part
    down = jnp.pad(w_down[0], ((0, spare_rows), (0, 0)))
    (shadow_blocks,) = after([shadow_blocks], x_z[0])
    shadow_kept, shadow_taken = exchange_cores(shadow_blocks)
    fenced = after([*x_plane[2:], down, *shadow_taken, *dy_z], hidden_near)
    x_plane[2:], down, shadow_taken, dy_z = fenced[:2], fenced[2], fenced[3:4], fenced[4:]

    dy_piece = stack_pieces(dy_z)
    dy_plane = send_plane(dy_piece)
    shadow_pieces = chip_pieces(shadow_kept, shadow_taken)
    for shift in range(1, steps - 1):
        shadow_pieces[shift] = send_piece(shadow_pieces[shift], shift)
    x_own = join_plane(tp_index, x_piece, *x_plane, earlier=[dy_piece])
    x_other = swap_cores(x_own)
    x_far = [(x_own, 0, later), (x_other, 0, later)]
    x_groups = [x_far[0], x_near[0], x_near[1], x_far[1]]
    hidden_far, slope_far, act_far = forward_rows(x_far, w_both, 2 * tile)
    shadow_pieces[-1:] = after(shadow_pieces[-1:], hidden_far)
    shadow_pieces[-1] = send_piece(shadow_pieces[-1], steps - 1)
    chip = ep_index // 2
    shadow_in, down = lay_out_shadow(shadow_pieces, down, shadow_part, chip, earlier=[hidden_far])
    hidden_s, slope_s, act_s = forward_rows(x_groups, shadow_in, 2 * tile, transposed=True)

    weighted, w_rows, w_shadow = weigh_hidden(
        hidden_near, hidden_far, hidden_s, shadow_pieces, 3 * shadow_part, tok_count, ep_index % 2
    )

    parts = 2 if steps % 2 == 0 else 1
    sent = output_other(weighted, down, tp_index, parts, tok_count, quarter)
    got = [swap_cores(array) for array in sent]
    dy_plane = after(dy_plane, *sent)

    dy_own = join_plane(tp_index, dy_piece, *dy_plane)
    dy_other = swap_cores(dy_own)
    dy_groups = [(dy_own, 0, later), (near_own, 1, tok_count), (near_other, 1, tok_count), (dy_other, 0, later)]
    segments = [
        (slope_far, act_far, 0),
        (slope_near, act_near, 0),
        (slope_near, act_near, tok_count),
        (slope_far, act_far, later),
    ]
    per_row = (slope_s, act_s, w_rows, w_shadow)
    pre_first, pre_s_first = backward_rows(dy_groups[:3], down, segments[:3], per_row, 0, 2 * tile)
    owns = output_own(weighted, got, down, tp_index, quarter, earlier=[pre_first])
    sums = [send_plane(*own[1:]) for own in owns]
    first_rows = sum(g[2] for g in dy_groups[:3])
    pre_last, pre_s_last = backward_rows(
        dy_groups[3:], down, segments[3:], per_row, first_rows, 2 * tile, earlier=[own[1] for own in owns]
    )
    pre, pre_s = [pre_first, pre_last], [pre_s_first, pre_s_last]
    grad_s = shadow_grads(x_groups, dy_groups, pre_s, weighted, shadow_part, block_width, 2 * tile)
    grad_pieces = chip_pieces(*exchange_cores(grad_s))

    def slot_rows(i):
        part = slice(i % (steps // parts) * tok_count, (i % (steps // parts) + 1) * tok_count)
        total = owns[i * parts // steps][0][part]
        for array in sums[i * parts // steps]:
            total = total + array[part].astype(jnp.float32)
        return total

    def send_rows(piece, i):
        return lax.ppermute(piece, "ep", swap_pairs(ep_count, 2 * (i + 1)))

    early = steps // parts if parts > 1 else 0
    sums[0] = after(sums[0], grad_s)
    rows = [slot_rows(i).astype(jnp.bfloat16) for i in range(early)]
    grad_down = down_grad(dy_groups, weighted, hidden_part, 2 * tile, earlier=[*rows, grad_pieces[0]])
    rows = [send_rows(piece, i) for i, piece in enumerate(rows)]
    fenced = after([*rows, *grad_pieces[1:]], grad_down)
    rows, grad_pieces[1:] = list(fenced[:early]), fenced[early:]
    grad_gate, grad_up = input_grads(x_groups, pre, 2 * tile, earlier=[grad_pieces[1]])
    for shift in range(1, steps - 1):
        grad_pieces[shift] = send_piece(grad_pieces[shift], shift)
    fenced = after([*sums[-1], *grad_pieces[1:]], grad_gate)
    sums[-1], grad_pieces[1:] = fenced[:3], fenced[3:]
    grad_pieces[-1] = send_piece(grad_pieces[-1], steps - 1)
    rows += [send_rows(slot_rows(i).astype(jnp.bfloat16), i) for i in range(early, steps - 1)]
    total = slot_rows(steps - 1)
    for piece in rows:
        total = total + piece.astype(jnp.float32)
    mixed = total.astype(jnp.bfloat16)

    grads_s = lay_out_grads(grad_pieces, shadow_part, chip)
    return (mixed, grad_gate[None], grad_up[None], grad_down[None], *grads_s)


def shards(tokens, cotangent, expert_ids, *others):
    tp_count, ep_count = lax.axis_size("tp"), lax.axis_size("ep")
    tok_count, top_count = expert_ids.shape
    rows = (5 * tok_count * top_count) // 4
    chips = ep_count // 2
    fits = tp_count == 4 and ep_count == 2 * chips and chips & (chips - 1) == 0 and tok_count % 128 == 0
    dense = fits and ep_count * tok_count <= 3 * rows
    return (dense_shards if dense else routed_shards)(tokens, cotangent, expert_ids, *others)


def solution(mesh):
    return jax.shard_map(
        shards,
        mesh=mesh,
        in_specs=(
            P("ep", "tp"),
            P("ep", "tp"),
            P("ep", None),
            P("ep", None),
            P("ep"),
            P("ep", None, "tp"),
            P("ep", None, "tp"),
            P("ep", "tp", None),
            P("ep", "tp"),
            P("ep", "tp"),
            P("tp", "ep"),
        ),
        out_specs=(
            P("ep", "tp"),
            P("ep", None, "tp"),
            P("ep", None, "tp"),
            P("ep", "tp", None),
            P("ep", "tp"),
            P("ep", "tp"),
            P("tp", "ep"),
        ),
        check_vma=False,
    )
```

```python
import functools

import jax
import jax.numpy as jnp
from jax import lax
from jax.experimental import pallas as pl
from jax.experimental.pallas import tpu as pltpu
from jax.sharding import PartitionSpec as P


def contract_rows(left, right):
    return lax.dot_general(
        left, right, (((0,), (0,)), ((), ())), preferred_element_type=jnp.float32
    )


def split_parts(values):
    upper_part = values.astype(jnp.bfloat16)
    lower_part = (values - upper_part.astype(jnp.float32)).astype(jnp.bfloat16)
    return (upper_part, lower_part)


def weigh_rows(weight_table, rows):
    weight_upper, weight_lower = split_parts(weight_table)
    return jnp.dot(weight_upper, rows, preferred_element_type=jnp.float32) + jnp.dot(
        weight_lower, rows, preferred_element_type=jnp.float32
    )


def expert_pass(rows_x, rows_dout, weight_gate, weight_up, weight_down):
    pre_gate = jnp.dot(rows_x, weight_gate, preferred_element_type=jnp.float32)
    pre_up = jnp.dot(rows_x, weight_up, preferred_element_type=jnp.float32)
    sigmoid_gate = jax.nn.sigmoid(pre_gate)
    activated = pre_gate * sigmoid_gate
    hidden = (activated * pre_up).astype(jnp.bfloat16)
    partial_out = jnp.dot(hidden, weight_down, preferred_element_type=jnp.float32).astype(
        jnp.bfloat16
    )
    hidden_grad = lax.dot_general(
        rows_dout, weight_down, (((1,), (1,)), ((), ())), preferred_element_type=jnp.float32
    )
    grad_pre_gate = (
        hidden_grad * pre_up * sigmoid_gate * (1.0 + pre_gate * (1.0 - sigmoid_gate))
    ).astype(jnp.bfloat16)
    grad_pre_up = (hidden_grad * activated).astype(jnp.bfloat16)
    return (partial_out, hidden, grad_pre_gate, grad_pre_up)


def routed_shards(
    tokens,
    cotangent,
    expert_ids,
    gate_weights,
    shadow_mask,
    w_gate,
    w_up,
    w_down,
    s_gate,
    s_up,
    s_down,
):
    ep_count = lax.axis_size("ep")
    tok_count, top_count = expert_ids.shape
    quarter_width = tokens.shape[1]
    width = quarter_width * lax.axis_size("tp")
    expert_count = w_gate.shape[0] * ep_count
    capacity = (5 * tok_count * top_count + 4 * expert_count - 1) // (4 * expert_count)
    slot_count = expert_count * capacity
    picks_flat = expert_ids.reshape(-1)
    onehot = (picks_flat[:, None] == jnp.arange(expert_count, dtype=jnp.int32)[None, :]).astype(
        jnp.int32
    )
    slot_rank = jnp.sum((jnp.cumsum(onehot, axis=0) - onehot) * onehot, axis=1)
    slot_index = (picks_flat * capacity + slot_rank).reshape(tok_count, top_count)
    matches = jnp.arange(slot_count, dtype=jnp.int32)[:, None, None] == slot_index[None, :, :]
    dispatch = jnp.any(matches, axis=2).astype(jnp.bfloat16)
    weighting = jnp.sum(jnp.where(matches, gate_weights[None, :, :top_count], 0.0), axis=2)
    slot_gate = jnp.sum(weighting, axis=1)
    shadow_weight = gate_weights[:, top_count] * shadow_mask.astype(jnp.float32)
    x_full, dy_full = (
        lax.all_gather(tokens, "tp", axis=1, tiled=True),
        lax.all_gather(cotangent, "tp", axis=1, tiled=True),
    )
    rows_x = jnp.dot(dispatch, tokens, preferred_element_type=jnp.float32).astype(jnp.bfloat16)
    rows_dy = jnp.dot(dispatch, cotangent, preferred_element_type=jnp.float32)
    rows_dout = (slot_gate[:, None] * rows_dy).astype(jnp.bfloat16)
    recv_x, recv_dout = (
        lax.all_to_all(
            rows_x.reshape(ep_count, -1, quarter_width),
            "ep",
            split_axis=0,
            concat_axis=0,
            tiled=True,
        ),
        lax.all_to_all(
            rows_dout.reshape(ep_count, -1, quarter_width),
            "ep",
            split_axis=0,
            concat_axis=0,
            tiled=True,
        ),
    )
    expert_x, expert_dout = (
        lax.all_gather(recv_x.reshape(-1, quarter_width), "tp", axis=1, tiled=True),
        lax.all_gather(recv_dout.reshape(-1, quarter_width), "tp", axis=1, tiled=True),
    )
    partial_out, hidden, grad_pre_gate, grad_pre_up = expert_pass(
        expert_x, expert_dout, w_gate[0], w_up[0], w_down[0]
    )
    grad_gate = contract_rows(expert_x, grad_pre_gate).astype(jnp.bfloat16)[None]
    grad_up = contract_rows(expert_x, grad_pre_up).astype(jnp.bfloat16)[None]
    grad_down = contract_rows(hidden, expert_dout).astype(jnp.bfloat16)[None]
    full_gate, full_up, full_down = (
        lax.all_gather(s_gate, "ep", axis=0, tiled=True),
        lax.all_gather(s_up, "ep", axis=0, tiled=True),
        lax.all_gather(s_down, "ep", axis=1, tiled=True),
    )
    shadow_dout = (shadow_weight[:, None] * dy_full.astype(jnp.float32)).astype(jnp.bfloat16)
    shadow_out, shadow_hidden, shadow_gate_pre, shadow_up_pre = expert_pass(
        x_full, shadow_dout, full_gate, full_up, full_down
    )
    shadow_sums = lax.psum_scatter(
        jnp.concatenate(
            [
                contract_rows(x_full, shadow_gate_pre),
                contract_rows(x_full, shadow_up_pre),
                contract_rows(shadow_dout, shadow_hidden),
            ],
            axis=1,
        ).astype(jnp.bfloat16),
        "ep",
        scatter_dimension=0,
        tiled=True,
    ).astype(jnp.float32)
    hidden_part = s_gate.shape[1]
    grad_s_gate = shadow_sums[:, :hidden_part].astype(jnp.bfloat16)
    grad_s_up = shadow_sums[:, hidden_part : 2 * hidden_part].astype(jnp.bfloat16)
    grad_s_down = shadow_sums[:, 2 * hidden_part :].T.astype(jnp.bfloat16)
    back_rows = lax.all_to_all(
        partial_out.reshape(ep_count, -1, width), "ep", split_axis=0, concat_axis=0, tiled=True
    ).reshape(-1, width)
    term = weigh_rows(weighting.T, back_rows)
    term = term + shadow_weight[:, None] * shadow_out.astype(jnp.float32)
    mixed = lax.psum_scatter(term.astype(jnp.bfloat16), "tp", scatter_dimension=1, tiled=True)
    return (mixed, grad_gate, grad_up, grad_down, grad_s_gate, grad_s_up, grad_s_down)


ANY = pl.BlockSpec(memory_space=pl.ANY)
VMEM_LIMIT = 60 * 1024 * 1024
SHORT = pl.CostEstimate(flops=1, bytes_accessed=1, transcendentals=0)


def swap_pairs(count, bit):
    return [(i, i ^ bit) for i in range(count)]


def dot32(left, right):
    return jnp.dot(left, right, preferred_element_type=jnp.float32)


def contract_last(left, right):
    return lax.dot_general(
        left, right, (((1,), (1,)), ((), ())), preferred_element_type=jnp.float32
    )


def shape_of(*dims, dtype=jnp.bfloat16):
    return jax.ShapeDtypeStruct(dims, dtype)


def after(arrays, *earlier):
    def nothing(*refs):
        del refs

    count = len(arrays)
    return pl.pallas_call(
        nothing,
        out_shape=[jax.ShapeDtypeStruct(a.shape, a.dtype) for a in arrays],
        in_specs=[ANY] * (count + len(earlier)),
        out_specs=[ANY] * count,
        input_output_aliases={i: i for i in range(count)},
        compiler_params=pltpu.CompilerParams(vmem_limit_bytes=VMEM_LIMIT),
        cost_estimate=SHORT,
        name="after",
    )(*arrays, *earlier)


def kernel_call(body, grid, in_specs, out_specs, out_shape, operands, scratch, name, column=None, earlier=()):
    count = len(operands)

    def run(column_ref, *refs):
        del column_ref
        body(*refs[:count], *refs[count + len(earlier) :])

    column = jnp.zeros((1,), jnp.int32) if column is None else column.reshape(1).astype(jnp.int32)
    return pl.pallas_call(
        run,
        out_shape=out_shape,
        grid_spec=pltpu.PrefetchScalarGridSpec(
            num_scalar_prefetch=1,
            grid=grid,
            in_specs=list(in_specs) + [ANY] * len(earlier),
            out_specs=out_specs,
            scratch_shapes=scratch,
        ),
        compiler_params=pltpu.CompilerParams(vmem_limit_bytes=VMEM_LIMIT),
        cost_estimate=SHORT,
        name=name,
    )(column, *operands, *earlier)


def whole(array):
    return pl.BlockSpec(array.shape, lambda *_: (0,) * len(array.shape))


def join_plane(column, *pieces, earlier=()):
    rows, quarter = pieces[0].shape
    count, halves = 4, len(pieces) - 3
    chunk = rows // 4
    per = 4 // halves

    def body(column_ref, *refs):
        out = refs[-1]
        for own_column in range(count):
            for j, from_diagonal in enumerate(refs[3 : 3 + halves]):

                @pl.when((column_ref[0] == own_column) & (pl.program_id(0) // per == j))
                def _(from_diagonal=from_diagonal, own_column=own_column):
                    for bit, source in enumerate(refs[:3] + (from_diagonal,)):
                        place = own_column ^ bit
                        out[:, place * quarter : (place + 1) * quarter] = source[...]

    def diagonal_spec(j):
        return pl.BlockSpec((chunk, quarter), lambda i, *_: (jnp.clip(i - j * per, 0, per - 1), 0))

    return pl.pallas_call(
        body,
        out_shape=shape_of(rows, count * quarter),
        grid_spec=pltpu.PrefetchScalarGridSpec(
            num_scalar_prefetch=1,
            grid=(4,),
            in_specs=[pl.BlockSpec((chunk, quarter), lambda i, *_: (i, 0))] * 3
            + [diagonal_spec(j) for j in range(halves)]
            + [ANY] * len(earlier),
            out_specs=pl.BlockSpec((chunk, count * quarter), lambda i, *_: (i, 0)),
        ),
        compiler_params=pltpu.CompilerParams(vmem_limit_bytes=VMEM_LIMIT),
        cost_estimate=SHORT,
        name="join_plane",
    )(column.reshape(1).astype(jnp.int32), *pieces, *earlier)


def stack_pieces(pieces, earlier=()):
    rows, columns = pieces[0].shape
    count = len(pieces)

    def body(*refs):
        for i, ref in enumerate(refs[:count]):

            @pl.when(pl.program_id(0) == i)
            def _():
                refs[-1][...] = ref[...]

    return pl.pallas_call(
        body,
        out_shape=shape_of(count * rows, columns),
        grid=(count,),
        in_specs=[pl.BlockSpec((rows, columns), lambda i: (0, 0))] * count + [ANY] * len(earlier),
        out_specs=pl.BlockSpec((rows, columns), lambda i: (i, 0)),
        compiler_params=pltpu.CompilerParams(vmem_limit_bytes=VMEM_LIMIT),
        cost_estimate=SHORT,
        name="stack_pieces",
    )(*pieces, *earlier)


def on_piece(chip_ref, refs, use):
    step = pl.program_id(0)
    shift = chip_ref[0] ^ (step // 2)
    for i, ref in enumerate(refs):
        for core in range(2):

            @pl.when((shift == i) & (lax.rem(step, 2) == core))
            def _(ref=ref, core=core):
                use(ref.at[0, core])


def lay_out_shadow(pieces, down, units, chip, earlier=()):
    count = len(pieces)
    ep_count = 2 * count
    block_width = pieces[0].shape[3]
    apart = units + -units % 128
    all_units, width = down.shape

    def body(chip_ref, *refs):
        shadow_ref, out = refs[-2:]

        def use(ref):
            shadow_ref[...] = jnp.zeros_like(shadow_ref)
            shadow_ref[:units, :] = ref[:units, :]
            shadow_ref[apart : apart + units, :] = ref[units : 2 * units, :]
            out[units:, :] = jnp.zeros((apart - units, block_width), jnp.bfloat16)
            out[:units, :] = ref[2 * units : 3 * units, :]

        on_piece(chip_ref, refs[:count], use)

    return pl.pallas_call(
        body,
        out_shape=[shape_of(2 * apart, width), shape_of(all_units, width)],
        grid_spec=pltpu.PrefetchScalarGridSpec(
            num_scalar_prefetch=1,
            grid=(ep_count,),
            in_specs=[whole(p) for p in pieces] + [ANY] * (1 + len(earlier)),
            out_specs=[
                pl.BlockSpec((2 * apart, block_width), lambda e, *_: (0, e)),
                pl.BlockSpec((apart, block_width), lambda e, *_: (all_units // apart - 1, e)),
            ],
        ),
        input_output_aliases={1 + count: 1},
        compiler_params=pltpu.CompilerParams(vmem_limit_bytes=VMEM_LIMIT),
        cost_estimate=SHORT,
        name="lay_out_shadow",
    )(chip.reshape(1).astype(jnp.int32), *pieces, down, *earlier)


def lay_out_grads(pieces, units, chip, earlier=()):
    count = len(pieces)
    ep_count = 2 * count
    block_width = pieces[0].shape[3]
    hidden = ep_count * units

    def body(chip_ref, *refs):
        gate_ref, up_ref, down_ref, gate_t, up_t = refs[-5:]
        place = pl.ds(pl.multiple_of(pl.program_id(0) * units, 16), units)

        def use(ref):
            gate_t[place, :] = ref[:units, :]
            up_t[place, :] = ref[units : 2 * units, :]
            down_ref[place, :] = ref[2 * units :, :]

        on_piece(chip_ref, refs[:count], use)

        @pl.when(pl.program_id(0) == ep_count - 1)
        def _():
            gate_ref[...] = gate_t[...].T
            up_ref[...] = up_t[...].T

    return pl.pallas_call(
        body,
        out_shape=[shape_of(block_width, hidden), shape_of(block_width, hidden), shape_of(hidden, block_width)],
        grid_spec=pltpu.PrefetchScalarGridSpec(
            num_scalar_prefetch=1,
            grid=(ep_count,),
            in_specs=[whole(p) for p in pieces] + [ANY] * len(earlier),
            out_specs=[pl.BlockSpec((block_width, hidden), lambda *_: (0, 0))] * 2
            + [pl.BlockSpec((hidden, block_width), lambda *_: (0, 0))],
            scratch_shapes=[pltpu.VMEM((hidden, block_width), jnp.bfloat16)] * 2,
        ),
        compiler_params=pltpu.CompilerParams(vmem_limit_bytes=VMEM_LIMIT),
        cost_estimate=SHORT,
        name="lay_out_grads",
    )(chip.reshape(1).astype(jnp.int32), *pieces, *earlier)


def row_specs(groups, tile):
    def spec(index, rows):
        return pl.BlockSpec((rows, tile), lambda k, *_: (index, k))

    return [spec(index, rows) for _, index, rows in groups]


def apply_gate(pre_gate, pre_up):
    sigmoid_gate = jax.nn.sigmoid(pre_gate)
    activated = pre_gate * sigmoid_gate
    hidden = (activated * pre_up).astype(jnp.bfloat16)
    return hidden, pre_up * sigmoid_gate * (1.0 + pre_gate * (1.0 - sigmoid_gate)), activated


def clear_first(acc):
    @pl.when(pl.program_id(0) == 0)
    def _():
        acc[...] = jnp.zeros_like(acc)


def rows_operand(refs, groups, held):
    if len(groups) == 1:
        return refs[0][...]
    return stage_rows(refs, groups, held)


def forward_rows(groups, w_both, tile, transposed=False, earlier=()):
    rows = sum(g[2] for g in groups)
    if transposed:
        units, width = w_both.shape[0] // 2, w_both.shape[1]
        tile_spec = pl.BlockSpec((2 * units, tile), lambda k, *_: (0, k))
    else:
        width, units = w_both.shape[0], w_both.shape[1] // 2
        tile_spec = pl.BlockSpec((tile, 2 * units), lambda k, *_: (k, 0))
    steps = width // tile

    def body(*refs):
        n = len(groups)
        both_ref, hidden_ref, slope_ref, act_ref, acc, held = refs[n:]
        clear_first(acc)
        operand = rows_operand(refs[:n], groups, held)
        acc[...] += contract_last(operand, both_ref[...]) if transposed else dot32(operand, both_ref[...])

        @pl.when(pl.program_id(0) == steps - 1)
        def _():
            chunk = 128

            @pl.loop(0, rows // chunk)
            def _(i):
                part = pl.ds(pl.multiple_of(i * chunk, chunk), chunk)
                hidden, slope, act = apply_gate(acc[part, :units], acc[part, units:])
                hidden_ref[part, :] = hidden
                slope_ref[part, :] = slope.astype(jnp.bfloat16)
                act_ref[part, :] = act.astype(jnp.bfloat16)

    out_spec = pl.BlockSpec((rows, units), lambda *_: (0, 0))
    return kernel_call(
        body,
        (steps,),
        row_specs(groups, tile) + [tile_spec],
        [out_spec] * 3,
        [shape_of(rows, units)] * 3,
        [g[0] for g in groups] + [w_both],
        [pltpu.VMEM((rows, 2 * units), jnp.float32), pltpu.VMEM((rows, tile), jnp.bfloat16)],
        "forward_rows",
        earlier=earlier,
    )


def weigh_hidden(hidden_near, hidden_far, hidden_s, pieces, first_row, slot_rows, core, earlier=()):
    count = len(pieces)
    rows, units_s = hidden_s.shape
    units = hidden_near.shape[1]
    slots = [(s, 0) for s in list(range(1, count)) + [0]] + [(s, 1) for s in range(count)]

    def body(core_ref, *refs):
        near_ref, far_ref, s_ref, *piece_refs = refs[: 3 + count]
        out, w_ref, w_s_ref = refs[-3:]
        near, far = 0, 0
        for i, (slot, other) in enumerate(slots):
            part = pl.ds(i * slot_rows, slot_rows)
            table = piece_refs[slot][0, core_ref[0] ^ other, first_row : first_row + 16, :][:1].astype(jnp.float32)

            def column(j):
                both = table[:, j * slot_rows : (j + 1) * slot_rows]
                both = both + table[:, (j + 2) * slot_rows : (j + 3) * slot_rows]
                return jnp.broadcast_to(both, (slot_rows, slot_rows)).T[:, :1]

            weight, weight_s = column(0), column(1)
            w_ref[part, :] = weight
            w_s_ref[part, :] = weight_s
            if slot == 0:
                hidden = near_ref[near : near + slot_rows, :]
                near += slot_rows
            else:
                hidden = far_ref[far : far + slot_rows, :]
                far += slot_rows
            out[part, :units] = (hidden.astype(jnp.float32) * weight).astype(jnp.bfloat16)
            out[part, units:] = (s_ref[part, :].astype(jnp.float32) * weight_s).astype(jnp.bfloat16)

    return pl.pallas_call(
        body,
        out_shape=[
            shape_of(rows, units + units_s),
            shape_of(rows, 1, dtype=jnp.float32),
            shape_of(rows, 1, dtype=jnp.float32),
        ],
        grid_spec=pltpu.PrefetchScalarGridSpec(
            num_scalar_prefetch=1,
            grid=(1,),
            in_specs=[whole(a) for a in (hidden_near, hidden_far, hidden_s, *pieces)] + [ANY] * len(earlier),
            out_specs=[
                pl.BlockSpec((rows, units + units_s), lambda *_: (0, 0)),
                pl.BlockSpec((rows, 1), lambda *_: (0, 0)),
                pl.BlockSpec((rows, 1), lambda *_: (0, 0)),
            ],
        ),
        compiler_params=pltpu.CompilerParams(vmem_limit_bytes=VMEM_LIMIT),
        cost_estimate=SHORT,
        name="weigh_hidden",
    )(core.reshape(1).astype(jnp.int32), hidden_near, hidden_far, hidden_s, *pieces, *earlier)


def output_other(weighted, down, column, parts, slot_rows, quarter, earlier=()):
    rows, units = weighted.shape
    count = rows // 2 // parts

    def body(weighted_ref, down_ref, *outs):
        value = dot32(weighted_ref[...], down_ref[...]).astype(jnp.bfloat16)
        for i, out in enumerate(outs):
            first, last = slot_rows + i * count, slot_rows + (i + 1) * count
            kept = min(last, rows // 2) - first
            out[:kept, :] = value[first : first + kept]
            if kept < count:
                out[kept:, :] = value[: count - kept]

    return kernel_call(
        body,
        (4,),
        [
            pl.BlockSpec((rows // 2, units), lambda *_: (1, 0)),
            pl.BlockSpec((units, quarter), lambda q, column_ref: (0, column_ref[0] ^ q)),
        ],
        [pl.BlockSpec((count, quarter), lambda q, *_: (0, q))] * parts,
        [shape_of(count, 4 * quarter)] * parts,
        [weighted, down],
        [],
        "output_other",
        column=column,
        earlier=earlier,
    )


def output_own(weighted, got, down, column, quarter, earlier=()):
    count, units = got[0].shape[0], weighted.shape[1]
    parts = len(got)

    def body(weighted_ref, down_ref, *refs):
        product = dot32(weighted_ref[...], down_ref[...])
        for i in range(parts):
            value = product[i * count : (i + 1) * count] + refs[i][...].astype(jnp.float32)
            for j, out in enumerate(refs[parts + 4 * i : parts + 4 * i + 4]):

                @pl.when(pl.program_id(0) == 3 - j)
                def _(out=out, value=value):
                    out[...] = value.astype(out.dtype)

    full = pl.BlockSpec((count, quarter), lambda *_: (0, 0))
    out = kernel_call(
        body,
        (4,),
        [
            pl.BlockSpec((parts * count, units), lambda *_: (0, 0)),
            pl.BlockSpec((units, quarter), lambda q, column_ref: (0, column_ref[0] ^ 3 ^ q)),
        ]
        + [pl.BlockSpec((count, quarter), lambda q, *_: (0, 3 - q))] * parts,
        [full] * (4 * parts),
        ([shape_of(count, quarter, dtype=jnp.float32)] + [shape_of(count, quarter)] * 3) * parts,
        [weighted, down] + list(got),
        [],
        "output_own",
        column=column,
        earlier=earlier,
    )
    return [out[4 * i : 4 * i + 4] for i in range(parts)]


def backward_rows(groups, down, parts, per_row, first_row, tile, earlier=()):
    slope_s, act_s, w_rows, w_shadow = per_row
    rows = sum(g[2] for g in groups)
    units_all, width = down.shape
    units_s = slope_s.shape[1]
    units = units_all - units_s
    steps = width // tile
    arrays = list({id(a): a for part in parts for a in part[:2]}.values())
    places = [[next(i for i, a in enumerate(arrays) if a is b) for b in part[:2]] for part in parts]

    def body(*refs):
        n, m = len(groups), len(arrays)
        down_ref = refs[n]
        array_refs = refs[n + 1 : n + 1 + m]
        slope_s_ref, act_s_ref, w_ref, w_s_ref, pre_ref, pre_s_ref, acc, held = refs[n + 1 + m :]
        clear_first(acc)
        acc[...] += contract_last(rows_operand(refs[:n], groups, held), down_ref[...])

        @pl.when(pl.program_id(0) == steps - 1)
        def _():
            chunk = 128
            start = 0
            for (_, _, count), (_, _, first), (slope_at, act_at) in zip(groups, parts, places):

                @pl.loop(0, count // chunk)
                def _(i, start=start, first=first, slope_ref=array_refs[slope_at], act_ref=array_refs[act_at]):
                    source = pl.ds(pl.multiple_of(first + i * chunk, chunk), chunk)
                    part = pl.ds(pl.multiple_of(start + i * chunk, chunk), chunk)
                    whole_part = pl.ds(pl.multiple_of(first_row + start + i * chunk, chunk), chunk)
                    grad = acc[part, :units] * w_ref[whole_part, :]
                    pre_ref[part, :units] = (grad * slope_ref[source, :]).astype(jnp.bfloat16)
                    pre_ref[part, units:] = (grad * act_ref[source, :]).astype(jnp.bfloat16)
                    grad = acc[part, units:] * w_s_ref[whole_part, :]
                    pre_s_ref[part, :units_s] = (grad * slope_s_ref[whole_part, :]).astype(jnp.bfloat16)
                    pre_s_ref[part, units_s:] = (grad * act_s_ref[whole_part, :]).astype(jnp.bfloat16)

                start += count

    extra = arrays + [slope_s, act_s, w_rows, w_shadow]
    return kernel_call(
        body,
        (steps,),
        row_specs(groups, tile) + [pl.BlockSpec((units_all, tile), lambda k, *_: (0, k))] + [whole(a) for a in extra],
        [pl.BlockSpec((rows, 2 * units), lambda *_: (0, 0)), pl.BlockSpec((rows, 2 * units_s), lambda *_: (0, 0))],
        [shape_of(rows, 2 * units), shape_of(rows, 2 * units_s)],
        [g[0] for g in groups] + [down] + extra,
        [pltpu.VMEM((rows, units_all), jnp.float32), pltpu.VMEM((rows, tile), jnp.bfloat16)],
        "backward_rows",
        earlier=earlier,
    )


def stage_rows(refs, groups, held):
    start = 0
    for ref, (_, _, count) in zip(refs, groups):
        held[pl.ds(start, count), :] = ref[...]
        start += count
    return held[...]


def shadow_grads(x_groups, dy_groups, pre_s, weighted, units, block, tile, earlier=()):
    rows, wide = weighted.shape[0], pre_s[0].shape[1]
    apart = wide // 2
    width = x_groups[0][0].shape[1]
    m = len(pre_s)

    def body(*refs):
        n = len(x_groups)
        pre_refs = refs[2 * n : 2 * n + m]
        hidden_ref, out, held, pre_t, hidden_t = refs[2 * n + m :]

        @pl.when(pl.program_id(0) == 0)
        def _():
            start = 0
            for ref in pre_refs:
                pre_t[:, start : start + ref.shape[0]] = ref[...].T
                start += ref.shape[0]
            hidden_t[...] = hidden_ref[...].T

        value = dot32(pre_t[...], stage_rows(refs[:n], x_groups, held)).astype(jnp.bfloat16)
        for i in range(tile // block):
            part = slice(i * block, (i + 1) * block)
            out[i, :units, :] = value[:units, part]
            out[i, units : 2 * units, :] = value[apart : apart + units, part]
        value = dot32(hidden_t[...], stage_rows(refs[n : 2 * n], dy_groups, held)).astype(jnp.bfloat16)
        for i in range(tile // block):
            out[i, 2 * units :, :] = value[:units, i * block : (i + 1) * block]

    (out,) = kernel_call(
        body,
        (width // tile,),
        row_specs(x_groups, tile)
        + row_specs(dy_groups, tile)
        + [whole(p) for p in pre_s]
        + [pl.BlockSpec((rows, apart), lambda *_: (0, weighted.shape[1] // apart - 1))],
        [pl.BlockSpec((tile // block, 3 * units, block), lambda k, *_: (k, 0, 0))],
        [shape_of(width // block, 3 * units, block)],
        [g[0] for g in x_groups + dy_groups] + list(pre_s) + [weighted],
        [
            pltpu.VMEM((rows, tile), jnp.bfloat16),
            pltpu.VMEM((wide, rows), jnp.bfloat16),
            pltpu.VMEM((apart, rows), jnp.bfloat16),
        ],
        "shadow_grads",
        earlier=earlier,
    )
    return out


def input_grads(groups, pre, tile, earlier=()):
    both = pre[0].shape[1]
    rows = sum(p.shape[0] for p in pre)
    units = both // 2
    width = groups[0][0].shape[1]
    m = len(pre)

    def body(*refs):
        n = len(groups)
        gate_ref, up_ref, held, pre_held = refs[n + m :]

        @pl.when(pl.program_id(0) == 0)
        def _():
            start = 0
            for ref in refs[n : n + m]:
                pre_held[start : start + ref.shape[0], :] = ref[...]
                start += ref.shape[0]

        value = contract_rows(stage_rows(refs[:n], groups, held), pre_held[...])
        gate_ref[...] = value[:, :units].astype(jnp.bfloat16)
        up_ref[...] = value[:, units:].astype(jnp.bfloat16)

    return kernel_call(
        body,
        (width // tile,),
        row_specs(groups, tile) + [whole(p) for p in pre],
        [pl.BlockSpec((tile, units), lambda k, *_: (k, 0))] * 2,
        [shape_of(width, units)] * 2,
        [g[0] for g in groups] + list(pre),
        [pltpu.VMEM((rows, tile), jnp.bfloat16), pltpu.VMEM((rows, both), jnp.bfloat16)],
        "input_grads",
        earlier=earlier,
    )


def down_grad(groups, weighted, units, tile, earlier=()):
    rows = weighted.shape[0]
    width = groups[0][0].shape[1]

    def body(*refs):
        n = len(groups)
        hidden_ref, out, held, hidden_t = refs[n:]

        @pl.when(pl.program_id(0) == 0)
        def _():
            hidden_t[...] = hidden_ref[...].T

        out[...] = dot32(hidden_t[...], stage_rows(refs[:n], groups, held)).astype(jnp.bfloat16)

    (out,) = kernel_call(
        body,
        (width // tile,),
        row_specs(groups, tile) + [pl.BlockSpec((rows, units), lambda *_: (0, 0))],
        [pl.BlockSpec((units, tile), lambda k, *_: (0, k))],
        [shape_of(units, width)],
        [g[0] for g in groups] + [weighted],
        [pltpu.VMEM((rows, tile), jnp.bfloat16), pltpu.VMEM((units, rows), jnp.bfloat16)],
        "down_grad",
        earlier=earlier,
    )
    return out


def send_along_z(own):
    ep_count = lax.axis_size("ep")
    return [lax.ppermute(own, "ep", swap_pairs(ep_count, 2 * s)) for s in range(1, ep_count // 2)]


def swap_cores(block):
    return lax.ppermute(block, "ep", swap_pairs(lax.axis_size("ep"), 1))


def send_plane(*pieces):
    pieces = pieces * 3 if len(pieces) == 1 else pieces
    return [lax.ppermute(p, "tp", swap_pairs(lax.axis_size("tp"), bit)) for p, bit in zip(pieces, (1, 2, 3))]


def send_diagonal(from_x, from_y):
    along, across = [swap_pairs(lax.axis_size("tp"), bit) for bit in (1, 2)]
    half = from_x.shape[0] // 2
    return [lax.ppermute(from_x[:half], "tp", across), lax.ppermute(from_y[half:], "tp", along)]


def exchange_cores(blocks, cuts=1):
    ep_count, core = lax.axis_size("ep"), lax.axis_index("ep") % 2
    pairs = blocks.reshape(ep_count // 2, 2, *blocks.shape[1:])
    kept = jnp.where(core == 0, pairs[:, 0], pairs[:, 1])
    given = jnp.where(core == 0, pairs[:, 1], pairs[:, 0])
    return kept, [swap_cores(part) for part in jnp.split(given, cuts)]


def chip_pieces(kept, taken):
    ep_count, me = lax.axis_size("ep"), lax.axis_index("ep")
    chips, chip, core = ep_count // 2, me // 2, me % 2
    taken = jnp.concatenate(taken, axis=0)
    both = jnp.stack([jnp.where(core == 0, kept, taken), jnp.where(core == 0, taken, kept)], axis=1)
    return [lax.dynamic_index_in_dim(both, chip ^ shift, 0) for shift in range(chips)]


def send_piece(piece, shift):
    return lax.ppermute(piece, "ep", swap_pairs(lax.axis_size("ep"), 2 * shift))


def dense_shards(
    tokens,
    cotangent,
    expert_ids,
    gate_weights,
    shadow_mask,
    w_gate,
    w_up,
    w_down,
    s_gate,
    s_up,
    s_down,
):
    ep_count, tp_count = lax.axis_size("ep"), lax.axis_size("tp")
    ep_index, tp_index = lax.axis_index("ep"), lax.axis_index("tp")
    tok_count, top_count = expert_ids.shape
    quarter = tokens.shape[1]
    width = quarter * tp_count
    hidden_part = w_gate.shape[2]
    shadow_part = hidden_part // ep_count
    block_width = s_gate.shape[0]
    steps = ep_count // 2
    later = (steps - 1) * tok_count
    tile = width // 8
    along, across = swap_pairs(tp_count, 1), swap_pairs(tp_count, 2)

    picked = expert_ids[None, :, :] == jnp.arange(ep_count, dtype=jnp.int32)[:, None, None]
    table = jnp.sum(jnp.where(picked, gate_weights[None, :, :top_count], 0.0), axis=2)
    shadow_weight = gate_weights[:, top_count] * shadow_mask.astype(jnp.float32)
    table = jnp.concatenate([table, jnp.broadcast_to(shadow_weight[None], table.shape)], axis=1)
    table = jnp.concatenate(split_parts(table), axis=1)
    table = jnp.pad(table[:, None, :], ((0, 0), (0, 15), (0, block_width - table.shape[1])))
    shadow_blocks = jnp.concatenate(
        [
            s_gate.T.reshape(ep_count, shadow_part, block_width),
            s_up.T.reshape(ep_count, shadow_part, block_width),
            s_down.reshape(ep_count, shadow_part, block_width),
            table,
        ],
        axis=1,
    )

    x_z = send_along_z(tokens)
    near = stack_pieces([tokens, cotangent])
    near_x, near_y = send_plane(near, near)
    near_x, near_y = after([near_x, near_y], x_z[0])
    near_d = send_diagonal(near_x, near_y)
    w_both = jnp.concatenate([w_gate[0], w_up[0]], axis=1)
    fenced = after([*near_d, *x_z], w_both, shadow_blocks)
    near_d, x_z = fenced[:2], fenced[2:]

    x_piece = stack_pieces(x_z)
    x_plane = send_plane(x_piece, x_piece)
    dy_z = send_along_z(cotangent)
    near_own = join_plane(tp_index, near, near_x, near_y, *near_d)
    near_other = swap_cores(near_own)
    x_near = [(near_own, 0, tok_count), (near_other, 0, tok_count)]
    hidden_near, slope_near, act_near = forward_rows(x_near, w_both, 2 * tile)
    spare_rows = -shadow_part % 128 + shadow_part
    down = jnp.pad(w_down[0], ((0, spare_rows), (0, 0)))
    *x_plane, down = after([*x_plane, down], *dy_z[:2], hidden_near)
    x_plane = [*x_plane, *send_diagonal(*x_plane)]
    (shadow_blocks,) = after([shadow_blocks], x_z[0])
    shadow_kept, shadow_taken = exchange_cores(shadow_blocks)
    shadow_pieces = chip_pieces(shadow_kept, shadow_taken)
    shadow_pieces[1] = send_piece(shadow_pieces[1], 1)
    fenced = after([*x_plane[2:], *shadow_pieces[1:], *dy_z])
    x_plane[2:], shadow_pieces[1:], dy_z = fenced[:2], fenced[2 : 1 + steps], fenced[1 + steps :]

    dy_piece = stack_pieces(dy_z)
    dy_plane = send_plane(dy_piece)
    for shift in range(2, steps - 1):
        shadow_pieces[shift] = send_piece(shadow_pieces[shift], shift)
    x_own = join_plane(tp_index, x_piece, *x_plane, earlier=[dy_piece])
    x_other = swap_cores(x_own)
    x_far = [(x_own, 0, later), (x_other, 0, later)]
    x_groups = [x_far[0], x_near[0], x_near[1], x_far[1]]
    hidden_far, slope_far, act_far = forward_rows(x_far, w_both, 2 * tile)
    shadow_pieces[-1:] = after(shadow_pieces[-1:], hidden_far)
    shadow_pieces[-1] = send_piece(shadow_pieces[-1], steps - 1)
    chip = ep_index // 2
    shadow_in, down = lay_out_shadow(shadow_pieces, down, shadow_part, chip, earlier=[hidden_far])
    hidden_s, slope_s, act_s = forward_rows(x_groups, shadow_in, 2 * tile, transposed=True)

    weighted, w_rows, w_shadow = weigh_hidden(
        hidden_near, hidden_far, hidden_s, shadow_pieces, 3 * shadow_part, tok_count, ep_index % 2
    )

    parts = 2 if steps % 2 == 0 else 1
    sent = output_other(weighted, down, tp_index, parts, tok_count, quarter)
    got = [swap_cores(array) for array in sent]
    dy_plane = after(dy_plane, *sent)

    dy_own = join_plane(tp_index, dy_piece, *dy_plane)
    dy_other = swap_cores(dy_own)
    dy_groups = [(dy_own, 0, later), (near_own, 1, tok_count), (near_other, 1, tok_count), (dy_other, 0, later)]
    segments = [
        (slope_far, act_far, 0),
        (slope_near, act_near, 0),
        (slope_near, act_near, tok_count),
        (slope_far, act_far, later),
    ]
    per_row = (slope_s, act_s, w_rows, w_shadow)
    pre_first, pre_s_first = backward_rows(dy_groups[:3], down, segments[:3], per_row, 0, 2 * tile)
    owns = output_own(weighted, got, down, tp_index, quarter, earlier=[pre_first])
    sums = [send_plane(*own[1:]) for own in owns]
    first_rows = sum(g[2] for g in dy_groups[:3])
    pre_last, pre_s_last = backward_rows(
        dy_groups[3:], down, segments[3:], per_row, first_rows, 2 * tile, earlier=[own[1] for own in owns]
    )
    pre, pre_s = [pre_first, pre_last], [pre_s_first, pre_s_last]
    grad_s = shadow_grads(x_groups, dy_groups, pre_s, weighted, shadow_part, block_width, 2 * tile)
    grad_pieces = chip_pieces(*exchange_cores(grad_s))

    def slot_rows(i):
        part = slice(i % (steps // parts) * tok_count, (i % (steps // parts) + 1) * tok_count)
        total = owns[i * parts // steps][0][part]
        for array in sums[i * parts // steps]:
            total = total + array[part].astype(jnp.float32)
        return total

    def send_rows(piece, i):
        return lax.ppermute(piece, "ep", swap_pairs(ep_count, 2 * (i + 1)))

    early = steps // parts if parts > 1 else 0
    sums[0] = after(sums[0], grad_s)
    rows = [slot_rows(i).astype(jnp.bfloat16) for i in range(early)]
    grad_down = down_grad(dy_groups, weighted, hidden_part, 2 * tile, earlier=[*rows, grad_pieces[0]])
    rows = [send_rows(piece, i) for i, piece in enumerate(rows)]
    fenced = after([*rows, *grad_pieces[1:]], grad_down)
    rows, grad_pieces[1:] = list(fenced[:early]), fenced[early:]
    grad_gate, grad_up = input_grads(x_groups, pre, 2 * tile, earlier=[grad_pieces[1]])
    for shift in range(1, steps - 1):
        grad_pieces[shift] = send_piece(grad_pieces[shift], shift)
    fenced = after([*sums[-1], *grad_pieces[1:]], grad_gate)
    sums[-1], grad_pieces[1:] = fenced[:3], fenced[3:]
    grad_pieces[-1] = send_piece(grad_pieces[-1], steps - 1)
    rows += [send_rows(slot_rows(i).astype(jnp.bfloat16), i) for i in range(early, steps - 1)]
    total = slot_rows(steps - 1)
    for piece in rows:
        total = total + piece.astype(jnp.float32)
    mixed = total.astype(jnp.bfloat16)

    grads_s = lay_out_grads(grad_pieces, shadow_part, chip)
    return (mixed, grad_gate[None], grad_up[None], grad_down[None], *grads_s)


def shards(tokens, cotangent, expert_ids, *others):
    tp_count, ep_count = lax.axis_size("tp"), lax.axis_size("ep")
    tok_count, top_count = expert_ids.shape
    rows = (5 * tok_count * top_count) // 4
    chips = ep_count // 2
    fits = tp_count == 4 and ep_count == 2 * chips and chips & (chips - 1) == 0 and tok_count % 128 == 0
    dense = fits and ep_count * tok_count <= 3 * rows
    return (dense_shards if dense else routed_shards)(tokens, cotangent, expert_ids, *others)


def solution(mesh):
    return jax.shard_map(
        shards,
        mesh=mesh,
        in_specs=(
            P("ep", "tp"),
            P("ep", "tp"),
            P("ep", None),
            P("ep", None),
            P("ep"),
            P("ep", None, "tp"),
            P("ep", None, "tp"),
            P("ep", "tp", None),
            P("ep", "tp"),
            P("ep", "tp"),
            P("tp", "ep"),
        ),
        out_specs=(
            P("ep", "tp"),
            P("ep", None, "tp"),
            P("ep", None, "tp"),
            P("ep", "tp", None),
            P("ep", "tp"),
            P("ep", "tp"),
            P("tp", "ep"),
        ),
        check_vma=False,
    )
```

```python
import functools

import jax
import jax.numpy as jnp
from jax import lax
from jax.experimental import pallas as pl
from jax.experimental.pallas import tpu as pltpu
from jax.sharding import PartitionSpec as P


def contract_rows(left, right):
    return lax.dot_general(
        left, right, (((0,), (0,)), ((), ())), preferred_element_type=jnp.float32
    )


def split_parts(values):
    upper_part = values.astype(jnp.bfloat16)
    lower_part = (values - upper_part.astype(jnp.float32)).astype(jnp.bfloat16)
    return (upper_part, lower_part)


def weigh_rows(weight_table, rows):
    weight_upper, weight_lower = split_parts(weight_table)
    return jnp.dot(weight_upper, rows, preferred_element_type=jnp.float32) + jnp.dot(
        weight_lower, rows, preferred_element_type=jnp.float32
    )


def expert_pass(rows_x, rows_dout, weight_gate, weight_up, weight_down):
    pre_gate = jnp.dot(rows_x, weight_gate, preferred_element_type=jnp.float32)
    pre_up = jnp.dot(rows_x, weight_up, preferred_element_type=jnp.float32)
    sigmoid_gate = jax.nn.sigmoid(pre_gate)
    activated = pre_gate * sigmoid_gate
    hidden = (activated * pre_up).astype(jnp.bfloat16)
    partial_out = jnp.dot(hidden, weight_down, preferred_element_type=jnp.float32).astype(
        jnp.bfloat16
    )
    hidden_grad = lax.dot_general(
        rows_dout, weight_down, (((1,), (1,)), ((), ())), preferred_element_type=jnp.float32
    )
    grad_pre_gate = (
        hidden_grad * pre_up * sigmoid_gate * (1.0 + pre_gate * (1.0 - sigmoid_gate))
    ).astype(jnp.bfloat16)
    grad_pre_up = (hidden_grad * activated).astype(jnp.bfloat16)
    return (partial_out, hidden, grad_pre_gate, grad_pre_up)


def routed_shards(
    tokens,
    cotangent,
    expert_ids,
    gate_weights,
    shadow_mask,
    w_gate,
    w_up,
    w_down,
    s_gate,
    s_up,
    s_down,
):
    ep_count = lax.axis_size("ep")
    tok_count, top_count = expert_ids.shape
    quarter_width = tokens.shape[1]
    width = quarter_width * lax.axis_size("tp")
    expert_count = w_gate.shape[0] * ep_count
    capacity = (5 * tok_count * top_count + 4 * expert_count - 1) // (4 * expert_count)
    slot_count = expert_count * capacity
    picks_flat = expert_ids.reshape(-1)
    onehot = (picks_flat[:, None] == jnp.arange(expert_count, dtype=jnp.int32)[None, :]).astype(
        jnp.int32
    )
    slot_rank = jnp.sum((jnp.cumsum(onehot, axis=0) - onehot) * onehot, axis=1)
    slot_index = (picks_flat * capacity + slot_rank).reshape(tok_count, top_count)
    matches = jnp.arange(slot_count, dtype=jnp.int32)[:, None, None] == slot_index[None, :, :]
    dispatch = jnp.any(matches, axis=2).astype(jnp.bfloat16)
    weighting = jnp.sum(jnp.where(matches, gate_weights[None, :, :top_count], 0.0), axis=2)
    slot_gate = jnp.sum(weighting, axis=1)
    shadow_weight = gate_weights[:, top_count] * shadow_mask.astype(jnp.float32)
    x_full, dy_full = (
        lax.all_gather(tokens, "tp", axis=1, tiled=True),
        lax.all_gather(cotangent, "tp", axis=1, tiled=True),
    )
    rows_x = jnp.dot(dispatch, tokens, preferred_element_type=jnp.float32).astype(jnp.bfloat16)
    rows_dy = jnp.dot(dispatch, cotangent, preferred_element_type=jnp.float32)
    rows_dout = (slot_gate[:, None] * rows_dy).astype(jnp.bfloat16)
    recv_x, recv_dout = (
        lax.all_to_all(
            rows_x.reshape(ep_count, -1, quarter_width),
            "ep",
            split_axis=0,
            concat_axis=0,
            tiled=True,
        ),
        lax.all_to_all(
            rows_dout.reshape(ep_count, -1, quarter_width),
            "ep",
            split_axis=0,
            concat_axis=0,
            tiled=True,
        ),
    )
    expert_x, expert_dout = (
        lax.all_gather(recv_x.reshape(-1, quarter_width), "tp", axis=1, tiled=True),
        lax.all_gather(recv_dout.reshape(-1, quarter_width), "tp", axis=1, tiled=True),
    )
    partial_out, hidden, grad_pre_gate, grad_pre_up = expert_pass(
        expert_x, expert_dout, w_gate[0], w_up[0], w_down[0]
    )
    grad_gate = contract_rows(expert_x, grad_pre_gate).astype(jnp.bfloat16)[None]
    grad_up = contract_rows(expert_x, grad_pre_up).astype(jnp.bfloat16)[None]
    grad_down = contract_rows(hidden, expert_dout).astype(jnp.bfloat16)[None]
    full_gate, full_up, full_down = (
        lax.all_gather(s_gate, "ep", axis=0, tiled=True),
        lax.all_gather(s_up, "ep", axis=0, tiled=True),
        lax.all_gather(s_down, "ep", axis=1, tiled=True),
    )
    shadow_dout = (shadow_weight[:, None] * dy_full.astype(jnp.float32)).astype(jnp.bfloat16)
    shadow_out, shadow_hidden, shadow_gate_pre, shadow_up_pre = expert_pass(
        x_full, shadow_dout, full_gate, full_up, full_down
    )
    shadow_sums = lax.psum_scatter(
        jnp.concatenate(
            [
                contract_rows(x_full, shadow_gate_pre),
                contract_rows(x_full, shadow_up_pre),
                contract_rows(shadow_dout, shadow_hidden),
            ],
            axis=1,
        ).astype(jnp.bfloat16),
        "ep",
        scatter_dimension=0,
        tiled=True,
    ).astype(jnp.float32)
    hidden_part = s_gate.shape[1]
    grad_s_gate = shadow_sums[:, :hidden_part].astype(jnp.bfloat16)
    grad_s_up = shadow_sums[:, hidden_part : 2 * hidden_part].astype(jnp.bfloat16)
    grad_s_down = shadow_sums[:, 2 * hidden_part :].T.astype(jnp.bfloat16)
    back_rows = lax.all_to_all(
        partial_out.reshape(ep_count, -1, width), "ep", split_axis=0, concat_axis=0, tiled=True
    ).reshape(-1, width)
    term = weigh_rows(weighting.T, back_rows)
    term = term + shadow_weight[:, None] * shadow_out.astype(jnp.float32)
    mixed = lax.psum_scatter(term.astype(jnp.bfloat16), "tp", scatter_dimension=1, tiled=True)
    return (mixed, grad_gate, grad_up, grad_down, grad_s_gate, grad_s_up, grad_s_down)


ANY = pl.BlockSpec(memory_space=pl.ANY)
VMEM_LIMIT = 60 * 1024 * 1024
SHORT = pl.CostEstimate(flops=1, bytes_accessed=1, transcendentals=0)


def swap_pairs(count, bit):
    return [(i, i ^ bit) for i in range(count)]


def dot32(left, right):
    return jnp.dot(left, right, preferred_element_type=jnp.float32)


def contract_last(left, right):
    return lax.dot_general(
        left, right, (((1,), (1,)), ((), ())), preferred_element_type=jnp.float32
    )


def shape_of(*dims, dtype=jnp.bfloat16):
    return jax.ShapeDtypeStruct(dims, dtype)


def after(arrays, *earlier):
    def nothing(*refs):
        del refs

    count = len(arrays)
    return pl.pallas_call(
        nothing,
        out_shape=[jax.ShapeDtypeStruct(a.shape, a.dtype) for a in arrays],
        in_specs=[ANY] * (count + len(earlier)),
        out_specs=[ANY] * count,
        input_output_aliases={i: i for i in range(count)},
        compiler_params=pltpu.CompilerParams(vmem_limit_bytes=VMEM_LIMIT),
        cost_estimate=SHORT,
        name="after",
    )(*arrays, *earlier)


def kernel_call(body, grid, in_specs, out_specs, out_shape, operands, scratch, name, column=None, earlier=()):
    count = len(operands)

    def run(column_ref, *refs):
        del column_ref
        body(*refs[:count], *refs[count + len(earlier) :])

    column = jnp.zeros((1,), jnp.int32) if column is None else column.reshape(1).astype(jnp.int32)
    return pl.pallas_call(
        run,
        out_shape=out_shape,
        grid_spec=pltpu.PrefetchScalarGridSpec(
            num_scalar_prefetch=1,
            grid=grid,
            in_specs=list(in_specs) + [ANY] * len(earlier),
            out_specs=out_specs,
            scratch_shapes=scratch,
        ),
        compiler_params=pltpu.CompilerParams(vmem_limit_bytes=VMEM_LIMIT),
        cost_estimate=SHORT,
        name=name,
    )(column, *operands, *earlier)


def whole(array):
    return pl.BlockSpec(array.shape, lambda *_: (0,) * len(array.shape))


def join_plane(column, *pieces, earlier=()):
    rows, quarter = pieces[0].shape
    count, halves = 4, len(pieces) - 3
    chunk = rows // 4
    per = 4 // halves

    def body(column_ref, *refs):
        out = refs[-1]
        for own_column in range(count):
            for j, from_diagonal in enumerate(refs[3 : 3 + halves]):

                @pl.when((column_ref[0] == own_column) & (pl.program_id(0) // per == j))
                def _(from_diagonal=from_diagonal, own_column=own_column):
                    for bit, source in enumerate(refs[:3] + (from_diagonal,)):
                        place = own_column ^ bit
                        out[:, place * quarter : (place + 1) * quarter] = source[...]

    def diagonal_spec(j):
        return pl.BlockSpec((chunk, quarter), lambda i, *_: (jnp.clip(i - j * per, 0, per - 1), 0))

    return pl.pallas_call(
        body,
        out_shape=shape_of(rows, count * quarter),
        grid_spec=pltpu.PrefetchScalarGridSpec(
            num_scalar_prefetch=1,
            grid=(4,),
            in_specs=[pl.BlockSpec((chunk, quarter), lambda i, *_: (i, 0))] * 3
            + [diagonal_spec(j) for j in range(halves)]
            + [ANY] * len(earlier),
            out_specs=pl.BlockSpec((chunk, count * quarter), lambda i, *_: (i, 0)),
        ),
        compiler_params=pltpu.CompilerParams(vmem_limit_bytes=VMEM_LIMIT),
        cost_estimate=SHORT,
        name="join_plane",
    )(column.reshape(1).astype(jnp.int32), *pieces, *earlier)


def stack_pieces(pieces, earlier=()):
    rows, columns = pieces[0].shape
    count = len(pieces)

    def body(*refs):
        for i, ref in enumerate(refs[:count]):

            @pl.when(pl.program_id(0) == i)
            def _():
                refs[-1][...] = ref[...]

    return pl.pallas_call(
        body,
        out_shape=shape_of(count * rows, columns),
        grid=(count,),
        in_specs=[pl.BlockSpec((rows, columns), lambda i: (0, 0))] * count + [ANY] * len(earlier),
        out_specs=pl.BlockSpec((rows, columns), lambda i: (i, 0)),
        compiler_params=pltpu.CompilerParams(vmem_limit_bytes=VMEM_LIMIT),
        cost_estimate=SHORT,
        name="stack_pieces",
    )(*pieces, *earlier)


def on_piece(chip_ref, refs, use):
    step = pl.program_id(0)
    shift = chip_ref[0] ^ (step // 2)
    for i, ref in enumerate(refs):
        for core in range(2):

            @pl.when((shift == i) & (lax.rem(step, 2) == core))
            def _(ref=ref, core=core):
                use(ref.at[0, core])


def lay_out_shadow(pieces, down, units, chip, earlier=()):
    count = len(pieces)
    ep_count = 2 * count
    block_width = pieces[0].shape[3]
    apart = units + -units % 128
    all_units, width = down.shape

    def body(chip_ref, *refs):
        shadow_ref, out = refs[-2:]

        def use(ref):
            shadow_ref[...] = jnp.zeros_like(shadow_ref)
            shadow_ref[:units, :] = ref[:units, :]
            shadow_ref[apart : apart + units, :] = ref[units : 2 * units, :]
            out[units:, :] = jnp.zeros((apart - units, block_width), jnp.bfloat16)
            out[:units, :] = ref[2 * units : 3 * units, :]

        on_piece(chip_ref, refs[:count], use)

    return pl.pallas_call(
        body,
        out_shape=[shape_of(2 * apart, width), shape_of(all_units, width)],
        grid_spec=pltpu.PrefetchScalarGridSpec(
            num_scalar_prefetch=1,
            grid=(ep_count,),
            in_specs=[whole(p) for p in pieces] + [ANY] * (1 + len(earlier)),
            out_specs=[
                pl.BlockSpec((2 * apart, block_width), lambda e, *_: (0, e)),
                pl.BlockSpec((apart, block_width), lambda e, *_: (all_units // apart - 1, e)),
            ],
        ),
        input_output_aliases={1 + count: 1},
        compiler_params=pltpu.CompilerParams(vmem_limit_bytes=VMEM_LIMIT),
        cost_estimate=SHORT,
        name="lay_out_shadow",
    )(chip.reshape(1).astype(jnp.int32), *pieces, down, *earlier)


def lay_out_grads(pieces, units, chip, earlier=()):
    count = len(pieces)
    ep_count = 2 * count
    block_width = pieces[0].shape[3]
    hidden = ep_count * units

    def body(chip_ref, *refs):
        gate_ref, up_ref, down_ref, gate_t, up_t = refs[-5:]
        place = pl.ds(pl.multiple_of(pl.program_id(0) * units, 16), units)

        def use(ref):
            gate_t[place, :] = ref[:units, :]
            up_t[place, :] = ref[units : 2 * units, :]
            down_ref[place, :] = ref[2 * units :, :]

        on_piece(chip_ref, refs[:count], use)

        @pl.when(pl.program_id(0) == ep_count - 1)
        def _():
            gate_ref[...] = gate_t[...].T
            up_ref[...] = up_t[...].T

    return pl.pallas_call(
        body,
        out_shape=[shape_of(block_width, hidden), shape_of(block_width, hidden), shape_of(hidden, block_width)],
        grid_spec=pltpu.PrefetchScalarGridSpec(
            num_scalar_prefetch=1,
            grid=(ep_count,),
            in_specs=[whole(p) for p in pieces] + [ANY] * len(earlier),
            out_specs=[pl.BlockSpec((block_width, hidden), lambda *_: (0, 0))] * 2
            + [pl.BlockSpec((hidden, block_width), lambda *_: (0, 0))],
            scratch_shapes=[pltpu.VMEM((hidden, block_width), jnp.bfloat16)] * 2,
        ),
        compiler_params=pltpu.CompilerParams(vmem_limit_bytes=VMEM_LIMIT),
        cost_estimate=SHORT,
        name="lay_out_grads",
    )(chip.reshape(1).astype(jnp.int32), *pieces, *earlier)


def row_specs(groups, tile):
    def spec(index, rows):
        return pl.BlockSpec((rows, tile), lambda k, *_: (index, k))

    return [spec(index, rows) for _, index, rows in groups]


def apply_gate(pre_gate, pre_up):
    sigmoid_gate = jax.nn.sigmoid(pre_gate)
    activated = pre_gate * sigmoid_gate
    hidden = (activated * pre_up).astype(jnp.bfloat16)
    return hidden, pre_up * sigmoid_gate * (1.0 + pre_gate * (1.0 - sigmoid_gate)), activated


def clear_first(acc):
    @pl.when(pl.program_id(0) == 0)
    def _():
        acc[...] = jnp.zeros_like(acc)


def rows_operand(refs, groups, held):
    if len(groups) == 1:
        return refs[0][...]
    return stage_rows(refs, groups, held)


def forward_rows(groups, w_both, tile, transposed=False, earlier=()):
    rows = sum(g[2] for g in groups)
    if transposed:
        units, width = w_both.shape[0] // 2, w_both.shape[1]
        tile_spec = pl.BlockSpec((2 * units, tile), lambda k, *_: (0, k))
    else:
        width, units = w_both.shape[0], w_both.shape[1] // 2
        tile_spec = pl.BlockSpec((tile, 2 * units), lambda k, *_: (k, 0))
    steps = width // tile

    def body(*refs):
        n = len(groups)
        both_ref, hidden_ref, slope_ref, act_ref, acc, held = refs[n:]
        clear_first(acc)
        operand = rows_operand(refs[:n], groups, held)
        acc[...] += contract_last(operand, both_ref[...]) if transposed else dot32(operand, both_ref[...])

        @pl.when(pl.program_id(0) == steps - 1)
        def _():
            chunk = 128

            @pl.loop(0, rows // chunk)
            def _(i):
                part = pl.ds(pl.multiple_of(i * chunk, chunk), chunk)
                hidden, slope, act = apply_gate(acc[part, :units], acc[part, units:])
                hidden_ref[part, :] = hidden
                slope_ref[part, :] = slope.astype(jnp.bfloat16)
                act_ref[part, :] = act.astype(jnp.bfloat16)

    out_spec = pl.BlockSpec((rows, units), lambda *_: (0, 0))
    return kernel_call(
        body,
        (steps,),
        row_specs(groups, tile) + [tile_spec],
        [out_spec] * 3,
        [shape_of(rows, units)] * 3,
        [g[0] for g in groups] + [w_both],
        [pltpu.VMEM((rows, 2 * units), jnp.float32), pltpu.VMEM((rows, tile), jnp.bfloat16)],
        "forward_rows",
        earlier=earlier,
    )


def weigh_hidden(hidden_near, hidden_far, hidden_s, pieces, first_row, slot_rows, core, earlier=()):
    count = len(pieces)
    rows, units_s = hidden_s.shape
    units = hidden_near.shape[1]
    slots = [(s, 0) for s in list(range(1, count)) + [0]] + [(s, 1) for s in range(count)]

    def body(core_ref, *refs):
        near_ref, far_ref, s_ref, *piece_refs = refs[: 3 + count]
        out, w_ref, w_s_ref = refs[-3:]
        near, far = 0, 0
        for i, (slot, other) in enumerate(slots):
            part = pl.ds(i * slot_rows, slot_rows)
            table = piece_refs[slot][0, core_ref[0] ^ other, first_row : first_row + 16, :][:1].astype(jnp.float32)

            def column(j):
                both = table[:, j * slot_rows : (j + 1) * slot_rows]
                both = both + table[:, (j + 2) * slot_rows : (j + 3) * slot_rows]
                return jnp.broadcast_to(both, (slot_rows, slot_rows)).T[:, :1]

            weight, weight_s = column(0), column(1)
            w_ref[part, :] = weight
            w_s_ref[part, :] = weight_s
            if slot == 0:
                hidden = near_ref[near : near + slot_rows, :]
                near += slot_rows
            else:
                hidden = far_ref[far : far + slot_rows, :]
                far += slot_rows
            out[part, :units] = (hidden.astype(jnp.float32) * weight).astype(jnp.bfloat16)
            out[part, units:] = (s_ref[part, :].astype(jnp.float32) * weight_s).astype(jnp.bfloat16)

    return pl.pallas_call(
        body,
        out_shape=[
            shape_of(rows, units + units_s),
            shape_of(rows, 1, dtype=jnp.float32),
            shape_of(rows, 1, dtype=jnp.float32),
        ],
        grid_spec=pltpu.PrefetchScalarGridSpec(
            num_scalar_prefetch=1,
            grid=(1,),
            in_specs=[whole(a) for a in (hidden_near, hidden_far, hidden_s, *pieces)] + [ANY] * len(earlier),
            out_specs=[
                pl.BlockSpec((rows, units + units_s), lambda *_: (0, 0)),
                pl.BlockSpec((rows, 1), lambda *_: (0, 0)),
                pl.BlockSpec((rows, 1), lambda *_: (0, 0)),
            ],
        ),
        compiler_params=pltpu.CompilerParams(vmem_limit_bytes=VMEM_LIMIT),
        cost_estimate=SHORT,
        name="weigh_hidden",
    )(core.reshape(1).astype(jnp.int32), hidden_near, hidden_far, hidden_s, *pieces, *earlier)


def output_other(weighted, down, column, parts, slot_rows, quarter, earlier=()):
    rows, units = weighted.shape
    count = rows // 2 // parts

    def body(weighted_ref, down_ref, *outs):
        value = dot32(weighted_ref[...], down_ref[...]).astype(jnp.bfloat16)
        for i, out in enumerate(outs):
            first, last = slot_rows + i * count, slot_rows + (i + 1) * count
            kept = min(last, rows // 2) - first
            out[:kept, :] = value[first : first + kept]
            if kept < count:
                out[kept:, :] = value[: count - kept]

    return kernel_call(
        body,
        (4,),
        [
            pl.BlockSpec((rows // 2, units), lambda *_: (1, 0)),
            pl.BlockSpec((units, quarter), lambda q, column_ref: (0, column_ref[0] ^ q)),
        ],
        [pl.BlockSpec((count, quarter), lambda q, *_: (0, q))] * parts,
        [shape_of(count, 4 * quarter)] * parts,
        [weighted, down],
        [],
        "output_other",
        column=column,
        earlier=earlier,
    )


def output_own(weighted, got, down, column, quarter, earlier=()):
    count, units = got[0].shape[0], weighted.shape[1]
    parts = len(got)

    def body(weighted_ref, down_ref, *refs):
        product = dot32(weighted_ref[...], down_ref[...])
        for i in range(parts):
            value = product[i * count : (i + 1) * count] + refs[i][...].astype(jnp.float32)
            for j, out in enumerate(refs[parts + 4 * i : parts + 4 * i + 4]):

                @pl.when(pl.program_id(0) == 3 - j)
                def _(out=out, value=value):
                    out[...] = value.astype(out.dtype)

    full = pl.BlockSpec((count, quarter), lambda *_: (0, 0))
    out = kernel_call(
        body,
        (4,),
        [
            pl.BlockSpec((parts * count, units), lambda *_: (0, 0)),
            pl.BlockSpec((units, quarter), lambda q, column_ref: (0, column_ref[0] ^ 3 ^ q)),
        ]
        + [pl.BlockSpec((count, quarter), lambda q, *_: (0, 3 - q))] * parts,
        [full] * (4 * parts),
        ([shape_of(count, quarter, dtype=jnp.float32)] + [shape_of(count, quarter)] * 3) * parts,
        [weighted, down] + list(got),
        [],
        "output_own",
        column=column,
        earlier=earlier,
    )
    return [out[4 * i : 4 * i + 4] for i in range(parts)]


def backward_rows(groups, down, parts, per_row, first_row, tile, earlier=()):
    slope_s, act_s, w_rows, w_shadow = per_row
    rows = sum(g[2] for g in groups)
    units_all, width = down.shape
    units_s = slope_s.shape[1]
    units = units_all - units_s
    steps = width // tile
    arrays = list({id(a): a for part in parts for a in part[:2]}.values())
    places = [[next(i for i, a in enumerate(arrays) if a is b) for b in part[:2]] for part in parts]

    def body(*refs):
        n, m = len(groups), len(arrays)
        down_ref = refs[n]
        array_refs = refs[n + 1 : n + 1 + m]
        slope_s_ref, act_s_ref, w_ref, w_s_ref, pre_ref, pre_s_ref, acc, held = refs[n + 1 + m :]
        clear_first(acc)
        acc[...] += contract_last(rows_operand(refs[:n], groups, held), down_ref[...])

        @pl.when(pl.program_id(0) == steps - 1)
        def _():
            chunk = 128
            start = 0
            for (_, _, count), (_, _, first), (slope_at, act_at) in zip(groups, parts, places):

                @pl.loop(0, count // chunk)
                def _(i, start=start, first=first, slope_ref=array_refs[slope_at], act_ref=array_refs[act_at]):
                    source = pl.ds(pl.multiple_of(first + i * chunk, chunk), chunk)
                    part = pl.ds(pl.multiple_of(start + i * chunk, chunk), chunk)
                    whole_part = pl.ds(pl.multiple_of(first_row + start + i * chunk, chunk), chunk)
                    grad = acc[part, :units] * w_ref[whole_part, :]
                    pre_ref[part, :units] = (grad * slope_ref[source, :]).astype(jnp.bfloat16)
                    pre_ref[part, units:] = (grad * act_ref[source, :]).astype(jnp.bfloat16)
                    grad = acc[part, units:] * w_s_ref[whole_part, :]
                    pre_s_ref[part, :units_s] = (grad * slope_s_ref[whole_part, :]).astype(jnp.bfloat16)
                    pre_s_ref[part, units_s:] = (grad * act_s_ref[whole_part, :]).astype(jnp.bfloat16)

                start += count

    extra = arrays + [slope_s, act_s, w_rows, w_shadow]
    return kernel_call(
        body,
        (steps,),
        row_specs(groups, tile) + [pl.BlockSpec((units_all, tile), lambda k, *_: (0, k))] + [whole(a) for a in extra],
        [pl.BlockSpec((rows, 2 * units), lambda *_: (0, 0)), pl.BlockSpec((rows, 2 * units_s), lambda *_: (0, 0))],
        [shape_of(rows, 2 * units), shape_of(rows, 2 * units_s)],
        [g[0] for g in groups] + [down] + extra,
        [pltpu.VMEM((rows, units_all), jnp.float32), pltpu.VMEM((rows, tile), jnp.bfloat16)],
        "backward_rows",
        earlier=earlier,
    )


def stage_rows(refs, groups, held):
    start = 0
    for ref, (_, _, count) in zip(refs, groups):
        held[pl.ds(start, count), :] = ref[...]
        start += count
    return held[...]


def shadow_grads(x_groups, dy_groups, pre_s, weighted, units, block, tile, earlier=()):
    rows, wide = weighted.shape[0], pre_s[0].shape[1]
    apart = wide // 2
    width = x_groups[0][0].shape[1]
    m = len(pre_s)

    def body(*refs):
        n = len(x_groups)
        pre_refs = refs[2 * n : 2 * n + m]
        hidden_ref, out, held, pre_t, hidden_t = refs[2 * n + m :]

        @pl.when(pl.program_id(0) == 0)
        def _():
            start = 0
            for ref in pre_refs:
                pre_t[:, start : start + ref.shape[0]] = ref[...].T
                start += ref.shape[0]
            hidden_t[...] = hidden_ref[...].T

        value = dot32(pre_t[...], stage_rows(refs[:n], x_groups, held)).astype(jnp.bfloat16)
        for i in range(tile // block):
            part = slice(i * block, (i + 1) * block)
            out[i, :units, :] = value[:units, part]
            out[i, units : 2 * units, :] = value[apart : apart + units, part]
        value = dot32(hidden_t[...], stage_rows(refs[n : 2 * n], dy_groups, held)).astype(jnp.bfloat16)
        for i in range(tile // block):
            out[i, 2 * units :, :] = value[:units, i * block : (i + 1) * block]

    (out,) = kernel_call(
        body,
        (width // tile,),
        row_specs(x_groups, tile)
        + row_specs(dy_groups, tile)
        + [whole(p) for p in pre_s]
        + [pl.BlockSpec((rows, apart), lambda *_: (0, weighted.shape[1] // apart - 1))],
        [pl.BlockSpec((tile // block, 3 * units, block), lambda k, *_: (k, 0, 0))],
        [shape_of(width // block, 3 * units, block)],
        [g[0] for g in x_groups + dy_groups] + list(pre_s) + [weighted],
        [
            pltpu.VMEM((rows, tile), jnp.bfloat16),
            pltpu.VMEM((wide, rows), jnp.bfloat16),
            pltpu.VMEM((apart, rows), jnp.bfloat16),
        ],
        "shadow_grads",
        earlier=earlier,
    )
    return out


def input_grads(groups, pre, tile, earlier=()):
    both = pre[0].shape[1]
    rows = sum(p.shape[0] for p in pre)
    units = both // 2
    width = groups[0][0].shape[1]
    m = len(pre)

    def body(*refs):
        n = len(groups)
        gate_ref, up_ref, held, pre_held = refs[n + m :]

        @pl.when(pl.program_id(0) == 0)
        def _():
            start = 0
            for ref in refs[n : n + m]:
                pre_held[start : start + ref.shape[0], :] = ref[...]
                start += ref.shape[0]

        value = contract_rows(stage_rows(refs[:n], groups, held), pre_held[...])
        gate_ref[...] = value[:, :units].astype(jnp.bfloat16)
        up_ref[...] = value[:, units:].astype(jnp.bfloat16)

    return kernel_call(
        body,
        (width // tile,),
        row_specs(groups, tile) + [whole(p) for p in pre],
        [pl.BlockSpec((tile, units), lambda k, *_: (k, 0))] * 2,
        [shape_of(width, units)] * 2,
        [g[0] for g in groups] + list(pre),
        [pltpu.VMEM((rows, tile), jnp.bfloat16), pltpu.VMEM((rows, both), jnp.bfloat16)],
        "input_grads",
        earlier=earlier,
    )


def down_grad(groups, weighted, units, tile, earlier=()):
    rows = weighted.shape[0]
    width = groups[0][0].shape[1]

    def body(*refs):
        n = len(groups)
        hidden_ref, out, held, hidden_t = refs[n:]

        @pl.when(pl.program_id(0) == 0)
        def _():
            hidden_t[...] = hidden_ref[...].T

        out[...] = dot32(hidden_t[...], stage_rows(refs[:n], groups, held)).astype(jnp.bfloat16)

    (out,) = kernel_call(
        body,
        (width // tile,),
        row_specs(groups, tile) + [pl.BlockSpec((rows, units), lambda *_: (0, 0))],
        [pl.BlockSpec((units, tile), lambda k, *_: (0, k))],
        [shape_of(units, width)],
        [g[0] for g in groups] + [weighted],
        [pltpu.VMEM((rows, tile), jnp.bfloat16), pltpu.VMEM((units, rows), jnp.bfloat16)],
        "down_grad",
        earlier=earlier,
    )
    return out


def send_along_z(own):
    ep_count = lax.axis_size("ep")
    return [lax.ppermute(own, "ep", swap_pairs(ep_count, 2 * s)) for s in range(1, ep_count // 2)]


def swap_cores(block):
    return lax.ppermute(block, "ep", swap_pairs(lax.axis_size("ep"), 1))


def send_plane(*pieces):
    pieces = pieces * 3 if len(pieces) == 1 else pieces
    return [lax.ppermute(p, "tp", swap_pairs(lax.axis_size("tp"), bit)) for p, bit in zip(pieces, (1, 2, 3))]


def send_diagonal(from_x, from_y):
    along, across = [swap_pairs(lax.axis_size("tp"), bit) for bit in (1, 2)]
    half = from_x.shape[0] // 2
    return [lax.ppermute(from_x[:half], "tp", across), lax.ppermute(from_y[half:], "tp", along)]


def exchange_cores(blocks, cuts=1):
    ep_count, core = lax.axis_size("ep"), lax.axis_index("ep") % 2
    pairs = blocks.reshape(ep_count // 2, 2, *blocks.shape[1:])
    kept = jnp.where(core == 0, pairs[:, 0], pairs[:, 1])
    given = jnp.where(core == 0, pairs[:, 1], pairs[:, 0])
    return kept, [swap_cores(part) for part in jnp.split(given, cuts)]


def chip_pieces(kept, taken):
    ep_count, me = lax.axis_size("ep"), lax.axis_index("ep")
    chips, chip, core = ep_count // 2, me // 2, me % 2
    taken = jnp.concatenate(taken, axis=0)
    both = jnp.stack([jnp.where(core == 0, kept, taken), jnp.where(core == 0, taken, kept)], axis=1)
    return [lax.dynamic_index_in_dim(both, chip ^ shift, 0) for shift in range(chips)]


def send_piece(piece, shift):
    return lax.ppermute(piece, "ep", swap_pairs(lax.axis_size("ep"), 2 * shift))


def dense_shards(
    tokens,
    cotangent,
    expert_ids,
    gate_weights,
    shadow_mask,
    w_gate,
    w_up,
    w_down,
    s_gate,
    s_up,
    s_down,
):
    ep_count, tp_count = lax.axis_size("ep"), lax.axis_size("tp")
    ep_index, tp_index = lax.axis_index("ep"), lax.axis_index("tp")
    tok_count, top_count = expert_ids.shape
    quarter = tokens.shape[1]
    width = quarter * tp_count
    hidden_part = w_gate.shape[2]
    shadow_part = hidden_part // ep_count
    block_width = s_gate.shape[0]
    steps = ep_count // 2
    later = (steps - 1) * tok_count
    tile = width // 8
    along, across = swap_pairs(tp_count, 1), swap_pairs(tp_count, 2)

    picked = expert_ids[None, :, :] == jnp.arange(ep_count, dtype=jnp.int32)[:, None, None]
    table = jnp.sum(jnp.where(picked, gate_weights[None, :, :top_count], 0.0), axis=2)
    shadow_weight = gate_weights[:, top_count] * shadow_mask.astype(jnp.float32)
    table = jnp.concatenate([table, jnp.broadcast_to(shadow_weight[None], table.shape)], axis=1)
    table = jnp.concatenate(split_parts(table), axis=1)
    table = jnp.pad(table[:, None, :], ((0, 0), (0, 15), (0, block_width - table.shape[1])))
    shadow_blocks = jnp.concatenate(
        [
            s_gate.T.reshape(ep_count, shadow_part, block_width),
            s_up.T.reshape(ep_count, shadow_part, block_width),
            s_down.reshape(ep_count, shadow_part, block_width),
            table,
        ],
        axis=1,
    )

    x_z = send_along_z(tokens)
    near = stack_pieces([tokens, cotangent])
    near_x, near_y = send_plane(near, near)
    near_x, near_y = after([near_x, near_y], x_z[0])
    near_d = send_diagonal(near_x, near_y)
    w_both = jnp.concatenate([w_gate[0], w_up[0]], axis=1)
    fenced = after([*near_d, *x_z], w_both, shadow_blocks)
    near_d, x_z = fenced[:2], fenced[2:]

    x_piece = stack_pieces(x_z)
    x_plane = send_plane(x_piece, x_piece)
    dy_z = send_along_z(cotangent)
    near_own = join_plane(tp_index, near, near_x, near_y, *near_d)
    near_other = swap_cores(near_own)
    x_near = [(near_own, 0, tok_count), (near_other, 0, tok_count)]
    hidden_near, slope_near, act_near = forward_rows(x_near, w_both, 2 * tile)
    spare_rows = -shadow_part % 128 + shadow_part
    down = jnp.pad(w_down[0], ((0, spare_rows), (0, 0)))
    *x_plane, down = after([*x_plane, down], *dy_z[:2], hidden_near)
    x_plane = [*x_plane, *send_diagonal(*x_plane)]
    (shadow_blocks,) = after([shadow_blocks], x_z[0])
    shadow_kept, shadow_taken = exchange_cores(shadow_blocks)
    fenced = after([*x_plane[2:], *shadow_taken, *dy_z])
    x_plane[2:], shadow_taken, dy_z = fenced[:2], fenced[2:3], fenced[3:]

    dy_piece = stack_pieces(dy_z)
    dy_plane = send_plane(dy_piece)
    shadow_pieces = chip_pieces(shadow_kept, shadow_taken)
    for shift in range(1, steps - 1):
        shadow_pieces[shift] = send_piece(shadow_pieces[shift], shift)
    x_own = join_plane(tp_index, x_piece, *x_plane, earlier=[dy_piece])
    x_other = swap_cores(x_own)
    x_far = [(x_own, 0, later), (x_other, 0, later)]
    x_groups = [x_far[0], x_near[0], x_near[1], x_far[1]]
    hidden_far, slope_far, act_far = forward_rows(x_far, w_both, 2 * tile)
    shadow_pieces[-1:] = after(shadow_pieces[-1:], hidden_far)
    shadow_pieces[-1] = send_piece(shadow_pieces[-1], steps - 1)
    chip = ep_index // 2
    shadow_in, down = lay_out_shadow(shadow_pieces, down, shadow_part, chip, earlier=[hidden_far])
    hidden_s, slope_s, act_s = forward_rows(x_groups, shadow_in, 2 * tile, transposed=True)

    weighted, w_rows, w_shadow = weigh_hidden(
        hidden_near, hidden_far, hidden_s, shadow_pieces, 3 * shadow_part, tok_count, ep_index % 2
    )

    parts = 2 if steps % 2 == 0 else 1
    sent = output_other(weighted, down, tp_index, parts, tok_count, quarter)
    got = [swap_cores(array) for array in sent]
    dy_plane = after(dy_plane, *sent)

    dy_own = join_plane(tp_index, dy_piece, *dy_plane)
    dy_other = swap_cores(dy_own)
    dy_groups = [(dy_own, 0, later), (near_own, 1, tok_count), (near_other, 1, tok_count), (dy_other, 0, later)]
    segments = [
        (slope_far, act_far, 0),
        (slope_near, act_near, 0),
        (slope_near, act_near, tok_count),
        (slope_far, act_far, later),
    ]
    per_row = (slope_s, act_s, w_rows, w_shadow)
    pre_first, pre_s_first = backward_rows(dy_groups[:3], down, segments[:3], per_row, 0, 2 * tile)
    owns = output_own(weighted, got, down, tp_index, quarter, earlier=[pre_first])
    sums = [send_plane(*own[1:]) for own in owns]
    first_rows = sum(g[2] for g in dy_groups[:3])
    pre_last, pre_s_last = backward_rows(
        dy_groups[3:], down, segments[3:], per_row, first_rows, 2 * tile, earlier=[own[1] for own in owns]
    )
    pre, pre_s = [pre_first, pre_last], [pre_s_first, pre_s_last]
    grad_s = shadow_grads(x_groups, dy_groups, pre_s, weighted, shadow_part, block_width, 2 * tile)
    grad_pieces = chip_pieces(*exchange_cores(grad_s))

    def slot_rows(i):
        part = slice(i % (steps // parts) * tok_count, (i % (steps // parts) + 1) * tok_count)
        total = owns[i * parts // steps][0][part]
        for array in sums[i * parts // steps]:
            total = total + array[part].astype(jnp.float32)
        return total

    def send_rows(piece, i):
        return lax.ppermute(piece, "ep", swap_pairs(ep_count, 2 * (i + 1)))

    early = steps // parts if parts > 1 else 0
    sums[0] = after(sums[0], grad_s)
    rows = [slot_rows(i).astype(jnp.bfloat16) for i in range(early)]
    grad_down = down_grad(dy_groups, weighted, hidden_part, 2 * tile, earlier=[*rows, grad_pieces[0]])
    rows = [send_rows(piece, i) for i, piece in enumerate(rows)]
    fenced = after([*rows, *grad_pieces[1:]], grad_down)
    rows, grad_pieces[1:] = list(fenced[:early]), fenced[early:]
    grad_gate, grad_up = input_grads(x_groups, pre, 2 * tile, earlier=[grad_pieces[1]])
    for shift in range(1, steps - 1):
        grad_pieces[shift] = send_piece(grad_pieces[shift], shift)
    fenced = after([*sums[-1], *grad_pieces[1:]], grad_gate)
    sums[-1], grad_pieces[1:] = fenced[:3], fenced[3:]
    grad_pieces[-1] = send_piece(grad_pieces[-1], steps - 1)
    rows += [send_rows(slot_rows(i).astype(jnp.bfloat16), i) for i in range(early, steps - 1)]
    total = slot_rows(steps - 1)
    for piece in rows:
        total = total + piece.astype(jnp.float32)
    mixed = total.astype(jnp.bfloat16)

    grads_s = lay_out_grads(grad_pieces, shadow_part, chip)
    return (mixed, grad_gate[None], grad_up[None], grad_down[None], *grads_s)


def shards(tokens, cotangent, expert_ids, *others):
    tp_count, ep_count = lax.axis_size("tp"), lax.axis_size("ep")
    tok_count, top_count = expert_ids.shape
    rows = (5 * tok_count * top_count) // 4
    chips = ep_count // 2
    fits = tp_count == 4 and ep_count == 2 * chips and chips & (chips - 1) == 0 and tok_count % 128 == 0
    dense = fits and ep_count * tok_count <= 3 * rows
    return (dense_shards if dense else routed_shards)(tokens, cotangent, expert_ids, *others)


def solution(mesh):
    return jax.shard_map(
        shards,
        mesh=mesh,
        in_specs=(
            P("ep", "tp"),
            P("ep", "tp"),
            P("ep", None),
            P("ep", None),
            P("ep"),
            P("ep", None, "tp"),
            P("ep", None, "tp"),
            P("ep", "tp", None),
            P("ep", "tp"),
            P("ep", "tp"),
            P("tp", "ep"),
        ),
        out_specs=(
            P("ep", "tp"),
            P("ep", None, "tp"),
            P("ep", None, "tp"),
            P("ep", "tp", None),
            P("ep", "tp"),
            P("ep", "tp"),
            P("tp", "ep"),
        ),
        check_vma=False,
    )
```

```python
import functools

import jax
import jax.numpy as jnp
from jax import lax
from jax.experimental import pallas as pl
from jax.experimental.pallas import tpu as pltpu
from jax.sharding import PartitionSpec as P


def contract_rows(left, right):
    return lax.dot_general(
        left, right, (((0,), (0,)), ((), ())), preferred_element_type=jnp.float32
    )


def split_parts(values):
    upper_part = values.astype(jnp.bfloat16)
    lower_part = (values - upper_part.astype(jnp.float32)).astype(jnp.bfloat16)
    return (upper_part, lower_part)


def weigh_rows(weight_table, rows):
    weight_upper, weight_lower = split_parts(weight_table)
    return jnp.dot(weight_upper, rows, preferred_element_type=jnp.float32) + jnp.dot(
        weight_lower, rows, preferred_element_type=jnp.float32
    )


def expert_pass(rows_x, rows_dout, weight_gate, weight_up, weight_down):
    pre_gate = jnp.dot(rows_x, weight_gate, preferred_element_type=jnp.float32)
    pre_up = jnp.dot(rows_x, weight_up, preferred_element_type=jnp.float32)
    sigmoid_gate = jax.nn.sigmoid(pre_gate)
    activated = pre_gate * sigmoid_gate
    hidden = (activated * pre_up).astype(jnp.bfloat16)
    partial_out = jnp.dot(hidden, weight_down, preferred_element_type=jnp.float32).astype(
        jnp.bfloat16
    )
    hidden_grad = lax.dot_general(
        rows_dout, weight_down, (((1,), (1,)), ((), ())), preferred_element_type=jnp.float32
    )
    grad_pre_gate = (
        hidden_grad * pre_up * sigmoid_gate * (1.0 + pre_gate * (1.0 - sigmoid_gate))
    ).astype(jnp.bfloat16)
    grad_pre_up = (hidden_grad * activated).astype(jnp.bfloat16)
    return (partial_out, hidden, grad_pre_gate, grad_pre_up)


def routed_shards(
    tokens,
    cotangent,
    expert_ids,
    gate_weights,
    shadow_mask,
    w_gate,
    w_up,
    w_down,
    s_gate,
    s_up,
    s_down,
):
    ep_count = lax.axis_size("ep")
    tok_count, top_count = expert_ids.shape
    quarter_width = tokens.shape[1]
    width = quarter_width * lax.axis_size("tp")
    expert_count = w_gate.shape[0] * ep_count
    capacity = (5 * tok_count * top_count + 4 * expert_count - 1) // (4 * expert_count)
    slot_count = expert_count * capacity
    picks_flat = expert_ids.reshape(-1)
    onehot = (picks_flat[:, None] == jnp.arange(expert_count, dtype=jnp.int32)[None, :]).astype(
        jnp.int32
    )
    slot_rank = jnp.sum((jnp.cumsum(onehot, axis=0) - onehot) * onehot, axis=1)
    slot_index = (picks_flat * capacity + slot_rank).reshape(tok_count, top_count)
    matches = jnp.arange(slot_count, dtype=jnp.int32)[:, None, None] == slot_index[None, :, :]
    dispatch = jnp.any(matches, axis=2).astype(jnp.bfloat16)
    weighting = jnp.sum(jnp.where(matches, gate_weights[None, :, :top_count], 0.0), axis=2)
    slot_gate = jnp.sum(weighting, axis=1)
    shadow_weight = gate_weights[:, top_count] * shadow_mask.astype(jnp.float32)
    x_full, dy_full = (
        lax.all_gather(tokens, "tp", axis=1, tiled=True),
        lax.all_gather(cotangent, "tp", axis=1, tiled=True),
    )
    rows_x = jnp.dot(dispatch, tokens, preferred_element_type=jnp.float32).astype(jnp.bfloat16)
    rows_dy = jnp.dot(dispatch, cotangent, preferred_element_type=jnp.float32)
    rows_dout = (slot_gate[:, None] * rows_dy).astype(jnp.bfloat16)
    recv_x, recv_dout = (
        lax.all_to_all(
            rows_x.reshape(ep_count, -1, quarter_width),
            "ep",
            split_axis=0,
            concat_axis=0,
            tiled=True,
        ),
        lax.all_to_all(
            rows_dout.reshape(ep_count, -1, quarter_width),
            "ep",
            split_axis=0,
            concat_axis=0,
            tiled=True,
        ),
    )
    expert_x, expert_dout = (
        lax.all_gather(recv_x.reshape(-1, quarter_width), "tp", axis=1, tiled=True),
        lax.all_gather(recv_dout.reshape(-1, quarter_width), "tp", axis=1, tiled=True),
    )
    partial_out, hidden, grad_pre_gate, grad_pre_up = expert_pass(
        expert_x, expert_dout, w_gate[0], w_up[0], w_down[0]
    )
    grad_gate = contract_rows(expert_x, grad_pre_gate).astype(jnp.bfloat16)[None]
    grad_up = contract_rows(expert_x, grad_pre_up).astype(jnp.bfloat16)[None]
    grad_down = contract_rows(hidden, expert_dout).astype(jnp.bfloat16)[None]
    full_gate, full_up, full_down = (
        lax.all_gather(s_gate, "ep", axis=0, tiled=True),
        lax.all_gather(s_up, "ep", axis=0, tiled=True),
        lax.all_gather(s_down, "ep", axis=1, tiled=True),
    )
    shadow_dout = (shadow_weight[:, None] * dy_full.astype(jnp.float32)).astype(jnp.bfloat16)
    shadow_out, shadow_hidden, shadow_gate_pre, shadow_up_pre = expert_pass(
        x_full, shadow_dout, full_gate, full_up, full_down
    )
    shadow_sums = lax.psum_scatter(
        jnp.concatenate(
            [
                contract_rows(x_full, shadow_gate_pre),
                contract_rows(x_full, shadow_up_pre),
                contract_rows(shadow_dout, shadow_hidden),
            ],
            axis=1,
        ).astype(jnp.bfloat16),
        "ep",
        scatter_dimension=0,
        tiled=True,
    ).astype(jnp.float32)
    hidden_part = s_gate.shape[1]
    grad_s_gate = shadow_sums[:, :hidden_part].astype(jnp.bfloat16)
    grad_s_up = shadow_sums[:, hidden_part : 2 * hidden_part].astype(jnp.bfloat16)
    grad_s_down = shadow_sums[:, 2 * hidden_part :].T.astype(jnp.bfloat16)
    back_rows = lax.all_to_all(
        partial_out.reshape(ep_count, -1, width), "ep", split_axis=0, concat_axis=0, tiled=True
    ).reshape(-1, width)
    term = weigh_rows(weighting.T, back_rows)
    term = term + shadow_weight[:, None] * shadow_out.astype(jnp.float32)
    mixed = lax.psum_scatter(term.astype(jnp.bfloat16), "tp", scatter_dimension=1, tiled=True)
    return (mixed, grad_gate, grad_up, grad_down, grad_s_gate, grad_s_up, grad_s_down)


ANY = pl.BlockSpec(memory_space=pl.ANY)
VMEM_LIMIT = 60 * 1024 * 1024
SHORT = pl.CostEstimate(flops=1, bytes_accessed=1, transcendentals=0)


def swap_pairs(count, bit):
    return [(i, i ^ bit) for i in range(count)]


def dot32(left, right):
    return jnp.dot(left, right, preferred_element_type=jnp.float32)


def contract_last(left, right):
    return lax.dot_general(
        left, right, (((1,), (1,)), ((), ())), preferred_element_type=jnp.float32
    )


def shape_of(*dims, dtype=jnp.bfloat16):
    return jax.ShapeDtypeStruct(dims, dtype)


def after(arrays, *earlier):
    def nothing(*refs):
        del refs

    count = len(arrays)
    return pl.pallas_call(
        nothing,
        out_shape=[jax.ShapeDtypeStruct(a.shape, a.dtype) for a in arrays],
        in_specs=[ANY] * (count + len(earlier)),
        out_specs=[ANY] * count,
        input_output_aliases={i: i for i in range(count)},
        compiler_params=pltpu.CompilerParams(vmem_limit_bytes=VMEM_LIMIT),
        cost_estimate=SHORT,
        name="after",
    )(*arrays, *earlier)


def kernel_call(body, grid, in_specs, out_specs, out_shape, operands, scratch, name, column=None, earlier=()):
    count = len(operands)

    def run(column_ref, *refs):
        del column_ref
        body(*refs[:count], *refs[count + len(earlier) :])

    column = jnp.zeros((1,), jnp.int32) if column is None else column.reshape(1).astype(jnp.int32)
    return pl.pallas_call(
        run,
        out_shape=out_shape,
        grid_spec=pltpu.PrefetchScalarGridSpec(
            num_scalar_prefetch=1,
            grid=grid,
            in_specs=list(in_specs) + [ANY] * len(earlier),
            out_specs=out_specs,
            scratch_shapes=scratch,
        ),
        compiler_params=pltpu.CompilerParams(vmem_limit_bytes=VMEM_LIMIT),
        cost_estimate=SHORT,
        name=name,
    )(column, *operands, *earlier)


def whole(array):
    return pl.BlockSpec(array.shape, lambda *_: (0,) * len(array.shape))


def join_plane(column, *pieces, earlier=()):
    rows, quarter = pieces[0].shape
    count, halves = 4, len(pieces) - 3
    chunk = rows // 4
    per = 4 // halves

    def body(column_ref, *refs):
        out = refs[-1]
        for own_column in range(count):
            for j, from_diagonal in enumerate(refs[3 : 3 + halves]):

                @pl.when((column_ref[0] == own_column) & (pl.program_id(0) // per == j))
                def _(from_diagonal=from_diagonal, own_column=own_column):
                    for bit, source in enumerate(refs[:3] + (from_diagonal,)):
                        place = own_column ^ bit
                        out[:, place * quarter : (place + 1) * quarter] = source[...]

    def diagonal_spec(j):
        return pl.BlockSpec((chunk, quarter), lambda i, *_: (jnp.clip(i - j * per, 0, per - 1), 0))

    return pl.pallas_call(
        body,
        out_shape=shape_of(rows, count * quarter),
        grid_spec=pltpu.PrefetchScalarGridSpec(
            num_scalar_prefetch=1,
            grid=(4,),
            in_specs=[pl.BlockSpec((chunk, quarter), lambda i, *_: (i, 0))] * 3
            + [diagonal_spec(j) for j in range(halves)]
            + [ANY] * len(earlier),
            out_specs=pl.BlockSpec((chunk, count * quarter), lambda i, *_: (i, 0)),
        ),
        compiler_params=pltpu.CompilerParams(vmem_limit_bytes=VMEM_LIMIT),
        cost_estimate=SHORT,
        name="join_plane",
    )(column.reshape(1).astype(jnp.int32), *pieces, *earlier)


def stack_pieces(pieces, earlier=()):
    rows, columns = pieces[0].shape
    count = len(pieces)

    def body(*refs):
        for i, ref in enumerate(refs[:count]):

            @pl.when(pl.program_id(0) == i)
            def _():
                refs[-1][...] = ref[...]

    return pl.pallas_call(
        body,
        out_shape=shape_of(count * rows, columns),
        grid=(count,),
        in_specs=[pl.BlockSpec((rows, columns), lambda i: (0, 0))] * count + [ANY] * len(earlier),
        out_specs=pl.BlockSpec((rows, columns), lambda i: (i, 0)),
        compiler_params=pltpu.CompilerParams(vmem_limit_bytes=VMEM_LIMIT),
        cost_estimate=SHORT,
        name="stack_pieces",
    )(*pieces, *earlier)


def on_piece(chip_ref, refs, use):
    step = pl.program_id(0)
    shift = chip_ref[0] ^ (step // 2)
    for i, ref in enumerate(refs):
        for core in range(2):

            @pl.when((shift == i) & (lax.rem(step, 2) == core))
            def _(ref=ref, core=core):
                use(ref.at[0, core])


def lay_out_shadow(pieces, down, units, chip, earlier=()):
    count = len(pieces)
    ep_count = 2 * count
    block_width = pieces[0].shape[3]
    apart = units + -units % 128
    all_units, width = down.shape

    def body(chip_ref, *refs):
        shadow_ref, out = refs[-2:]

        def use(ref):
            shadow_ref[...] = jnp.zeros_like(shadow_ref)
            shadow_ref[:units, :] = ref[:units, :]
            shadow_ref[apart : apart + units, :] = ref[units : 2 * units, :]
            out[units:, :] = jnp.zeros((apart - units, block_width), jnp.bfloat16)
            out[:units, :] = ref[2 * units : 3 * units, :]

        on_piece(chip_ref, refs[:count], use)

    return pl.pallas_call(
        body,
        out_shape=[shape_of(2 * apart, width), shape_of(all_units, width)],
        grid_spec=pltpu.PrefetchScalarGridSpec(
            num_scalar_prefetch=1,
            grid=(ep_count,),
            in_specs=[whole(p) for p in pieces] + [ANY] * (1 + len(earlier)),
            out_specs=[
                pl.BlockSpec((2 * apart, block_width), lambda e, *_: (0, e)),
                pl.BlockSpec((apart, block_width), lambda e, *_: (all_units // apart - 1, e)),
            ],
        ),
        input_output_aliases={1 + count: 1},
        compiler_params=pltpu.CompilerParams(vmem_limit_bytes=VMEM_LIMIT),
        cost_estimate=SHORT,
        name="lay_out_shadow",
    )(chip.reshape(1).astype(jnp.int32), *pieces, down, *earlier)


def lay_out_grads(pieces, units, chip, earlier=()):
    count = len(pieces)
    ep_count = 2 * count
    block_width = pieces[0].shape[3]
    hidden = ep_count * units

    def body(chip_ref, *refs):
        gate_ref, up_ref, down_ref, gate_t, up_t = refs[-5:]
        place = pl.ds(pl.multiple_of(pl.program_id(0) * units, 16), units)

        def use(ref):
            gate_t[place, :] = ref[:units, :]
            up_t[place, :] = ref[units : 2 * units, :]
            down_ref[place, :] = ref[2 * units :, :]

        on_piece(chip_ref, refs[:count], use)

        @pl.when(pl.program_id(0) == ep_count - 1)
        def _():
            gate_ref[...] = gate_t[...].T
            up_ref[...] = up_t[...].T

    return pl.pallas_call(
        body,
        out_shape=[shape_of(block_width, hidden), shape_of(block_width, hidden), shape_of(hidden, block_width)],
        grid_spec=pltpu.PrefetchScalarGridSpec(
            num_scalar_prefetch=1,
            grid=(ep_count,),
            in_specs=[whole(p) for p in pieces] + [ANY] * len(earlier),
            out_specs=[pl.BlockSpec((block_width, hidden), lambda *_: (0, 0))] * 2
            + [pl.BlockSpec((hidden, block_width), lambda *_: (0, 0))],
            scratch_shapes=[pltpu.VMEM((hidden, block_width), jnp.bfloat16)] * 2,
        ),
        compiler_params=pltpu.CompilerParams(vmem_limit_bytes=VMEM_LIMIT),
        cost_estimate=SHORT,
        name="lay_out_grads",
    )(chip.reshape(1).astype(jnp.int32), *pieces, *earlier)


def row_specs(groups, tile):
    def spec(index, rows):
        return pl.BlockSpec((rows, tile), lambda k, *_: (index, k))

    return [spec(index, rows) for _, index, rows in groups]


def apply_gate(pre_gate, pre_up):
    sigmoid_gate = jax.nn.sigmoid(pre_gate)
    activated = pre_gate * sigmoid_gate
    hidden = (activated * pre_up).astype(jnp.bfloat16)
    return hidden, pre_up * sigmoid_gate * (1.0 + pre_gate * (1.0 - sigmoid_gate)), activated


def clear_first(acc):
    @pl.when(pl.program_id(0) == 0)
    def _():
        acc[...] = jnp.zeros_like(acc)


def rows_operand(refs, groups, held):
    if len(groups) == 1:
        return refs[0][...]
    return stage_rows(refs, groups, held)


def forward_rows(groups, w_both, tile, transposed=False, earlier=()):
    rows = sum(g[2] for g in groups)
    if transposed:
        units, width = w_both.shape[0] // 2, w_both.shape[1]
        tile_spec = pl.BlockSpec((2 * units, tile), lambda k, *_: (0, k))
    else:
        width, units = w_both.shape[0], w_both.shape[1] // 2
        tile_spec = pl.BlockSpec((tile, 2 * units), lambda k, *_: (k, 0))
    steps = width // tile

    def body(*refs):
        n = len(groups)
        both_ref, hidden_ref, slope_ref, act_ref, acc, held = refs[n:]
        clear_first(acc)
        operand = rows_operand(refs[:n], groups, held)
        acc[...] += contract_last(operand, both_ref[...]) if transposed else dot32(operand, both_ref[...])

        @pl.when(pl.program_id(0) == steps - 1)
        def _():
            chunk = 128

            @pl.loop(0, rows // chunk)
            def _(i):
                part = pl.ds(pl.multiple_of(i * chunk, chunk), chunk)
                hidden, slope, act = apply_gate(acc[part, :units], acc[part, units:])
                hidden_ref[part, :] = hidden
                slope_ref[part, :] = slope.astype(jnp.bfloat16)
                act_ref[part, :] = act.astype(jnp.bfloat16)

    out_spec = pl.BlockSpec((rows, units), lambda *_: (0, 0))
    return kernel_call(
        body,
        (steps,),
        row_specs(groups, tile) + [tile_spec],
        [out_spec] * 3,
        [shape_of(rows, units)] * 3,
        [g[0] for g in groups] + [w_both],
        [pltpu.VMEM((rows, 2 * units), jnp.float32), pltpu.VMEM((rows, tile), jnp.bfloat16)],
        "forward_rows",
        earlier=earlier,
    )


def weigh_hidden(hidden_near, hidden_far, hidden_s, pieces, first_row, slot_rows, core, earlier=()):
    count = len(pieces)
    rows, units_s = hidden_s.shape
    units = hidden_near.shape[1]
    slots = [(s, 0) for s in list(range(1, count)) + [0]] + [(s, 1) for s in range(count)]

    def body(core_ref, *refs):
        near_ref, far_ref, s_ref, *piece_refs = refs[: 3 + count]
        out, w_ref, w_s_ref = refs[-3:]
        near, far = 0, 0
        for i, (slot, other) in enumerate(slots):
            part = pl.ds(i * slot_rows, slot_rows)
            table = piece_refs[slot][0, core_ref[0] ^ other, first_row : first_row + 16, :][:1].astype(jnp.float32)

            def column(j):
                both = table[:, j * slot_rows : (j + 1) * slot_rows]
                both = both + table[:, (j + 2) * slot_rows : (j + 3) * slot_rows]
                return jnp.broadcast_to(both, (slot_rows, slot_rows)).T[:, :1]

            weight, weight_s = column(0), column(1)
            w_ref[part, :] = weight
            w_s_ref[part, :] = weight_s
            if slot == 0:
                hidden = near_ref[near : near + slot_rows, :]
                near += slot_rows
            else:
                hidden = far_ref[far : far + slot_rows, :]
                far += slot_rows
            out[part, :units] = (hidden.astype(jnp.float32) * weight).astype(jnp.bfloat16)
            out[part, units:] = (s_ref[part, :].astype(jnp.float32) * weight_s).astype(jnp.bfloat16)

    return pl.pallas_call(
        body,
        out_shape=[
            shape_of(rows, units + units_s),
            shape_of(rows, 1, dtype=jnp.float32),
            shape_of(rows, 1, dtype=jnp.float32),
        ],
        grid_spec=pltpu.PrefetchScalarGridSpec(
            num_scalar_prefetch=1,
            grid=(1,),
            in_specs=[whole(a) for a in (hidden_near, hidden_far, hidden_s, *pieces)] + [ANY] * len(earlier),
            out_specs=[
                pl.BlockSpec((rows, units + units_s), lambda *_: (0, 0)),
                pl.BlockSpec((rows, 1), lambda *_: (0, 0)),
                pl.BlockSpec((rows, 1), lambda *_: (0, 0)),
            ],
        ),
        compiler_params=pltpu.CompilerParams(vmem_limit_bytes=VMEM_LIMIT),
        cost_estimate=SHORT,
        name="weigh_hidden",
    )(core.reshape(1).astype(jnp.int32), hidden_near, hidden_far, hidden_s, *pieces, *earlier)


def output_other(weighted, down, column, parts, slot_rows, quarter, earlier=()):
    rows, units = weighted.shape
    count = rows // 2 // parts

    def body(weighted_ref, down_ref, *outs):
        value = dot32(weighted_ref[...], down_ref[...]).astype(jnp.bfloat16)
        for i, out in enumerate(outs):
            first, last = slot_rows + i * count, slot_rows + (i + 1) * count
            kept = min(last, rows // 2) - first
            out[:kept, :] = value[first : first + kept]
            if kept < count:
                out[kept:, :] = value[: count - kept]

    return kernel_call(
        body,
        (4,),
        [
            pl.BlockSpec((rows // 2, units), lambda *_: (1, 0)),
            pl.BlockSpec((units, quarter), lambda q, column_ref: (0, column_ref[0] ^ q)),
        ],
        [pl.BlockSpec((count, quarter), lambda q, *_: (0, q))] * parts,
        [shape_of(count, 4 * quarter)] * parts,
        [weighted, down],
        [],
        "output_other",
        column=column,
        earlier=earlier,
    )


def output_own(weighted, got, down, column, quarter, earlier=()):
    count, units = got[0].shape[0], weighted.shape[1]
    parts = len(got)

    def body(weighted_ref, down_ref, *refs):
        product = dot32(weighted_ref[...], down_ref[...])
        for i in range(parts):
            value = product[i * count : (i + 1) * count] + refs[i][...].astype(jnp.float32)
            for j, out in enumerate(refs[parts + 4 * i : parts + 4 * i + 4]):

                @pl.when(pl.program_id(0) == 3 - j)
                def _(out=out, value=value):
                    out[...] = value.astype(out.dtype)

    full = pl.BlockSpec((count, quarter), lambda *_: (0, 0))
    out = kernel_call(
        body,
        (4,),
        [
            pl.BlockSpec((parts * count, units), lambda *_: (0, 0)),
            pl.BlockSpec((units, quarter), lambda q, column_ref: (0, column_ref[0] ^ 3 ^ q)),
        ]
        + [pl.BlockSpec((count, quarter), lambda q, *_: (0, 3 - q))] * parts,
        [full] * (4 * parts),
        ([shape_of(count, quarter, dtype=jnp.float32)] + [shape_of(count, quarter)] * 3) * parts,
        [weighted, down] + list(got),
        [],
        "output_own",
        column=column,
        earlier=earlier,
    )
    return [out[4 * i : 4 * i + 4] for i in range(parts)]


def backward_rows(groups, down, parts, per_row, first_row, tile, earlier=()):
    slope_s, act_s, w_rows, w_shadow = per_row
    rows = sum(g[2] for g in groups)
    units_all, width = down.shape
    units_s = slope_s.shape[1]
    units = units_all - units_s
    steps = width // tile
    arrays = list({id(a): a for part in parts for a in part[:2]}.values())
    places = [[next(i for i, a in enumerate(arrays) if a is b) for b in part[:2]] for part in parts]

    def body(*refs):
        n, m = len(groups), len(arrays)
        down_ref = refs[n]
        array_refs = refs[n + 1 : n + 1 + m]
        slope_s_ref, act_s_ref, w_ref, w_s_ref, pre_ref, pre_s_ref, acc, held = refs[n + 1 + m :]
        clear_first(acc)
        acc[...] += contract_last(rows_operand(refs[:n], groups, held), down_ref[...])

        @pl.when(pl.program_id(0) == steps - 1)
        def _():
            chunk = 128
            start = 0
            for (_, _, count), (_, _, first), (slope_at, act_at) in zip(groups, parts, places):

                @pl.loop(0, count // chunk)
                def _(i, start=start, first=first, slope_ref=array_refs[slope_at], act_ref=array_refs[act_at]):
                    source = pl.ds(pl.multiple_of(first + i * chunk, chunk), chunk)
                    part = pl.ds(pl.multiple_of(start + i * chunk, chunk), chunk)
                    whole_part = pl.ds(pl.multiple_of(first_row + start + i * chunk, chunk), chunk)
                    grad = acc[part, :units] * w_ref[whole_part, :]
                    pre_ref[part, :units] = (grad * slope_ref[source, :]).astype(jnp.bfloat16)
                    pre_ref[part, units:] = (grad * act_ref[source, :]).astype(jnp.bfloat16)
                    grad = acc[part, units:] * w_s_ref[whole_part, :]
                    pre_s_ref[part, :units_s] = (grad * slope_s_ref[whole_part, :]).astype(jnp.bfloat16)
                    pre_s_ref[part, units_s:] = (grad * act_s_ref[whole_part, :]).astype(jnp.bfloat16)

                start += count

    extra = arrays + [slope_s, act_s, w_rows, w_shadow]
    return kernel_call(
        body,
        (steps,),
        row_specs(groups, tile) + [pl.BlockSpec((units_all, tile), lambda k, *_: (0, k))] + [whole(a) for a in extra],
        [pl.BlockSpec((rows, 2 * units), lambda *_: (0, 0)), pl.BlockSpec((rows, 2 * units_s), lambda *_: (0, 0))],
        [shape_of(rows, 2 * units), shape_of(rows, 2 * units_s)],
        [g[0] for g in groups] + [down] + extra,
        [pltpu.VMEM((rows, units_all), jnp.float32), pltpu.VMEM((rows, tile), jnp.bfloat16)],
        "backward_rows",
        earlier=earlier,
    )


def stage_rows(refs, groups, held):
    start = 0
    for ref, (_, _, count) in zip(refs, groups):
        held[pl.ds(start, count), :] = ref[...]
        start += count
    return held[...]


def shadow_grads(x_groups, dy_groups, pre_s, weighted, units, block, tile, earlier=()):
    rows, wide = weighted.shape[0], pre_s[0].shape[1]
    apart = wide // 2
    width = x_groups[0][0].shape[1]
    m = len(pre_s)

    def body(*refs):
        n = len(x_groups)
        pre_refs = refs[2 * n : 2 * n + m]
        hidden_ref, out, held, pre_t, hidden_t = refs[2 * n + m :]

        @pl.when(pl.program_id(0) == 0)
        def _():
            start = 0
            for ref in pre_refs:
                pre_t[:, start : start + ref.shape[0]] = ref[...].T
                start += ref.shape[0]
            hidden_t[...] = hidden_ref[...].T

        value = dot32(pre_t[...], stage_rows(refs[:n], x_groups, held)).astype(jnp.bfloat16)
        for i in range(tile // block):
            part = slice(i * block, (i + 1) * block)
            out[i, :units, :] = value[:units, part]
            out[i, units : 2 * units, :] = value[apart : apart + units, part]
        value = dot32(hidden_t[...], stage_rows(refs[n : 2 * n], dy_groups, held)).astype(jnp.bfloat16)
        for i in range(tile // block):
            out[i, 2 * units :, :] = value[:units, i * block : (i + 1) * block]

    (out,) = kernel_call(
        body,
        (width // tile,),
        row_specs(x_groups, tile)
        + row_specs(dy_groups, tile)
        + [whole(p) for p in pre_s]
        + [pl.BlockSpec((rows, apart), lambda *_: (0, weighted.shape[1] // apart - 1))],
        [pl.BlockSpec((tile // block, 3 * units, block), lambda k, *_: (k, 0, 0))],
        [shape_of(width // block, 3 * units, block)],
        [g[0] for g in x_groups + dy_groups] + list(pre_s) + [weighted],
        [
            pltpu.VMEM((rows, tile), jnp.bfloat16),
            pltpu.VMEM((wide, rows), jnp.bfloat16),
            pltpu.VMEM((apart, rows), jnp.bfloat16),
        ],
        "shadow_grads",
        earlier=earlier,
    )
    return out


def input_grads(groups, pre, tile, earlier=()):
    both = pre[0].shape[1]
    rows = sum(p.shape[0] for p in pre)
    units = both // 2
    width = groups[0][0].shape[1]
    m = len(pre)

    def body(*refs):
        n = len(groups)
        gate_ref, up_ref, held, pre_held = refs[n + m :]

        @pl.when(pl.program_id(0) == 0)
        def _():
            start = 0
            for ref in refs[n : n + m]:
                pre_held[start : start + ref.shape[0], :] = ref[...]
                start += ref.shape[0]

        value = contract_rows(stage_rows(refs[:n], groups, held), pre_held[...])
        gate_ref[...] = value[:, :units].astype(jnp.bfloat16)
        up_ref[...] = value[:, units:].astype(jnp.bfloat16)

    return kernel_call(
        body,
        (width // tile,),
        row_specs(groups, tile) + [whole(p) for p in pre],
        [pl.BlockSpec((tile, units), lambda k, *_: (k, 0))] * 2,
        [shape_of(width, units)] * 2,
        [g[0] for g in groups] + list(pre),
        [pltpu.VMEM((rows, tile), jnp.bfloat16), pltpu.VMEM((rows, both), jnp.bfloat16)],
        "input_grads",
        earlier=earlier,
    )


def down_grad(groups, weighted, units, tile, earlier=()):
    rows = weighted.shape[0]
    width = groups[0][0].shape[1]

    def body(*refs):
        n = len(groups)
        hidden_ref, out, held, hidden_t = refs[n:]

        @pl.when(pl.program_id(0) == 0)
        def _():
            hidden_t[...] = hidden_ref[...].T

        out[...] = dot32(hidden_t[...], stage_rows(refs[:n], groups, held)).astype(jnp.bfloat16)

    (out,) = kernel_call(
        body,
        (width // tile,),
        row_specs(groups, tile) + [pl.BlockSpec((rows, units), lambda *_: (0, 0))],
        [pl.BlockSpec((units, tile), lambda k, *_: (0, k))],
        [shape_of(units, width)],
        [g[0] for g in groups] + [weighted],
        [pltpu.VMEM((rows, tile), jnp.bfloat16), pltpu.VMEM((units, rows), jnp.bfloat16)],
        "down_grad",
        earlier=earlier,
    )
    return out


def send_along_z(own):
    ep_count = lax.axis_size("ep")
    return [lax.ppermute(own, "ep", swap_pairs(ep_count, 2 * s)) for s in range(1, ep_count // 2)]


def swap_cores(block):
    return lax.ppermute(block, "ep", swap_pairs(lax.axis_size("ep"), 1))


def send_plane(*pieces):
    pieces = pieces * 3 if len(pieces) == 1 else pieces
    return [lax.ppermute(p, "tp", swap_pairs(lax.axis_size("tp"), bit)) for p, bit in zip(pieces, (1, 2, 3))]


def send_diagonal(from_x, from_y):
    along, across = [swap_pairs(lax.axis_size("tp"), bit) for bit in (1, 2)]
    half = from_x.shape[0] // 2
    return [lax.ppermute(from_x[:half], "tp", across), lax.ppermute(from_y[half:], "tp", along)]


def exchange_cores(blocks, cuts=1):
    ep_count, core = lax.axis_size("ep"), lax.axis_index("ep") % 2
    pairs = blocks.reshape(ep_count // 2, 2, *blocks.shape[1:])
    kept = jnp.where(core == 0, pairs[:, 0], pairs[:, 1])
    given = jnp.where(core == 0, pairs[:, 1], pairs[:, 0])
    return kept, [swap_cores(part) for part in jnp.split(given, cuts)]


def chip_pieces(kept, taken):
    ep_count, me = lax.axis_size("ep"), lax.axis_index("ep")
    chips, chip, core = ep_count // 2, me // 2, me % 2
    taken = jnp.concatenate(taken, axis=0)
    both = jnp.stack([jnp.where(core == 0, kept, taken), jnp.where(core == 0, taken, kept)], axis=1)
    return [lax.dynamic_index_in_dim(both, chip ^ shift, 0) for shift in range(chips)]


def send_piece(piece, shift):
    return lax.ppermute(piece, "ep", swap_pairs(lax.axis_size("ep"), 2 * shift))


def dense_shards(
    tokens,
    cotangent,
    expert_ids,
    gate_weights,
    shadow_mask,
    w_gate,
    w_up,
    w_down,
    s_gate,
    s_up,
    s_down,
):
    ep_count, tp_count = lax.axis_size("ep"), lax.axis_size("tp")
    ep_index, tp_index = lax.axis_index("ep"), lax.axis_index("tp")
    tok_count, top_count = expert_ids.shape
    quarter = tokens.shape[1]
    width = quarter * tp_count
    hidden_part = w_gate.shape[2]
    shadow_part = hidden_part // ep_count
    block_width = s_gate.shape[0]
    steps = ep_count // 2
    later = (steps - 1) * tok_count
    tile = width // 8
    along, across = swap_pairs(tp_count, 1), swap_pairs(tp_count, 2)

    picked = expert_ids[None, :, :] == jnp.arange(ep_count, dtype=jnp.int32)[:, None, None]
    table = jnp.sum(jnp.where(picked, gate_weights[None, :, :top_count], 0.0), axis=2)
    shadow_weight = gate_weights[:, top_count] * shadow_mask.astype(jnp.float32)
    table = jnp.concatenate([table, jnp.broadcast_to(shadow_weight[None], table.shape)], axis=1)
    table = jnp.concatenate(split_parts(table), axis=1)
    table = jnp.pad(table[:, None, :], ((0, 0), (0, 15), (0, block_width - table.shape[1])))
    shadow_blocks = jnp.concatenate(
        [
            s_gate.T.reshape(ep_count, shadow_part, block_width),
            s_up.T.reshape(ep_count, shadow_part, block_width),
            s_down.reshape(ep_count, shadow_part, block_width),
            table,
        ],
        axis=1,
    )

    x_z = send_along_z(tokens)
    near = stack_pieces([tokens, cotangent])
    near_x, near_y = send_plane(near, near)
    near_x, near_y = after([near_x, near_y], x_z[0])
    near_d = send_diagonal(near_x, near_y)
    w_both = jnp.concatenate([w_gate[0], w_up[0]], axis=1)
    fenced = after([*near_d, *x_z], w_both, shadow_blocks)
    near_d, x_z = fenced[:2], fenced[2:]

    x_piece = stack_pieces(x_z)
    x_plane = send_plane(x_piece, x_piece)
    dy_z = send_along_z(cotangent)
    near_own = join_plane(tp_index, near, near_x, near_y, *near_d)
    near_other = swap_cores(near_own)
    x_near = [(near_own, 0, tok_count), (near_other, 0, tok_count)]
    hidden_near, slope_near, act_near = forward_rows(x_near, w_both, 2 * tile)
    spare_rows = -shadow_part % 128 + shadow_part
    down = jnp.pad(w_down[0], ((0, spare_rows), (0, 0)))
    *x_plane, down = after([*x_plane, down], *dy_z, hidden_near)
    x_plane = [*x_plane, *send_diagonal(*x_plane)]
    (shadow_blocks,) = after([shadow_blocks], x_z[0])
    shadow_kept, shadow_taken = exchange_cores(shadow_blocks)
    fenced = after([*x_plane[2:], *shadow_taken, *dy_z])
    x_plane[2:], shadow_taken, dy_z = fenced[:2], fenced[2:3], fenced[3:]

    dy_piece = stack_pieces(dy_z)
    dy_plane = send_plane(dy_piece)
    shadow_pieces = chip_pieces(shadow_kept, shadow_taken)
    for shift in range(1, steps - 1):
        shadow_pieces[shift] = send_piece(shadow_pieces[shift], shift)
    x_own = join_plane(tp_index, x_piece, *x_plane, earlier=[dy_piece])
    x_other = swap_cores(x_own)
    x_far = [(x_own, 0, later), (x_other, 0, later)]
    x_groups = [x_far[0], x_near[0], x_near[1], x_far[1]]
    hidden_far, slope_far, act_far = forward_rows(x_far, w_both, 2 * tile)
    shadow_pieces[-1:] = after(shadow_pieces[-1:], hidden_far)
    shadow_pieces[-1] = send_piece(shadow_pieces[-1], steps - 1)
    chip = ep_index // 2
    shadow_in, down = lay_out_shadow(shadow_pieces, down, shadow_part, chip, earlier=[hidden_far])
    hidden_s, slope_s, act_s = forward_rows(x_groups, shadow_in, 2 * tile, transposed=True)

    weighted, w_rows, w_shadow = weigh_hidden(
        hidden_near, hidden_far, hidden_s, shadow_pieces, 3 * shadow_part, tok_count, ep_index % 2
    )

    parts = 2 if steps % 2 == 0 else 1
    sent = output_other(weighted, down, tp_index, parts, tok_count, quarter)
    got = [swap_cores(array) for array in sent]
    dy_plane = after(dy_plane, *sent)

    dy_own = join_plane(tp_index, dy_piece, *dy_plane)
    dy_other = swap_cores(dy_own)
    dy_groups = [(dy_own, 0, later), (near_own, 1, tok_count), (near_other, 1, tok_count), (dy_other, 0, later)]
    segments = [
        (slope_far, act_far, 0),
        (slope_near, act_near, 0),
        (slope_near, act_near, tok_count),
        (slope_far, act_far, later),
    ]
    per_row = (slope_s, act_s, w_rows, w_shadow)
    pre_first, pre_s_first = backward_rows(dy_groups[:3], down, segments[:3], per_row, 0, 2 * tile)
    owns = output_own(weighted, got, down, tp_index, quarter, earlier=[pre_first])
    sums = [send_plane(*own[1:]) for own in owns]
    first_rows = sum(g[2] for g in dy_groups[:3])
    pre_last, pre_s_last = backward_rows(
        dy_groups[3:], down, segments[3:], per_row, first_rows, 2 * tile, earlier=[own[1] for own in owns]
    )
    pre, pre_s = [pre_first, pre_last], [pre_s_first, pre_s_last]
    grad_s = shadow_grads(x_groups, dy_groups, pre_s, weighted, shadow_part, block_width, 2 * tile)
    grad_pieces = chip_pieces(*exchange_cores(grad_s))

    def slot_rows(i):
        part = slice(i % (steps // parts) * tok_count, (i % (steps // parts) + 1) * tok_count)
        total = owns[i * parts // steps][0][part]
        for array in sums[i * parts // steps]:
            total = total + array[part].astype(jnp.float32)
        return total

    def send_rows(piece, i):
        return lax.ppermute(piece, "ep", swap_pairs(ep_count, 2 * (i + 1)))

    early = steps // parts if parts > 1 else 0
    sums[0] = after(sums[0], grad_s)
    rows = [slot_rows(i).astype(jnp.bfloat16) for i in range(early)]
    grad_down = down_grad(dy_groups, weighted, hidden_part, 2 * tile, earlier=[*rows, grad_pieces[0]])
    rows = [send_rows(piece, i) for i, piece in enumerate(rows)]
    fenced = after([*rows, *grad_pieces[1:]], grad_down)
    rows, grad_pieces[1:] = list(fenced[:early]), fenced[early:]
    grad_gate, grad_up = input_grads(x_groups, pre, 2 * tile, earlier=[grad_pieces[1]])
    for shift in range(1, steps - 1):
        grad_pieces[shift] = send_piece(grad_pieces[shift], shift)
    fenced = after([*sums[-1], *grad_pieces[1:]], grad_gate)
    sums[-1], grad_pieces[1:] = fenced[:3], fenced[3:]
    grad_pieces[-1] = send_piece(grad_pieces[-1], steps - 1)
    rows += [send_rows(slot_rows(i).astype(jnp.bfloat16), i) for i in range(early, steps - 1)]
    total = slot_rows(steps - 1)
    for piece in rows:
        total = total + piece.astype(jnp.float32)
    mixed = total.astype(jnp.bfloat16)

    grads_s = lay_out_grads(grad_pieces, shadow_part, chip)
    return (mixed, grad_gate[None], grad_up[None], grad_down[None], *grads_s)


def shards(tokens, cotangent, expert_ids, *others):
    tp_count, ep_count = lax.axis_size("tp"), lax.axis_size("ep")
    tok_count, top_count = expert_ids.shape
    rows = (5 * tok_count * top_count) // 4
    chips = ep_count // 2
    fits = tp_count == 4 and ep_count == 2 * chips and chips & (chips - 1) == 0 and tok_count % 128 == 0
    dense = fits and ep_count * tok_count <= 3 * rows
    return (dense_shards if dense else routed_shards)(tokens, cotangent, expert_ids, *others)


def solution(mesh):
    return jax.shard_map(
        shards,
        mesh=mesh,
        in_specs=(
            P("ep", "tp"),
            P("ep", "tp"),
            P("ep", None),
            P("ep", None),
            P("ep"),
            P("ep", None, "tp"),
            P("ep", None, "tp"),
            P("ep", "tp", None),
            P("ep", "tp"),
            P("ep", "tp"),
            P("tp", "ep"),
        ),
        out_specs=(
            P("ep", "tp"),
            P("ep", None, "tp"),
            P("ep", None, "tp"),
            P("ep", "tp", None),
            P("ep", "tp"),
            P("ep", "tp"),
            P("tp", "ep"),
        ),
        check_vma=False,
    )
```

```python
import functools

import jax
import jax.numpy as jnp
from jax import lax
from jax.experimental import pallas as pl
from jax.experimental.pallas import tpu as pltpu
from jax.sharding import PartitionSpec as P


def contract_rows(left, right):
    return lax.dot_general(
        left, right, (((0,), (0,)), ((), ())), preferred_element_type=jnp.float32
    )


def split_parts(values):
    upper_part = values.astype(jnp.bfloat16)
    lower_part = (values - upper_part.astype(jnp.float32)).astype(jnp.bfloat16)
    return (upper_part, lower_part)


def weigh_rows(weight_table, rows):
    weight_upper, weight_lower = split_parts(weight_table)
    return jnp.dot(weight_upper, rows, preferred_element_type=jnp.float32) + jnp.dot(
        weight_lower, rows, preferred_element_type=jnp.float32
    )


def expert_pass(rows_x, rows_dout, weight_gate, weight_up, weight_down):
    pre_gate = jnp.dot(rows_x, weight_gate, preferred_element_type=jnp.float32)
    pre_up = jnp.dot(rows_x, weight_up, preferred_element_type=jnp.float32)
    sigmoid_gate = jax.nn.sigmoid(pre_gate)
    activated = pre_gate * sigmoid_gate
    hidden = (activated * pre_up).astype(jnp.bfloat16)
    partial_out = jnp.dot(hidden, weight_down, preferred_element_type=jnp.float32).astype(
        jnp.bfloat16
    )
    hidden_grad = lax.dot_general(
        rows_dout, weight_down, (((1,), (1,)), ((), ())), preferred_element_type=jnp.float32
    )
    grad_pre_gate = (
        hidden_grad * pre_up * sigmoid_gate * (1.0 + pre_gate * (1.0 - sigmoid_gate))
    ).astype(jnp.bfloat16)
    grad_pre_up = (hidden_grad * activated).astype(jnp.bfloat16)
    return (partial_out, hidden, grad_pre_gate, grad_pre_up)


def routed_shards(
    tokens,
    cotangent,
    expert_ids,
    gate_weights,
    shadow_mask,
    w_gate,
    w_up,
    w_down,
    s_gate,
    s_up,
    s_down,
):
    ep_count = lax.axis_size("ep")
    tok_count, top_count = expert_ids.shape
    quarter_width = tokens.shape[1]
    width = quarter_width * lax.axis_size("tp")
    expert_count = w_gate.shape[0] * ep_count
    capacity = (5 * tok_count * top_count + 4 * expert_count - 1) // (4 * expert_count)
    slot_count = expert_count * capacity
    picks_flat = expert_ids.reshape(-1)
    onehot = (picks_flat[:, None] == jnp.arange(expert_count, dtype=jnp.int32)[None, :]).astype(
        jnp.int32
    )
    slot_rank = jnp.sum((jnp.cumsum(onehot, axis=0) - onehot) * onehot, axis=1)
    slot_index = (picks_flat * capacity + slot_rank).reshape(tok_count, top_count)
    matches = jnp.arange(slot_count, dtype=jnp.int32)[:, None, None] == slot_index[None, :, :]
    dispatch = jnp.any(matches, axis=2).astype(jnp.bfloat16)
    weighting = jnp.sum(jnp.where(matches, gate_weights[None, :, :top_count], 0.0), axis=2)
    slot_gate = jnp.sum(weighting, axis=1)
    shadow_weight = gate_weights[:, top_count] * shadow_mask.astype(jnp.float32)
    x_full, dy_full = (
        lax.all_gather(tokens, "tp", axis=1, tiled=True),
        lax.all_gather(cotangent, "tp", axis=1, tiled=True),
    )
    rows_x = jnp.dot(dispatch, tokens, preferred_element_type=jnp.float32).astype(jnp.bfloat16)
    rows_dy = jnp.dot(dispatch, cotangent, preferred_element_type=jnp.float32)
    rows_dout = (slot_gate[:, None] * rows_dy).astype(jnp.bfloat16)
    recv_x, recv_dout = (
        lax.all_to_all(
            rows_x.reshape(ep_count, -1, quarter_width),
            "ep",
            split_axis=0,
            concat_axis=0,
            tiled=True,
        ),
        lax.all_to_all(
            rows_dout.reshape(ep_count, -1, quarter_width),
            "ep",
            split_axis=0,
            concat_axis=0,
            tiled=True,
        ),
    )
    expert_x, expert_dout = (
        lax.all_gather(recv_x.reshape(-1, quarter_width), "tp", axis=1, tiled=True),
        lax.all_gather(recv_dout.reshape(-1, quarter_width), "tp", axis=1, tiled=True),
    )
    partial_out, hidden, grad_pre_gate, grad_pre_up = expert_pass(
        expert_x, expert_dout, w_gate[0], w_up[0], w_down[0]
    )
    grad_gate = contract_rows(expert_x, grad_pre_gate).astype(jnp.bfloat16)[None]
    grad_up = contract_rows(expert_x, grad_pre_up).astype(jnp.bfloat16)[None]
    grad_down = contract_rows(hidden, expert_dout).astype(jnp.bfloat16)[None]
    full_gate, full_up, full_down = (
        lax.all_gather(s_gate, "ep", axis=0, tiled=True),
        lax.all_gather(s_up, "ep", axis=0, tiled=True),
        lax.all_gather(s_down, "ep", axis=1, tiled=True),
    )
    shadow_dout = (shadow_weight[:, None] * dy_full.astype(jnp.float32)).astype(jnp.bfloat16)
    shadow_out, shadow_hidden, shadow_gate_pre, shadow_up_pre = expert_pass(
        x_full, shadow_dout, full_gate, full_up, full_down
    )
    shadow_sums = lax.psum_scatter(
        jnp.concatenate(
            [
                contract_rows(x_full, shadow_gate_pre),
                contract_rows(x_full, shadow_up_pre),
                contract_rows(shadow_dout, shadow_hidden),
            ],
            axis=1,
        ).astype(jnp.bfloat16),
        "ep",
        scatter_dimension=0,
        tiled=True,
    ).astype(jnp.float32)
    hidden_part = s_gate.shape[1]
    grad_s_gate = shadow_sums[:, :hidden_part].astype(jnp.bfloat16)
    grad_s_up = shadow_sums[:, hidden_part : 2 * hidden_part].astype(jnp.bfloat16)
    grad_s_down = shadow_sums[:, 2 * hidden_part :].T.astype(jnp.bfloat16)
    back_rows = lax.all_to_all(
        partial_out.reshape(ep_count, -1, width), "ep", split_axis=0, concat_axis=0, tiled=True
    ).reshape(-1, width)
    term = weigh_rows(weighting.T, back_rows)
    term = term + shadow_weight[:, None] * shadow_out.astype(jnp.float32)
    mixed = lax.psum_scatter(term.astype(jnp.bfloat16), "tp", scatter_dimension=1, tiled=True)
    return (mixed, grad_gate, grad_up, grad_down, grad_s_gate, grad_s_up, grad_s_down)


ANY = pl.BlockSpec(memory_space=pl.ANY)
VMEM_LIMIT = 60 * 1024 * 1024
SHORT = pl.CostEstimate(flops=1, bytes_accessed=1, transcendentals=0)


def swap_pairs(count, bit):
    return [(i, i ^ bit) for i in range(count)]


def dot32(left, right):
    return jnp.dot(left, right, preferred_element_type=jnp.float32)


def contract_last(left, right):
    return lax.dot_general(
        left, right, (((1,), (1,)), ((), ())), preferred_element_type=jnp.float32
    )


def shape_of(*dims, dtype=jnp.bfloat16):
    return jax.ShapeDtypeStruct(dims, dtype)


def after(arrays, *earlier):
    def nothing(*refs):
        del refs

    count = len(arrays)
    return pl.pallas_call(
        nothing,
        out_shape=[jax.ShapeDtypeStruct(a.shape, a.dtype) for a in arrays],
        in_specs=[ANY] * (count + len(earlier)),
        out_specs=[ANY] * count,
        input_output_aliases={i: i for i in range(count)},
        compiler_params=pltpu.CompilerParams(vmem_limit_bytes=VMEM_LIMIT),
        cost_estimate=SHORT,
        name="after",
    )(*arrays, *earlier)


def kernel_call(body, grid, in_specs, out_specs, out_shape, operands, scratch, name, column=None, earlier=()):
    count = len(operands)

    def run(column_ref, *refs):
        del column_ref
        body(*refs[:count], *refs[count + len(earlier) :])

    column = jnp.zeros((1,), jnp.int32) if column is None else column.reshape(1).astype(jnp.int32)
    return pl.pallas_call(
        run,
        out_shape=out_shape,
        grid_spec=pltpu.PrefetchScalarGridSpec(
            num_scalar_prefetch=1,
            grid=grid,
            in_specs=list(in_specs) + [ANY] * len(earlier),
            out_specs=out_specs,
            scratch_shapes=scratch,
        ),
        compiler_params=pltpu.CompilerParams(vmem_limit_bytes=VMEM_LIMIT),
        cost_estimate=SHORT,
        name=name,
    )(column, *operands, *earlier)


def whole(array):
    return pl.BlockSpec(array.shape, lambda *_: (0,) * len(array.shape))


def join_plane(column, *pieces, earlier=()):
    rows, quarter = pieces[0].shape
    count, halves = 4, len(pieces) - 3
    chunk = rows // 4
    per = 4 // halves

    def body(column_ref, *refs):
        out = refs[-1]
        for own_column in range(count):
            for j, from_diagonal in enumerate(refs[3 : 3 + halves]):

                @pl.when((column_ref[0] == own_column) & (pl.program_id(0) // per == j))
                def _(from_diagonal=from_diagonal, own_column=own_column):
                    for bit, source in enumerate(refs[:3] + (from_diagonal,)):
                        place = own_column ^ bit
                        out[:, place * quarter : (place + 1) * quarter] = source[...]

    def diagonal_spec(j):
        return pl.BlockSpec((chunk, quarter), lambda i, *_: (jnp.clip(i - j * per, 0, per - 1), 0))

    return pl.pallas_call(
        body,
        out_shape=shape_of(rows, count * quarter),
        grid_spec=pltpu.PrefetchScalarGridSpec(
            num_scalar_prefetch=1,
            grid=(4,),
            in_specs=[pl.BlockSpec((chunk, quarter), lambda i, *_: (i, 0))] * 3
            + [diagonal_spec(j) for j in range(halves)]
            + [ANY] * len(earlier),
            out_specs=pl.BlockSpec((chunk, count * quarter), lambda i, *_: (i, 0)),
        ),
        compiler_params=pltpu.CompilerParams(vmem_limit_bytes=VMEM_LIMIT),
        cost_estimate=SHORT,
        name="join_plane",
    )(column.reshape(1).astype(jnp.int32), *pieces, *earlier)


def stack_pieces(pieces, earlier=()):
    rows, columns = pieces[0].shape
    count = len(pieces)

    def body(*refs):
        for i, ref in enumerate(refs[:count]):

            @pl.when(pl.program_id(0) == i)
            def _():
                refs[-1][...] = ref[...]

    return pl.pallas_call(
        body,
        out_shape=shape_of(count * rows, columns),
        grid=(count,),
        in_specs=[pl.BlockSpec((rows, columns), lambda i: (0, 0))] * count + [ANY] * len(earlier),
        out_specs=pl.BlockSpec((rows, columns), lambda i: (i, 0)),
        compiler_params=pltpu.CompilerParams(vmem_limit_bytes=VMEM_LIMIT),
        cost_estimate=SHORT,
        name="stack_pieces",
    )(*pieces, *earlier)


def on_piece(chip_ref, refs, use):
    step = pl.program_id(0)
    shift = chip_ref[0] ^ (step // 2)
    for i, ref in enumerate(refs):
        for core in range(2):

            @pl.when((shift == i) & (lax.rem(step, 2) == core))
            def _(ref=ref, core=core):
                use(ref.at[0, core])


def lay_out_shadow(pieces, down, units, chip, earlier=()):
    count = len(pieces)
    ep_count = 2 * count
    block_width = pieces[0].shape[3]
    apart = units + -units % 128
    all_units, width = down.shape

    def body(chip_ref, *refs):
        shadow_ref, out = refs[-2:]

        def use(ref):
            shadow_ref[...] = jnp.zeros_like(shadow_ref)
            shadow_ref[:units, :] = ref[:units, :]
            shadow_ref[apart : apart + units, :] = ref[units : 2 * units, :]
            out[units:, :] = jnp.zeros((apart - units, block_width), jnp.bfloat16)
            out[:units, :] = ref[2 * units : 3 * units, :]

        on_piece(chip_ref, refs[:count], use)

    return pl.pallas_call(
        body,
        out_shape=[shape_of(2 * apart, width), shape_of(all_units, width)],
        grid_spec=pltpu.PrefetchScalarGridSpec(
            num_scalar_prefetch=1,
            grid=(ep_count,),
            in_specs=[whole(p) for p in pieces] + [ANY] * (1 + len(earlier)),
            out_specs=[
                pl.BlockSpec((2 * apart, block_width), lambda e, *_: (0, e)),
                pl.BlockSpec((apart, block_width), lambda e, *_: (all_units // apart - 1, e)),
            ],
        ),
        input_output_aliases={1 + count: 1},
        compiler_params=pltpu.CompilerParams(vmem_limit_bytes=VMEM_LIMIT),
        cost_estimate=SHORT,
        name="lay_out_shadow",
    )(chip.reshape(1).astype(jnp.int32), *pieces, down, *earlier)


def lay_out_grads(pieces, units, chip, earlier=()):
    count = len(pieces)
    ep_count = 2 * count
    block_width = pieces[0].shape[3]
    hidden = ep_count * units

    def body(chip_ref, *refs):
        gate_ref, up_ref, down_ref, gate_t, up_t = refs[-5:]
        place = pl.ds(pl.multiple_of(pl.program_id(0) * units, 16), units)

        def use(ref):
            gate_t[place, :] = ref[:units, :]
            up_t[place, :] = ref[units : 2 * units, :]
            down_ref[place, :] = ref[2 * units :, :]

        on_piece(chip_ref, refs[:count], use)

        @pl.when(pl.program_id(0) == ep_count - 1)
        def _():
            gate_ref[...] = gate_t[...].T
            up_ref[...] = up_t[...].T

    return pl.pallas_call(
        body,
        out_shape=[shape_of(block_width, hidden), shape_of(block_width, hidden), shape_of(hidden, block_width)],
        grid_spec=pltpu.PrefetchScalarGridSpec(
            num_scalar_prefetch=1,
            grid=(ep_count,),
            in_specs=[whole(p) for p in pieces] + [ANY] * len(earlier),
            out_specs=[pl.BlockSpec((block_width, hidden), lambda *_: (0, 0))] * 2
            + [pl.BlockSpec((hidden, block_width), lambda *_: (0, 0))],
            scratch_shapes=[pltpu.VMEM((hidden, block_width), jnp.bfloat16)] * 2,
        ),
        compiler_params=pltpu.CompilerParams(vmem_limit_bytes=VMEM_LIMIT),
        cost_estimate=SHORT,
        name="lay_out_grads",
    )(chip.reshape(1).astype(jnp.int32), *pieces, *earlier)


def row_specs(groups, tile):
    def spec(index, rows):
        return pl.BlockSpec((rows, tile), lambda k, *_: (index, k))

    return [spec(index, rows) for _, index, rows in groups]


def apply_gate(pre_gate, pre_up):
    sigmoid_gate = jax.nn.sigmoid(pre_gate)
    activated = pre_gate * sigmoid_gate
    hidden = (activated * pre_up).astype(jnp.bfloat16)
    return hidden, pre_up * sigmoid_gate * (1.0 + pre_gate * (1.0 - sigmoid_gate)), activated


def clear_first(acc):
    @pl.when(pl.program_id(0) == 0)
    def _():
        acc[...] = jnp.zeros_like(acc)


def rows_operand(refs, groups, held):
    if len(groups) == 1:
        return refs[0][...]
    return stage_rows(refs, groups, held)


def forward_rows(groups, w_both, tile, transposed=False, earlier=()):
    rows = sum(g[2] for g in groups)
    if transposed:
        units, width = w_both.shape[0] // 2, w_both.shape[1]
        tile_spec = pl.BlockSpec((2 * units, tile), lambda k, *_: (0, k))
    else:
        width, units = w_both.shape[0], w_both.shape[1] // 2
        tile_spec = pl.BlockSpec((tile, 2 * units), lambda k, *_: (k, 0))
    steps = width // tile

    def body(*refs):
        n = len(groups)
        both_ref, hidden_ref, slope_ref, act_ref, acc, held = refs[n:]
        clear_first(acc)
        operand = rows_operand(refs[:n], groups, held)
        acc[...] += contract_last(operand, both_ref[...]) if transposed else dot32(operand, both_ref[...])

        @pl.when(pl.program_id(0) == steps - 1)
        def _():
            chunk = 128

            @pl.loop(0, rows // chunk)
            def _(i):
                part = pl.ds(pl.multiple_of(i * chunk, chunk), chunk)
                hidden, slope, act = apply_gate(acc[part, :units], acc[part, units:])
                hidden_ref[part, :] = hidden
                slope_ref[part, :] = slope.astype(jnp.bfloat16)
                act_ref[part, :] = act.astype(jnp.bfloat16)

    out_spec = pl.BlockSpec((rows, units), lambda *_: (0, 0))
    return kernel_call(
        body,
        (steps,),
        row_specs(groups, tile) + [tile_spec],
        [out_spec] * 3,
        [shape_of(rows, units)] * 3,
        [g[0] for g in groups] + [w_both],
        [pltpu.VMEM((rows, 2 * units), jnp.float32), pltpu.VMEM((rows, tile), jnp.bfloat16)],
        "forward_rows",
        earlier=earlier,
    )


def weigh_hidden(hidden_near, hidden_far, hidden_s, pieces, first_row, slot_rows, core, earlier=()):
    count = len(pieces)
    rows, units_s = hidden_s.shape
    units = hidden_near.shape[1]
    slots = [(s, 0) for s in list(range(1, count)) + [0]] + [(s, 1) for s in range(count)]

    def body(core_ref, *refs):
        near_ref, far_ref, s_ref, *piece_refs = refs[: 3 + count]
        out, w_ref, w_s_ref = refs[-3:]
        near, far = 0, 0
        for i, (slot, other) in enumerate(slots):
            part = pl.ds(i * slot_rows, slot_rows)
            table = piece_refs[slot][0, core_ref[0] ^ other, first_row : first_row + 16, :][:1].astype(jnp.float32)

            def column(j):
                both = table[:, j * slot_rows : (j + 1) * slot_rows]
                both = both + table[:, (j + 2) * slot_rows : (j + 3) * slot_rows]
                return jnp.broadcast_to(both, (slot_rows, slot_rows)).T[:, :1]

            weight, weight_s = column(0), column(1)
            w_ref[part, :] = weight
            w_s_ref[part, :] = weight_s
            if slot == 0:
                hidden = near_ref[near : near + slot_rows, :]
                near += slot_rows
            else:
                hidden = far_ref[far : far + slot_rows, :]
                far += slot_rows
            out[part, :units] = (hidden.astype(jnp.float32) * weight).astype(jnp.bfloat16)
            out[part, units:] = (s_ref[part, :].astype(jnp.float32) * weight_s).astype(jnp.bfloat16)

    return pl.pallas_call(
        body,
        out_shape=[
            shape_of(rows, units + units_s),
            shape_of(rows, 1, dtype=jnp.float32),
            shape_of(rows, 1, dtype=jnp.float32),
        ],
        grid_spec=pltpu.PrefetchScalarGridSpec(
            num_scalar_prefetch=1,
            grid=(1,),
            in_specs=[whole(a) for a in (hidden_near, hidden_far, hidden_s, *pieces)] + [ANY] * len(earlier),
            out_specs=[
                pl.BlockSpec((rows, units + units_s), lambda *_: (0, 0)),
                pl.BlockSpec((rows, 1), lambda *_: (0, 0)),
                pl.BlockSpec((rows, 1), lambda *_: (0, 0)),
            ],
        ),
        compiler_params=pltpu.CompilerParams(vmem_limit_bytes=VMEM_LIMIT),
        cost_estimate=SHORT,
        name="weigh_hidden",
    )(core.reshape(1).astype(jnp.int32), hidden_near, hidden_far, hidden_s, *pieces, *earlier)


def output_other(weighted, down, column, parts, slot_rows, quarter, earlier=()):
    rows, units = weighted.shape
    count = rows // 2 // parts

    def body(weighted_ref, down_ref, *outs):
        value = dot32(weighted_ref[...], down_ref[...]).astype(jnp.bfloat16)
        for i, out in enumerate(outs):
            first, last = slot_rows + i * count, slot_rows + (i + 1) * count
            kept = min(last, rows // 2) - first
            out[:kept, :] = value[first : first + kept]
            if kept < count:
                out[kept:, :] = value[: count - kept]

    return kernel_call(
        body,
        (4,),
        [
            pl.BlockSpec((rows // 2, units), lambda *_: (1, 0)),
            pl.BlockSpec((units, quarter), lambda q, column_ref: (0, column_ref[0] ^ q)),
        ],
        [pl.BlockSpec((count, quarter), lambda q, *_: (0, q))] * parts,
        [shape_of(count, 4 * quarter)] * parts,
        [weighted, down],
        [],
        "output_other",
        column=column,
        earlier=earlier,
    )


def output_own(weighted, got, down, column, quarter, earlier=()):
    count, units = got[0].shape[0], weighted.shape[1]
    parts = len(got)

    def body(weighted_ref, down_ref, *refs):
        product = dot32(weighted_ref[...], down_ref[...])
        for i in range(parts):
            value = product[i * count : (i + 1) * count] + refs[i][...].astype(jnp.float32)
            for j, out in enumerate(refs[parts + 4 * i : parts + 4 * i + 4]):

                @pl.when(pl.program_id(0) == 3 - j)
                def _(out=out, value=value):
                    out[...] = value.astype(out.dtype)

    full = pl.BlockSpec((count, quarter), lambda *_: (0, 0))
    out = kernel_call(
        body,
        (4,),
        [
            pl.BlockSpec((parts * count, units), lambda *_: (0, 0)),
            pl.BlockSpec((units, quarter), lambda q, column_ref: (0, column_ref[0] ^ 3 ^ q)),
        ]
        + [pl.BlockSpec((count, quarter), lambda q, *_: (0, 3 - q))] * parts,
        [full] * (4 * parts),
        ([shape_of(count, quarter, dtype=jnp.float32)] + [shape_of(count, quarter)] * 3) * parts,
        [weighted, down] + list(got),
        [],
        "output_own",
        column=column,
        earlier=earlier,
    )
    return [out[4 * i : 4 * i + 4] for i in range(parts)]


def backward_rows(groups, down, parts, per_row, first_row, tile, earlier=()):
    slope_s, act_s, w_rows, w_shadow = per_row
    rows = sum(g[2] for g in groups)
    units_all, width = down.shape
    units_s = slope_s.shape[1]
    units = units_all - units_s
    steps = width // tile
    arrays = list({id(a): a for part in parts for a in part[:2]}.values())
    places = [[next(i for i, a in enumerate(arrays) if a is b) for b in part[:2]] for part in parts]

    def body(*refs):
        n, m = len(groups), len(arrays)
        down_ref = refs[n]
        array_refs = refs[n + 1 : n + 1 + m]
        slope_s_ref, act_s_ref, w_ref, w_s_ref, pre_ref, pre_s_ref, acc, held = refs[n + 1 + m :]
        clear_first(acc)
        acc[...] += contract_last(rows_operand(refs[:n], groups, held), down_ref[...])

        @pl.when(pl.program_id(0) == steps - 1)
        def _():
            chunk = 128
            start = 0
            for (_, _, count), (_, _, first), (slope_at, act_at) in zip(groups, parts, places):

                @pl.loop(0, count // chunk)
                def _(i, start=start, first=first, slope_ref=array_refs[slope_at], act_ref=array_refs[act_at]):
                    source = pl.ds(pl.multiple_of(first + i * chunk, chunk), chunk)
                    part = pl.ds(pl.multiple_of(start + i * chunk, chunk), chunk)
                    whole_part = pl.ds(pl.multiple_of(first_row + start + i * chunk, chunk), chunk)
                    grad = acc[part, :units] * w_ref[whole_part, :]
                    pre_ref[part, :units] = (grad * slope_ref[source, :]).astype(jnp.bfloat16)
                    pre_ref[part, units:] = (grad * act_ref[source, :]).astype(jnp.bfloat16)
                    grad = acc[part, units:] * w_s_ref[whole_part, :]
                    pre_s_ref[part, :units_s] = (grad * slope_s_ref[whole_part, :]).astype(jnp.bfloat16)
                    pre_s_ref[part, units_s:] = (grad * act_s_ref[whole_part, :]).astype(jnp.bfloat16)

                start += count

    extra = arrays + [slope_s, act_s, w_rows, w_shadow]
    return kernel_call(
        body,
        (steps,),
        row_specs(groups, tile) + [pl.BlockSpec((units_all, tile), lambda k, *_: (0, k))] + [whole(a) for a in extra],
        [pl.BlockSpec((rows, 2 * units), lambda *_: (0, 0)), pl.BlockSpec((rows, 2 * units_s), lambda *_: (0, 0))],
        [shape_of(rows, 2 * units), shape_of(rows, 2 * units_s)],
        [g[0] for g in groups] + [down] + extra,
        [pltpu.VMEM((rows, units_all), jnp.float32), pltpu.VMEM((rows, tile), jnp.bfloat16)],
        "backward_rows",
        earlier=earlier,
    )


def stage_rows(refs, groups, held):
    start = 0
    for ref, (_, _, count) in zip(refs, groups):
        held[pl.ds(start, count), :] = ref[...]
        start += count
    return held[...]


def shadow_grads(x_groups, dy_groups, pre_s, weighted, units, block, tile, earlier=()):
    rows, wide = weighted.shape[0], pre_s[0].shape[1]
    apart = wide // 2
    width = x_groups[0][0].shape[1]
    m = len(pre_s)

    def body(*refs):
        n = len(x_groups)
        pre_refs = refs[2 * n : 2 * n + m]
        hidden_ref, out, held, pre_t, hidden_t = refs[2 * n + m :]

        @pl.when(pl.program_id(0) == 0)
        def _():
            start = 0
            for ref in pre_refs:
                pre_t[:, start : start + ref.shape[0]] = ref[...].T
                start += ref.shape[0]
            hidden_t[...] = hidden_ref[...].T

        value = dot32(pre_t[...], stage_rows(refs[:n], x_groups, held)).astype(jnp.bfloat16)
        for i in range(tile // block):
            part = slice(i * block, (i + 1) * block)
            out[i, :units, :] = value[:units, part]
            out[i, units : 2 * units, :] = value[apart : apart + units, part]
        value = dot32(hidden_t[...], stage_rows(refs[n : 2 * n], dy_groups, held)).astype(jnp.bfloat16)
        for i in range(tile // block):
            out[i, 2 * units :, :] = value[:units, i * block : (i + 1) * block]

    (out,) = kernel_call(
        body,
        (width // tile,),
        row_specs(x_groups, tile)
        + row_specs(dy_groups, tile)
        + [whole(p) for p in pre_s]
        + [pl.BlockSpec((rows, apart), lambda *_: (0, weighted.shape[1] // apart - 1))],
        [pl.BlockSpec((tile // block, 3 * units, block), lambda k, *_: (k, 0, 0))],
        [shape_of(width // block, 3 * units, block)],
        [g[0] for g in x_groups + dy_groups] + list(pre_s) + [weighted],
        [
            pltpu.VMEM((rows, tile), jnp.bfloat16),
            pltpu.VMEM((wide, rows), jnp.bfloat16),
            pltpu.VMEM((apart, rows), jnp.bfloat16),
        ],
        "shadow_grads",
        earlier=earlier,
    )
    return out


def input_grads(groups, pre, tile, earlier=()):
    both = pre[0].shape[1]
    rows = sum(p.shape[0] for p in pre)
    units = both // 2
    width = groups[0][0].shape[1]
    m = len(pre)

    def body(*refs):
        n = len(groups)
        gate_ref, up_ref, held, pre_held = refs[n + m :]

        @pl.when(pl.program_id(0) == 0)
        def _():
            start = 0
            for ref in refs[n : n + m]:
                pre_held[start : start + ref.shape[0], :] = ref[...]
                start += ref.shape[0]

        value = contract_rows(stage_rows(refs[:n], groups, held), pre_held[...])
        gate_ref[...] = value[:, :units].astype(jnp.bfloat16)
        up_ref[...] = value[:, units:].astype(jnp.bfloat16)

    return kernel_call(
        body,
        (width // tile,),
        row_specs(groups, tile) + [whole(p) for p in pre],
        [pl.BlockSpec((tile, units), lambda k, *_: (k, 0))] * 2,
        [shape_of(width, units)] * 2,
        [g[0] for g in groups] + list(pre),
        [pltpu.VMEM((rows, tile), jnp.bfloat16), pltpu.VMEM((rows, both), jnp.bfloat16)],
        "input_grads",
        earlier=earlier,
    )


def down_grad(groups, weighted, units, tile, earlier=()):
    rows = weighted.shape[0]
    width = groups[0][0].shape[1]

    def body(*refs):
        n = len(groups)
        hidden_ref, out, held, hidden_t = refs[n:]

        @pl.when(pl.program_id(0) == 0)
        def _():
            hidden_t[...] = hidden_ref[...].T

        out[...] = dot32(hidden_t[...], stage_rows(refs[:n], groups, held)).astype(jnp.bfloat16)

    (out,) = kernel_call(
        body,
        (width // tile,),
        row_specs(groups, tile) + [pl.BlockSpec((rows, units), lambda *_: (0, 0))],
        [pl.BlockSpec((units, tile), lambda k, *_: (0, k))],
        [shape_of(units, width)],
        [g[0] for g in groups] + [weighted],
        [pltpu.VMEM((rows, tile), jnp.bfloat16), pltpu.VMEM((units, rows), jnp.bfloat16)],
        "down_grad",
        earlier=earlier,
    )
    return out


def send_along_z(own):
    ep_count = lax.axis_size("ep")
    return [lax.ppermute(own, "ep", swap_pairs(ep_count, 2 * s)) for s in range(1, ep_count // 2)]


def swap_cores(block):
    return lax.ppermute(block, "ep", swap_pairs(lax.axis_size("ep"), 1))


def send_plane(*pieces):
    pieces = pieces * 3 if len(pieces) == 1 else pieces
    return [lax.ppermute(p, "tp", swap_pairs(lax.axis_size("tp"), bit)) for p, bit in zip(pieces, (1, 2, 3))]


def send_diagonal(from_x, from_y):
    along, across = [swap_pairs(lax.axis_size("tp"), bit) for bit in (1, 2)]
    half = from_x.shape[0] // 2
    return [lax.ppermute(from_x[:half], "tp", across), lax.ppermute(from_y[half:], "tp", along)]


def exchange_cores(blocks, cuts=1):
    ep_count, core = lax.axis_size("ep"), lax.axis_index("ep") % 2
    pairs = blocks.reshape(ep_count // 2, 2, *blocks.shape[1:])
    kept = jnp.where(core == 0, pairs[:, 0], pairs[:, 1])
    given = jnp.where(core == 0, pairs[:, 1], pairs[:, 0])
    return kept, [swap_cores(part) for part in jnp.split(given, cuts)]


def chip_pieces(kept, taken):
    ep_count, me = lax.axis_size("ep"), lax.axis_index("ep")
    chips, chip, core = ep_count // 2, me // 2, me % 2
    taken = jnp.concatenate(taken, axis=0)
    both = jnp.stack([jnp.where(core == 0, kept, taken), jnp.where(core == 0, taken, kept)], axis=1)
    return [lax.dynamic_index_in_dim(both, chip ^ shift, 0) for shift in range(chips)]


def send_piece(piece, shift):
    return lax.ppermute(piece, "ep", swap_pairs(lax.axis_size("ep"), 2 * shift))


def dense_shards(
    tokens,
    cotangent,
    expert_ids,
    gate_weights,
    shadow_mask,
    w_gate,
    w_up,
    w_down,
    s_gate,
    s_up,
    s_down,
):
    ep_count, tp_count = lax.axis_size("ep"), lax.axis_size("tp")
    ep_index, tp_index = lax.axis_index("ep"), lax.axis_index("tp")
    tok_count, top_count = expert_ids.shape
    quarter = tokens.shape[1]
    width = quarter * tp_count
    hidden_part = w_gate.shape[2]
    shadow_part = hidden_part // ep_count
    block_width = s_gate.shape[0]
    steps = ep_count // 2
    later = (steps - 1) * tok_count
    tile = width // 8
    along, across = swap_pairs(tp_count, 1), swap_pairs(tp_count, 2)

    picked = expert_ids[None, :, :] == jnp.arange(ep_count, dtype=jnp.int32)[:, None, None]
    table = jnp.sum(jnp.where(picked, gate_weights[None, :, :top_count], 0.0), axis=2)
    shadow_weight = gate_weights[:, top_count] * shadow_mask.astype(jnp.float32)
    table = jnp.concatenate([table, jnp.broadcast_to(shadow_weight[None], table.shape)], axis=1)
    table = jnp.concatenate(split_parts(table), axis=1)
    table = jnp.pad(table[:, None, :], ((0, 0), (0, 15), (0, block_width - table.shape[1])))
    shadow_blocks = jnp.concatenate(
        [
            s_gate.T.reshape(ep_count, shadow_part, block_width),
            s_up.T.reshape(ep_count, shadow_part, block_width),
            s_down.reshape(ep_count, shadow_part, block_width),
            table,
        ],
        axis=1,
    )

    x_z = send_along_z(tokens)
    near = stack_pieces([tokens, cotangent])
    near_x, near_y = send_plane(near, near)
    near_x, near_y = after([near_x, near_y], x_z[0])
    near_d = send_diagonal(near_x, near_y)
    w_both = jnp.concatenate([w_gate[0], w_up[0]], axis=1)
    fenced = after([*near_d, *x_z], w_both, shadow_blocks)
    near_d, x_z = fenced[:2], fenced[2:]

    x_piece = stack_pieces(x_z)
    x_plane = send_plane(x_piece, x_piece)
    dy_z = send_along_z(cotangent)
    near_own = join_plane(tp_index, near, near_x, near_y, *near_d)
    near_other = swap_cores(near_own)
    x_near = [(near_own, 0, tok_count), (near_other, 0, tok_count)]
    hidden_near, slope_near, act_near = forward_rows(x_near, w_both, 2 * tile)
    spare_rows = -shadow_part % 128 + shadow_part
    down = jnp.pad(w_down[0], ((0, spare_rows), (0, 0)))
    (shadow_blocks,) = after([shadow_blocks], x_z[0])
    shadow_kept, shadow_taken = exchange_cores(shadow_blocks)
    shadow_pieces = chip_pieces(shadow_kept, shadow_taken)
    shadow_pieces[-1] = send_piece(shadow_pieces[-1], steps - 1)
    fenced = after([*x_plane, down, *shadow_pieces[1:]], *dy_z[:2], hidden_near)
    x_plane, down, shadow_pieces[1:] = fenced[:2], fenced[2], fenced[3:]
    x_plane = [*x_plane, *send_diagonal(*x_plane)]
    fenced = after([*x_plane[2:], *shadow_pieces[1:], *dy_z])
    x_plane[2:], shadow_pieces[1:], dy_z = fenced[:2], fenced[2 : 1 + steps], fenced[1 + steps :]

    dy_piece = stack_pieces(dy_z)
    dy_plane = send_plane(dy_piece)
    for shift in range(1, steps - 1):
        shadow_pieces[shift] = send_piece(shadow_pieces[shift], shift)
    x_own = join_plane(tp_index, x_piece, *x_plane, earlier=[dy_piece])
    x_other = swap_cores(x_own)
    x_far = [(x_own, 0, later), (x_other, 0, later)]
    x_groups = [x_far[0], x_near[0], x_near[1], x_far[1]]
    hidden_far, slope_far, act_far = forward_rows(x_far, w_both, 2 * tile)
    chip = ep_index // 2
    shadow_in, down = lay_out_shadow(shadow_pieces, down, shadow_part, chip, earlier=[hidden_far])
    hidden_s, slope_s, act_s = forward_rows(x_groups, shadow_in, 2 * tile, transposed=True)

    weighted, w_rows, w_shadow = weigh_hidden(
        hidden_near, hidden_far, hidden_s, shadow_pieces, 3 * shadow_part, tok_count, ep_index % 2
    )

    parts = 2 if steps % 2 == 0 else 1
    sent = output_other(weighted, down, tp_index, parts, tok_count, quarter)
    got = [swap_cores(array) for array in sent]
    dy_plane = after(dy_plane, *sent)

    dy_own = join_plane(tp_index, dy_piece, *dy_plane)
    dy_other = swap_cores(dy_own)
    dy_groups = [(dy_own, 0, later), (near_own, 1, tok_count), (near_other, 1, tok_count), (dy_other, 0, later)]
    segments = [
        (slope_far, act_far, 0),
        (slope_near, act_near, 0),
        (slope_near, act_near, tok_count),
        (slope_far, act_far, later),
    ]
    per_row = (slope_s, act_s, w_rows, w_shadow)
    pre_first, pre_s_first = backward_rows(dy_groups[:3], down, segments[:3], per_row, 0, 2 * tile)
    owns = output_own(weighted, got, down, tp_index, quarter, earlier=[pre_first])
    sums = [send_plane(*own[1:]) for own in owns]
    first_rows = sum(g[2] for g in dy_groups[:3])
    pre_last, pre_s_last = backward_rows(
        dy_groups[3:], down, segments[3:], per_row, first_rows, 2 * tile, earlier=[own[1] for own in owns]
    )
    pre, pre_s = [pre_first, pre_last], [pre_s_first, pre_s_last]
    grad_s = shadow_grads(x_groups, dy_groups, pre_s, weighted, shadow_part, block_width, 2 * tile)
    grad_pieces = chip_pieces(*exchange_cores(grad_s))

    def slot_rows(i):
        part = slice(i % (steps // parts) * tok_count, (i % (steps // parts) + 1) * tok_count)
        total = owns[i * parts // steps][0][part]
        for array in sums[i * parts // steps]:
            total = total + array[part].astype(jnp.float32)
        return total

    def send_rows(piece, i):
        return lax.ppermute(piece, "ep", swap_pairs(ep_count, 2 * (i + 1)))

    early = steps // parts if parts > 1 else 0
    sums[0] = after(sums[0], grad_s)
    rows = [slot_rows(i).astype(jnp.bfloat16) for i in range(early)]
    grad_down = down_grad(dy_groups, weighted, hidden_part, 2 * tile, earlier=[*rows, grad_pieces[0]])
    rows = [send_rows(piece, i) for i, piece in enumerate(rows)]
    fenced = after([*rows, *grad_pieces[1:]], grad_down)
    rows, grad_pieces[1:] = list(fenced[:early]), fenced[early:]
    grad_gate, grad_up = input_grads(x_groups, pre, 2 * tile, earlier=[grad_pieces[1]])
    for shift in range(1, steps - 1):
        grad_pieces[shift] = send_piece(grad_pieces[shift], shift)
    fenced = after([*sums[-1], *grad_pieces[1:]], grad_gate)
    sums[-1], grad_pieces[1:] = fenced[:3], fenced[3:]
    grad_pieces[-1] = send_piece(grad_pieces[-1], steps - 1)
    rows += [send_rows(slot_rows(i).astype(jnp.bfloat16), i) for i in range(early, steps - 1)]
    total = slot_rows(steps - 1)
    for piece in rows:
        total = total + piece.astype(jnp.float32)
    mixed = total.astype(jnp.bfloat16)

    grads_s = lay_out_grads(grad_pieces, shadow_part, chip)
    return (mixed, grad_gate[None], grad_up[None], grad_down[None], *grads_s)


def shards(tokens, cotangent, expert_ids, *others):
    tp_count, ep_count = lax.axis_size("tp"), lax.axis_size("ep")
    tok_count, top_count = expert_ids.shape
    rows = (5 * tok_count * top_count) // 4
    chips = ep_count // 2
    fits = tp_count == 4 and ep_count == 2 * chips and chips & (chips - 1) == 0 and tok_count % 128 == 0
    dense = fits and ep_count * tok_count <= 3 * rows
    return (dense_shards if dense else routed_shards)(tokens, cotangent, expert_ids, *others)


def solution(mesh):
    return jax.shard_map(
        shards,
        mesh=mesh,
        in_specs=(
            P("ep", "tp"),
            P("ep", "tp"),
            P("ep", None),
            P("ep", None),
            P("ep"),
            P("ep", None, "tp"),
            P("ep", None, "tp"),
            P("ep", "tp", None),
            P("ep", "tp"),
            P("ep", "tp"),
            P("tp", "ep"),
        ),
        out_specs=(
            P("ep", "tp"),
            P("ep", None, "tp"),
            P("ep", None, "tp"),
            P("ep", "tp", None),
            P("ep", "tp"),
            P("ep", "tp"),
            P("tp", "ep"),
        ),
        check_vma=False,
    )
```
